32 devices in a mesh: dp: 16 (over z, x, core), tensor: 2 (over y).
Axes of the slice: x: 2, y: 2, z: 4, core: 2. Of those that a mesh axis runs over, the one named last changes fastest.
Arguments:
- tokens: bfloat16 [2, 16384, 1024], P(None, ('dp', 'tensor')), may hold values from -6 to 6
- cotangent: bfloat16 [2, 16384, 1024], P(None, ('dp', 'tensor')), may hold values from -6 to 6
- piece_starts: int32 [2, 16, 2], P(None, 'dp'), may hold values from 0 to 768, as said below
- w_qkv: float32 [3, 1024, 1024], P(None, 'dp', 'tensor'), may hold values from -0.1875 to 0.1875
- w_out: float32 [1024, 1024], P('tensor', 'dp'), may hold values from -0.5 to 0.5
- w_up: float32 [1024, 4096], P('dp', 'tensor'), as said below
- w_down: float32 [4096, 1024], P('tensor', 'dp'), may hold values from -0.09375 to 0.09375
- vectors: float32 [12, 1024], replicated, as said below
- m_qkv: float32 [3, 1024, 1024], P(None, 'dp', 'tensor'), may hold values from -112 to 112
- m_out: float32 [1024, 1024], P('tensor', 'dp'), may hold values from -512 to 512
- m_up: float32 [1024, 4096], P('dp', 'tensor'), may hold values from -256 to 256
- m_down: float32 [4096, 1024], P('tensor', 'dp'), may hold values from -512 to 512
- m_vec: float32 [12, 1024], replicated, may hold values from -512 to 512
Outputs:
- block_output: bfloat16 [2, 16384, 1024], P(None, ('dp', 'tensor'))
- grad_tokens: float32 [2, 16384, 1024], P(None, ('dp', 'tensor'))
- grad_qkv: float32 [3, 1024, 1024], P(None, 'dp', 'tensor')
- grad_out: float32 [1024, 1024], P('tensor', 'dp')
- grad_up: float32 [1024, 4096], P('dp', 'tensor')
- grad_down: float32 [4096, 1024], P('tensor', 'dp')
- grad_vec: float32 [12, 1024], replicated
- moment_qkv: float32 [3, 1024, 1024], P(None, 'dp', 'tensor')
- moment_out: float32 [1024, 1024], P('tensor', 'dp')
- moment_up: float32 [1024, 4096], P('dp', 'tensor')
- moment_down: float32 [4096, 1024], P('tensor', 'dp')
- moment_vec: float32 [12, 1024], replicated
- new_qkv: float32 [3, 1024, 1024], P(None, 'dp', 'tensor')
- new_out: float32 [1024, 1024], P('tensor', 'dp')
- new_up: float32 [1024, 4096], P('dp', 'tensor')
- new_down: float32 [4096, 1024], P('tensor', 'dp')
- new_vec: float32 [12, 1024], replicated
The draws below stay inside these ranges and needn't reach their ends.
Inputs may be any that keep to these rules, and one draw needn't show every extreme that they name: `piece_starts`: in each sequence piece k starts within [k * 512, (k + 1) * 512 - 256], so pieces lie inside the sequence and never intersect. `vectors`: rows 0 and 5 are gains near one. `w_up`: entries are at most six times 1024 to the power minus one half in magnitude.
All inputs are finite; a program needn't handle non-finite values.
Results may differ from the reference program's by a relative error of at most 0.019.
Values may be sent and summed in bfloat16 or wider, within the bound.
A program may use at most 320 MiB of HBM per device.

```python
import math
import jax
import jax.numpy as jnp
from jax import lax

D = 1024
H = 16
HD = 64
FF = 4096
LEN = 1024
PIECE = 256
NPIECE = 2
MB = 2
NS_ITERS = 3
NSEQ = 16
TOKENS = 16384


def draw_piece_starts(key, part):
    room_size = LEN // NPIECE - PIECE + 1
    offsets = jax.random.randint(key, (MB, NSEQ, NPIECE), 0, room_size, dtype=jnp.int32)
    offsets = offsets.at[0, 0, 0].set(0)
    offsets = offsets.at[0, 0, NPIECE - 1].set(room_size - 1)
    base_starts = jnp.arange(NPIECE, dtype=jnp.int32) * (LEN // NPIECE)
    return (offsets + base_starts[None, None, :]).astype(jnp.int32)


def draw_vectors(key, part):
    first_key = jax.random.fold_in(key, 11)
    second_key = jax.random.fold_in(key, 23)
    noise = 0.3 * jax.random.normal(first_key, (12, D), jnp.float32)
    gains = 1.0 + 0.25 * jax.random.normal(second_key, (12, D), jnp.float32)
    row_ids = jnp.arange(12, dtype=jnp.int32)[:, None]
    gain_rows = (row_ids == 0) | (row_ids == 5)
    return jnp.where(gain_rows, gains, noise).astype(jnp.float32)


def draw_w_up(key, part):
    first_key = jax.random.fold_in(key, 31)
    entries = jnp.clip(jax.random.normal(first_key, (D, FF), jnp.float32), -6.0, 6.0)
    return (entries * (1.0 / math.sqrt(D))).astype(jnp.float32)


def shard_levels(stream_key, extent, cuts, smallest, high):
    def one(position, shards_of):
        draws = jax.random.uniform(jax.random.fold_in(jax.random.fold_in(stream_key, 6), position), (shards_of,), jnp.float32, smallest / len(cuts), high / len(cuts))
        return jnp.repeat(jnp.exp(draws), extent[position] // shards_of).reshape((-1,) + (1,) * (len(extent) - position - 1))

    gain = one(*cuts[0])
    for cut in cuts[1:]:
        gain = gain * one(*cut)
    return gain


def centred(rng, extent, scale, limit, shards=(), kind=jnp.bfloat16):
    array = jax.random.normal(rng, extent, jnp.float32) * scale
    if len(shards) > 0:
        array = shard_levels(rng, extent, shards, -0.22, 0.18) * array
    return jnp.clip(array, min=-limit, max=limit).astype(kind)


def setup_inputs(seed: int = 0) -> dict:
    keys = jax.random.split(jax.random.key(seed), 14)
    return {
        "tokens": centred(keys[0], (MB, TOKENS, D), 1.0, 6.0, ((1, 32),)),
        "cotangent": centred(keys[1], (MB, TOKENS, D), 1.0, 6.0, ((1, 32),)),
        "piece_starts": draw_piece_starts(jax.random.fold_in(keys[13], 71), 0),
        "w_qkv": centred(keys[3], (3, D, D), D ** -0.5, 0.1875, ((1, 16), (2, 2)), jnp.float32),
        "w_out": centred(keys[4], (D, D), (D // 8) ** -0.5, 0.5, ((0, 2), (1, 16)), jnp.float32),
        "w_up": draw_w_up(jax.random.fold_in(keys[13], 71), 0),
        "w_down": centred(keys[6], (FF, D), FF ** -0.5, 0.09375, ((0, 2), (1, 16)), jnp.float32),
        "vectors": draw_vectors(jax.random.fold_in(keys[13], 71), 0),
        "m_qkv": centred(keys[8], (3, D, D), (0.1 * (MB * TOKENS) ** 0.5), 112.0, ((1, 16), (2, 2)), jnp.float32),
        "m_out": centred(keys[9], (D, D), (0.5 * (MB * TOKENS) ** 0.5), 512.0, ((0, 2), (1, 16)), jnp.float32),
        "m_up": centred(keys[10], (D, FF), (0.25 * (MB * TOKENS) ** 0.5), 256.0, ((0, 16), (1, 2)), jnp.float32),
        "m_down": centred(keys[11], (FF, D), (0.5 * (MB * TOKENS) ** 0.5), 512.0, ((0, 2), (1, 16)), jnp.float32),
        "m_vec": centred(keys[12], (12, D), (0.5 * (MB * TOKENS) ** 0.5), 512.0, (), jnp.float32),
    }


NORM_EPSILON = 1e-05
SQUARE_EPSILON = 1e-06
MASKED_SCORE = -1e+30
SCHULZ_FIRST = 3.4445
SCHULZ_SECOND = -4.775
SCHULZ_THIRD = 2.0315
MOMENTUM_DECAY = 0.5
MATRIX_RATE = 0.5
VECTOR_RATE = 0.05

@jax.custom_vjp
def low(v):
    return lax.optimization_barrier(v.astype(jnp.bfloat16)).astype(jnp.float32)

@jax.custom_vjp
def low_back(v):
    return v

def low_keep(v):
    return (low(v), None)

def low_pass(kept, grad):
    return (grad,)

def back_keep(v):
    return (v, None)

def back_low(kept, grad):
    return (low(grad),)
low.defvjp(low_keep, low_pass)
low_back.defvjp(back_keep, back_low)

def product(former, latter):
    return jnp.dot(former, latter, precision=lax.Precision.HIGHEST, preferred_element_type=jnp.float32)

def layer_norm(inputs, gain_row, shift_row):
    average = lax.optimization_barrier(jnp.mean(inputs, axis=-1, keepdims=True))
    centered = inputs - average
    variance = lax.optimization_barrier(jnp.mean(centered * centered, axis=-1, keepdims=True))
    return centered * lax.rsqrt(variance + NORM_EPSILON) * gain_row + shift_row

def score_layout(starts, slopes):
    positions = jnp.arange(LEN, dtype=jnp.int32)
    inside = (positions[None, :] >= starts[:, None]) & (positions[None, :] < starts[:, None] + PIECE)
    labels = jnp.arange(1, NPIECE + 1, dtype=jnp.int32)
    piece_label = lax.optimization_barrier(jnp.sum(jnp.where(inside, labels[:, None], 0), axis=0))
    same_piece = (piece_label[:, None] == piece_label[None, :]) & (piece_label[:, None] > 0)
    visible = (positions[None, :] <= positions[:, None]) | same_piece
    distance = jnp.abs(positions[:, None] - positions[None, :]).astype(jnp.float32)
    penalty = -slopes[:, None, None] * distance[None, :, :]
    return (visible, penalty)

def block(inputs, starts, params):
    w_qkv, w_out, w_up, w_down, vectors = params
    slopes = jnp.exp2(-8.0 * jnp.arange(1, H + 1, dtype=jnp.float32) / H)
    normed = low(layer_norm(inputs, vectors[0], vectors[1]))
    weights_qkv = low(w_qkv)
    queries = low(low_back(product(normed, weights_qkv[0]) + vectors[2]))
    key_rows = low(low_back(product(normed, weights_qkv[1])))
    values = low(low_back(product(normed, weights_qkv[2]) + vectors[3]))
    query_heads = queries.reshape(LEN, H, HD)
    key_heads = key_rows.reshape(LEN, H, HD)
    value_heads = values.reshape(LEN, H, HD)
    visible, penalty = score_layout(starts, slopes)
    scores = jnp.einsum('qhd,khd->hqk', query_heads, key_heads, precision=lax.Precision.HIGHEST) * (1.0 / math.sqrt(HD)) + penalty
    scores = low_back(scores)
    scores = jnp.where(visible[None, :, :], scores, MASKED_SCORE)
    probabilities = low(jax.nn.softmax(scores, axis=-1))
    context = jnp.einsum('hqk,khd->qhd', probabilities, value_heads, precision=lax.Precision.HIGHEST).reshape(LEN, D)
    context = low(low_back(context))
    attended = low_back(product(context, low(w_out)))
    middle = inputs + attended + vectors[4]
    normed_two = low(layer_norm(middle, vectors[5], vectors[6]))
    before = low_back(product(normed_two, low(w_up)) + vectors[7:11].reshape(FF))
    activated = low(jax.nn.gelu(before, approximate=True))
    expanded = low_back(product(activated, low(w_down)))
    return middle + expanded + vectors[11]

def orthogonal(matrix):
    square = jnp.sum(matrix * matrix)
    state = low(matrix * lax.rsqrt(square + SQUARE_EPSILON))
    for sweep_index in range(NS_ITERS):
        gram_matrix = low(product(state.T, state))
        turned = product(state, gram_matrix)
        mixed = low(SCHULZ_SECOND * state + SCHULZ_THIRD * turned)
        state = low(SCHULZ_FIRST * state + product(mixed, gram_matrix))
    return state

def reference(tokens, cotangent, piece_starts, w_qkv, w_out, w_up, w_down, vectors, m_qkv, m_out, m_up, m_down, m_vec):
    seq_count = MB * NSEQ
    token_seqs = tokens.astype(jnp.float32).reshape(seq_count, LEN, D)
    cot_seqs = cotangent.astype(jnp.float32).reshape(seq_count, LEN, D)
    start_seqs = piece_starts.reshape(seq_count, NPIECE)
    params = (w_qkv, w_out, w_up, w_down, vectors)

    def visit(totals, element):
        token_seq, cot_seq, start_seq = element

        def forward(inputs, weights):
            return block(inputs, start_seq, weights)
        result, pullback = jax.vjp(forward, token_seq, params)
        grad_rows, grad_weights = pullback(cot_seq)
        totals = jax.tree.map(lambda former, latter: former + latter, totals, grad_weights)
        return (totals, (result, grad_rows))
    initial = jax.tree.map(jnp.zeros_like, params)
    totals, (results, grad_rows) = lax.scan(visit, initial, (token_seqs, cot_seqs, start_seqs))
    grad_qkv, grad_out, grad_up, grad_down, grad_vec = totals
    block_output = results.reshape(MB, TOKENS, D).astype(jnp.bfloat16)
    grad_tokens = grad_rows.reshape(MB, TOKENS, D)
    moment_qkv = MOMENTUM_DECAY * m_qkv + grad_qkv
    moment_out = MOMENTUM_DECAY * m_out + grad_out
    moment_up = MOMENTUM_DECAY * m_up + grad_up
    moment_down = MOMENTUM_DECAY * m_down + grad_down
    moment_vec = MOMENTUM_DECAY * m_vec + grad_vec
    wide_factor = math.sqrt(FF / D)
    update_qkv = jnp.stack([orthogonal(moment_qkv[0].T).T, orthogonal(moment_qkv[1].T).T, orthogonal(moment_qkv[2].T).T])
    new_qkv = w_qkv - MATRIX_RATE * update_qkv
    new_out = w_out - MATRIX_RATE * orthogonal(moment_out)
    new_up = w_up - MATRIX_RATE * wide_factor * orthogonal(moment_up.T).T
    new_down = w_down - MATRIX_RATE * wide_factor * orthogonal(moment_down)
    new_vec = vectors - VECTOR_RATE * moment_vec * lax.rsqrt(lax.optimization_barrier(jnp.mean(moment_vec * moment_vec, axis=1, keepdims=True)) + SQUARE_EPSILON)
    return (block_output, grad_tokens, grad_qkv, grad_out, grad_up, grad_down, grad_vec, moment_qkv, moment_out, moment_up, moment_down, moment_vec, new_qkv, new_out, new_up, new_down, new_vec)
```

```python
import math

import jax
import jax.numpy as jnp
from jax import lax
from jax.experimental import pallas as pl
from jax.experimental.pallas import tpu as pltpu
from jax.sharding import PartitionSpec as P

D = 1024
H = 16
HD = 64
FF = 4096
LEN = 1024
PIECE = 256
NPIECE = 2
MB = 2
NS_ITERS = 3


NORM_EPSILON = 1e-05
SQUARE_EPSILON = 1e-06
MASKED_SCORE = -1e30
SCHULZ_FIRST = 3.4445
SCHULZ_SECOND = -4.775
SCHULZ_THIRD = 2.0315
MOMENTUM_DECAY = 0.5
MATRIX_RATE = 0.5
VECTOR_RATE = 0.05


def layer_norm(inputs, gain_row, shift_row):
    average = jnp.mean(inputs, axis=-1, keepdims=True)
    centered = inputs - average
    variance = jnp.mean(centered * centered, axis=-1, keepdims=True)
    return centered * lax.rsqrt(variance + NORM_EPSILON) * gain_row + shift_row


def gelu_tanh(inputs):
    return jax.nn.gelu(inputs, approximate=True)


def score_layout(starts, slopes):
    positions = jnp.arange(LEN, dtype=jnp.int32)
    inside = (positions[None, :] >= starts[:, None]) & (
        positions[None, :] < starts[:, None] + PIECE
    )
    labels = jnp.arange(1, NPIECE + 1, dtype=jnp.int32)
    piece_label = jnp.sum(jnp.where(inside, labels[:, None], 0), axis=0)
    same_piece = (piece_label[:, None] == piece_label[None, :]) & (piece_label[:, None] > 0)
    visible = (positions[None, :] <= positions[:, None]) | same_piece
    distance = jnp.abs(positions[:, None] - positions[None, :]).astype(jnp.float32)
    penalty = -slopes[:, None, None] * distance[None, :, :]
    return (visible, penalty)


def head_scores(query_heads, key_heads, starts, slopes):
    visible, penalty = score_layout(starts, slopes)
    raw_scores = jnp.einsum(
        "qhd,khd->hqk", query_heads, key_heads, preferred_element_type=jnp.float32
    )
    scores = raw_scores * (1.0 / math.sqrt(HD)) + penalty
    return jnp.where(visible[None, :, :], scores, MASKED_SCORE)


def attend_forward(element, slopes):
    query_seq, key_seq, value_seq, starts = element
    heads_here = slopes.shape[0]
    query_heads = query_seq.reshape(LEN, heads_here, HD)
    key_heads = key_seq.reshape(LEN, heads_here, HD)
    value_heads = value_seq.reshape(LEN, heads_here, HD)
    scores = head_scores(query_heads, key_heads, starts, slopes)
    maximum = jnp.max(scores, axis=-1, keepdims=True)
    weights_raw = jnp.exp(scores - maximum)
    denominator = jnp.sum(weights_raw, axis=-1, keepdims=True)
    probabilities = weights_raw / denominator
    context = jnp.einsum(
        "hqk,khd->qhd",
        probabilities.astype(jnp.bfloat16),
        value_heads,
        preferred_element_type=jnp.float32,
    )
    logsum = (maximum + jnp.log(denominator))[..., 0]
    return (context.reshape(LEN, heads_here * HD), logsum)


def attend_backward(element, slopes):
    query_seq, key_seq, value_seq, context_grad, logsum, starts = element
    heads_here = slopes.shape[0]
    query_heads = query_seq.reshape(LEN, heads_here, HD)
    key_heads = key_seq.reshape(LEN, heads_here, HD)
    value_heads = value_seq.reshape(LEN, heads_here, HD)
    grad_heads = context_grad.reshape(LEN, heads_here, HD)
    scores = head_scores(query_heads, key_heads, starts, slopes)
    probabilities = jnp.exp(scores - logsum[..., None])
    grad_probs = jnp.einsum(
        "qhd,khd->hqk", grad_heads, value_heads, preferred_element_type=jnp.float32
    )
    inner_sum = jnp.sum(probabilities * grad_probs, axis=-1, keepdims=True)
    grad_scores = (probabilities * (grad_probs - inner_sum)).astype(jnp.bfloat16)
    scale_factor = 1.0 / math.sqrt(HD)
    grad_query = (
        jnp.einsum("hqk,khd->qhd", grad_scores, key_heads, preferred_element_type=jnp.float32)
        * scale_factor
    )
    grad_key = (
        jnp.einsum("hqk,qhd->khd", grad_scores, query_heads, preferred_element_type=jnp.float32)
        * scale_factor
    )
    grad_value = jnp.einsum(
        "hqk,qhd->khd",
        probabilities.astype(jnp.bfloat16),
        grad_heads,
        preferred_element_type=jnp.float32,
    )
    width_here = heads_here * HD
    return (
        grad_query.astype(jnp.bfloat16).reshape(LEN, width_here),
        grad_key.astype(jnp.bfloat16).reshape(LEN, width_here),
        grad_value.astype(jnp.bfloat16).reshape(LEN, width_here),
    )


def placed(values, offset, length):
    return lax.dynamic_update_slice_in_dim(jnp.zeros((length,), jnp.float32), values, offset, 0)


def accumulate(totals, addend):
    if totals is None:
        return addend
    return tuple((former + latter for former, latter in zip(totals, addend)))


def gram_term(narrow_rows, wide_rows):
    part_narrow = jnp.einsum(
        "mrc,mrd->cmd", narrow_rows, narrow_rows, preferred_element_type=jnp.float32
    )
    part_wide = jnp.einsum("mrc,mrd->cmd", wide_rows, wide_rows, preferred_element_type=jnp.float32)
    return jnp.concatenate([part_narrow, part_wide], axis=1)


def schulz_step(state, gram_matrix):
    turned = jnp.einsum("mrc,cmd->mrd", state, gram_matrix, preferred_element_type=jnp.float32)
    mixed = (SCHULZ_SECOND * state.astype(jnp.float32) + SCHULZ_THIRD * turned).astype(jnp.bfloat16)
    return (
        SCHULZ_FIRST * state.astype(jnp.float32)
        + jnp.einsum("mrc,cmd->mrd", mixed, gram_matrix, preferred_element_type=jnp.float32)
    ).astype(jnp.bfloat16)


def slice_term(source, weights, pattern):
    return jnp.einsum(pattern, source, weights, preferred_element_type=jnp.float32)


def on_device(
    tokens,
    cotangent,
    piece_starts,
    w_qkv,
    w_out,
    w_up,
    w_down,
    vectors,
    m_qkv,
    m_out,
    m_up,
    m_down,
    m_vec,
):
    tensor_count = lax.axis_size("tensor")
    tensor_rank = lax.axis_index("tensor")
    shard_rank = lax.axis_index("dp")
    heads_here = H // tensor_count
    width_here = heads_here * HD
    hidden_here = FF // tensor_count
    rows_here = tokens.shape[1]
    group_rows = rows_here * tensor_count
    seqs_here = piece_starts.shape[1]
    shard_rows = w_qkv.shape[1]
    head_ids = tensor_rank * heads_here + jnp.arange(heads_here, dtype=jnp.int32) + 1
    slopes = jnp.exp2(-8.0 * head_ids.astype(jnp.float32) / H)
    query_shift = lax.dynamic_slice_in_dim(vectors[2], tensor_rank * width_here, width_here, 0)
    value_shift = lax.dynamic_slice_in_dim(vectors[3], tensor_rank * width_here, width_here, 0)
    up_shift = lax.dynamic_slice_in_dim(
        vectors[7:11].reshape(FF), tensor_rank * hidden_here, hidden_here, 0
    )
    low_qkv = w_qkv.astype(jnp.bfloat16)
    low_out = w_out.astype(jnp.bfloat16)
    low_up = w_up.astype(jnp.bfloat16)
    low_down = w_down.astype(jnp.bfloat16)
    outputs_list = []
    input_grads = []
    vector_total = jnp.zeros((12, D), jnp.float32)
    grad_total = None

    def forward_one(element):
        return attend_forward(element, slopes)

    def backward_one(element):
        return attend_backward(element, slopes)

    for batch_index in range(MB):
        full_qkv, full_out, full_up, full_down = (
            lax.all_gather(low_qkv, "dp", axis=1, tiled=True),
            lax.all_gather(low_out, "dp", axis=1, tiled=True),
            lax.all_gather(low_up, "dp", axis=0, tiled=True),
            lax.all_gather(low_down, "dp", axis=1, tiled=True),
        )
        token_rows = tokens[batch_index].astype(jnp.float32)
        cotangent_rows = cotangent[batch_index]
        normed_one = layer_norm(token_rows, vectors[0], vectors[1])
        normed_all, cotangent_all = (
            lax.all_gather(normed_one.astype(jnp.bfloat16), "tensor", axis=0, tiled=True),
            lax.all_gather(cotangent_rows, "tensor", axis=0, tiled=True),
        )
        projected = jnp.einsum(
            "td,cde->cte", normed_all, full_qkv, preferred_element_type=jnp.float32
        )
        query_low = (projected[0] + query_shift).astype(jnp.bfloat16)
        key_low = projected[1].astype(jnp.bfloat16)
        value_low = (projected[2] + value_shift).astype(jnp.bfloat16)
        query_seqs = query_low.reshape(seqs_here, LEN, width_here)
        key_seqs = key_low.reshape(seqs_here, LEN, width_here)
        value_seqs = value_low.reshape(seqs_here, LEN, width_here)
        starts_here = piece_starts[batch_index]
        context_seq, logsum = lax.map(forward_one, (query_seqs, key_seqs, value_seqs, starts_here))
        context_low = context_seq.reshape(group_rows, width_here).astype(jnp.bfloat16)
        attended = lax.psum_scatter(
            slice_term(context_low, full_out, "tc,cd->td").astype(jnp.bfloat16),
            "tensor",
            scatter_dimension=0,
            tiled=True,
        ).astype(jnp.float32)
        middle = token_rows + attended + vectors[4]
        normed_two = layer_norm(middle, vectors[5], vectors[6])
        normed_two_all = lax.all_gather(
            normed_two.astype(jnp.bfloat16), "tensor", axis=0, tiled=True
        )
        before = jnp.dot(normed_two_all, full_up, preferred_element_type=jnp.float32) + up_shift
        activated = gelu_tanh(before).astype(jnp.bfloat16)
        expanded = lax.psum_scatter(
            slice_term(activated, full_down, "tf,fd->td").astype(jnp.bfloat16),
            "tensor",
            scatter_dimension=0,
            tiled=True,
        ).astype(jnp.float32)
        outputs_list.append((middle + expanded + vectors[11]).astype(jnp.bfloat16))
        grad_down = jnp.einsum(
            "tf,td->fd", activated, cotangent_all, preferred_element_type=jnp.float32
        )
        grad_activated = jnp.einsum(
            "td,fd->tf", cotangent_all, full_down, preferred_element_type=jnp.float32
        )
        gelu_pull = jax.vjp(gelu_tanh, before)[1]
        grad_before = gelu_pull(grad_activated)[0].astype(jnp.bfloat16)
        grad_up = jnp.einsum(
            "td,tf->df", normed_two_all, grad_before, preferred_element_type=jnp.float32
        )
        grad_normed_two = lax.psum_scatter(
            slice_term(grad_before, full_up, "tf,df->td").astype(jnp.bfloat16),
            "tensor",
            scatter_dimension=0,
            tiled=True,
        ).astype(jnp.float32)
        second_pull = jax.vjp(layer_norm, middle, vectors[5], vectors[6])[1]
        middle_from_norm, gain_two_grad, shift_two_grad = second_pull(grad_normed_two)
        grad_middle = cotangent_rows.astype(jnp.float32) + middle_from_norm
        grad_middle_all = lax.all_gather(
            grad_middle.astype(jnp.bfloat16), "tensor", axis=0, tiled=True
        )
        grad_out = jnp.einsum(
            "tc,td->cd", context_low, grad_middle_all, preferred_element_type=jnp.float32
        )
        grad_context = jnp.einsum(
            "td,cd->tc", grad_middle_all, full_out, preferred_element_type=jnp.float32
        ).astype(jnp.bfloat16)
        grad_query, grad_key, grad_value = lax.map(
            backward_one,
            (
                query_seqs,
                key_seqs,
                value_seqs,
                grad_context.reshape(seqs_here, LEN, width_here),
                logsum,
                starts_here,
            ),
        )
        grad_stack = jnp.stack(
            [
                grad_query.reshape(group_rows, width_here),
                grad_key.reshape(group_rows, width_here),
                grad_value.reshape(group_rows, width_here),
            ]
        )
        grad_qkv = jnp.einsum(
            "td,cte->cde", normed_all, grad_stack, preferred_element_type=jnp.float32
        )
        grad_normed_one = lax.psum_scatter(
            slice_term(grad_stack, full_qkv, "cte,cde->td").astype(jnp.bfloat16),
            "tensor",
            scatter_dimension=0,
            tiled=True,
        ).astype(jnp.float32)
        first_pull = jax.vjp(layer_norm, token_rows, vectors[0], vectors[1])[1]
        token_from_norm, gain_one_grad, shift_one_grad = first_pull(grad_normed_one)
        input_grads.append(grad_middle + token_from_norm)
        query_bias = jnp.sum(grad_stack[0], axis=0, dtype=jnp.float32)
        value_bias = jnp.sum(grad_stack[2], axis=0, dtype=jnp.float32)
        up_bias = jnp.sum(grad_before, axis=0, dtype=jnp.float32)
        head_rows = jnp.stack(
            [
                gain_one_grad,
                shift_one_grad,
                placed(query_bias, tensor_rank * width_here, D),
                placed(value_bias, tensor_rank * width_here, D),
                jnp.sum(grad_middle, axis=0),
                gain_two_grad,
                shift_two_grad,
            ]
        )
        up_rows = placed(up_bias, tensor_rank * hidden_here, FF).reshape(4, D)
        tail_row = jnp.sum(cotangent_rows, axis=0, dtype=jnp.float32)[None, :]
        vector_total = vector_total + jnp.concatenate([head_rows, up_rows, tail_row], axis=0)
        shard_grads = (
            lax.psum_scatter(
                grad_qkv.astype(jnp.bfloat16), "dp", scatter_dimension=1, tiled=True
            ).astype(jnp.float32),
            lax.psum_scatter(
                grad_out.astype(jnp.bfloat16), "dp", scatter_dimension=1, tiled=True
            ).astype(jnp.float32),
            lax.psum_scatter(
                grad_up.astype(jnp.bfloat16), "dp", scatter_dimension=0, tiled=True
            ).astype(jnp.float32),
            lax.psum_scatter(
                grad_down.astype(jnp.bfloat16), "dp", scatter_dimension=1, tiled=True
            ).astype(jnp.float32),
        )
        grad_total = accumulate(grad_total, shard_grads)
    grad_qkv_shard, grad_out_shard, grad_up_shard, grad_down_shard = grad_total
    moment_qkv = MOMENTUM_DECAY * m_qkv + grad_qkv_shard
    moment_out = MOMENTUM_DECAY * m_out + grad_out_shard
    moment_up = MOMENTUM_DECAY * m_up + grad_up_shard
    moment_down = MOMENTUM_DECAY * m_down + grad_down_shard
    squares = jnp.concatenate(
        [
            jnp.sum(moment_qkv * moment_qkv, axis=(1, 2)),
            jnp.stack(
                [
                    jnp.sum(moment_out * moment_out),
                    jnp.sum(moment_up * moment_up),
                    jnp.sum(moment_down * moment_down),
                ]
            ),
        ]
    )
    vector_grad, square_total = lax.psum((vector_total, squares), ("dp", "tensor"))
    factors = lax.rsqrt(square_total + SQUARE_EPSILON)
    scaled_qkv = (moment_qkv * factors[0:3][:, None, None]).astype(jnp.bfloat16)
    scaled_out = (moment_out * factors[3]).astype(jnp.bfloat16)
    scaled_up = (moment_up * factors[4]).astype(jnp.bfloat16)
    scaled_down = (moment_down * factors[5]).astype(jnp.bfloat16)
    gathered_qkv, gathered_out, gathered_up, gathered_down = (
        lax.all_gather(scaled_qkv, "dp", axis=1, tiled=True),
        lax.all_gather(scaled_out, "dp", axis=1, tiled=True),
        lax.all_gather(scaled_up, "dp", axis=0, tiled=True),
        lax.all_gather(scaled_down, "dp", axis=1, tiled=True),
    )
    offset = shard_rank * shard_rows
    narrow_rows = jnp.concatenate([jnp.swapaxes(gathered_qkv, 1, 2), gathered_out[None]], axis=0)
    wide_rows = jnp.stack([gathered_up.T, gathered_down])
    for sweep_index in range(NS_ITERS):
        gram_share = lax.psum_scatter(
            gram_term(narrow_rows, wide_rows).astype(jnp.bfloat16),
            "tensor",
            scatter_dimension=0,
            tiled=True,
        )
        gram_matrix = lax.all_gather(gram_share, "tensor", axis=0, tiled=True)
        narrow_rows = schulz_step(narrow_rows, gram_matrix[:, 0:4])
        wide_rows = schulz_step(wide_rows, gram_matrix[:, 4:6])
    final_narrow = narrow_rows.astype(jnp.float32)
    final_wide = wide_rows.astype(jnp.float32)
    update_qkv = lax.dynamic_slice_in_dim(
        jnp.swapaxes(final_narrow[0:3], 1, 2), offset, shard_rows, 1
    )
    update_out = lax.dynamic_slice_in_dim(final_narrow[3], offset, shard_rows, 1)
    update_up = lax.dynamic_slice_in_dim(final_wide[0].T, offset, shard_rows, 0)
    update_down = lax.dynamic_slice_in_dim(final_wide[1], offset, shard_rows, 1)
    wide_factor = math.sqrt(FF / D)
    new_qkv = w_qkv - MATRIX_RATE * update_qkv
    new_out = w_out - MATRIX_RATE * update_out
    new_up = w_up - MATRIX_RATE * wide_factor * update_up
    new_down = w_down - MATRIX_RATE * wide_factor * update_down
    moment_vec = MOMENTUM_DECAY * m_vec + vector_grad
    new_vec = vectors - VECTOR_RATE * moment_vec * lax.rsqrt(
        jnp.mean(moment_vec * moment_vec, axis=1, keepdims=True) + SQUARE_EPSILON
    )
    return (
        jnp.stack(outputs_list),
        jnp.stack(input_grads),
        grad_qkv_shard,
        grad_out_shard,
        grad_up_shard,
        grad_down_shard,
        vector_grad,
        moment_qkv,
        moment_out,
        moment_up,
        moment_down,
        moment_vec,
        new_qkv,
        new_out,
        new_up,
        new_down,
        new_vec,
    )


def layout_grid(starts_ref, dist_ref):
    key_pos = lax.broadcasted_iota(jnp.int32, (LEN, LEN), 0)
    query_pos = lax.broadcasted_iota(jnp.int32, (LEN, LEN), 1)
    gap = query_pos - key_pos
    visible = gap >= 0
    for piece in range(NPIECE):
        start = starts_ref[piece]
        inside_key = (key_pos >= start) & (key_pos < start + PIECE)
        inside_query = (query_pos >= start) & (query_pos < start + PIECE)
        visible = visible | (inside_key & inside_query)
    dist_ref[...] = jnp.where(visible, jnp.abs(gap).astype(jnp.float32), -MASKED_SCORE)


def attend_fwd_kernel(starts_ref, slopes_ref, q_ref, k_ref, v_ref, ctx_ref, exps_ref, stat_ref, dist_ref):
    head = pl.program_id(0)

    @pl.when(head == 0)
    def _():
        layout_grid(starts_ref, dist_ref)

    slope = slopes_ref[head]
    keys = k_ref[0, 0, 0].T
    queries = q_ref[0, 0, 0] * (1.0 / math.sqrt(HD))
    for block in range(LEN // QB):
        span = min(LEN, QB * block + QB + PIECE)
        cols = slice(block * QB, block * QB + QB)
        scores = jnp.dot(keys[:span], queries[:, cols], preferred_element_type=jnp.float32)
        scores = scores - slope * dist_ref[:span, cols]
        top = jnp.max(scores, axis=0, keepdims=True)
        raw = jnp.exp(scores - top)
        inverse = 1.0 / jnp.sum(raw, axis=0, keepdims=True)
        low = raw.astype(jnp.bfloat16)
        exps_ref[0, :span, cols] = low
        context = jnp.dot(v_ref[0, 0, 0, :, :span], low, preferred_element_type=jnp.float32)
        ctx_ref[0, :, cols] = (context * inverse).astype(jnp.bfloat16)
        stat_ref[0, :, cols] = inverse


def attend_bwd_kernel(q_ref, k_ref, v_ref, ctx_ref, grad_ref, exps_ref, stat_ref, dq_ref, dk_ref, dv_ref, dk_sum, dv_sum):
    scale = 1.0 / math.sqrt(HD)
    keys_t = k_ref[0, 0, 0]
    values = v_ref[0, 0, 0].T
    queries = q_ref[0, 0, 0].T
    dk_sum[...] = jnp.zeros_like(dk_sum)
    dv_sum[...] = jnp.zeros_like(dv_sum)
    for block in reversed(range(LEN // QB)):
        span = min(LEN, QB * block + QB + PIECE)
        cols = slice(block * QB, block * QB + QB)
        grad = grad_ref[0, :, cols].astype(jnp.float32) * stat_ref[0, :, cols]
        inner = jnp.sum(grad * ctx_ref[0, :, cols].astype(jnp.float32), axis=0, keepdims=True)
        grad_low = grad.astype(jnp.bfloat16)
        exps = exps_ref[0, :span, cols]
        grad_probs = jnp.dot(values[:span], grad_low, preferred_element_type=jnp.float32)
        grad_scores = (exps.astype(jnp.float32) * (grad_probs - inner)).astype(jnp.bfloat16)
        dv_sum[:span, :] += jnp.dot(exps, grad_low.T, preferred_element_type=jnp.float32)
        dk_sum[:span, :] += jnp.dot(grad_scores, queries[cols], preferred_element_type=jnp.float32)
        dq = jnp.dot(keys_t[:, :span], grad_scores, preferred_element_type=jnp.float32)
        dq_ref[0, :, cols] = (dq * scale).astype(jnp.bfloat16)
    dk_ref[0] = (dk_sum[...] * scale).T.astype(jnp.bfloat16)
    dv_ref[0] = dv_sum[...].T.astype(jnp.bfloat16)


QB = 256


def part_spec(part, heads_each):
    return pl.BlockSpec((1, 1, 1, HD, LEN), lambda h: (h // heads_each, part, h % heads_each, 0, 0))


HEAD_ROWS = pl.BlockSpec((1, HD, LEN), lambda h: (h, 0, 0))
HEAD_GRID = pl.BlockSpec((1, LEN, LEN), lambda h: (h, 0, 0))
HEAD_STAT = pl.BlockSpec((1, 1, LEN), lambda h: (h, 0, 0))
SCALARS = pl.BlockSpec(memory_space=pltpu.SMEM)
VMEM_LIMIT = 56 * 1024 * 1024


def attention_forward(starts, slopes, packed):
    heads_each = packed.shape[2]
    return pl.pallas_call(
        attend_fwd_kernel,
        grid=(H,),
        in_specs=[SCALARS, SCALARS] + [part_spec(part, heads_each) for part in range(3)],
        out_specs=[HEAD_ROWS, HEAD_GRID, HEAD_STAT],
        out_shape=[
            jax.ShapeDtypeStruct((H, HD, LEN), jnp.bfloat16),
            jax.ShapeDtypeStruct((H, LEN, LEN), jnp.bfloat16),
            jax.ShapeDtypeStruct((H, 1, LEN), jnp.float32),
        ],
        scratch_shapes=[pltpu.VMEM((LEN, LEN), jnp.float32)],
        compiler_params=pltpu.CompilerParams(vmem_limit_bytes=VMEM_LIMIT),
        cost_estimate=pl.CostEstimate(flops=4 * LEN * LEN * D * 4, bytes_accessed=44 * 1024 * 1024, transcendentals=H * LEN * LEN),
    )(starts, slopes, packed, packed, packed)


def attention_backward(packed, context, grad_context, exps, stats):
    heads_each = packed.shape[2]
    return pl.pallas_call(
        attend_bwd_kernel,
        grid=(H,),
        in_specs=[part_spec(part, heads_each) for part in range(3)]
        + [HEAD_ROWS, HEAD_ROWS, HEAD_GRID, HEAD_STAT],
        out_specs=[HEAD_ROWS, HEAD_ROWS, HEAD_ROWS],
        out_shape=[jax.ShapeDtypeStruct((H, HD, LEN), jnp.bfloat16)] * 3,
        scratch_shapes=[pltpu.VMEM((LEN, HD), jnp.float32), pltpu.VMEM((LEN, HD), jnp.float32)],
        compiler_params=pltpu.CompilerParams(vmem_limit_bytes=VMEM_LIMIT),
        cost_estimate=pl.CostEstimate(flops=8 * LEN * LEN * D * 4, bytes_accessed=50 * 1024 * 1024, transcendentals=0),
    )(packed, packed, packed, context, grad_context, exps, stats)


BOTH = ("tensor", "dp")
SWAP = [(0, 1), (1, 0)]


def narrow(rows):
    return rows.astype(jnp.bfloat16)


def contract(left, right, left_dim, right_dim):
    return lax.dot_general(
        left, right, (((left_dim,), (right_dim,)), ((), ())), preferred_element_type=jnp.float32
    )


def swap_halves(mine, rank):
    rows = mine.shape[0] // 2
    kept = lax.dynamic_slice_in_dim(mine, rank * rows, rows, 0)
    sent = lax.dynamic_slice_in_dim(mine, (1 - rank) * rows, rows, 0)
    got = lax.ppermute(sent, "tensor", SWAP)
    return jnp.where(rank == 0, jnp.stack([kept, got]), jnp.stack([got, kept]))


def join_halves(pair, rank):
    kept = lax.dynamic_index_in_dim(pair, rank, 0, keepdims=False)
    sent = lax.dynamic_index_in_dim(pair, 1 - rank, 0, keepdims=False)
    got = lax.ppermute(sent, "tensor", SWAP)
    return jnp.where(rank == 0, jnp.concatenate([kept, got]), jnp.concatenate([got, kept]))


def sequence_step(
    tokens,
    cotangent,
    piece_starts,
    w_qkv,
    w_out,
    w_up,
    w_down,
    vectors,
    m_qkv,
    m_out,
    m_up,
    m_down,
    m_vec,
):
    rank = lax.axis_index("tensor")
    parts = lax.axis_size("tensor")
    width = D // parts
    hidden = FF // parts
    shard_rows = w_qkv.shape[1]
    slopes = jnp.exp2(-8.0 * jnp.arange(1, H + 1, dtype=jnp.float32) / H)

    def spread(rows):
        whole = lax.all_gather(rows, BOTH, axis=0, tiled=True)
        return whole.reshape(parts, D, rows.shape[1])

    def collect(grads):
        return lax.psum_scatter(
            grads.reshape(parts * D, -1), BOTH, scatter_dimension=0, tiled=True
        ).astype(jnp.float32)

    full_qkv = spread(narrow(jnp.swapaxes(w_qkv, 0, 1)).reshape(shard_rows, 3 * width))
    token_rows = join_halves(tokens, rank).astype(jnp.float32)
    full_out = spread(narrow(w_out.T))
    full_up = spread(narrow(w_up))
    full_down = spread(narrow(w_down.T))
    cotangent_low = join_halves(cotangent, rank)
    cotangent_rows = cotangent_low.astype(jnp.float32)
    starts = lax.dynamic_slice_in_dim(piece_starts[:, 0], rank, 1, 0)[0]

    normed_one = narrow(layer_norm(token_rows, vectors[0], vectors[1]))
    shifts = jnp.stack([vectors[2], jnp.zeros((D,), jnp.float32), vectors[3]])
    shifts = jnp.swapaxes(shifts.reshape(3, parts, width), 0, 1).reshape(parts, 3 * width, 1)
    packed = jnp.stack(
        [narrow(contract(full_qkv[part], normed_one, 0, 1) + shifts[part]) for part in range(parts)]
    )
    packed = packed.reshape(parts, 3, width // HD, HD, LEN)
    context, exps, stats = attention_forward(starts, slopes, packed)
    context_rows = context.reshape(parts, width, LEN)
    attended = sum(contract(context_rows[part], full_out[part], 0, 1) for part in range(parts))
    middle = token_rows + attended + vectors[4]
    normed_two = narrow(layer_norm(middle, vectors[5], vectors[6]))
    up_shift = vectors[7:11].reshape(parts, hidden)
    before = [contract(normed_two, full_up[part], 1, 0) + up_shift[part] for part in range(parts)]
    activated = [narrow(gelu_tanh(rows)) for rows in before]
    expanded = sum(contract(activated[part], full_down[part], 1, 1) for part in range(parts))
    block_rows = narrow(middle + expanded + vectors[11])

    grad_down = jnp.stack([narrow(contract(cotangent_low, rows, 0, 0)) for rows in activated])
    grad_before = []
    for part in range(parts):
        grad_activated = contract(cotangent_low, full_down[part], 1, 0)
        gelu_pull = jax.vjp(gelu_tanh, before[part])[1]
        grad_before.append(narrow(gelu_pull(grad_activated)[0]))
    grad_up = jnp.stack([narrow(contract(normed_two, rows, 0, 0)) for rows in grad_before])
    grad_down_shard = collect(grad_down)
    grad_up_shard = collect(grad_up)
    grad_normed_two = sum(contract(grad_before[part], full_up[part], 1, 1) for part in range(parts))
    second_pull = jax.vjp(layer_norm, middle, vectors[5], vectors[6])[1]
    middle_from_norm, gain_two_grad, shift_two_grad = second_pull(grad_normed_two)
    grad_middle = cotangent_rows + middle_from_norm
    grad_middle_low = narrow(grad_middle)
    grad_out = jnp.stack(
        [narrow(contract(grad_middle_low, context_rows[part], 0, 1)) for part in range(parts)]
    )
    grad_out_shard = collect(grad_out)
    grad_context = jnp.stack(
        [narrow(contract(full_out[part], grad_middle_low, 0, 1)) for part in range(parts)]
    ).reshape(H, HD, LEN)
    grad_parts = attention_backward(packed, context, grad_context, exps, stats)
    grad_packed = jnp.stack([rows.reshape(parts, width, LEN) for rows in grad_parts], axis=1)
    grad_packed = grad_packed.reshape(parts, 3 * width, LEN)
    grad_qkv = jnp.stack([narrow(contract(normed_one, grad_packed[part], 0, 1)) for part in range(parts)])
    grad_qkv_shard = collect(grad_qkv)
    grad_normed_one = sum(contract(grad_packed[part], full_qkv[part], 0, 1) for part in range(parts))
    first_pull = jax.vjp(layer_norm, token_rows, vectors[0], vectors[1])[1]
    token_from_norm, gain_one_grad, shift_one_grad = first_pull(grad_normed_one)
    grad_token_rows = grad_middle + token_from_norm
    output_pair = swap_halves(block_rows, rank)
    token_pair = swap_halves(narrow(grad_token_rows), rank).astype(jnp.float32)

    row_sums = [
        jnp.sum(rows.astype(jnp.float32), axis=2).reshape(D) for rows in (grad_parts[0], grad_parts[2])
    ]
    up_bias = jnp.concatenate([jnp.sum(rows, axis=0, dtype=jnp.float32) for rows in grad_before])
    vector_total = jnp.concatenate(
        [
            jnp.stack(
                [
                    gain_one_grad,
                    shift_one_grad,
                    row_sums[0],
                    row_sums[1],
                    jnp.sum(grad_middle, axis=0),
                    gain_two_grad,
                    shift_two_grad,
                ]
            ),
            up_bias.reshape(4, D),
            jnp.sum(cotangent_rows, axis=0)[None],
        ]
    )
    grad_qkv_shard = jnp.swapaxes(grad_qkv_shard.reshape(shard_rows, 3, width), 0, 1)
    shards = (grad_qkv_shard, grad_out_shard.T, grad_up_shard, grad_down_shard.T)
    outputs = muon_step(shards, vector_total, w_qkv, w_out, w_up, w_down, vectors, m_qkv, m_out, m_up, m_down, m_vec)
    return (output_pair, token_pair) + outputs


def muon_step(
    shards, vector_total, w_qkv, w_out, w_up, w_down, vectors, m_qkv, m_out, m_up, m_down, m_vec
):
    shard_rank = lax.axis_index("dp")
    shard_rows = w_qkv.shape[1]
    grad_qkv_shard, grad_out_shard, grad_up_shard, grad_down_shard = shards
    moment_qkv = MOMENTUM_DECAY * m_qkv + grad_qkv_shard
    moment_out = MOMENTUM_DECAY * m_out + grad_out_shard
    moment_up = MOMENTUM_DECAY * m_up + grad_up_shard
    moment_down = MOMENTUM_DECAY * m_down + grad_down_shard
    squares = jnp.concatenate(
        [
            jnp.sum(moment_qkv * moment_qkv, axis=(1, 2)),
            jnp.stack(
                [
                    jnp.sum(moment_out * moment_out),
                    jnp.sum(moment_up * moment_up),
                    jnp.sum(moment_down * moment_down),
                ]
            ),
        ]
    )
    vector_grad, square_total = lax.psum((vector_total, squares), ("dp", "tensor"))
    factors = lax.rsqrt(square_total + SQUARE_EPSILON)
    scaled_qkv = (moment_qkv * factors[0:3][:, None, None]).astype(jnp.bfloat16)
    scaled_out = (moment_out * factors[3]).astype(jnp.bfloat16)
    scaled_up = (moment_up * factors[4]).astype(jnp.bfloat16)
    scaled_down = (moment_down * factors[5]).astype(jnp.bfloat16)
    gathered_qkv, gathered_out, gathered_up, gathered_down = (
        lax.all_gather(scaled_qkv, "dp", axis=1, tiled=True),
        lax.all_gather(scaled_out, "dp", axis=1, tiled=True),
        lax.all_gather(scaled_up, "dp", axis=0, tiled=True),
        lax.all_gather(scaled_down, "dp", axis=1, tiled=True),
    )
    offset = shard_rank * shard_rows
    narrow_rows = jnp.concatenate([jnp.swapaxes(gathered_qkv, 1, 2), gathered_out[None]], axis=0)
    wide_rows = jnp.stack([gathered_up.T, gathered_down])
    for sweep_index in range(NS_ITERS):
        gram_share = lax.psum_scatter(
            gram_term(narrow_rows, wide_rows).astype(jnp.bfloat16),
            "tensor",
            scatter_dimension=0,
            tiled=True,
        )
        gram_matrix = lax.all_gather(gram_share, "tensor", axis=0, tiled=True)
        narrow_rows = schulz_step(narrow_rows, gram_matrix[:, 0:4])
        wide_rows = schulz_step(wide_rows, gram_matrix[:, 4:6])
    final_narrow = narrow_rows.astype(jnp.float32)
    final_wide = wide_rows.astype(jnp.float32)
    update_qkv = lax.dynamic_slice_in_dim(
        jnp.swapaxes(final_narrow[0:3], 1, 2), offset, shard_rows, 1
    )
    update_out = lax.dynamic_slice_in_dim(final_narrow[3], offset, shard_rows, 1)
    update_up = lax.dynamic_slice_in_dim(final_wide[0].T, offset, shard_rows, 0)
    update_down = lax.dynamic_slice_in_dim(final_wide[1], offset, shard_rows, 1)
    wide_factor = math.sqrt(FF / D)
    new_qkv = w_qkv - MATRIX_RATE * update_qkv
    new_out = w_out - MATRIX_RATE * update_out
    new_up = w_up - MATRIX_RATE * wide_factor * update_up
    new_down = w_down - MATRIX_RATE * wide_factor * update_down
    moment_vec = MOMENTUM_DECAY * m_vec + vector_grad
    new_vec = vectors - VECTOR_RATE * moment_vec * lax.rsqrt(
        jnp.mean(moment_vec * moment_vec, axis=1, keepdims=True) + SQUARE_EPSILON
    )
    return (
        grad_qkv_shard,
        grad_out_shard,
        grad_up_shard,
        grad_down_shard,
        vector_grad,
        moment_qkv,
        moment_out,
        moment_up,
        moment_down,
        moment_vec,
        new_qkv,
        new_out,
        new_up,
        new_down,
        new_vec,
    )


def solution(mesh):
    in_specs = (
        P(None, ("dp", "tensor"), None),
        P(None, ("dp", "tensor"), None),
        P(None, "dp", None),
        P(None, "dp", "tensor"),
        P("tensor", "dp"),
        P("dp", "tensor"),
        P("tensor", "dp"),
        P(),
        P(None, "dp", "tensor"),
        P("tensor", "dp"),
        P("dp", "tensor"),
        P("tensor", "dp"),
        P(),
    )
    out_specs = (
        P(None, ("dp", "tensor"), None),
        P(None, ("dp", "tensor"), None),
        P(None, "dp", "tensor"),
        P("tensor", "dp"),
        P("dp", "tensor"),
        P("tensor", "dp"),
        P(),
        P(None, "dp", "tensor"),
        P("tensor", "dp"),
        P("dp", "tensor"),
        P("tensor", "dp"),
        P(),
        P(None, "dp", "tensor"),
        P("tensor", "dp"),
        P("dp", "tensor"),
        P("tensor", "dp"),
        P(),
    )
    groups_fit = mesh.shape["tensor"] == MB

    def pick(*arrays):
        if groups_fit and arrays[2].shape[1] == 1:
            return sequence_step(*arrays)
        return on_device(*arrays)

    return jax.shard_map(
        pick, mesh=mesh, in_specs=in_specs, out_specs=out_specs, check_vma=False
    )
```

```python
import math

import jax
import jax.numpy as jnp
from jax import lax
from jax.experimental import pallas as pl
from jax.experimental.pallas import tpu as pltpu
from jax.sharding import PartitionSpec as P

D = 1024
H = 16
HD = 64
FF = 4096
LEN = 1024
PIECE = 256
NPIECE = 2
MB = 2
NS_ITERS = 3


NORM_EPSILON = 1e-05
SQUARE_EPSILON = 1e-06
MASKED_SCORE = -1e30
SCHULZ_FIRST = 3.4445
SCHULZ_SECOND = -4.775
SCHULZ_THIRD = 2.0315
MOMENTUM_DECAY = 0.5
MATRIX_RATE = 0.5
VECTOR_RATE = 0.05


def layer_norm(inputs, gain_row, shift_row):
    average = jnp.mean(inputs, axis=-1, keepdims=True)
    centered = inputs - average
    variance = jnp.mean(centered * centered, axis=-1, keepdims=True)
    return centered * lax.rsqrt(variance + NORM_EPSILON) * gain_row + shift_row


def gelu_tanh(inputs):
    return jax.nn.gelu(inputs, approximate=True)


def score_layout(starts, slopes):
    positions = jnp.arange(LEN, dtype=jnp.int32)
    inside = (positions[None, :] >= starts[:, None]) & (
        positions[None, :] < starts[:, None] + PIECE
    )
    labels = jnp.arange(1, NPIECE + 1, dtype=jnp.int32)
    piece_label = jnp.sum(jnp.where(inside, labels[:, None], 0), axis=0)
    same_piece = (piece_label[:, None] == piece_label[None, :]) & (piece_label[:, None] > 0)
    visible = (positions[None, :] <= positions[:, None]) | same_piece
    distance = jnp.abs(positions[:, None] - positions[None, :]).astype(jnp.float32)
    penalty = -slopes[:, None, None] * distance[None, :, :]
    return (visible, penalty)


def head_scores(query_heads, key_heads, starts, slopes):
    visible, penalty = score_layout(starts, slopes)
    raw_scores = jnp.einsum(
        "qhd,khd->hqk", query_heads, key_heads, preferred_element_type=jnp.float32
    )
    scores = raw_scores * (1.0 / math.sqrt(HD)) + penalty
    return jnp.where(visible[None, :, :], scores, MASKED_SCORE)


def attend_forward(element, slopes):
    query_seq, key_seq, value_seq, starts = element
    heads_here = slopes.shape[0]
    query_heads = query_seq.reshape(LEN, heads_here, HD)
    key_heads = key_seq.reshape(LEN, heads_here, HD)
    value_heads = value_seq.reshape(LEN, heads_here, HD)
    scores = head_scores(query_heads, key_heads, starts, slopes)
    maximum = jnp.max(scores, axis=-1, keepdims=True)
    weights_raw = jnp.exp(scores - maximum)
    denominator = jnp.sum(weights_raw, axis=-1, keepdims=True)
    probabilities = weights_raw / denominator
    context = jnp.einsum(
        "hqk,khd->qhd",
        probabilities.astype(jnp.bfloat16),
        value_heads,
        preferred_element_type=jnp.float32,
    )
    logsum = (maximum + jnp.log(denominator))[..., 0]
    return (context.reshape(LEN, heads_here * HD), logsum)


def attend_backward(element, slopes):
    query_seq, key_seq, value_seq, context_grad, logsum, starts = element
    heads_here = slopes.shape[0]
    query_heads = query_seq.reshape(LEN, heads_here, HD)
    key_heads = key_seq.reshape(LEN, heads_here, HD)
    value_heads = value_seq.reshape(LEN, heads_here, HD)
    grad_heads = context_grad.reshape(LEN, heads_here, HD)
    scores = head_scores(query_heads, key_heads, starts, slopes)
    probabilities = jnp.exp(scores - logsum[..., None])
    grad_probs = jnp.einsum(
        "qhd,khd->hqk", grad_heads, value_heads, preferred_element_type=jnp.float32
    )
    inner_sum = jnp.sum(probabilities * grad_probs, axis=-1, keepdims=True)
    grad_scores = (probabilities * (grad_probs - inner_sum)).astype(jnp.bfloat16)
    scale_factor = 1.0 / math.sqrt(HD)
    grad_query = (
        jnp.einsum("hqk,khd->qhd", grad_scores, key_heads, preferred_element_type=jnp.float32)
        * scale_factor
    )
    grad_key = (
        jnp.einsum("hqk,qhd->khd", grad_scores, query_heads, preferred_element_type=jnp.float32)
        * scale_factor
    )
    grad_value = jnp.einsum(
        "hqk,qhd->khd",
        probabilities.astype(jnp.bfloat16),
        grad_heads,
        preferred_element_type=jnp.float32,
    )
    width_here = heads_here * HD
    return (
        grad_query.astype(jnp.bfloat16).reshape(LEN, width_here),
        grad_key.astype(jnp.bfloat16).reshape(LEN, width_here),
        grad_value.astype(jnp.bfloat16).reshape(LEN, width_here),
    )


def placed(values, offset, length):
    return lax.dynamic_update_slice_in_dim(jnp.zeros((length,), jnp.float32), values, offset, 0)


def accumulate(totals, addend):
    if totals is None:
        return addend
    return tuple((former + latter for former, latter in zip(totals, addend)))


def gram_term(narrow_rows, wide_rows):
    part_narrow = jnp.einsum(
        "mrc,mrd->cmd", narrow_rows, narrow_rows, preferred_element_type=jnp.float32
    )
    part_wide = jnp.einsum("mrc,mrd->cmd", wide_rows, wide_rows, preferred_element_type=jnp.float32)
    return jnp.concatenate([part_narrow, part_wide], axis=1)


def schulz_step(state, gram_matrix):
    turned = jnp.einsum("mrc,cmd->mrd", state, gram_matrix, preferred_element_type=jnp.float32)
    mixed = (SCHULZ_SECOND * state.astype(jnp.float32) + SCHULZ_THIRD * turned).astype(jnp.bfloat16)
    return (
        SCHULZ_FIRST * state.astype(jnp.float32)
        + jnp.einsum("mrc,cmd->mrd", mixed, gram_matrix, preferred_element_type=jnp.float32)
    ).astype(jnp.bfloat16)


def slice_term(source, weights, pattern):
    return jnp.einsum(pattern, source, weights, preferred_element_type=jnp.float32)


def on_device(
    tokens,
    cotangent,
    piece_starts,
    w_qkv,
    w_out,
    w_up,
    w_down,
    vectors,
    m_qkv,
    m_out,
    m_up,
    m_down,
    m_vec,
):
    tensor_count = lax.axis_size("tensor")
    tensor_rank = lax.axis_index("tensor")
    shard_rank = lax.axis_index("dp")
    heads_here = H // tensor_count
    width_here = heads_here * HD
    hidden_here = FF // tensor_count
    rows_here = tokens.shape[1]
    group_rows = rows_here * tensor_count
    seqs_here = piece_starts.shape[1]
    shard_rows = w_qkv.shape[1]
    head_ids = tensor_rank * heads_here + jnp.arange(heads_here, dtype=jnp.int32) + 1
    slopes = jnp.exp2(-8.0 * head_ids.astype(jnp.float32) / H)
    query_shift = lax.dynamic_slice_in_dim(vectors[2], tensor_rank * width_here, width_here, 0)
    value_shift = lax.dynamic_slice_in_dim(vectors[3], tensor_rank * width_here, width_here, 0)
    up_shift = lax.dynamic_slice_in_dim(
        vectors[7:11].reshape(FF), tensor_rank * hidden_here, hidden_here, 0
    )
    low_qkv = w_qkv.astype(jnp.bfloat16)
    low_out = w_out.astype(jnp.bfloat16)
    low_up = w_up.astype(jnp.bfloat16)
    low_down = w_down.astype(jnp.bfloat16)
    outputs_list = []
    input_grads = []
    vector_total = jnp.zeros((12, D), jnp.float32)
    grad_total = None

    def forward_one(element):
        return attend_forward(element, slopes)

    def backward_one(element):
        return attend_backward(element, slopes)

    for batch_index in range(MB):
        full_qkv, full_out, full_up, full_down = (
            lax.all_gather(low_qkv, "dp", axis=1, tiled=True),
            lax.all_gather(low_out, "dp", axis=1, tiled=True),
            lax.all_gather(low_up, "dp", axis=0, tiled=True),
            lax.all_gather(low_down, "dp", axis=1, tiled=True),
        )
        token_rows = tokens[batch_index].astype(jnp.float32)
        cotangent_rows = cotangent[batch_index]
        normed_one = layer_norm(token_rows, vectors[0], vectors[1])
        normed_all, cotangent_all = (
            lax.all_gather(normed_one.astype(jnp.bfloat16), "tensor", axis=0, tiled=True),
            lax.all_gather(cotangent_rows, "tensor", axis=0, tiled=True),
        )
        projected = jnp.einsum(
            "td,cde->cte", normed_all, full_qkv, preferred_element_type=jnp.float32
        )
        query_low = (projected[0] + query_shift).astype(jnp.bfloat16)
        key_low = projected[1].astype(jnp.bfloat16)
        value_low = (projected[2] + value_shift).astype(jnp.bfloat16)
        query_seqs = query_low.reshape(seqs_here, LEN, width_here)
        key_seqs = key_low.reshape(seqs_here, LEN, width_here)
        value_seqs = value_low.reshape(seqs_here, LEN, width_here)
        starts_here = piece_starts[batch_index]
        context_seq, logsum = lax.map(forward_one, (query_seqs, key_seqs, value_seqs, starts_here))
        context_low = context_seq.reshape(group_rows, width_here).astype(jnp.bfloat16)
        attended = lax.psum_scatter(
            slice_term(context_low, full_out, "tc,cd->td").astype(jnp.bfloat16),
            "tensor",
            scatter_dimension=0,
            tiled=True,
        ).astype(jnp.float32)
        middle = token_rows + attended + vectors[4]
        normed_two = layer_norm(middle, vectors[5], vectors[6])
        normed_two_all = lax.all_gather(
            normed_two.astype(jnp.bfloat16), "tensor", axis=0, tiled=True
        )
        before = jnp.dot(normed_two_all, full_up, preferred_element_type=jnp.float32) + up_shift
        activated = gelu_tanh(before).astype(jnp.bfloat16)
        expanded = lax.psum_scatter(
            slice_term(activated, full_down, "tf,fd->td").astype(jnp.bfloat16),
            "tensor",
            scatter_dimension=0,
            tiled=True,
        ).astype(jnp.float32)
        outputs_list.append((middle + expanded + vectors[11]).astype(jnp.bfloat16))
        grad_down = jnp.einsum(
            "tf,td->fd", activated, cotangent_all, preferred_element_type=jnp.float32
        )
        grad_activated = jnp.einsum(
            "td,fd->tf", cotangent_all, full_down, preferred_element_type=jnp.float32
        )
        gelu_pull = jax.vjp(gelu_tanh, before)[1]
        grad_before = gelu_pull(grad_activated)[0].astype(jnp.bfloat16)
        grad_up = jnp.einsum(
            "td,tf->df", normed_two_all, grad_before, preferred_element_type=jnp.float32
        )
        grad_normed_two = lax.psum_scatter(
            slice_term(grad_before, full_up, "tf,df->td").astype(jnp.bfloat16),
            "tensor",
            scatter_dimension=0,
            tiled=True,
        ).astype(jnp.float32)
        second_pull = jax.vjp(layer_norm, middle, vectors[5], vectors[6])[1]
        middle_from_norm, gain_two_grad, shift_two_grad = second_pull(grad_normed_two)
        grad_middle = cotangent_rows.astype(jnp.float32) + middle_from_norm
        grad_middle_all = lax.all_gather(
            grad_middle.astype(jnp.bfloat16), "tensor", axis=0, tiled=True
        )
        grad_out = jnp.einsum(
            "tc,td->cd", context_low, grad_middle_all, preferred_element_type=jnp.float32
        )
        grad_context = jnp.einsum(
            "td,cd->tc", grad_middle_all, full_out, preferred_element_type=jnp.float32
        ).astype(jnp.bfloat16)
        grad_query, grad_key, grad_value = lax.map(
            backward_one,
            (
                query_seqs,
                key_seqs,
                value_seqs,
                grad_context.reshape(seqs_here, LEN, width_here),
                logsum,
                starts_here,
            ),
        )
        grad_stack = jnp.stack(
            [
                grad_query.reshape(group_rows, width_here),
                grad_key.reshape(group_rows, width_here),
                grad_value.reshape(group_rows, width_here),
            ]
        )
        grad_qkv = jnp.einsum(
            "td,cte->cde", normed_all, grad_stack, preferred_element_type=jnp.float32
        )
        grad_normed_one = lax.psum_scatter(
            slice_term(grad_stack, full_qkv, "cte,cde->td").astype(jnp.bfloat16),
            "tensor",
            scatter_dimension=0,
            tiled=True,
        ).astype(jnp.float32)
        first_pull = jax.vjp(layer_norm, token_rows, vectors[0], vectors[1])[1]
        token_from_norm, gain_one_grad, shift_one_grad = first_pull(grad_normed_one)
        input_grads.append(grad_middle + token_from_norm)
        query_bias = jnp.sum(grad_stack[0], axis=0, dtype=jnp.float32)
        value_bias = jnp.sum(grad_stack[2], axis=0, dtype=jnp.float32)
        up_bias = jnp.sum(grad_before, axis=0, dtype=jnp.float32)
        head_rows = jnp.stack(
            [
                gain_one_grad,
                shift_one_grad,
                placed(query_bias, tensor_rank * width_here, D),
                placed(value_bias, tensor_rank * width_here, D),
                jnp.sum(grad_middle, axis=0),
                gain_two_grad,
                shift_two_grad,
            ]
        )
        up_rows = placed(up_bias, tensor_rank * hidden_here, FF).reshape(4, D)
        tail_row = jnp.sum(cotangent_rows, axis=0, dtype=jnp.float32)[None, :]
        vector_total = vector_total + jnp.concatenate([head_rows, up_rows, tail_row], axis=0)
        shard_grads = (
            lax.psum_scatter(
                grad_qkv.astype(jnp.bfloat16), "dp", scatter_dimension=1, tiled=True
            ).astype(jnp.float32),
            lax.psum_scatter(
                grad_out.astype(jnp.bfloat16), "dp", scatter_dimension=1, tiled=True
            ).astype(jnp.float32),
            lax.psum_scatter(
                grad_up.astype(jnp.bfloat16), "dp", scatter_dimension=0, tiled=True
            ).astype(jnp.float32),
            lax.psum_scatter(
                grad_down.astype(jnp.bfloat16), "dp", scatter_dimension=1, tiled=True
            ).astype(jnp.float32),
        )
        grad_total = accumulate(grad_total, shard_grads)
    grad_qkv_shard, grad_out_shard, grad_up_shard, grad_down_shard = grad_total
    moment_qkv = MOMENTUM_DECAY * m_qkv + grad_qkv_shard
    moment_out = MOMENTUM_DECAY * m_out + grad_out_shard
    moment_up = MOMENTUM_DECAY * m_up + grad_up_shard
    moment_down = MOMENTUM_DECAY * m_down + grad_down_shard
    squares = jnp.concatenate(
        [
            jnp.sum(moment_qkv * moment_qkv, axis=(1, 2)),
            jnp.stack(
                [
                    jnp.sum(moment_out * moment_out),
                    jnp.sum(moment_up * moment_up),
                    jnp.sum(moment_down * moment_down),
                ]
            ),
        ]
    )
    vector_grad, square_total = lax.psum((vector_total, squares), ("dp", "tensor"))
    factors = lax.rsqrt(square_total + SQUARE_EPSILON)
    scaled_qkv = (moment_qkv * factors[0:3][:, None, None]).astype(jnp.bfloat16)
    scaled_out = (moment_out * factors[3]).astype(jnp.bfloat16)
    scaled_up = (moment_up * factors[4]).astype(jnp.bfloat16)
    scaled_down = (moment_down * factors[5]).astype(jnp.bfloat16)
    gathered_qkv, gathered_out, gathered_up, gathered_down = (
        lax.all_gather(scaled_qkv, "dp", axis=1, tiled=True),
        lax.all_gather(scaled_out, "dp", axis=1, tiled=True),
        lax.all_gather(scaled_up, "dp", axis=0, tiled=True),
        lax.all_gather(scaled_down, "dp", axis=1, tiled=True),
    )
    offset = shard_rank * shard_rows
    narrow_rows = jnp.concatenate([jnp.swapaxes(gathered_qkv, 1, 2), gathered_out[None]], axis=0)
    wide_rows = jnp.stack([gathered_up.T, gathered_down])
    for sweep_index in range(NS_ITERS):
        gram_share = lax.psum_scatter(
            gram_term(narrow_rows, wide_rows).astype(jnp.bfloat16),
            "tensor",
            scatter_dimension=0,
            tiled=True,
        )
        gram_matrix = lax.all_gather(gram_share, "tensor", axis=0, tiled=True)
        narrow_rows = schulz_step(narrow_rows, gram_matrix[:, 0:4])
        wide_rows = schulz_step(wide_rows, gram_matrix[:, 4:6])
    final_narrow = narrow_rows.astype(jnp.float32)
    final_wide = wide_rows.astype(jnp.float32)
    update_qkv = lax.dynamic_slice_in_dim(
        jnp.swapaxes(final_narrow[0:3], 1, 2), offset, shard_rows, 1
    )
    update_out = lax.dynamic_slice_in_dim(final_narrow[3], offset, shard_rows, 1)
    update_up = lax.dynamic_slice_in_dim(final_wide[0].T, offset, shard_rows, 0)
    update_down = lax.dynamic_slice_in_dim(final_wide[1], offset, shard_rows, 1)
    wide_factor = math.sqrt(FF / D)
    new_qkv = w_qkv - MATRIX_RATE * update_qkv
    new_out = w_out - MATRIX_RATE * update_out
    new_up = w_up - MATRIX_RATE * wide_factor * update_up
    new_down = w_down - MATRIX_RATE * wide_factor * update_down
    moment_vec = MOMENTUM_DECAY * m_vec + vector_grad
    new_vec = vectors - VECTOR_RATE * moment_vec * lax.rsqrt(
        jnp.mean(moment_vec * moment_vec, axis=1, keepdims=True) + SQUARE_EPSILON
    )
    return (
        jnp.stack(outputs_list),
        jnp.stack(input_grads),
        grad_qkv_shard,
        grad_out_shard,
        grad_up_shard,
        grad_down_shard,
        vector_grad,
        moment_qkv,
        moment_out,
        moment_up,
        moment_down,
        moment_vec,
        new_qkv,
        new_out,
        new_up,
        new_down,
        new_vec,
    )


def layout_grid(starts_ref, dist_ref):
    key_pos = lax.broadcasted_iota(jnp.int32, (LEN, LEN), 0)
    query_pos = lax.broadcasted_iota(jnp.int32, (LEN, LEN), 1)
    gap = query_pos - key_pos
    visible = gap >= 0
    for piece in range(NPIECE):
        start = starts_ref[piece]
        inside_key = (key_pos >= start) & (key_pos < start + PIECE)
        inside_query = (query_pos >= start) & (query_pos < start + PIECE)
        visible = visible | (inside_key & inside_query)
    dist_ref[...] = jnp.where(visible, jnp.abs(gap).astype(jnp.float32), -MASKED_SCORE)


def attend_fwd_kernel(starts_ref, slopes_ref, q_ref, k_ref, v_ref, ctx_ref, exps_ref, stat_ref, dist_ref):
    head = pl.program_id(0)

    @pl.when(head == 0)
    def _():
        layout_grid(starts_ref, dist_ref)

    slope = slopes_ref[head]
    keys = k_ref[0, 0, 0].T
    queries = q_ref[0, 0, 0] * (1.0 / math.sqrt(HD))
    for block in range(LEN // QB):
        span = min(LEN, QB * block + QB + PIECE)
        cols = slice(block * QB, block * QB + QB)
        scores = jnp.dot(keys[:span], queries[:, cols], preferred_element_type=jnp.float32)
        scores = scores - slope * dist_ref[:span, cols]
        top = jnp.max(scores, axis=0, keepdims=True)
        raw = jnp.exp(scores - top)
        inverse = 1.0 / jnp.sum(raw, axis=0, keepdims=True)
        low = raw.astype(jnp.bfloat16)
        exps_ref[0, :span, cols] = low
        context = jnp.dot(v_ref[0, 0, 0, :, :span], low, preferred_element_type=jnp.float32)
        ctx_ref[0, :, cols] = (context * inverse).astype(jnp.bfloat16)
        stat_ref[0, :, cols] = inverse


def attend_bwd_kernel(q_ref, k_ref, v_ref, ctx_ref, grad_ref, exps_ref, stat_ref, dq_ref, dk_ref, dv_ref, dk_sum, dv_sum):
    scale = 1.0 / math.sqrt(HD)
    keys_t = k_ref[0, 0, 0]
    values = v_ref[0, 0, 0].T
    queries = q_ref[0, 0, 0].T
    dk_sum[...] = jnp.zeros_like(dk_sum)
    dv_sum[...] = jnp.zeros_like(dv_sum)
    for block in reversed(range(LEN // QB)):
        span = min(LEN, QB * block + QB + PIECE)
        cols = slice(block * QB, block * QB + QB)
        grad = grad_ref[0, :, cols].astype(jnp.float32) * stat_ref[0, :, cols]
        inner = jnp.sum(grad * ctx_ref[0, :, cols].astype(jnp.float32), axis=0, keepdims=True)
        grad_low = grad.astype(jnp.bfloat16)
        exps = exps_ref[0, :span, cols]
        grad_probs = jnp.dot(values[:span], grad_low, preferred_element_type=jnp.float32)
        grad_scores = (exps.astype(jnp.float32) * (grad_probs - inner)).astype(jnp.bfloat16)
        dv_sum[:span, :] += jnp.dot(exps, grad_low.T, preferred_element_type=jnp.float32)
        dk_sum[:span, :] += jnp.dot(grad_scores, queries[cols], preferred_element_type=jnp.float32)
        dq = jnp.dot(keys_t[:, :span], grad_scores, preferred_element_type=jnp.float32)
        dq_ref[0, :, cols] = (dq * scale).astype(jnp.bfloat16)
    dk_ref[0] = (dk_sum[...] * scale).T.astype(jnp.bfloat16)
    dv_ref[0] = dv_sum[...].T.astype(jnp.bfloat16)


QB = 256


def part_spec(part, heads_each):
    return pl.BlockSpec((1, 1, 1, HD, LEN), lambda h: (h // heads_each, part, h % heads_each, 0, 0))


HEAD_ROWS = pl.BlockSpec((1, HD, LEN), lambda h: (h, 0, 0))
HEAD_GRID = pl.BlockSpec((1, LEN, LEN), lambda h: (h, 0, 0))
HEAD_STAT = pl.BlockSpec((1, 1, LEN), lambda h: (h, 0, 0))
SCALARS = pl.BlockSpec(memory_space=pltpu.SMEM)
VMEM_LIMIT = 56 * 1024 * 1024


def attention_forward(starts, slopes, packed):
    heads_each = packed.shape[2]
    return pl.pallas_call(
        attend_fwd_kernel,
        grid=(H,),
        in_specs=[SCALARS, SCALARS] + [part_spec(part, heads_each) for part in range(3)],
        out_specs=[HEAD_ROWS, HEAD_GRID, HEAD_STAT],
        out_shape=[
            jax.ShapeDtypeStruct((H, HD, LEN), jnp.bfloat16),
            jax.ShapeDtypeStruct((H, LEN, LEN), jnp.bfloat16),
            jax.ShapeDtypeStruct((H, 1, LEN), jnp.float32),
        ],
        scratch_shapes=[pltpu.VMEM((LEN, LEN), jnp.float32)],
        compiler_params=pltpu.CompilerParams(vmem_limit_bytes=VMEM_LIMIT),
        cost_estimate=pl.CostEstimate(flops=4 * LEN * LEN * D * 4, bytes_accessed=44 * 1024 * 1024, transcendentals=H * LEN * LEN),
    )(starts, slopes, packed, packed, packed)


def attention_backward(packed, context, grad_context, exps, stats):
    heads_each = packed.shape[2]
    return pl.pallas_call(
        attend_bwd_kernel,
        grid=(H,),
        in_specs=[part_spec(part, heads_each) for part in range(3)]
        + [HEAD_ROWS, HEAD_ROWS, HEAD_GRID, HEAD_STAT],
        out_specs=[HEAD_ROWS, HEAD_ROWS, HEAD_ROWS],
        out_shape=[jax.ShapeDtypeStruct((H, HD, LEN), jnp.bfloat16)] * 3,
        scratch_shapes=[pltpu.VMEM((LEN, HD), jnp.float32), pltpu.VMEM((LEN, HD), jnp.float32)],
        compiler_params=pltpu.CompilerParams(vmem_limit_bytes=VMEM_LIMIT),
        cost_estimate=pl.CostEstimate(flops=8 * LEN * LEN * D * 4, bytes_accessed=50 * 1024 * 1024, transcendentals=0),
    )(packed, packed, packed, context, grad_context, exps, stats)


SLOTS = 12
SLOT = 512
TILE = 256
MESH_IDS = pl.DeviceIdType.MESH


def handler_of(slot):
    wide = slot - 4
    square = slot < 4
    dp_index = jnp.where(square, jnp.where(slot < 2, 2, 12), 4 + 6 * (wide // 4) + wide % 2)
    tensor_index = jnp.where(square, slot % 2, (wide // 2) % 2)
    return dp_index, tensor_index


def muon_kernel(
    moments_ref,
    vec_ref,
    updates_ref,
    vec_out_ref,
    pieces,
    turned,
    vec_pieces,
    vec_sum,
    gram,
    gram_low,
    poly_low,
    half_low,
    chain_low,
    chain_next,
    out_half,
    in_half,
    local_sem,
    send_sem,
    recv_sem,
    half_send,
    half_recv,
):
    groups = lax.axis_size("dp")
    parts = lax.axis_size("tensor")
    count = groups * parts
    dp_me = lax.axis_index("dp")
    t_me = lax.axis_index("tensor")
    me = t_me * groups + dp_me
    is_square = (dp_me == 2) | (dp_me == 12)
    is_up = (dp_me == 4) | (dp_me == 5)
    is_down = (dp_me == 10) | (dp_me == 11)
    is_wide = is_up | is_down
    is_handler = is_square | is_wide
    wide_slot = jnp.where(is_up, 4 + (dp_me - 4), 8 + (dp_me - 10)) + 2 * t_me
    slot_me = jnp.where(is_square, t_me + jnp.where(dp_me == 12, 2, 0), wide_slot)
    slot_me = jnp.where(is_handler, slot_me, 0)

    barrier = pltpu.get_barrier_semaphore()

    def greet(step, carry):
        other = lax.rem(me + step, count)
        pl.semaphore_signal(
            barrier, inc=1, device_id=(lax.rem(other, groups), other // groups), device_id_type=MESH_IDS
        )
        return carry

    lax.fori_loop(1, count, greet, 0)
    pl.semaphore_wait(barrier, count - 1)

    def give(step, carry):
        slot = lax.rem(me + step, SLOTS)
        dp_to, t_to = handler_of(slot)
        away = (dp_to != dp_me) | (t_to != t_me)

        @pl.when(away)
        def _():
            pltpu.make_async_remote_copy(
                src_ref=vec_ref.at[slot],
                dst_ref=vec_pieces.at[me],
                send_sem=send_sem.at[1],
                recv_sem=recv_sem.at[1],
                device_id=(dp_to, t_to),
                device_id_type=MESH_IDS,
            ).start()
            pltpu.make_async_remote_copy(
                src_ref=moments_ref.at[slot],
                dst_ref=pieces.at[me],
                send_sem=send_sem.at[0],
                recv_sem=recv_sem.at[0],
                device_id=(dp_to, t_to),
                device_id_type=MESH_IDS,
            ).start()

        return carry

    lax.fori_loop(0, SLOTS, give, 0)

    def give_back(source, sem, target):
        def one(step, carry):
            other = lax.rem(me + step, count)
            pltpu.make_async_remote_copy(
                src_ref=source.at[other] if source is turned else source,
                dst_ref=target.at[slot_me],
                send_sem=send_sem.at[sem],
                recv_sem=recv_sem.at[sem],
                device_id=(lax.rem(other, groups), other // groups),
                device_id_type=MESH_IDS,
            ).start()
            return carry

        lax.fori_loop(1, count, one, 0)

    @pl.when(is_handler)
    def _():
        own = [
            pltpu.make_async_copy(vec_ref.at[slot_me], vec_pieces.at[me], local_sem.at[0]),
            pltpu.make_async_copy(moments_ref.at[slot_me], pieces.at[me], local_sem.at[1]),
        ]
        for copy in own:
            copy.start()
        for copy in own:
            copy.wait()
        rest = pl.ds(0, count - 1)
        pltpu.make_async_copy(vec_pieces.at[rest], vec_pieces.at[rest], recv_sem.at[1]).wait()
        vec_sum[...] = jnp.sum(vec_pieces[...], axis=0)
        give_back(vec_sum, 2, vec_out_ref)
        own_vec = pltpu.make_async_copy(vec_sum, vec_out_ref.at[slot_me], local_sem.at[0])
        own_vec.start()
        own_vec.wait()
        pltpu.make_async_copy(pieces.at[rest], pieces.at[rest], recv_sem.at[0]).wait()

        rows_of = TILE // 64

        def gram_tile(tile, carry):
            rows = pl.ds(pl.multiple_of(tile * TILE, TILE), TILE)
            total = jnp.zeros((TILE, D), jnp.float32)
            for part in range(parts):
                left = pieces[pl.ds(part * groups + tile * rows_of, rows_of)].reshape(TILE, SLOT)
                right = pieces[part * groups : (part + 1) * groups].reshape(D, SLOT)
                total += lax.dot_general(
                    left, right, (((1,), (1,)), ((), ())), preferred_element_type=jnp.float32
                )
            gram[rows, :] = total
            return carry

        lax.fori_loop(0, D // TILE, gram_tile, 0)

        @pl.when(is_wide)
        def _():
            core = lax.rem(dp_me, 2)
            half = D // 2
            mine = pl.ds(pl.multiple_of(core * half, half), half)
            theirs = pl.ds(pl.multiple_of((1 - core) * half, half), half)
            sibling = (dp_me + 1 - 2 * core, t_me)
            across = (dp_me, 1 - t_me)

            def exchange(stage, place):
                copy = pltpu.make_async_remote_copy(
                    src_ref=out_half.at[stage],
                    dst_ref=in_half.at[stage],
                    send_sem=half_send.at[stage],
                    recv_sem=half_recv.at[stage],
                    device_id=place,
                    device_id_type=MESH_IDS,
                )
                copy.start()
                copy.wait()

            out_half[0] = gram[theirs, :].astype(jnp.bfloat16)
            exchange(0, sibling)
            out_half[1] = (gram[mine, :] + in_half[0].astype(jnp.float32)).astype(jnp.bfloat16)
            exchange(1, across)
            total = out_half[1].astype(jnp.float32) + in_half[1].astype(jnp.float32)
            out_half[2] = total.astype(jnp.bfloat16)
            exchange(2, sibling)
            gram[mine, :] = out_half[2].astype(jnp.float32)
            gram[theirs, :] = in_half[2].astype(jnp.float32)

        def trace_tile(tile, total):
            rows = pl.ds(pl.multiple_of(tile * TILE, TILE), TILE)
            row_ids = lax.broadcasted_iota(jnp.int32, (TILE, D), 0) + tile * TILE
            col_ids = lax.broadcasted_iota(jnp.int32, (TILE, D), 1)
            diagonal = jnp.where(row_ids == col_ids, gram[rows, :], 0.0)
            return total + jnp.sum(jnp.sum(diagonal, axis=0, keepdims=True), axis=1, keepdims=True)

        square_total = lax.fori_loop(0, D // TILE, trace_tile, jnp.zeros((1, 1), jnp.float32))
        factor = lax.rsqrt(square_total + SQUARE_EPSILON)
        gram_low[...] = (gram[...] * (factor * factor)).astype(jnp.bfloat16)

        first, second, third = SCHULZ_FIRST, SCHULZ_SECOND, SCHULZ_THIRD

        def tiles(body):
            def one(tile, carry):
                body(pl.ds(pl.multiple_of(tile * TILE, TILE), TILE))
                return carry

            lax.fori_loop(0, D // TILE, one, 0)

        def mul(left, right):
            return jnp.dot(left, right, preferred_element_type=jnp.float32)

        chain = chain_low
        other = chain_next
        for sweep in range(NS_ITERS):
            target = chain if sweep == 0 else poly_low

            def poly(rows):
                square = mul(gram_low[rows, :], gram_low[...])
                grown = (second / first) * gram_low[rows, :].astype(jnp.float32) + (third / first) * square
                target[rows, :] = grown.astype(jnp.bfloat16)

            tiles(poly)
            if sweep > 0:

                def join(rows, chain=chain, other=other):
                    total = chain[rows, :].astype(jnp.float32) + poly_low[rows, :].astype(jnp.float32)
                    other[rows, :] = (total + mul(chain[rows, :], poly_low[...])).astype(jnp.bfloat16)

                tiles(join)
                chain, other = other, chain
            if sweep < NS_ITERS - 1:

                def half(rows):
                    grown = gram_low[rows, :].astype(jnp.float32) + mul(gram_low[rows, :], target[...])
                    half_low[rows, :] = grown.astype(jnp.bfloat16)

                def full(rows):
                    grown = half_low[rows, :].astype(jnp.float32) + mul(half_low[rows, :], target[...])
                    gram_low[rows, :] = (grown * (first * first)).astype(jnp.bfloat16)

                tiles(half)
                tiles(full)

        scale = factor * (first**NS_ITERS)

        def turn_tile(tile, carry):
            rows = pl.ds(pl.multiple_of(tile * TILE, TILE), TILE)
            for part in range(parts):
                at = pl.ds(part * groups + tile * rows_of, rows_of)
                whole = pieces[part * groups : (part + 1) * groups].reshape(D, SLOT)
                kept = pieces[at].reshape(TILE, SLOT).astype(jnp.float32)
                fresh = (kept + mul(chain[rows, :], whole)) * scale
                turned[at] = fresh.astype(jnp.bfloat16).reshape(rows_of, 64, SLOT)
            return carry

        lax.fori_loop(0, D // TILE, turn_tile, 0)
        give_back(turned, 3, updates_ref)
        own_turned = pltpu.make_async_copy(turned.at[me], updates_ref.at[slot_me], local_sem.at[1])
        own_turned.start()
        own_turned.wait()

    def finish(length):
        here = pl.ds(0, length)
        pltpu.make_async_copy(vec_ref.at[here], vec_ref.at[here], send_sem.at[1]).wait()
        pltpu.make_async_copy(moments_ref.at[here], moments_ref.at[here], send_sem.at[0]).wait()
        pltpu.make_async_copy(vec_out_ref.at[here], vec_out_ref.at[here], recv_sem.at[2]).wait()
        pltpu.make_async_copy(updates_ref.at[here], updates_ref.at[here], recv_sem.at[3]).wait()

    @pl.when(is_handler)
    def _():
        finish(SLOTS - 1)
        rest = pl.ds(0, count - 1)
        pltpu.make_async_copy(vec_pieces.at[rest], vec_pieces.at[rest], send_sem.at[2]).wait()
        pltpu.make_async_copy(turned.at[rest], turned.at[rest], send_sem.at[3]).wait()

    @pl.when(jnp.logical_not(is_handler))
    def _():
        finish(SLOTS)


def muon_call(moments, vec_parts):
    count = lax.axis_size("dp") * lax.axis_size("tensor")
    rows = moments.shape[1]
    vmem = pl.BlockSpec(memory_space=pltpu.VMEM)
    low = pltpu.VMEM((D, D), jnp.bfloat16)
    return pl.pallas_call(
        muon_kernel,
        in_specs=[vmem, vmem],
        out_specs=[vmem, vmem],
        out_shape=[
            jax.ShapeDtypeStruct(moments.shape, jnp.bfloat16),
            jax.ShapeDtypeStruct(vec_parts.shape, jnp.float32),
        ],
        scratch_shapes=[
            pltpu.VMEM((count, rows, SLOT), jnp.bfloat16),
            pltpu.VMEM((count, rows, SLOT), jnp.bfloat16),
            pltpu.VMEM((count,) + vec_parts.shape[1:], jnp.float32),
            pltpu.VMEM(vec_parts.shape[1:], jnp.float32),
            pltpu.VMEM((D, D), jnp.float32),
            low,
            low,
            low,
            low,
            low,
            pltpu.VMEM((3, D // 2, D), jnp.bfloat16),
            pltpu.VMEM((3, D // 2, D), jnp.bfloat16),
            pltpu.SemaphoreType.DMA((2,)),
            pltpu.SemaphoreType.DMA((4,)),
            pltpu.SemaphoreType.DMA((4,)),
            pltpu.SemaphoreType.DMA((3,)),
            pltpu.SemaphoreType.DMA((3,)),
        ],
        compiler_params=pltpu.CompilerParams(
            collective_id=1, has_side_effects=True, vmem_limit_bytes=VMEM_LIMIT
        ),
        cost_estimate=pl.CostEstimate(flops=12 * 2 * D**3, bytes_accessed=4 * 1024 * 1024, transcendentals=0),
    )(moments, vec_parts)


def by_slots(rows):
    return jnp.swapaxes(rows.reshape(rows.shape[0], -1, SLOT), 0, 1)


def from_slots(rows):
    return jnp.swapaxes(rows, 0, 1).reshape(rows.shape[1], -1)


def muon_step(
    shards, vector_total, w_qkv, w_out, w_up, w_down, vectors, m_qkv, m_out, m_up, m_down, m_vec
):
    grad_qkv_shard, grad_out_shard, grad_up_shard, grad_down_shard = shards
    moment_qkv = MOMENTUM_DECAY * m_qkv + grad_qkv_shard
    moment_out = MOMENTUM_DECAY * m_out + grad_out_shard
    moment_up = MOMENTUM_DECAY * m_up + grad_up_shard
    moment_down = MOMENTUM_DECAY * m_down + grad_down_shard
    slots = jnp.concatenate(
        [
            narrow(moment_qkv),
            narrow(moment_out).T[None],
            by_slots(narrow(moment_up)),
            by_slots(narrow(moment_down).T),
        ]
    )
    updates, vector_rows = muon_call(slots, vector_total.reshape(SLOTS, 8, 128))
    vector_grad = vector_rows.reshape(12, D)
    wide_factor = math.sqrt(FF / D)
    new_qkv = w_qkv - MATRIX_RATE * updates[0:3].astype(jnp.float32)
    new_out = w_out - MATRIX_RATE * updates[3].T.astype(jnp.float32)
    new_up = w_up - MATRIX_RATE * wide_factor * from_slots(updates[4:8]).astype(jnp.float32)
    new_down = w_down - MATRIX_RATE * wide_factor * from_slots(updates[8:12]).T.astype(jnp.float32)
    moment_vec = MOMENTUM_DECAY * m_vec + vector_grad
    new_vec = vectors - VECTOR_RATE * moment_vec * lax.rsqrt(
        jnp.mean(moment_vec * moment_vec, axis=1, keepdims=True) + SQUARE_EPSILON
    )
    return (
        grad_qkv_shard,
        grad_out_shard,
        grad_up_shard,
        grad_down_shard,
        vector_grad,
        moment_qkv,
        moment_out,
        moment_up,
        moment_down,
        moment_vec,
        new_qkv,
        new_out,
        new_up,
        new_down,
        new_vec,
    )


BOTH = ("tensor", "dp")
SWAP = [(0, 1), (1, 0)]


def narrow(rows):
    return rows.astype(jnp.bfloat16)


def contract(left, right, left_dim, right_dim):
    return lax.dot_general(
        left, right, (((left_dim,), (right_dim,)), ((), ())), preferred_element_type=jnp.float32
    )


def swap_halves(mine, rank):
    rows = mine.shape[0] // 2
    kept = lax.dynamic_slice_in_dim(mine, rank * rows, rows, 0)
    sent = lax.dynamic_slice_in_dim(mine, (1 - rank) * rows, rows, 0)
    got = lax.ppermute(sent, "tensor", SWAP)
    return jnp.where(rank == 0, jnp.stack([kept, got]), jnp.stack([got, kept]))


def join_halves(pair, rank):
    kept = lax.dynamic_index_in_dim(pair, rank, 0, keepdims=False)
    sent = lax.dynamic_index_in_dim(pair, 1 - rank, 0, keepdims=False)
    got = lax.ppermute(sent, "tensor", SWAP)
    return jnp.where(rank == 0, jnp.concatenate([kept, got]), jnp.concatenate([got, kept]))


def sequence_step(
    tokens,
    cotangent,
    piece_starts,
    w_qkv,
    w_out,
    w_up,
    w_down,
    vectors,
    m_qkv,
    m_out,
    m_up,
    m_down,
    m_vec,
):
    rank = lax.axis_index("tensor")
    parts = lax.axis_size("tensor")
    width = D // parts
    hidden = FF // parts
    shard_rows = w_qkv.shape[1]
    slopes = jnp.exp2(-8.0 * jnp.arange(1, H + 1, dtype=jnp.float32) / H)

    def spread(rows):
        whole = lax.all_gather(rows, BOTH, axis=0, tiled=True)
        return whole.reshape(parts, D, rows.shape[1])

    def collect(grads):
        return lax.psum_scatter(
            grads.reshape(parts * D, -1), BOTH, scatter_dimension=0, tiled=True
        ).astype(jnp.float32)

    full_qkv = spread(narrow(jnp.swapaxes(w_qkv, 0, 1)).reshape(shard_rows, 3 * width))
    token_rows = join_halves(tokens, rank).astype(jnp.float32)
    full_out = spread(narrow(w_out.T))
    full_up = spread(narrow(w_up))
    full_down = spread(narrow(w_down.T))
    cotangent_low = join_halves(cotangent, rank)
    cotangent_rows = cotangent_low.astype(jnp.float32)
    starts = lax.dynamic_slice_in_dim(piece_starts[:, 0], rank, 1, 0)[0]

    normed_one = narrow(layer_norm(token_rows, vectors[0], vectors[1]))
    shifts = jnp.stack([vectors[2], jnp.zeros((D,), jnp.float32), vectors[3]])
    shifts = jnp.swapaxes(shifts.reshape(3, parts, width), 0, 1).reshape(parts, 3 * width, 1)
    packed = jnp.stack(
        [narrow(contract(full_qkv[part], normed_one, 0, 1) + shifts[part]) for part in range(parts)]
    )
    packed = packed.reshape(parts, 3, width // HD, HD, LEN)
    context, exps, stats = attention_forward(starts, slopes, packed)
    context_rows = context.reshape(parts, width, LEN)
    attended = sum(contract(context_rows[part], full_out[part], 0, 1) for part in range(parts))
    middle = token_rows + attended + vectors[4]
    normed_two = narrow(layer_norm(middle, vectors[5], vectors[6]))
    up_shift = vectors[7:11].reshape(parts, hidden)
    before = [contract(normed_two, full_up[part], 1, 0) + up_shift[part] for part in range(parts)]
    activated = [narrow(gelu_tanh(rows)) for rows in before]
    expanded = sum(contract(activated[part], full_down[part], 1, 1) for part in range(parts))
    block_rows = narrow(middle + expanded + vectors[11])

    grad_down = jnp.stack([narrow(contract(cotangent_low, rows, 0, 0)) for rows in activated])
    grad_before = []
    for part in range(parts):
        grad_activated = contract(cotangent_low, full_down[part], 1, 0)
        gelu_pull = jax.vjp(gelu_tanh, before[part])[1]
        grad_before.append(narrow(gelu_pull(grad_activated)[0]))
    grad_up = jnp.stack([narrow(contract(normed_two, rows, 0, 0)) for rows in grad_before])
    grad_down_shard = collect(grad_down)
    grad_up_shard = collect(grad_up)
    grad_normed_two = sum(contract(grad_before[part], full_up[part], 1, 1) for part in range(parts))
    second_pull = jax.vjp(layer_norm, middle, vectors[5], vectors[6])[1]
    middle_from_norm, gain_two_grad, shift_two_grad = second_pull(grad_normed_two)
    grad_middle = cotangent_rows + middle_from_norm
    grad_middle_low = narrow(grad_middle)
    grad_out = jnp.stack(
        [narrow(contract(grad_middle_low, context_rows[part], 0, 1)) for part in range(parts)]
    )
    grad_out_shard = collect(grad_out)
    grad_context = jnp.stack(
        [narrow(contract(full_out[part], grad_middle_low, 0, 1)) for part in range(parts)]
    ).reshape(H, HD, LEN)
    grad_parts = attention_backward(packed, context, grad_context, exps, stats)
    grad_packed = jnp.stack([rows.reshape(parts, width, LEN) for rows in grad_parts], axis=1)
    grad_packed = grad_packed.reshape(parts, 3 * width, LEN)
    grad_qkv = jnp.stack([narrow(contract(normed_one, grad_packed[part], 0, 1)) for part in range(parts)])
    grad_qkv_shard = collect(grad_qkv)
    grad_normed_one = sum(contract(grad_packed[part], full_qkv[part], 0, 1) for part in range(parts))
    first_pull = jax.vjp(layer_norm, token_rows, vectors[0], vectors[1])[1]
    token_from_norm, gain_one_grad, shift_one_grad = first_pull(grad_normed_one)
    grad_token_rows = grad_middle + token_from_norm
    output_pair = swap_halves(block_rows, rank)
    token_pair = swap_halves(narrow(grad_token_rows), rank).astype(jnp.float32)

    row_sums = [
        jnp.sum(rows.astype(jnp.float32), axis=2).reshape(D) for rows in (grad_parts[0], grad_parts[2])
    ]
    up_bias = jnp.concatenate([jnp.sum(rows, axis=0, dtype=jnp.float32) for rows in grad_before])
    vector_total = jnp.concatenate(
        [
            jnp.stack(
                [
                    gain_one_grad,
                    shift_one_grad,
                    row_sums[0],
                    row_sums[1],
                    jnp.sum(grad_middle, axis=0),
                    gain_two_grad,
                    shift_two_grad,
                ]
            ),
            up_bias.reshape(4, D),
            jnp.sum(cotangent_rows, axis=0)[None],
        ]
    )
    grad_qkv_shard = jnp.swapaxes(grad_qkv_shard.reshape(shard_rows, 3, width), 0, 1)
    shards = (grad_qkv_shard, grad_out_shard.T, grad_up_shard, grad_down_shard.T)
    outputs = muon_step(shards, vector_total, w_qkv, w_out, w_up, w_down, vectors, m_qkv, m_out, m_up, m_down, m_vec)
    return (output_pair, token_pair) + outputs


def solution(mesh):
    in_specs = (
        P(None, ("dp", "tensor"), None),
        P(None, ("dp", "tensor"), None),
        P(None, "dp", None),
        P(None, "dp", "tensor"),
        P("tensor", "dp"),
        P("dp", "tensor"),
        P("tensor", "dp"),
        P(),
        P(None, "dp", "tensor"),
        P("tensor", "dp"),
        P("dp", "tensor"),
        P("tensor", "dp"),
        P(),
    )
    out_specs = (
        P(None, ("dp", "tensor"), None),
        P(None, ("dp", "tensor"), None),
        P(None, "dp", "tensor"),
        P("tensor", "dp"),
        P("dp", "tensor"),
        P("tensor", "dp"),
        P(),
        P(None, "dp", "tensor"),
        P("tensor", "dp"),
        P("dp", "tensor"),
        P("tensor", "dp"),
        P(),
        P(None, "dp", "tensor"),
        P("tensor", "dp"),
        P("dp", "tensor"),
        P("tensor", "dp"),
        P(),
    )
    groups_fit = mesh.shape["tensor"] == MB and mesh.shape["dp"] == 16

    def pick(*arrays):
        if groups_fit and arrays[2].shape[1] == 1:
            return sequence_step(*arrays)
        return on_device(*arrays)

    return jax.shard_map(
        pick, mesh=mesh, in_specs=in_specs, out_specs=out_specs, check_vma=False
    )
```

```python
import math

import jax
import jax.numpy as jnp
from jax import lax
from jax.experimental import pallas as pl
from jax.experimental.pallas import tpu as pltpu
from jax.sharding import PartitionSpec as P

D = 1024
H = 16
HD = 64
FF = 4096
LEN = 1024
PIECE = 256
NPIECE = 2
MB = 2
NS_ITERS = 3


NORM_EPSILON = 1e-05
SQUARE_EPSILON = 1e-06
MASKED_SCORE = -1e30
SCHULZ_FIRST = 3.4445
SCHULZ_SECOND = -4.775
SCHULZ_THIRD = 2.0315
MOMENTUM_DECAY = 0.5
MATRIX_RATE = 0.5
VECTOR_RATE = 0.05


def layer_norm(inputs, gain_row, shift_row):
    average = jnp.mean(inputs, axis=-1, keepdims=True)
    centered = inputs - average
    variance = jnp.mean(centered * centered, axis=-1, keepdims=True)
    return centered * lax.rsqrt(variance + NORM_EPSILON) * gain_row + shift_row


def gelu_tanh(inputs):
    return jax.nn.gelu(inputs, approximate=True)


def score_layout(starts, slopes):
    positions = jnp.arange(LEN, dtype=jnp.int32)
    inside = (positions[None, :] >= starts[:, None]) & (
        positions[None, :] < starts[:, None] + PIECE
    )
    labels = jnp.arange(1, NPIECE + 1, dtype=jnp.int32)
    piece_label = jnp.sum(jnp.where(inside, labels[:, None], 0), axis=0)
    same_piece = (piece_label[:, None] == piece_label[None, :]) & (piece_label[:, None] > 0)
    visible = (positions[None, :] <= positions[:, None]) | same_piece
    distance = jnp.abs(positions[:, None] - positions[None, :]).astype(jnp.float32)
    penalty = -slopes[:, None, None] * distance[None, :, :]
    return (visible, penalty)


def head_scores(query_heads, key_heads, starts, slopes):
    visible, penalty = score_layout(starts, slopes)
    raw_scores = jnp.einsum(
        "qhd,khd->hqk", query_heads, key_heads, preferred_element_type=jnp.float32
    )
    scores = raw_scores * (1.0 / math.sqrt(HD)) + penalty
    return jnp.where(visible[None, :, :], scores, MASKED_SCORE)


def attend_forward(element, slopes):
    query_seq, key_seq, value_seq, starts = element
    heads_here = slopes.shape[0]
    query_heads = query_seq.reshape(LEN, heads_here, HD)
    key_heads = key_seq.reshape(LEN, heads_here, HD)
    value_heads = value_seq.reshape(LEN, heads_here, HD)
    scores = head_scores(query_heads, key_heads, starts, slopes)
    maximum = jnp.max(scores, axis=-1, keepdims=True)
    weights_raw = jnp.exp(scores - maximum)
    denominator = jnp.sum(weights_raw, axis=-1, keepdims=True)
    probabilities = weights_raw / denominator
    context = jnp.einsum(
        "hqk,khd->qhd",
        probabilities.astype(jnp.bfloat16),
        value_heads,
        preferred_element_type=jnp.float32,
    )
    logsum = (maximum + jnp.log(denominator))[..., 0]
    return (context.reshape(LEN, heads_here * HD), logsum)


def attend_backward(element, slopes):
    query_seq, key_seq, value_seq, context_grad, logsum, starts = element
    heads_here = slopes.shape[0]
    query_heads = query_seq.reshape(LEN, heads_here, HD)
    key_heads = key_seq.reshape(LEN, heads_here, HD)
    value_heads = value_seq.reshape(LEN, heads_here, HD)
    grad_heads = context_grad.reshape(LEN, heads_here, HD)
    scores = head_scores(query_heads, key_heads, starts, slopes)
    probabilities = jnp.exp(scores - logsum[..., None])
    grad_probs = jnp.einsum(
        "qhd,khd->hqk", grad_heads, value_heads, preferred_element_type=jnp.float32
    )
    inner_sum = jnp.sum(probabilities * grad_probs, axis=-1, keepdims=True)
    grad_scores = (probabilities * (grad_probs - inner_sum)).astype(jnp.bfloat16)
    scale_factor = 1.0 / math.sqrt(HD)
    grad_query = (
        jnp.einsum("hqk,khd->qhd", grad_scores, key_heads, preferred_element_type=jnp.float32)
        * scale_factor
    )
    grad_key = (
        jnp.einsum("hqk,qhd->khd", grad_scores, query_heads, preferred_element_type=jnp.float32)
        * scale_factor
    )
    grad_value = jnp.einsum(
        "hqk,qhd->khd",
        probabilities.astype(jnp.bfloat16),
        grad_heads,
        preferred_element_type=jnp.float32,
    )
    width_here = heads_here * HD
    return (
        grad_query.astype(jnp.bfloat16).reshape(LEN, width_here),
        grad_key.astype(jnp.bfloat16).reshape(LEN, width_here),
        grad_value.astype(jnp.bfloat16).reshape(LEN, width_here),
    )


def placed(values, offset, length):
    return lax.dynamic_update_slice_in_dim(jnp.zeros((length,), jnp.float32), values, offset, 0)


def accumulate(totals, addend):
    if totals is None:
        return addend
    return tuple((former + latter for former, latter in zip(totals, addend)))


def gram_term(narrow_rows, wide_rows):
    part_narrow = jnp.einsum(
        "mrc,mrd->cmd", narrow_rows, narrow_rows, preferred_element_type=jnp.float32
    )
    part_wide = jnp.einsum("mrc,mrd->cmd", wide_rows, wide_rows, preferred_element_type=jnp.float32)
    return jnp.concatenate([part_narrow, part_wide], axis=1)


def schulz_step(state, gram_matrix):
    turned = jnp.einsum("mrc,cmd->mrd", state, gram_matrix, preferred_element_type=jnp.float32)
    mixed = (SCHULZ_SECOND * state.astype(jnp.float32) + SCHULZ_THIRD * turned).astype(jnp.bfloat16)
    return (
        SCHULZ_FIRST * state.astype(jnp.float32)
        + jnp.einsum("mrc,cmd->mrd", mixed, gram_matrix, preferred_element_type=jnp.float32)
    ).astype(jnp.bfloat16)


def slice_term(source, weights, pattern):
    return jnp.einsum(pattern, source, weights, preferred_element_type=jnp.float32)


def on_device(
    tokens,
    cotangent,
    piece_starts,
    w_qkv,
    w_out,
    w_up,
    w_down,
    vectors,
    m_qkv,
    m_out,
    m_up,
    m_down,
    m_vec,
):
    tensor_count = lax.axis_size("tensor")
    tensor_rank = lax.axis_index("tensor")
    shard_rank = lax.axis_index("dp")
    heads_here = H // tensor_count
    width_here = heads_here * HD
    hidden_here = FF // tensor_count
    rows_here = tokens.shape[1]
    group_rows = rows_here * tensor_count
    seqs_here = piece_starts.shape[1]
    shard_rows = w_qkv.shape[1]
    head_ids = tensor_rank * heads_here + jnp.arange(heads_here, dtype=jnp.int32) + 1
    slopes = jnp.exp2(-8.0 * head_ids.astype(jnp.float32) / H)
    query_shift = lax.dynamic_slice_in_dim(vectors[2], tensor_rank * width_here, width_here, 0)
    value_shift = lax.dynamic_slice_in_dim(vectors[3], tensor_rank * width_here, width_here, 0)
    up_shift = lax.dynamic_slice_in_dim(
        vectors[7:11].reshape(FF), tensor_rank * hidden_here, hidden_here, 0
    )
    low_qkv = w_qkv.astype(jnp.bfloat16)
    low_out = w_out.astype(jnp.bfloat16)
    low_up = w_up.astype(jnp.bfloat16)
    low_down = w_down.astype(jnp.bfloat16)
    outputs_list = []
    input_grads = []
    vector_total = jnp.zeros((12, D), jnp.float32)
    grad_total = None

    def forward_one(element):
        return attend_forward(element, slopes)

    def backward_one(element):
        return attend_backward(element, slopes)

    for batch_index in range(MB):
        full_qkv, full_out, full_up, full_down = (
            lax.all_gather(low_qkv, "dp", axis=1, tiled=True),
            lax.all_gather(low_out, "dp", axis=1, tiled=True),
            lax.all_gather(low_up, "dp", axis=0, tiled=True),
            lax.all_gather(low_down, "dp", axis=1, tiled=True),
        )
        token_rows = tokens[batch_index].astype(jnp.float32)
        cotangent_rows = cotangent[batch_index]
        normed_one = layer_norm(token_rows, vectors[0], vectors[1])
        normed_all, cotangent_all = (
            lax.all_gather(normed_one.astype(jnp.bfloat16), "tensor", axis=0, tiled=True),
            lax.all_gather(cotangent_rows, "tensor", axis=0, tiled=True),
        )
        projected = jnp.einsum(
            "td,cde->cte", normed_all, full_qkv, preferred_element_type=jnp.float32
        )
        query_low = (projected[0] + query_shift).astype(jnp.bfloat16)
        key_low = projected[1].astype(jnp.bfloat16)
        value_low = (projected[2] + value_shift).astype(jnp.bfloat16)
        query_seqs = query_low.reshape(seqs_here, LEN, width_here)
        key_seqs = key_low.reshape(seqs_here, LEN, width_here)
        value_seqs = value_low.reshape(seqs_here, LEN, width_here)
        starts_here = piece_starts[batch_index]
        context_seq, logsum = lax.map(forward_one, (query_seqs, key_seqs, value_seqs, starts_here))
        context_low = context_seq.reshape(group_rows, width_here).astype(jnp.bfloat16)
        attended = lax.psum_scatter(
            slice_term(context_low, full_out, "tc,cd->td").astype(jnp.bfloat16),
            "tensor",
            scatter_dimension=0,
            tiled=True,
        ).astype(jnp.float32)
        middle = token_rows + attended + vectors[4]
        normed_two = layer_norm(middle, vectors[5], vectors[6])
        normed_two_all = lax.all_gather(
            normed_two.astype(jnp.bfloat16), "tensor", axis=0, tiled=True
        )
        before = jnp.dot(normed_two_all, full_up, preferred_element_type=jnp.float32) + up_shift
        activated = gelu_tanh(before).astype(jnp.bfloat16)
        expanded = lax.psum_scatter(
            slice_term(activated, full_down, "tf,fd->td").astype(jnp.bfloat16),
            "tensor",
            scatter_dimension=0,
            tiled=True,
        ).astype(jnp.float32)
        outputs_list.append((middle + expanded + vectors[11]).astype(jnp.bfloat16))
        grad_down = jnp.einsum(
            "tf,td->fd", activated, cotangent_all, preferred_element_type=jnp.float32
        )
        grad_activated = jnp.einsum(
            "td,fd->tf", cotangent_all, full_down, preferred_element_type=jnp.float32
        )
        gelu_pull = jax.vjp(gelu_tanh, before)[1]
        grad_before = gelu_pull(grad_activated)[0].astype(jnp.bfloat16)
        grad_up = jnp.einsum(
            "td,tf->df", normed_two_all, grad_before, preferred_element_type=jnp.float32
        )
        grad_normed_two = lax.psum_scatter(
            slice_term(grad_before, full_up, "tf,df->td").astype(jnp.bfloat16),
            "tensor",
            scatter_dimension=0,
            tiled=True,
        ).astype(jnp.float32)
        second_pull = jax.vjp(layer_norm, middle, vectors[5], vectors[6])[1]
        middle_from_norm, gain_two_grad, shift_two_grad = second_pull(grad_normed_two)
        grad_middle = cotangent_rows.astype(jnp.float32) + middle_from_norm
        grad_middle_all = lax.all_gather(
            grad_middle.astype(jnp.bfloat16), "tensor", axis=0, tiled=True
        )
        grad_out = jnp.einsum(
            "tc,td->cd", context_low, grad_middle_all, preferred_element_type=jnp.float32
        )
        grad_context = jnp.einsum(
            "td,cd->tc", grad_middle_all, full_out, preferred_element_type=jnp.float32
        ).astype(jnp.bfloat16)
        grad_query, grad_key, grad_value = lax.map(
            backward_one,
            (
                query_seqs,
                key_seqs,
                value_seqs,
                grad_context.reshape(seqs_here, LEN, width_here),
                logsum,
                starts_here,
            ),
        )
        grad_stack = jnp.stack(
            [
                grad_query.reshape(group_rows, width_here),
                grad_key.reshape(group_rows, width_here),
                grad_value.reshape(group_rows, width_here),
            ]
        )
        grad_qkv = jnp.einsum(
            "td,cte->cde", normed_all, grad_stack, preferred_element_type=jnp.float32
        )
        grad_normed_one = lax.psum_scatter(
            slice_term(grad_stack, full_qkv, "cte,cde->td").astype(jnp.bfloat16),
            "tensor",
            scatter_dimension=0,
            tiled=True,
        ).astype(jnp.float32)
        first_pull = jax.vjp(layer_norm, token_rows, vectors[0], vectors[1])[1]
        token_from_norm, gain_one_grad, shift_one_grad = first_pull(grad_normed_one)
        input_grads.append(grad_middle + token_from_norm)
        query_bias = jnp.sum(grad_stack[0], axis=0, dtype=jnp.float32)
        value_bias = jnp.sum(grad_stack[2], axis=0, dtype=jnp.float32)
        up_bias = jnp.sum(grad_before, axis=0, dtype=jnp.float32)
        head_rows = jnp.stack(
            [
                gain_one_grad,
                shift_one_grad,
                placed(query_bias, tensor_rank * width_here, D),
                placed(value_bias, tensor_rank * width_here, D),
                jnp.sum(grad_middle, axis=0),
                gain_two_grad,
                shift_two_grad,
            ]
        )
        up_rows = placed(up_bias, tensor_rank * hidden_here, FF).reshape(4, D)
        tail_row = jnp.sum(cotangent_rows, axis=0, dtype=jnp.float32)[None, :]
        vector_total = vector_total + jnp.concatenate([head_rows, up_rows, tail_row], axis=0)
        shard_grads = (
            lax.psum_scatter(
                grad_qkv.astype(jnp.bfloat16), "dp", scatter_dimension=1, tiled=True
            ).astype(jnp.float32),
            lax.psum_scatter(
                grad_out.astype(jnp.bfloat16), "dp", scatter_dimension=1, tiled=True
            ).astype(jnp.float32),
            lax.psum_scatter(
                grad_up.astype(jnp.bfloat16), "dp", scatter_dimension=0, tiled=True
            ).astype(jnp.float32),
            lax.psum_scatter(
                grad_down.astype(jnp.bfloat16), "dp", scatter_dimension=1, tiled=True
            ).astype(jnp.float32),
        )
        grad_total = accumulate(grad_total, shard_grads)
    grad_qkv_shard, grad_out_shard, grad_up_shard, grad_down_shard = grad_total
    moment_qkv = MOMENTUM_DECAY * m_qkv + grad_qkv_shard
    moment_out = MOMENTUM_DECAY * m_out + grad_out_shard
    moment_up = MOMENTUM_DECAY * m_up + grad_up_shard
    moment_down = MOMENTUM_DECAY * m_down + grad_down_shard
    squares = jnp.concatenate(
        [
            jnp.sum(moment_qkv * moment_qkv, axis=(1, 2)),
            jnp.stack(
                [
                    jnp.sum(moment_out * moment_out),
                    jnp.sum(moment_up * moment_up),
                    jnp.sum(moment_down * moment_down),
                ]
            ),
        ]
    )
    vector_grad, square_total = lax.psum((vector_total, squares), ("dp", "tensor"))
    factors = lax.rsqrt(square_total + SQUARE_EPSILON)
    scaled_qkv = (moment_qkv * factors[0:3][:, None, None]).astype(jnp.bfloat16)
    scaled_out = (moment_out * factors[3]).astype(jnp.bfloat16)
    scaled_up = (moment_up * factors[4]).astype(jnp.bfloat16)
    scaled_down = (moment_down * factors[5]).astype(jnp.bfloat16)
    gathered_qkv, gathered_out, gathered_up, gathered_down = (
        lax.all_gather(scaled_qkv, "dp", axis=1, tiled=True),
        lax.all_gather(scaled_out, "dp", axis=1, tiled=True),
        lax.all_gather(scaled_up, "dp", axis=0, tiled=True),
        lax.all_gather(scaled_down, "dp", axis=1, tiled=True),
    )
    offset = shard_rank * shard_rows
    narrow_rows = jnp.concatenate([jnp.swapaxes(gathered_qkv, 1, 2), gathered_out[None]], axis=0)
    wide_rows = jnp.stack([gathered_up.T, gathered_down])
    for sweep_index in range(NS_ITERS):
        gram_share = lax.psum_scatter(
            gram_term(narrow_rows, wide_rows).astype(jnp.bfloat16),
            "tensor",
            scatter_dimension=0,
            tiled=True,
        )
        gram_matrix = lax.all_gather(gram_share, "tensor", axis=0, tiled=True)
        narrow_rows = schulz_step(narrow_rows, gram_matrix[:, 0:4])
        wide_rows = schulz_step(wide_rows, gram_matrix[:, 4:6])
    final_narrow = narrow_rows.astype(jnp.float32)
    final_wide = wide_rows.astype(jnp.float32)
    update_qkv = lax.dynamic_slice_in_dim(
        jnp.swapaxes(final_narrow[0:3], 1, 2), offset, shard_rows, 1
    )
    update_out = lax.dynamic_slice_in_dim(final_narrow[3], offset, shard_rows, 1)
    update_up = lax.dynamic_slice_in_dim(final_wide[0].T, offset, shard_rows, 0)
    update_down = lax.dynamic_slice_in_dim(final_wide[1], offset, shard_rows, 1)
    wide_factor = math.sqrt(FF / D)
    new_qkv = w_qkv - MATRIX_RATE * update_qkv
    new_out = w_out - MATRIX_RATE * update_out
    new_up = w_up - MATRIX_RATE * wide_factor * update_up
    new_down = w_down - MATRIX_RATE * wide_factor * update_down
    moment_vec = MOMENTUM_DECAY * m_vec + vector_grad
    new_vec = vectors - VECTOR_RATE * moment_vec * lax.rsqrt(
        jnp.mean(moment_vec * moment_vec, axis=1, keepdims=True) + SQUARE_EPSILON
    )
    return (
        jnp.stack(outputs_list),
        jnp.stack(input_grads),
        grad_qkv_shard,
        grad_out_shard,
        grad_up_shard,
        grad_down_shard,
        vector_grad,
        moment_qkv,
        moment_out,
        moment_up,
        moment_down,
        moment_vec,
        new_qkv,
        new_out,
        new_up,
        new_down,
        new_vec,
    )


QB = 256
PAIR = 2 * HD
PAIRS = D // PAIR
VMEM_LIMIT = 56 * 1024 * 1024


def layout_grid(starts_ref, dist_ref):
    key_pos = lax.broadcasted_iota(jnp.int32, (LEN, LEN), 0)
    query_pos = lax.broadcasted_iota(jnp.int32, (LEN, LEN), 1)
    gap = query_pos - key_pos
    visible = gap >= 0
    for piece in range(NPIECE):
        start = starts_ref[piece]
        inside_key = (key_pos >= start) & (key_pos < start + PIECE)
        inside_query = (query_pos >= start) & (query_pos < start + PIECE)
        visible = visible | (inside_key & inside_query)
    dist_ref[...] = jnp.where(visible, jnp.abs(gap).astype(jnp.float32), -MASKED_SCORE)


def only_rows(pair, half):
    rows = lax.broadcasted_iota(jnp.int32, pair.shape, 0)
    return jnp.where((rows >= HD) if half else (rows < HD), pair, jnp.zeros_like(pair))


def only_cols(pair, half):
    cols = lax.broadcasted_iota(jnp.int32, pair.shape, 1)
    return jnp.where((cols >= HD) if half else (cols < HD), pair, jnp.zeros_like(pair))


def mul(left, right):
    return jnp.dot(left, right, preferred_element_type=jnp.float32)


def attend_fwd_kernel(starts_ref, slopes_ref, packed_ref, ctx_ref, exps_ref, stat_ref, dist_ref, ctx_t):
    pair = pl.program_id(0)

    @pl.when(pair == 0)
    def _():
        layout_grid(starts_ref, dist_ref)

    keys = packed_ref[:, PAIR : 2 * PAIR]
    values_t = packed_ref[:, 2 * PAIR :].T
    queries_t = (packed_ref[:, :PAIR] * (1.0 / math.sqrt(HD))).T
    for half in (0, 1):
        slope = slopes_ref[2 * pair + half]
        queries = only_rows(queries_t, half)
        heads = slice(half * HD, half * HD + HD)
        for block in range(LEN // QB):
            span = min(LEN, QB * block + QB + PIECE)
            cols = slice(block * QB, block * QB + QB)
            scores = mul(keys[:span], queries[:, cols]) - slope * dist_ref[:span, cols]
            top = jnp.max(scores, axis=0, keepdims=True)
            raw = jnp.exp(scores - top)
            inverse = 1.0 / jnp.sum(raw, axis=0, keepdims=True)
            low = raw.astype(jnp.bfloat16)
            exps_ref[half, :span, cols] = low
            ctx_t[heads, cols] = mul(values_t[heads, :span], low) * inverse
            stat_ref[0, half : half + 1, cols] = inverse
    ctx_ref[...] = ctx_t[...].T.astype(jnp.bfloat16)


def attend_bwd_kernel(packed_ref, ctx_ref, grad_ref, exps_ref, stat_ref, out_ref, dq_t, dk_sum, dv_sum):
    scale = 1.0 / math.sqrt(HD)
    queries = packed_ref[:, :PAIR]
    keys_t = packed_ref[:, PAIR : 2 * PAIR].T
    values = packed_ref[:, 2 * PAIR :]
    grads_t = grad_ref[...].T.astype(jnp.float32)
    context_t = ctx_ref[...].T.astype(jnp.float32)
    scaled = []
    inner_rows = []
    for half in (0, 1):
        heads = slice(half * HD, half * HD + HD)
        scaled.append(grads_t[heads] * stat_ref[0, half : half + 1, :])
        inner_rows.append(jnp.sum(scaled[half] * context_t[heads], axis=0, keepdims=True))
    scaled_t = jnp.concatenate(scaled, axis=0).astype(jnp.bfloat16)
    scaled_rows = scaled_t.T
    dk_sum[...] = jnp.zeros_like(dk_sum)
    dv_sum[...] = jnp.zeros_like(dv_sum)
    for half in (0, 1):
        heads = slice(half * HD, half * HD + HD)
        half_t = only_rows(scaled_t, half)
        half_rows = only_cols(scaled_rows, half)
        half_queries = only_cols(queries, half)
        for block in range(LEN // QB):
            span = min(LEN, QB * block + QB + PIECE)
            cols = slice(block * QB, block * QB + QB)
            exps = exps_ref[half, :span, cols]
            grad_probs = mul(values[:span], half_t[:, cols])
            grad_scores = (exps.astype(jnp.float32) * (grad_probs - inner_rows[half][:, cols])).astype(jnp.bfloat16)
            dv_sum[:span, :] += mul(exps, half_rows[cols])
            dk_sum[:span, :] += mul(grad_scores, half_queries[cols])
            dq_t[heads, cols] = mul(keys_t[heads, :span], grad_scores)
    out_ref[:, :PAIR] = (dq_t[...] * scale).T.astype(jnp.bfloat16)
    out_ref[:, PAIR : 2 * PAIR] = (dk_sum[...] * scale).astype(jnp.bfloat16)
    out_ref[:, 2 * PAIR :] = dv_sum[...].astype(jnp.bfloat16)


PACKED_COLS = pl.BlockSpec((LEN, 3 * PAIR), lambda p: (0, p))
PAIR_COLS = pl.BlockSpec((LEN, PAIR), lambda p: (0, p))
PAIR_GRID = pl.BlockSpec((2, LEN, LEN), lambda p: (p, 0, 0))
PAIR_STAT = pl.BlockSpec((1, 2, LEN), lambda p: (p, 0, 0))
SCALARS = pl.BlockSpec(memory_space=pltpu.SMEM)


def attention_forward(starts, slopes, packed):
    return pl.pallas_call(
        attend_fwd_kernel,
        grid=(PAIRS,),
        in_specs=[SCALARS, SCALARS, PACKED_COLS],
        out_specs=[PAIR_COLS, PAIR_GRID, PAIR_STAT],
        out_shape=[
            jax.ShapeDtypeStruct((LEN, D), jnp.bfloat16),
            jax.ShapeDtypeStruct((H, LEN, LEN), jnp.bfloat16),
            jax.ShapeDtypeStruct((PAIRS, 2, LEN), jnp.float32),
        ],
        scratch_shapes=[pltpu.VMEM((LEN, LEN), jnp.float32), pltpu.VMEM((PAIR, LEN), jnp.float32)],
        compiler_params=pltpu.CompilerParams(vmem_limit_bytes=VMEM_LIMIT),
        cost_estimate=pl.CostEstimate(
            flops=16 * LEN * LEN * D, bytes_accessed=44 * 1024 * 1024, transcendentals=H * LEN * LEN
        ),
    )(starts, slopes, packed)


def attention_backward(packed, context, grad_context, exps, stats):
    return pl.pallas_call(
        attend_bwd_kernel,
        grid=(PAIRS,),
        in_specs=[PACKED_COLS, PAIR_COLS, PAIR_COLS, PAIR_GRID, PAIR_STAT],
        out_specs=PACKED_COLS,
        out_shape=jax.ShapeDtypeStruct((LEN, 3 * D), jnp.bfloat16),
        scratch_shapes=[
            pltpu.VMEM((PAIR, LEN), jnp.float32),
            pltpu.VMEM((LEN, PAIR), jnp.float32),
            pltpu.VMEM((LEN, PAIR), jnp.float32),
        ],
        compiler_params=pltpu.CompilerParams(vmem_limit_bytes=VMEM_LIMIT),
        cost_estimate=pl.CostEstimate(flops=32 * LEN * LEN * D, bytes_accessed=50 * 1024 * 1024, transcendentals=0),
    )(packed, context, grad_context, exps, stats)


SLOTS = 12
SLOT = 512
HALF_SLOT = SLOT // 2
TILE = 256
MESH_IDS = pl.DeviceIdType.MESH


def handler_of(slot):
    wide = slot - 4
    square = slot < 4
    dp_index = jnp.where(square, jnp.where(slot < 2, 2, 12), 4 + 6 * (wide // 4) + wide % 2)
    tensor_index = jnp.where(square, slot % 2, (wide // 2) % 2)
    return dp_index, tensor_index


def muon_kernel(
    moments_ref,
    vec_ref,
    updates_ref,
    vec_out_ref,
    pieces,
    turned,
    vec_pieces,
    vec_sum,
    gram,
    gram_low,
    poly_low,
    half_low,
    chain_low,
    chain_next,
    out_half,
    in_half,
    local_sem,
    send_sem,
    recv_sem,
    half_send,
    half_recv,
):
    groups = lax.axis_size("dp")
    parts = lax.axis_size("tensor")
    count = groups * parts
    dp_me = lax.axis_index("dp")
    t_me = lax.axis_index("tensor")
    me = t_me * groups + dp_me
    is_square = (dp_me == 2) | (dp_me == 12)
    is_up = (dp_me == 4) | (dp_me == 5)
    is_down = (dp_me == 10) | (dp_me == 11)
    is_wide = is_up | is_down
    is_handler = is_square | is_wide
    wide_slot = jnp.where(is_up, 4 + (dp_me - 4), 8 + (dp_me - 10)) + 2 * t_me
    slot_me = jnp.where(is_square, t_me + jnp.where(dp_me == 12, 2, 0), wide_slot)
    slot_me = jnp.where(is_handler, slot_me, 0)

    barrier = pltpu.get_barrier_semaphore()

    def greet(step, carry):
        other = lax.rem(me + step, count)
        pl.semaphore_signal(
            barrier, inc=1, device_id=(lax.rem(other, groups), other // groups), device_id_type=MESH_IDS
        )
        return carry

    lax.fori_loop(1, count, greet, 0)
    pl.semaphore_wait(barrier, count - 1)

    def give(step, carry):
        slot = lax.rem(me + step, SLOTS)
        dp_to, t_to = handler_of(slot)
        away = (dp_to != dp_me) | (t_to != t_me)

        @pl.when(away)
        def _():
            pltpu.make_async_remote_copy(
                src_ref=vec_ref.at[slot],
                dst_ref=vec_pieces.at[me],
                send_sem=send_sem.at[1],
                recv_sem=recv_sem.at[1],
                device_id=(dp_to, t_to),
                device_id_type=MESH_IDS,
            ).start()
            pltpu.make_async_remote_copy(
                src_ref=moments_ref.at[slot],
                dst_ref=pieces.at[me],
                send_sem=send_sem.at[0],
                recv_sem=recv_sem.at[0],
                device_id=(dp_to, t_to),
                device_id_type=MESH_IDS,
            ).start()

        return carry

    lax.fori_loop(0, SLOTS, give, 0)

    def give_back(source, sem, target):
        def one(step, carry):
            other = lax.rem(me + step, count)
            pltpu.make_async_remote_copy(
                src_ref=source.at[other] if source is turned else source,
                dst_ref=target.at[slot_me],
                send_sem=send_sem.at[sem],
                recv_sem=recv_sem.at[sem],
                device_id=(lax.rem(other, groups), other // groups),
                device_id_type=MESH_IDS,
            ).start()
            return carry

        lax.fori_loop(1, count, one, 0)

    @pl.when(is_handler)
    def _():
        own = [
            pltpu.make_async_copy(vec_ref.at[slot_me], vec_pieces.at[me], local_sem.at[0]),
            pltpu.make_async_copy(moments_ref.at[slot_me], pieces.at[me], local_sem.at[1]),
        ]
        for copy in own:
            copy.start()
        for copy in own:
            copy.wait()
        rest = pl.ds(0, count - 1)
        pltpu.make_async_copy(vec_pieces.at[rest], vec_pieces.at[rest], recv_sem.at[1]).wait()
        vec_sum[...] = jnp.sum(vec_pieces[...], axis=0)
        give_back(vec_sum, 2, vec_out_ref)
        own_vec = pltpu.make_async_copy(vec_sum, vec_out_ref.at[slot_me], local_sem.at[0])
        own_vec.start()
        own_vec.wait()
        pltpu.make_async_copy(pieces.at[rest], pieces.at[rest], recv_sem.at[0]).wait()

        rows_of = TILE // 64

        def gram_tile(tile, carry):
            rows = pl.ds(pl.multiple_of(tile * TILE, TILE), TILE)
            total = jnp.zeros((TILE, D), jnp.float32)
            for part in range(parts):
                left = pieces[pl.ds(part * groups + tile * rows_of, rows_of)].reshape(TILE, SLOT)
                right = pieces[part * groups : (part + 1) * groups].reshape(D, SLOT)
                total += lax.dot_general(
                    left, right, (((1,), (1,)), ((), ())), preferred_element_type=jnp.float32
                )
            gram[rows, :] = total
            return carry

        lax.fori_loop(0, D // TILE, gram_tile, 0)

        @pl.when(is_wide)
        def _():
            core = lax.rem(dp_me, 2)
            half = D // 2
            mine = pl.ds(pl.multiple_of(core * half, half), half)
            theirs = pl.ds(pl.multiple_of((1 - core) * half, half), half)
            sibling = (dp_me + 1 - 2 * core, t_me)
            across = (dp_me, 1 - t_me)

            def exchange(stage, place):
                copy = pltpu.make_async_remote_copy(
                    src_ref=out_half.at[stage],
                    dst_ref=in_half.at[stage],
                    send_sem=half_send.at[stage],
                    recv_sem=half_recv.at[stage],
                    device_id=place,
                    device_id_type=MESH_IDS,
                )
                copy.start()
                copy.wait()

            out_half[0] = gram[theirs, :].astype(jnp.bfloat16)
            exchange(0, sibling)
            out_half[1] = (gram[mine, :] + in_half[0].astype(jnp.float32)).astype(jnp.bfloat16)
            exchange(1, across)
            total = out_half[1].astype(jnp.float32) + in_half[1].astype(jnp.float32)
            out_half[2] = total.astype(jnp.bfloat16)
            exchange(2, sibling)
            gram[mine, :] = out_half[2].astype(jnp.float32)
            gram[theirs, :] = in_half[2].astype(jnp.float32)

        def trace_tile(tile, total):
            rows = pl.ds(pl.multiple_of(tile * TILE, TILE), TILE)
            row_ids = lax.broadcasted_iota(jnp.int32, (TILE, D), 0) + tile * TILE
            col_ids = lax.broadcasted_iota(jnp.int32, (TILE, D), 1)
            diagonal = jnp.where(row_ids == col_ids, gram[rows, :], 0.0)
            return total + jnp.sum(jnp.sum(diagonal, axis=0, keepdims=True), axis=1, keepdims=True)

        square_total = lax.fori_loop(0, D // TILE, trace_tile, jnp.zeros((1, 1), jnp.float32))
        factor = lax.rsqrt(square_total + SQUARE_EPSILON)
        gram_low[...] = (gram[...] * (factor * factor)).astype(jnp.bfloat16)

        first, second, third = SCHULZ_FIRST, SCHULZ_SECOND, SCHULZ_THIRD

        def tiles(body):
            def one(tile, carry):
                body(pl.ds(pl.multiple_of(tile * TILE, TILE), TILE))
                return carry

            lax.fori_loop(0, D // TILE, one, 0)

        chain = chain_low
        other = chain_next
        for sweep in range(NS_ITERS):
            target = chain if sweep == 0 else poly_low

            def poly(rows):
                square = mul(gram_low[rows, :], gram_low[...])
                grown = (second / first) * gram_low[rows, :].astype(jnp.float32) + (third / first) * square
                target[rows, :] = grown.astype(jnp.bfloat16)

            tiles(poly)
            if sweep > 0:

                def join(rows, chain=chain, other=other):
                    total = chain[rows, :].astype(jnp.float32) + poly_low[rows, :].astype(jnp.float32)
                    other[rows, :] = (total + mul(chain[rows, :], poly_low[...])).astype(jnp.bfloat16)

                tiles(join)
                chain, other = other, chain
            if sweep < NS_ITERS - 1:

                def half(rows):
                    grown = gram_low[rows, :].astype(jnp.float32) + mul(gram_low[rows, :], target[...])
                    half_low[rows, :] = grown.astype(jnp.bfloat16)

                def full(rows):
                    grown = half_low[rows, :].astype(jnp.float32) + mul(half_low[rows, :], target[...])
                    gram_low[rows, :] = (grown * (first * first)).astype(jnp.bfloat16)

                tiles(half)
                tiles(full)

        scale = factor * (first**NS_ITERS)

        def turn_tile(tile, carry):
            rows = pl.ds(pl.multiple_of(tile * TILE, TILE), TILE)
            for part in range(parts):
                at = pl.ds(part * groups + tile * rows_of, rows_of)
                whole = pieces[part * groups : (part + 1) * groups].reshape(D, SLOT)
                kept = pieces[at].reshape(TILE, SLOT).astype(jnp.float32)
                fresh = (kept + mul(chain[rows, :], whole)) * scale
                turned[at] = fresh.astype(jnp.bfloat16).reshape(rows_of, 64, SLOT)
            return carry

        lax.fori_loop(0, D // TILE, turn_tile, 0)
        give_back(turned, 3, updates_ref)
        own_turned = pltpu.make_async_copy(turned.at[me], updates_ref.at[slot_me], local_sem.at[1])
        own_turned.start()
        own_turned.wait()

    def finish(length):
        here = pl.ds(0, length)
        pltpu.make_async_copy(vec_ref.at[here], vec_ref.at[here], send_sem.at[1]).wait()
        pltpu.make_async_copy(moments_ref.at[here], moments_ref.at[here], send_sem.at[0]).wait()
        pltpu.make_async_copy(vec_out_ref.at[here], vec_out_ref.at[here], recv_sem.at[2]).wait()
        pltpu.make_async_copy(updates_ref.at[here], updates_ref.at[here], recv_sem.at[3]).wait()

    @pl.when(is_handler)
    def _():
        finish(SLOTS - 1)
        rest = pl.ds(0, count - 1)
        pltpu.make_async_copy(vec_pieces.at[rest], vec_pieces.at[rest], send_sem.at[2]).wait()
        pltpu.make_async_copy(turned.at[rest], turned.at[rest], send_sem.at[3]).wait()

    @pl.when(jnp.logical_not(is_handler))
    def _():
        finish(SLOTS)


def muon_call(moments, vec_parts):
    count = lax.axis_size("dp") * lax.axis_size("tensor")
    rows = moments.shape[1]
    vmem = pl.BlockSpec(memory_space=pltpu.VMEM)
    low = pltpu.VMEM((D, D), jnp.bfloat16)
    return pl.pallas_call(
        muon_kernel,
        in_specs=[vmem, vmem],
        out_specs=[vmem, vmem],
        out_shape=[
            jax.ShapeDtypeStruct(moments.shape, jnp.bfloat16),
            jax.ShapeDtypeStruct(vec_parts.shape, jnp.float32),
        ],
        scratch_shapes=[
            pltpu.VMEM((count, rows, SLOT), jnp.bfloat16),
            pltpu.VMEM((count, rows, SLOT), jnp.bfloat16),
            pltpu.VMEM((count,) + vec_parts.shape[1:], jnp.float32),
            pltpu.VMEM(vec_parts.shape[1:], jnp.float32),
            pltpu.VMEM((D, D), jnp.float32),
            low,
            low,
            low,
            low,
            low,
            pltpu.VMEM((3, D // 2, D), jnp.bfloat16),
            pltpu.VMEM((3, D // 2, D), jnp.bfloat16),
            pltpu.SemaphoreType.DMA((2,)),
            pltpu.SemaphoreType.DMA((4,)),
            pltpu.SemaphoreType.DMA((4,)),
            pltpu.SemaphoreType.DMA((3,)),
            pltpu.SemaphoreType.DMA((3,)),
        ],
        compiler_params=pltpu.CompilerParams(
            collective_id=1, has_side_effects=True, vmem_limit_bytes=VMEM_LIMIT
        ),
        cost_estimate=pl.CostEstimate(flops=12 * 2 * D**3, bytes_accessed=4 * 1024 * 1024, transcendentals=0),
    )(moments, vec_parts)


def by_slots(rows):
    return jnp.swapaxes(rows.reshape(rows.shape[0], -1, SLOT), 0, 1)


def from_slots(rows):
    return jnp.swapaxes(rows, 0, 1).reshape(rows.shape[1], -1)


def muon_step(
    shards, vector_total, w_qkv, w_out, w_up, w_down, vectors, m_qkv, m_out, m_up, m_down, m_vec
):
    grad_qkv_shard, grad_out_shard, grad_up_shard, grad_down_shard = shards
    moment_qkv = MOMENTUM_DECAY * m_qkv + grad_qkv_shard
    moment_out = MOMENTUM_DECAY * m_out + grad_out_shard
    moment_up = MOMENTUM_DECAY * m_up + grad_up_shard
    moment_down = MOMENTUM_DECAY * m_down + grad_down_shard
    slots = jnp.concatenate(
        [
            narrow(moment_qkv),
            narrow(moment_out).T[None],
            by_slots(narrow(moment_up)),
            by_slots(narrow(moment_down).T),
        ]
    )
    updates, vector_rows = muon_call(slots, vector_total.reshape(SLOTS, 8, 128))
    vector_grad = vector_rows.reshape(12, D)
    wide_factor = math.sqrt(FF / D)
    new_qkv = w_qkv - MATRIX_RATE * updates[0:3].astype(jnp.float32)
    new_out = w_out - MATRIX_RATE * updates[3].T.astype(jnp.float32)
    new_up = w_up - MATRIX_RATE * wide_factor * from_slots(updates[4:8]).astype(jnp.float32)
    new_down = w_down - MATRIX_RATE * wide_factor * from_slots(updates[8:12]).T.astype(jnp.float32)
    moment_vec = MOMENTUM_DECAY * m_vec + vector_grad
    new_vec = vectors - VECTOR_RATE * moment_vec * lax.rsqrt(
        jnp.mean(moment_vec * moment_vec, axis=1, keepdims=True) + SQUARE_EPSILON
    )
    return (
        grad_qkv_shard,
        grad_out_shard,
        grad_up_shard,
        grad_down_shard,
        vector_grad,
        moment_qkv,
        moment_out,
        moment_up,
        moment_down,
        moment_vec,
        new_qkv,
        new_out,
        new_up,
        new_down,
        new_vec,
    )


def neighbours():
    dp_me = lax.axis_index("dp")
    y = lax.axis_index("tensor")
    core = lax.rem(dp_me, 2)
    x = lax.rem(dp_me // 2, 2)
    z = dp_me // 4
    sibling = (dp_me + 1 - 2 * core, y)
    beside = (dp_me + 2 - 4 * x, y)
    across = (dp_me, 1 - y)
    stations = [(lax.rem(dp_me + 4 * hop, 16), y) for hop in (1, 2, 3)]
    return (z, x, core, y), sibling, beside, across, stations


def greet_neighbours(places):
    barrier = pltpu.get_barrier_semaphore()
    for place in places:
        pl.semaphore_signal(barrier, inc=1, device_id=place, device_id_type=MESH_IDS)
    pl.semaphore_wait(barrier, len(places))


SWAP_AT = 2
SPREAD_LAG = 1


class Spread:
    def __init__(self, slots_ref, table, local_sem, send_sem, recv_sem):
        self.slots_ref, self.table = slots_ref, table
        self.local_sem, self.send_sem, self.recv_sem = local_sem, send_sem, recv_sem
        (self.z, self.x, self.core, self.y), self.sibling, self.beside, self.across, self.stations = neighbours()

    def remote(self, source, target, stage, slot, place):
        return pltpu.make_async_remote_copy(
            src_ref=source,
            dst_ref=target,
            send_sem=self.send_sem.at[stage, slot],
            recv_sem=self.recv_sem.at[stage, slot],
            device_id=place,
            device_id_type=MESH_IDS,
        )

    def cols(self, slot, part, start=0, size=SLOT):
        _, column, distance, _ = self.table[slot]
        if isinstance(part, int):
            return pl.ds(column + part * distance + start, size)
        return pl.ds(pl.multiple_of(column + part * distance + start, 128), size)

    def own(self, slot):
        here = self.table[slot][0].at[self.z, self.x, self.core, :, self.cols(slot, self.y)]
        return pltpu.make_async_copy(self.slots_ref.at[slot], here, self.local_sem.at[slot])

    def along_z(self, slot):
        here = self.table[slot][0].at[self.z, self.x, self.core, :, self.cols(slot, self.y)]
        return [
            self.remote(self.slots_ref.at[slot], here, hop, slot, place)
            for hop, place in enumerate(self.stations)
        ]

    def second(self, slot):
        whole, _, _, size = self.table[slot]
        copies = []
        if size:
            part = whole.at[:, self.x, self.core, :, self.cols(slot, self.y, 0, size)]
            copies.append(self.remote(part, part, 3, slot, self.beside))
        if size < SLOT:
            part = whole.at[:, self.x, self.core, :, self.cols(slot, self.y, size, SLOT - size)]
            copies.append(self.remote(part, part, 4, slot, self.across))
        return copies

    def third(self, slot):
        whole, _, _, size = self.table[slot]
        copies = []
        if size:
            part = whole.at[:, :, self.core, :, self.cols(slot, self.y, 0, size)]
            copies.append(self.remote(part, part, 5, slot, self.across))
        if size < SLOT:
            for index in (0, 1):
                part = whole.at[:, self.x, self.core, :, self.cols(slot, index, size, SLOT - size)]
                copies.append(self.remote(part, part, 6 + index, slot, self.beside))
        return copies

    def fourth(self, slot):
        whole = self.table[slot][0]
        copies = []
        for index in (0, 1):
            part = whole.at[:, :, self.core, :, self.cols(slot, index)]
            copies.append(self.remote(part, part, 8 + index, slot, self.sibling))
        return copies

    def begin(self):
        for slot in range(len(self.table)):
            self.own(slot).start()
            for copy in self.along_z(slot):
                copy.start()

    def tick(self, index):
        count = len(self.table)
        if index < count:
            self.own(index).wait()
            for copy in self.along_z(index):
                copy.wait_recv()
            for copy in self.second(index):
                copy.start()
        if 0 <= index - SPREAD_LAG < count:
            for copy in self.second(index - SPREAD_LAG):
                copy.wait_recv()
            for copy in self.third(index - SPREAD_LAG):
                copy.start()
        if 0 <= index - 2 * SPREAD_LAG < count:
            for copy in self.third(index - 2 * SPREAD_LAG):
                copy.wait_recv()
            for copy in self.fourth(index - 2 * SPREAD_LAG):
                copy.start()

    def ticks(self):
        return len(self.table) + 2 * SPREAD_LAG

    def finish(self):
        for slot in range(len(self.table)):
            for copy in self.along_z(slot) + self.second(slot) + self.third(slot):
                copy.wait_send()
            for copy in self.fourth(slot):
                copy.wait()


def spread_semaphores(count):
    return [
        pltpu.SemaphoreType.DMA((count,)),
        pltpu.SemaphoreType.DMA((10, count)),
        pltpu.SemaphoreType.DMA((10, count)),
    ]


def first_spread_kernel(slots_ref, tokens_ref, whole_ref, got_ref, local_sem, send_sem, recv_sem, token_sem):
    table = [(whole_ref, index * SLOT, 3 * SLOT, 0) for index in range(3)]
    spread = Spread(slots_ref, table, local_sem, send_sem, recv_sem)
    greet_neighbours([spread.sibling, spread.beside, spread.across] + spread.stations)
    swap = pltpu.make_async_remote_copy(
        src_ref=tokens_ref.at[1 - spread.y],
        dst_ref=got_ref,
        send_sem=token_sem.at[0],
        recv_sem=token_sem.at[1],
        device_id=spread.across,
        device_id_type=MESH_IDS,
    )
    spread.begin()
    for index in range(spread.ticks()):
        spread.tick(index)
        if index == SWAP_AT:
            swap.start()
    spread.finish()
    swap.wait()


def second_spread_kernel(
    slots_ref, cotangent_ref, out_ref, up_ref, down_ref, got_ref, local_sem, send_sem, recv_sem, token_sem
):
    table = [(out_ref, 0, SLOT, 0)]
    table += [(up_ref, index * SLOT, 4 * SLOT, HALF_SLOT if index % 2 else 0) for index in range(4)]
    table += [(down_ref, index * SLOT, 4 * SLOT, HALF_SLOT if index % 2 else 0) for index in range(4)]
    spread = Spread(slots_ref, table, local_sem, send_sem, recv_sem)
    greet_neighbours([spread.sibling, spread.beside, spread.across] + spread.stations)
    swap = pltpu.make_async_remote_copy(
        src_ref=cotangent_ref.at[1 - spread.y],
        dst_ref=got_ref,
        send_sem=token_sem.at[0],
        recv_sem=token_sem.at[1],
        device_id=spread.across,
        device_id_type=MESH_IDS,
    )
    spread.begin()
    for index in range(spread.ticks()):
        spread.tick(index)
        if index == SWAP_AT:
            swap.start()
    spread.finish()
    swap.wait()


def whole_shape(columns):
    return jax.ShapeDtypeStruct((4, 2, 2, 64, columns), jnp.bfloat16)


def first_spread(slots, tokens):
    anywhere = pl.BlockSpec(memory_space=pl.ANY)
    whole, got = pl.pallas_call(
        first_spread_kernel,
        in_specs=[anywhere] * 2,
        out_specs=[anywhere] * 2,
        out_shape=[whole_shape(3 * D), jax.ShapeDtypeStruct(tokens.shape[1:], tokens.dtype)],
        scratch_shapes=spread_semaphores(3) + [pltpu.SemaphoreType.DMA((2,))],
        compiler_params=pltpu.CompilerParams(collective_id=3, has_side_effects=True),
    )(slots, tokens)
    return whole.reshape(D, 3 * D), got


def second_spread(slots, cotangent):
    anywhere = pl.BlockSpec(memory_space=pl.ANY)
    out, up, down, got = pl.pallas_call(
        second_spread_kernel,
        in_specs=[anywhere] * 2,
        out_specs=[anywhere] * 4,
        out_shape=[
            whole_shape(D),
            whole_shape(FF),
            whole_shape(FF),
            jax.ShapeDtypeStruct(cotangent.shape[1:], cotangent.dtype),
        ],
        scratch_shapes=spread_semaphores(9) + [pltpu.SemaphoreType.DMA((2,))],
        compiler_params=pltpu.CompilerParams(collective_id=4, has_side_effects=True),
    )(slots, cotangent)
    return out.reshape(D, D), up.reshape(D, FF), down.reshape(D, FF), got


GROUP_SLOTS = (3, 1, 4, 4)
LAG = 2


def sum_kernel(
    qkv_ref,
    out_ref,
    up_ref,
    down_ref,
    total_ref,
    mine,
    first,
    second_y,
    second_x,
    third,
    fourth,
    load_sem,
    send_sem,
    recv_sem,
):
    (z, x, core, y), sibling, beside, across, stations = neighbours()
    low_cols = pl.ds(0, HALF_SLOT)
    high_cols = pl.ds(HALF_SLOT, HALF_SLOT)

    greet_neighbours([sibling, beside, across] + stations)

    def remote(source, target, stage, slot, place):
        return pltpu.make_async_remote_copy(
            src_ref=source,
            dst_ref=target,
            send_sem=send_sem.at[stage, slot],
            recv_sem=recv_sem.at[stage, slot],
            device_id=place,
            device_id_type=MESH_IDS,
        )

    slot = 0
    for ref, number in zip((qkv_ref, out_ref, up_ref, down_ref), GROUP_SLOTS):
        for index in range(number):
            for part in (0, 1):
                cols = pl.ds((part * number + index) * SLOT, SLOT)
                remote(ref.at[:, :, 1 - core, :, cols], first.at[slot, part], 0, slot, sibling).start()
                pltpu.make_async_copy(
                    ref.at[:, :, core, :, cols], mine.at[slot, part], load_sem.at[slot]
                ).start()
            slot += 1

    def second_copies(slot):
        return (
            remote(first.at[slot, 1 - y, :, :, :, low_cols], second_y.at[slot], 1, slot, across),
            remote(first.at[slot, :, :, 1 - x, :, high_cols], second_x.at[slot], 2, slot, beside),
        )

    def third_copies(slot):
        return (
            remote(second_y.at[slot, :, 1 - x], third.at[slot, :, :, low_cols], 3, slot, beside),
            remote(second_x.at[slot, 1 - y], third.at[slot, :, :, high_cols], 4, slot, across),
        )

    def fourth_copies(slot):
        return [
            remote(third.at[slot, lax.rem(z + hop, 4)], fourth.at[slot, hop - 1], 4 + hop, slot, place)
            for hop, place in zip((1, 2, 3), stations)
        ]

    def landed(ref, stage, slot):
        pltpu.make_async_copy(ref, ref, recv_sem.at[stage, slot]).wait()

    def step(index, carry):
        @pl.when(index < SLOTS)
        def _():
            slot = index
            pltpu.make_async_copy(mine.at[slot], mine.at[slot], load_sem.at[slot]).wait()
            landed(first.at[slot], 0, slot)
            first[slot] = first[slot] + mine[slot]
            for copy in second_copies(slot):
                copy.start()

        @pl.when((index >= LAG) & (index < SLOTS + LAG))
        def _():
            slot = index - LAG
            landed(second_y.at[slot], 1, slot)
            second_y[slot] = second_y[slot] + first[slot, y, :, :, :, :HALF_SLOT]
            landed(second_x.at[slot], 2, slot)
            second_x[slot] = second_x[slot] + first[slot, :, :, x, :, HALF_SLOT:]
            for copy in third_copies(slot):
                copy.start()

        @pl.when((index >= 2 * LAG) & (index < SLOTS + 2 * LAG))
        def _():
            slot = index - 2 * LAG
            landed(third.at[slot, :, :, low_cols], 3, slot)
            landed(third.at[slot, :, :, high_cols], 4, slot)
            third[slot, :, :, :HALF_SLOT] = third[slot, :, :, :HALF_SLOT] + second_y[slot, :, x]
            third[slot, :, :, HALF_SLOT:] = third[slot, :, :, HALF_SLOT:] + second_x[slot, y]
            for copy in fourth_copies(slot):
                copy.start()

        @pl.when(index >= 3 * LAG)
        def _():
            slot = index - 3 * LAG
            total = third[slot, z].astype(jnp.float32)
            for hop in (1, 2, 3):
                landed(fourth.at[slot, hop - 1], 4 + hop, slot)
                total = total + fourth[slot, hop - 1].astype(jnp.float32)
            total_ref[slot] = total

        return carry

    lax.fori_loop(0, SLOTS + 3 * LAG, step, 0)

    def sent(slot, carry):
        pltpu.make_async_copy(mine.at[slot], mine.at[slot], send_sem.at[0, slot]).wait()
        for copy in second_copies(slot) + third_copies(slot) + tuple(fourth_copies(slot)):
            copy.wait_send()
        return carry

    lax.fori_loop(0, SLOTS, sent, 0)


def sum_over_devices(grads):
    rows = 64
    refs = [grad.reshape(4, 2, 2, rows, grad.shape[-1]) for grad in grads]
    part = (SLOTS, 2, 4, 2, rows, SLOT)
    anywhere = pl.BlockSpec(memory_space=pl.ANY)
    return pl.pallas_call(
        sum_kernel,
        in_specs=[anywhere] * 4,
        out_specs=pl.BlockSpec(memory_space=pltpu.VMEM),
        out_shape=jax.ShapeDtypeStruct((SLOTS, rows, SLOT), jnp.float32),
        scratch_shapes=[
            pltpu.VMEM(part, jnp.bfloat16),
            pltpu.VMEM(part, jnp.bfloat16),
            pltpu.VMEM((SLOTS, 4, 2, rows, HALF_SLOT), jnp.bfloat16),
            pltpu.VMEM((SLOTS, 2, 4, rows, HALF_SLOT), jnp.bfloat16),
            pltpu.VMEM((SLOTS, 4, rows, SLOT), jnp.bfloat16),
            pltpu.VMEM((SLOTS, 3, rows, SLOT), jnp.bfloat16),
            pltpu.SemaphoreType.DMA((SLOTS,)),
            pltpu.SemaphoreType.DMA((8, SLOTS)),
            pltpu.SemaphoreType.DMA((8, SLOTS)),
        ],
        compiler_params=pltpu.CompilerParams(
            collective_id=2, has_side_effects=True, vmem_limit_bytes=VMEM_LIMIT
        ),
        cost_estimate=pl.CostEstimate(flops=0, bytes_accessed=300 * 1024 * 1024, transcendentals=0),
    )(*refs)


def narrow(rows):
    return rows.astype(jnp.bfloat16)


def contract(left, right, left_dim, right_dim):
    return lax.dot_general(
        left, right, (((left_dim,), (right_dim,)), ((), ())), preferred_element_type=jnp.float32
    )


def in_order(rank, own, got):
    return jnp.where(rank == 0, jnp.concatenate([own, got]), jnp.concatenate([got, own]))


def swap_halves(mine, rank):
    rows = mine.shape[0] // 2
    kept = lax.dynamic_slice_in_dim(mine, rank * rows, rows, 0)
    sent = lax.dynamic_slice_in_dim(mine, (1 - rank) * rows, rows, 0)
    got = lax.ppermute(sent, "tensor", [(0, 1), (1, 0)])
    return jnp.where(rank == 0, jnp.stack([kept, got]), jnp.stack([got, kept]))


def by_pairs(rows):
    count, height, width = rows.shape
    return jnp.transpose(rows.reshape(count, height, width // PAIR, PAIR), (1, 2, 0, 3)).reshape(height, -1)


def from_pairs(rows):
    height = rows.shape[0]
    return jnp.transpose(rows.reshape(height, -1, 3, PAIR), (2, 0, 1, 3)).reshape(3, height, -1)


def sequence_step(
    tokens,
    cotangent,
    piece_starts,
    w_qkv,
    w_out,
    w_up,
    w_down,
    vectors,
    m_qkv,
    m_out,
    m_up,
    m_down,
    m_vec,
):
    rank = lax.axis_index("tensor")
    slopes = jnp.exp2(-8.0 * jnp.arange(1, H + 1, dtype=jnp.float32) / H)
    starts = lax.dynamic_slice_in_dim(piece_starts[:, 0], rank, 1, 0)[0]
    own_tokens = lax.dynamic_index_in_dim(tokens, rank, 0, keepdims=False)
    own_cotangent = lax.dynamic_index_in_dim(cotangent, rank, 0, keepdims=False)

    full_qkv, other_tokens = first_spread(by_slots(by_pairs(narrow(w_qkv))), tokens)
    token_rows = in_order(rank, own_tokens, other_tokens).astype(jnp.float32)
    normed_one = narrow(layer_norm(token_rows, vectors[0], vectors[1]))
    shifts = by_pairs(jnp.stack([vectors[2], jnp.zeros((D,), jnp.float32), vectors[3]])[:, None])
    packed = narrow(contract(normed_one, full_qkv, 1, 0) + shifts)
    context, exps, stats = attention_forward(starts, slopes, packed)

    later_slots = jnp.concatenate(
        [narrow(w_out).T[None], by_slots(narrow(w_up)), by_slots(narrow(w_down).T)]
    )
    full_out, full_up, full_down, other_cotangent = second_spread(later_slots, cotangent)
    cotangent_low = in_order(rank, own_cotangent, other_cotangent)
    cotangent_rows = cotangent_low.astype(jnp.float32)

    middle = token_rows + contract(context, full_out, 1, 1) + vectors[4]
    normed_two = narrow(layer_norm(middle, vectors[5], vectors[6]))
    before = contract(normed_two, full_up, 1, 0) + vectors[7:11].reshape(FF)
    activated = narrow(gelu_tanh(before))
    block_rows = narrow(middle + contract(activated, full_down, 1, 1) + vectors[11])
    output_pair = swap_halves(block_rows, rank)

    grad_down = narrow(contract(cotangent_low, activated, 0, 0))
    gelu_pull = jax.vjp(gelu_tanh, before)[1]
    grad_before = narrow(gelu_pull(contract(cotangent_low, full_down, 1, 0))[0])
    grad_up = narrow(contract(normed_two, grad_before, 0, 0))
    second_pull = jax.vjp(layer_norm, middle, vectors[5], vectors[6])[1]
    middle_from_norm, gain_two_grad, shift_two_grad = second_pull(contract(grad_before, full_up, 1, 1))
    grad_middle = cotangent_rows + middle_from_norm
    grad_middle_low = narrow(grad_middle)
    grad_out = narrow(contract(grad_middle_low, context, 0, 0))
    grad_context = narrow(contract(grad_middle_low, full_out, 1, 0))
    grad_packed = attention_backward(packed, context, grad_context, exps, stats)
    grad_qkv = narrow(contract(normed_one, grad_packed, 0, 0))
    sums = sum_over_devices((grad_qkv, grad_out, grad_up, grad_down))
    first_pull = jax.vjp(layer_norm, token_rows, vectors[0], vectors[1])[1]
    token_from_norm, gain_one_grad, shift_one_grad = first_pull(contract(grad_packed, full_qkv, 1, 1))
    grad_token_rows = grad_middle + token_from_norm
    token_pair = swap_halves(narrow(grad_token_rows), rank).astype(jnp.float32)

    packed_sums = from_pairs(jnp.sum(grad_packed, axis=0, dtype=jnp.float32)[None])[:, 0]
    vector_total = jnp.concatenate(
        [
            jnp.stack(
                [
                    gain_one_grad,
                    shift_one_grad,
                    packed_sums[0],
                    packed_sums[2],
                    jnp.sum(grad_middle, axis=0),
                    gain_two_grad,
                    shift_two_grad,
                ]
            ),
            jnp.sum(grad_before, axis=0, dtype=jnp.float32).reshape(4, D),
            jnp.sum(cotangent_rows, axis=0)[None],
        ]
    )
    shards = (
        from_pairs(from_slots(sums[0:3])),
        sums[3].T,
        from_slots(sums[4:8]),
        from_slots(sums[8:12]).T,
    )
    outputs = muon_step(shards, vector_total, w_qkv, w_out, w_up, w_down, vectors, m_qkv, m_out, m_up, m_down, m_vec)
    return (output_pair, token_pair) + outputs


def solution(mesh):
    in_specs = (
        P(None, ("dp", "tensor"), None),
        P(None, ("dp", "tensor"), None),
        P(None, "dp", None),
        P(None, "dp", "tensor"),
        P("tensor", "dp"),
        P("dp", "tensor"),
        P("tensor", "dp"),
        P(),
        P(None, "dp", "tensor"),
        P("tensor", "dp"),
        P("dp", "tensor"),
        P("tensor", "dp"),
        P(),
    )
    out_specs = (
        P(None, ("dp", "tensor"), None),
        P(None, ("dp", "tensor"), None),
        P(None, "dp", "tensor"),
        P("tensor", "dp"),
        P("dp", "tensor"),
        P("tensor", "dp"),
        P(),
        P(None, "dp", "tensor"),
        P("tensor", "dp"),
        P("dp", "tensor"),
        P("tensor", "dp"),
        P(),
        P(None, "dp", "tensor"),
        P("tensor", "dp"),
        P("dp", "tensor"),
        P("tensor", "dp"),
        P(),
    )
    groups_fit = mesh.shape["tensor"] == MB and mesh.shape["dp"] == 16

    def pick(*arrays):
        if groups_fit and arrays[2].shape[1] == 1:
            return sequence_step(*arrays)
        return on_device(*arrays)

    return jax.shard_map(
        pick, mesh=mesh, in_specs=in_specs, out_specs=out_specs, check_vma=False
    )
```

```python
import math

import jax
import jax.numpy as jnp
from jax import lax
from jax.experimental import pallas as pl
from jax.experimental.pallas import tpu as pltpu
from jax.sharding import PartitionSpec as P

D = 1024
H = 16
HD = 64
FF = 4096
LEN = 1024
PIECE = 256
NPIECE = 2
MB = 2
NS_ITERS = 3


NORM_EPSILON = 1e-05
SQUARE_EPSILON = 1e-06
MASKED_SCORE = -1e30
SCHULZ_FIRST = 3.4445
SCHULZ_SECOND = -4.775
SCHULZ_THIRD = 2.0315
MOMENTUM_DECAY = 0.5
MATRIX_RATE = 0.5
VECTOR_RATE = 0.05


def layer_norm(inputs, gain_row, shift_row):
    average = jnp.mean(inputs, axis=-1, keepdims=True)
    centered = inputs - average
    variance = jnp.mean(centered * centered, axis=-1, keepdims=True)
    return centered * lax.rsqrt(variance + NORM_EPSILON) * gain_row + shift_row


def gelu_tanh(inputs):
    return jax.nn.gelu(inputs, approximate=True)


def score_layout(starts, slopes):
    positions = jnp.arange(LEN, dtype=jnp.int32)
    inside = (positions[None, :] >= starts[:, None]) & (
        positions[None, :] < starts[:, None] + PIECE
    )
    labels = jnp.arange(1, NPIECE + 1, dtype=jnp.int32)
    piece_label = jnp.sum(jnp.where(inside, labels[:, None], 0), axis=0)
    same_piece = (piece_label[:, None] == piece_label[None, :]) & (piece_label[:, None] > 0)
    visible = (positions[None, :] <= positions[:, None]) | same_piece
    distance = jnp.abs(positions[:, None] - positions[None, :]).astype(jnp.float32)
    penalty = -slopes[:, None, None] * distance[None, :, :]
    return (visible, penalty)


def head_scores(query_heads, key_heads, starts, slopes):
    visible, penalty = score_layout(starts, slopes)
    raw_scores = jnp.einsum(
        "qhd,khd->hqk", query_heads, key_heads, preferred_element_type=jnp.float32
    )
    scores = raw_scores * (1.0 / math.sqrt(HD)) + penalty
    return jnp.where(visible[None, :, :], scores, MASKED_SCORE)


def attend_forward(element, slopes):
    query_seq, key_seq, value_seq, starts = element
    heads_here = slopes.shape[0]
    query_heads = query_seq.reshape(LEN, heads_here, HD)
    key_heads = key_seq.reshape(LEN, heads_here, HD)
    value_heads = value_seq.reshape(LEN, heads_here, HD)
    scores = head_scores(query_heads, key_heads, starts, slopes)
    maximum = jnp.max(scores, axis=-1, keepdims=True)
    weights_raw = jnp.exp(scores - maximum)
    denominator = jnp.sum(weights_raw, axis=-1, keepdims=True)
    probabilities = weights_raw / denominator
    context = jnp.einsum(
        "hqk,khd->qhd",
        probabilities.astype(jnp.bfloat16),
        value_heads,
        preferred_element_type=jnp.float32,
    )
    logsum = (maximum + jnp.log(denominator))[..., 0]
    return (context.reshape(LEN, heads_here * HD), logsum)


def attend_backward(element, slopes):
    query_seq, key_seq, value_seq, context_grad, logsum, starts = element
    heads_here = slopes.shape[0]
    query_heads = query_seq.reshape(LEN, heads_here, HD)
    key_heads = key_seq.reshape(LEN, heads_here, HD)
    value_heads = value_seq.reshape(LEN, heads_here, HD)
    grad_heads = context_grad.reshape(LEN, heads_here, HD)
    scores = head_scores(query_heads, key_heads, starts, slopes)
    probabilities = jnp.exp(scores - logsum[..., None])
    grad_probs = jnp.einsum(
        "qhd,khd->hqk", grad_heads, value_heads, preferred_element_type=jnp.float32
    )
    inner_sum = jnp.sum(probabilities * grad_probs, axis=-1, keepdims=True)
    grad_scores = (probabilities * (grad_probs - inner_sum)).astype(jnp.bfloat16)
    scale_factor = 1.0 / math.sqrt(HD)
    grad_query = (
        jnp.einsum("hqk,khd->qhd", grad_scores, key_heads, preferred_element_type=jnp.float32)
        * scale_factor
    )
    grad_key = (
        jnp.einsum("hqk,qhd->khd", grad_scores, query_heads, preferred_element_type=jnp.float32)
        * scale_factor
    )
    grad_value = jnp.einsum(
        "hqk,qhd->khd",
        probabilities.astype(jnp.bfloat16),
        grad_heads,
        preferred_element_type=jnp.float32,
    )
    width_here = heads_here * HD
    return (
        grad_query.astype(jnp.bfloat16).reshape(LEN, width_here),
        grad_key.astype(jnp.bfloat16).reshape(LEN, width_here),
        grad_value.astype(jnp.bfloat16).reshape(LEN, width_here),
    )


def placed(values, offset, length):
    return lax.dynamic_update_slice_in_dim(jnp.zeros((length,), jnp.float32), values, offset, 0)


def accumulate(totals, addend):
    if totals is None:
        return addend
    return tuple((former + latter for former, latter in zip(totals, addend)))


def gram_term(narrow_rows, wide_rows):
    part_narrow = jnp.einsum(
        "mrc,mrd->cmd", narrow_rows, narrow_rows, preferred_element_type=jnp.float32
    )
    part_wide = jnp.einsum("mrc,mrd->cmd", wide_rows, wide_rows, preferred_element_type=jnp.float32)
    return jnp.concatenate([part_narrow, part_wide], axis=1)


def schulz_step(state, gram_matrix):
    turned = jnp.einsum("mrc,cmd->mrd", state, gram_matrix, preferred_element_type=jnp.float32)
    mixed = (SCHULZ_SECOND * state.astype(jnp.float32) + SCHULZ_THIRD * turned).astype(jnp.bfloat16)
    return (
        SCHULZ_FIRST * state.astype(jnp.float32)
        + jnp.einsum("mrc,cmd->mrd", mixed, gram_matrix, preferred_element_type=jnp.float32)
    ).astype(jnp.bfloat16)


def slice_term(source, weights, pattern):
    return jnp.einsum(pattern, source, weights, preferred_element_type=jnp.float32)


def on_device(
    tokens,
    cotangent,
    piece_starts,
    w_qkv,
    w_out,
    w_up,
    w_down,
    vectors,
    m_qkv,
    m_out,
    m_up,
    m_down,
    m_vec,
):
    tensor_count = lax.axis_size("tensor")
    tensor_rank = lax.axis_index("tensor")
    shard_rank = lax.axis_index("dp")
    heads_here = H // tensor_count
    width_here = heads_here * HD
    hidden_here = FF // tensor_count
    rows_here = tokens.shape[1]
    group_rows = rows_here * tensor_count
    seqs_here = piece_starts.shape[1]
    shard_rows = w_qkv.shape[1]
    head_ids = tensor_rank * heads_here + jnp.arange(heads_here, dtype=jnp.int32) + 1
    slopes = jnp.exp2(-8.0 * head_ids.astype(jnp.float32) / H)
    query_shift = lax.dynamic_slice_in_dim(vectors[2], tensor_rank * width_here, width_here, 0)
    value_shift = lax.dynamic_slice_in_dim(vectors[3], tensor_rank * width_here, width_here, 0)
    up_shift = lax.dynamic_slice_in_dim(
        vectors[7:11].reshape(FF), tensor_rank * hidden_here, hidden_here, 0
    )
    low_qkv = w_qkv.astype(jnp.bfloat16)
    low_out = w_out.astype(jnp.bfloat16)
    low_up = w_up.astype(jnp.bfloat16)
    low_down = w_down.astype(jnp.bfloat16)
    outputs_list = []
    input_grads = []
    vector_total = jnp.zeros((12, D), jnp.float32)
    grad_total = None

    def forward_one(element):
        return attend_forward(element, slopes)

    def backward_one(element):
        return attend_backward(element, slopes)

    for batch_index in range(MB):
        full_qkv, full_out, full_up, full_down = (
            lax.all_gather(low_qkv, "dp", axis=1, tiled=True),
            lax.all_gather(low_out, "dp", axis=1, tiled=True),
            lax.all_gather(low_up, "dp", axis=0, tiled=True),
            lax.all_gather(low_down, "dp", axis=1, tiled=True),
        )
        token_rows = tokens[batch_index].astype(jnp.float32)
        cotangent_rows = cotangent[batch_index]
        normed_one = layer_norm(token_rows, vectors[0], vectors[1])
        normed_all, cotangent_all = (
            lax.all_gather(normed_one.astype(jnp.bfloat16), "tensor", axis=0, tiled=True),
            lax.all_gather(cotangent_rows, "tensor", axis=0, tiled=True),
        )
        projected = jnp.einsum(
            "td,cde->cte", normed_all, full_qkv, preferred_element_type=jnp.float32
        )
        query_low = (projected[0] + query_shift).astype(jnp.bfloat16)
        key_low = projected[1].astype(jnp.bfloat16)
        value_low = (projected[2] + value_shift).astype(jnp.bfloat16)
        query_seqs = query_low.reshape(seqs_here, LEN, width_here)
        key_seqs = key_low.reshape(seqs_here, LEN, width_here)
        value_seqs = value_low.reshape(seqs_here, LEN, width_here)
        starts_here = piece_starts[batch_index]
        context_seq, logsum = lax.map(forward_one, (query_seqs, key_seqs, value_seqs, starts_here))
        context_low = context_seq.reshape(group_rows, width_here).astype(jnp.bfloat16)
        attended = lax.psum_scatter(
            slice_term(context_low, full_out, "tc,cd->td").astype(jnp.bfloat16),
            "tensor",
            scatter_dimension=0,
            tiled=True,
        ).astype(jnp.float32)
        middle = token_rows + attended + vectors[4]
        normed_two = layer_norm(middle, vectors[5], vectors[6])
        normed_two_all = lax.all_gather(
            normed_two.astype(jnp.bfloat16), "tensor", axis=0, tiled=True
        )
        before = jnp.dot(normed_two_all, full_up, preferred_element_type=jnp.float32) + up_shift
        activated = gelu_tanh(before).astype(jnp.bfloat16)
        expanded = lax.psum_scatter(
            slice_term(activated, full_down, "tf,fd->td").astype(jnp.bfloat16),
            "tensor",
            scatter_dimension=0,
            tiled=True,
        ).astype(jnp.float32)
        outputs_list.append((middle + expanded + vectors[11]).astype(jnp.bfloat16))
        grad_down = jnp.einsum(
            "tf,td->fd", activated, cotangent_all, preferred_element_type=jnp.float32
        )
        grad_activated = jnp.einsum(
            "td,fd->tf", cotangent_all, full_down, preferred_element_type=jnp.float32
        )
        gelu_pull = jax.vjp(gelu_tanh, before)[1]
        grad_before = gelu_pull(grad_activated)[0].astype(jnp.bfloat16)
        grad_up = jnp.einsum(
            "td,tf->df", normed_two_all, grad_before, preferred_element_type=jnp.float32
        )
        grad_normed_two = lax.psum_scatter(
            slice_term(grad_before, full_up, "tf,df->td").astype(jnp.bfloat16),
            "tensor",
            scatter_dimension=0,
            tiled=True,
        ).astype(jnp.float32)
        second_pull = jax.vjp(layer_norm, middle, vectors[5], vectors[6])[1]
        middle_from_norm, gain_two_grad, shift_two_grad = second_pull(grad_normed_two)
        grad_middle = cotangent_rows.astype(jnp.float32) + middle_from_norm
        grad_middle_all = lax.all_gather(
            grad_middle.astype(jnp.bfloat16), "tensor", axis=0, tiled=True
        )
        grad_out = jnp.einsum(
            "tc,td->cd", context_low, grad_middle_all, preferred_element_type=jnp.float32
        )
        grad_context = jnp.einsum(
            "td,cd->tc", grad_middle_all, full_out, preferred_element_type=jnp.float32
        ).astype(jnp.bfloat16)
        grad_query, grad_key, grad_value = lax.map(
            backward_one,
            (
                query_seqs,
                key_seqs,
                value_seqs,
                grad_context.reshape(seqs_here, LEN, width_here),
                logsum,
                starts_here,
            ),
        )
        grad_stack = jnp.stack(
            [
                grad_query.reshape(group_rows, width_here),
                grad_key.reshape(group_rows, width_here),
                grad_value.reshape(group_rows, width_here),
            ]
        )
        grad_qkv = jnp.einsum(
            "td,cte->cde", normed_all, grad_stack, preferred_element_type=jnp.float32
        )
        grad_normed_one = lax.psum_scatter(
            slice_term(grad_stack, full_qkv, "cte,cde->td").astype(jnp.bfloat16),
            "tensor",
            scatter_dimension=0,
            tiled=True,
        ).astype(jnp.float32)
        first_pull = jax.vjp(layer_norm, token_rows, vectors[0], vectors[1])[1]
        token_from_norm, gain_one_grad, shift_one_grad = first_pull(grad_normed_one)
        input_grads.append(grad_middle + token_from_norm)
        query_bias = jnp.sum(grad_stack[0], axis=0, dtype=jnp.float32)
        value_bias = jnp.sum(grad_stack[2], axis=0, dtype=jnp.float32)
        up_bias = jnp.sum(grad_before, axis=0, dtype=jnp.float32)
        head_rows = jnp.stack(
            [
                gain_one_grad,
                shift_one_grad,
                placed(query_bias, tensor_rank * width_here, D),
                placed(value_bias, tensor_rank * width_here, D),
                jnp.sum(grad_middle, axis=0),
                gain_two_grad,
                shift_two_grad,
            ]
        )
        up_rows = placed(up_bias, tensor_rank * hidden_here, FF).reshape(4, D)
        tail_row = jnp.sum(cotangent_rows, axis=0, dtype=jnp.float32)[None, :]
        vector_total = vector_total + jnp.concatenate([head_rows, up_rows, tail_row], axis=0)
        shard_grads = (
            lax.psum_scatter(
                grad_qkv.astype(jnp.bfloat16), "dp", scatter_dimension=1, tiled=True
            ).astype(jnp.float32),
            lax.psum_scatter(
                grad_out.astype(jnp.bfloat16), "dp", scatter_dimension=1, tiled=True
            ).astype(jnp.float32),
            lax.psum_scatter(
                grad_up.astype(jnp.bfloat16), "dp", scatter_dimension=0, tiled=True
            ).astype(jnp.float32),
            lax.psum_scatter(
                grad_down.astype(jnp.bfloat16), "dp", scatter_dimension=1, tiled=True
            ).astype(jnp.float32),
        )
        grad_total = accumulate(grad_total, shard_grads)
    grad_qkv_shard, grad_out_shard, grad_up_shard, grad_down_shard = grad_total
    moment_qkv = MOMENTUM_DECAY * m_qkv + grad_qkv_shard
    moment_out = MOMENTUM_DECAY * m_out + grad_out_shard
    moment_up = MOMENTUM_DECAY * m_up + grad_up_shard
    moment_down = MOMENTUM_DECAY * m_down + grad_down_shard
    squares = jnp.concatenate(
        [
            jnp.sum(moment_qkv * moment_qkv, axis=(1, 2)),
            jnp.stack(
                [
                    jnp.sum(moment_out * moment_out),
                    jnp.sum(moment_up * moment_up),
                    jnp.sum(moment_down * moment_down),
                ]
            ),
        ]
    )
    vector_grad, square_total = lax.psum((vector_total, squares), ("dp", "tensor"))
    factors = lax.rsqrt(square_total + SQUARE_EPSILON)
    scaled_qkv = (moment_qkv * factors[0:3][:, None, None]).astype(jnp.bfloat16)
    scaled_out = (moment_out * factors[3]).astype(jnp.bfloat16)
    scaled_up = (moment_up * factors[4]).astype(jnp.bfloat16)
    scaled_down = (moment_down * factors[5]).astype(jnp.bfloat16)
    gathered_qkv, gathered_out, gathered_up, gathered_down = (
        lax.all_gather(scaled_qkv, "dp", axis=1, tiled=True),
        lax.all_gather(scaled_out, "dp", axis=1, tiled=True),
        lax.all_gather(scaled_up, "dp", axis=0, tiled=True),
        lax.all_gather(scaled_down, "dp", axis=1, tiled=True),
    )
    offset = shard_rank * shard_rows
    narrow_rows = jnp.concatenate([jnp.swapaxes(gathered_qkv, 1, 2), gathered_out[None]], axis=0)
    wide_rows = jnp.stack([gathered_up.T, gathered_down])
    for sweep_index in range(NS_ITERS):
        gram_share = lax.psum_scatter(
            gram_term(narrow_rows, wide_rows).astype(jnp.bfloat16),
            "tensor",
            scatter_dimension=0,
            tiled=True,
        )
        gram_matrix = lax.all_gather(gram_share, "tensor", axis=0, tiled=True)
        narrow_rows = schulz_step(narrow_rows, gram_matrix[:, 0:4])
        wide_rows = schulz_step(wide_rows, gram_matrix[:, 4:6])
    final_narrow = narrow_rows.astype(jnp.float32)
    final_wide = wide_rows.astype(jnp.float32)
    update_qkv = lax.dynamic_slice_in_dim(
        jnp.swapaxes(final_narrow[0:3], 1, 2), offset, shard_rows, 1
    )
    update_out = lax.dynamic_slice_in_dim(final_narrow[3], offset, shard_rows, 1)
    update_up = lax.dynamic_slice_in_dim(final_wide[0].T, offset, shard_rows, 0)
    update_down = lax.dynamic_slice_in_dim(final_wide[1], offset, shard_rows, 1)
    wide_factor = math.sqrt(FF / D)
    new_qkv = w_qkv - MATRIX_RATE * update_qkv
    new_out = w_out - MATRIX_RATE * update_out
    new_up = w_up - MATRIX_RATE * wide_factor * update_up
    new_down = w_down - MATRIX_RATE * wide_factor * update_down
    moment_vec = MOMENTUM_DECAY * m_vec + vector_grad
    new_vec = vectors - VECTOR_RATE * moment_vec * lax.rsqrt(
        jnp.mean(moment_vec * moment_vec, axis=1, keepdims=True) + SQUARE_EPSILON
    )
    return (
        jnp.stack(outputs_list),
        jnp.stack(input_grads),
        grad_qkv_shard,
        grad_out_shard,
        grad_up_shard,
        grad_down_shard,
        vector_grad,
        moment_qkv,
        moment_out,
        moment_up,
        moment_down,
        moment_vec,
        new_qkv,
        new_out,
        new_up,
        new_down,
        new_vec,
    )


QB = 256
PAIR = 2 * HD
PAIRS = D // PAIR
VMEM_LIMIT = 56 * 1024 * 1024


def layout_grid(starts_ref, dist_ref):
    key_pos = lax.broadcasted_iota(jnp.int32, (LEN, LEN), 0)
    query_pos = lax.broadcasted_iota(jnp.int32, (LEN, LEN), 1)
    gap = query_pos - key_pos
    visible = gap >= 0
    for piece in range(NPIECE):
        start = starts_ref[piece]
        inside_key = (key_pos >= start) & (key_pos < start + PIECE)
        inside_query = (query_pos >= start) & (query_pos < start + PIECE)
        visible = visible | (inside_key & inside_query)
    dist_ref[...] = jnp.where(visible, jnp.abs(gap).astype(jnp.float32), -MASKED_SCORE)


def only_rows(pair, half):
    rows = lax.broadcasted_iota(jnp.int32, pair.shape, 0)
    return jnp.where((rows >= HD) if half else (rows < HD), pair, jnp.zeros_like(pair))


def only_cols(pair, half):
    cols = lax.broadcasted_iota(jnp.int32, pair.shape, 1)
    return jnp.where((cols >= HD) if half else (cols < HD), pair, jnp.zeros_like(pair))


def mul(left, right):
    return jnp.dot(left, right, preferred_element_type=jnp.float32)


def attend_pair(pair, slopes_ref, packed, dist_ref, ctx_ref, exps_ref, stat_ref, ctx_t):
    keys = packed[:, PAIR : 2 * PAIR]
    values_t = packed[:, 2 * PAIR :].T
    queries_t = (packed[:, :PAIR] * (1.0 / math.sqrt(HD))).T
    for half in (0, 1):
        slope = slopes_ref[2 * pair + half]
        queries = only_rows(queries_t, half)
        heads = slice(half * HD, half * HD + HD)
        for block in range(LEN // QB):
            span = min(LEN, QB * block + QB + PIECE)
            cols = slice(block * QB, block * QB + QB)
            scores = mul(keys[:span], queries[:, cols]) - slope * dist_ref[:span, cols]
            top = jnp.max(scores, axis=0, keepdims=True)
            raw = jnp.exp(scores - top)
            inverse = 1.0 / jnp.sum(raw, axis=0, keepdims=True)
            low = raw.astype(jnp.bfloat16)
            exps_ref[half, :span, cols] = low
            ctx_t[heads, cols] = mul(values_t[heads, :span], low) * inverse
            stat_ref[0, half : half + 1, cols] = inverse
    ctx_ref[...] = ctx_t[...].T.astype(jnp.bfloat16)


def attend_bwd_kernel(packed_ref, ctx_ref, grad_ref, exps_ref, stat_ref, out_ref, dq_t, dk_sum, dv_sum):
    scale = 1.0 / math.sqrt(HD)
    queries = packed_ref[:, :PAIR]
    keys_t = packed_ref[:, PAIR : 2 * PAIR].T
    values = packed_ref[:, 2 * PAIR :]
    grads_t = grad_ref[...].T.astype(jnp.float32)
    context_t = ctx_ref[...].T.astype(jnp.float32)
    scaled = []
    inner_rows = []
    for half in (0, 1):
        heads = slice(half * HD, half * HD + HD)
        scaled.append(grads_t[heads] * stat_ref[0, half : half + 1, :])
        inner_rows.append(jnp.sum(scaled[half] * context_t[heads], axis=0, keepdims=True))
    scaled_t = jnp.concatenate(scaled, axis=0).astype(jnp.bfloat16)
    scaled_rows = scaled_t.T
    dk_sum[...] = jnp.zeros_like(dk_sum)
    dv_sum[...] = jnp.zeros_like(dv_sum)
    for half in (0, 1):
        heads = slice(half * HD, half * HD + HD)
        half_t = only_rows(scaled_t, half)
        half_rows = only_cols(scaled_rows, half)
        half_queries = only_cols(queries, half)
        for block in range(LEN // QB):
            span = min(LEN, QB * block + QB + PIECE)
            cols = slice(block * QB, block * QB + QB)
            exps = exps_ref[half, :span, cols]
            grad_probs = mul(values[:span], half_t[:, cols])
            grad_scores = (exps.astype(jnp.float32) * (grad_probs - inner_rows[half][:, cols])).astype(jnp.bfloat16)
            dv_sum[:span, :] += mul(exps, half_rows[cols])
            dk_sum[:span, :] += mul(grad_scores, half_queries[cols])
            dq_t[heads, cols] = mul(keys_t[heads, :span], grad_scores)
    out_ref[:, :PAIR] = (dq_t[...] * scale).T.astype(jnp.bfloat16)
    out_ref[:, PAIR : 2 * PAIR] = (dk_sum[...] * scale).astype(jnp.bfloat16)
    out_ref[:, 2 * PAIR :] = dv_sum[...].astype(jnp.bfloat16)


PACKED_COLS = pl.BlockSpec((LEN, 3 * PAIR), lambda p: (0, p))
PAIR_COLS = pl.BlockSpec((LEN, PAIR), lambda p: (0, p))
PAIR_GRID = pl.BlockSpec((2, LEN, LEN), lambda p: (p, 0, 0))
PAIR_STAT = pl.BlockSpec((1, 2, LEN), lambda p: (p, 0, 0))
SCALARS = pl.BlockSpec(memory_space=pltpu.SMEM)


def attention_backward(packed, context, grad_context, exps, stats):
    return pl.pallas_call(
        attend_bwd_kernel,
        grid=(PAIRS,),
        in_specs=[PACKED_COLS, PAIR_COLS, PAIR_COLS, PAIR_GRID, PAIR_STAT],
        out_specs=PACKED_COLS,
        out_shape=jax.ShapeDtypeStruct((LEN, 3 * D), jnp.bfloat16),
        scratch_shapes=[
            pltpu.VMEM((PAIR, LEN), jnp.float32),
            pltpu.VMEM((LEN, PAIR), jnp.float32),
            pltpu.VMEM((LEN, PAIR), jnp.float32),
        ],
        compiler_params=pltpu.CompilerParams(vmem_limit_bytes=VMEM_LIMIT),
        cost_estimate=pl.CostEstimate(flops=32 * LEN * LEN * D, bytes_accessed=50 * 1024 * 1024, transcendentals=0),
    )(packed, context, grad_context, exps, stats)


SLOTS = 12
SLOT = 512
HALF_SLOT = SLOT // 2
TILE = 256
MESH_IDS = pl.DeviceIdType.MESH


def handler_of(slot):
    wide = slot - 4
    square = slot < 4
    dp_index = jnp.where(square, jnp.where(slot < 2, 2, 12), 4 + 6 * (wide // 4) + wide % 2)
    tensor_index = jnp.where(square, slot % 2, (wide // 2) % 2)
    return dp_index, tensor_index


def muon_kernel(
    moments_ref,
    vec_ref,
    updates_ref,
    vec_out_ref,
    pieces,
    turned,
    vec_pieces,
    vec_sum,
    gram,
    gram_low,
    poly_low,
    half_low,
    chain_low,
    chain_next,
    out_half,
    in_half,
    local_sem,
    send_sem,
    recv_sem,
    half_send,
    half_recv,
):
    groups = lax.axis_size("dp")
    parts = lax.axis_size("tensor")
    count = groups * parts
    dp_me = lax.axis_index("dp")
    t_me = lax.axis_index("tensor")
    me = t_me * groups + dp_me
    is_square = (dp_me == 2) | (dp_me == 12)
    is_up = (dp_me == 4) | (dp_me == 5)
    is_down = (dp_me == 10) | (dp_me == 11)
    is_wide = is_up | is_down
    is_handler = is_square | is_wide
    wide_slot = jnp.where(is_up, 4 + (dp_me - 4), 8 + (dp_me - 10)) + 2 * t_me
    slot_me = jnp.where(is_square, t_me + jnp.where(dp_me == 12, 2, 0), wide_slot)
    slot_me = jnp.where(is_handler, slot_me, 0)

    barrier = pltpu.get_barrier_semaphore()

    def greet(step, carry):
        other = lax.rem(me + step, count)
        pl.semaphore_signal(
            barrier, inc=1, device_id=(lax.rem(other, groups), other // groups), device_id_type=MESH_IDS
        )
        return carry

    lax.fori_loop(1, count, greet, 0)
    pl.semaphore_wait(barrier, count - 1)

    def give(step, carry):
        slot = lax.rem(me + step, SLOTS)
        dp_to, t_to = handler_of(slot)
        away = (dp_to != dp_me) | (t_to != t_me)

        @pl.when(away)
        def _():
            pltpu.make_async_remote_copy(
                src_ref=vec_ref.at[slot],
                dst_ref=vec_pieces.at[me],
                send_sem=send_sem.at[1],
                recv_sem=recv_sem.at[1],
                device_id=(dp_to, t_to),
                device_id_type=MESH_IDS,
            ).start()
            pltpu.make_async_remote_copy(
                src_ref=moments_ref.at[slot],
                dst_ref=pieces.at[me],
                send_sem=send_sem.at[0],
                recv_sem=recv_sem.at[0],
                device_id=(dp_to, t_to),
                device_id_type=MESH_IDS,
            ).start()

        return carry

    lax.fori_loop(0, SLOTS, give, 0)

    def give_back(source, sem, target):
        def one(step, carry):
            other = lax.rem(me + step, count)
            pltpu.make_async_remote_copy(
                src_ref=source.at[other] if source is turned else source,
                dst_ref=target.at[slot_me],
                send_sem=send_sem.at[sem],
                recv_sem=recv_sem.at[sem],
                device_id=(lax.rem(other, groups), other // groups),
                device_id_type=MESH_IDS,
            ).start()
            return carry

        lax.fori_loop(1, count, one, 0)

    @pl.when(is_handler)
    def _():
        own = [
            pltpu.make_async_copy(vec_ref.at[slot_me], vec_pieces.at[me], local_sem.at[0]),
            pltpu.make_async_copy(moments_ref.at[slot_me], pieces.at[me], local_sem.at[1]),
        ]
        for copy in own:
            copy.start()
        for copy in own:
            copy.wait()
        rest = pl.ds(0, count - 1)
        pltpu.make_async_copy(vec_pieces.at[rest], vec_pieces.at[rest], recv_sem.at[1]).wait()
        vec_sum[...] = jnp.sum(vec_pieces[...], axis=0)
        give_back(vec_sum, 2, vec_out_ref)
        own_vec = pltpu.make_async_copy(vec_sum, vec_out_ref.at[slot_me], local_sem.at[0])
        own_vec.start()
        own_vec.wait()
        pltpu.make_async_copy(pieces.at[rest], pieces.at[rest], recv_sem.at[0]).wait()

        rows_of = TILE // 64

        def gram_tile(tile, carry):
            rows = pl.ds(pl.multiple_of(tile * TILE, TILE), TILE)
            total = jnp.zeros((TILE, D), jnp.float32)
            for part in range(parts):
                left = pieces[pl.ds(part * groups + tile * rows_of, rows_of)].reshape(TILE, SLOT)
                right = pieces[part * groups : (part + 1) * groups].reshape(D, SLOT)
                total += lax.dot_general(
                    left, right, (((1,), (1,)), ((), ())), preferred_element_type=jnp.float32
                )
            gram[rows, :] = total
            return carry

        lax.fori_loop(0, D // TILE, gram_tile, 0)

        @pl.when(is_wide)
        def _():
            core = lax.rem(dp_me, 2)
            half = D // 2
            mine = pl.ds(pl.multiple_of(core * half, half), half)
            theirs = pl.ds(pl.multiple_of((1 - core) * half, half), half)
            sibling = (dp_me + 1 - 2 * core, t_me)
            across = (dp_me, 1 - t_me)

            def exchange(stage, place):
                copy = pltpu.make_async_remote_copy(
                    src_ref=out_half.at[stage],
                    dst_ref=in_half.at[stage],
                    send_sem=half_send.at[stage],
                    recv_sem=half_recv.at[stage],
                    device_id=place,
                    device_id_type=MESH_IDS,
                )
                copy.start()
                copy.wait()

            out_half[0] = gram[theirs, :].astype(jnp.bfloat16)
            exchange(0, sibling)
            out_half[1] = (gram[mine, :] + in_half[0].astype(jnp.float32)).astype(jnp.bfloat16)
            exchange(1, across)
            total = out_half[1].astype(jnp.float32) + in_half[1].astype(jnp.float32)
            out_half[2] = total.astype(jnp.bfloat16)
            exchange(2, sibling)
            gram[mine, :] = out_half[2].astype(jnp.float32)
            gram[theirs, :] = in_half[2].astype(jnp.float32)

        def trace_tile(tile, total):
            rows = pl.ds(pl.multiple_of(tile * TILE, TILE), TILE)
            row_ids = lax.broadcasted_iota(jnp.int32, (TILE, D), 0) + tile * TILE
            col_ids = lax.broadcasted_iota(jnp.int32, (TILE, D), 1)
            diagonal = jnp.where(row_ids == col_ids, gram[rows, :], 0.0)
            return total + jnp.sum(jnp.sum(diagonal, axis=0, keepdims=True), axis=1, keepdims=True)

        square_total = lax.fori_loop(0, D // TILE, trace_tile, jnp.zeros((1, 1), jnp.float32))
        factor = lax.rsqrt(square_total + SQUARE_EPSILON)
        gram_low[...] = (gram[...] * (factor * factor)).astype(jnp.bfloat16)

        first, second, third = SCHULZ_FIRST, SCHULZ_SECOND, SCHULZ_THIRD

        def tiles(body):
            def one(tile, carry):
                body(pl.ds(pl.multiple_of(tile * TILE, TILE), TILE))
                return carry

            lax.fori_loop(0, D // TILE, one, 0)

        chain = chain_low
        other = chain_next
        for sweep in range(NS_ITERS):
            target = chain if sweep == 0 else poly_low

            def poly(rows):
                square = mul(gram_low[rows, :], gram_low[...])
                grown = (second / first) * gram_low[rows, :].astype(jnp.float32) + (third / first) * square
                target[rows, :] = grown.astype(jnp.bfloat16)

            tiles(poly)
            if sweep > 0:

                def join(rows, chain=chain, other=other):
                    total = chain[rows, :].astype(jnp.float32) + poly_low[rows, :].astype(jnp.float32)
                    other[rows, :] = (total + mul(chain[rows, :], poly_low[...])).astype(jnp.bfloat16)

                tiles(join)
                chain, other = other, chain
            if sweep < NS_ITERS - 1:

                def half(rows):
                    grown = gram_low[rows, :].astype(jnp.float32) + mul(gram_low[rows, :], target[...])
                    half_low[rows, :] = grown.astype(jnp.bfloat16)

                def full(rows):
                    grown = half_low[rows, :].astype(jnp.float32) + mul(half_low[rows, :], target[...])
                    gram_low[rows, :] = (grown * (first * first)).astype(jnp.bfloat16)

                tiles(half)
                tiles(full)

        scale = factor * (first**NS_ITERS)

        def turn_tile(tile, carry):
            rows = pl.ds(pl.multiple_of(tile * TILE, TILE), TILE)
            for part in range(parts):
                at = pl.ds(part * groups + tile * rows_of, rows_of)
                whole = pieces[part * groups : (part + 1) * groups].reshape(D, SLOT)
                kept = pieces[at].reshape(TILE, SLOT).astype(jnp.float32)
                fresh = (kept + mul(chain[rows, :], whole)) * scale
                turned[at] = fresh.astype(jnp.bfloat16).reshape(rows_of, 64, SLOT)
            return carry

        lax.fori_loop(0, D // TILE, turn_tile, 0)
        give_back(turned, 3, updates_ref)
        own_turned = pltpu.make_async_copy(turned.at[me], updates_ref.at[slot_me], local_sem.at[1])
        own_turned.start()
        own_turned.wait()

    def finish(length):
        here = pl.ds(0, length)
        pltpu.make_async_copy(vec_ref.at[here], vec_ref.at[here], send_sem.at[1]).wait()
        pltpu.make_async_copy(moments_ref.at[here], moments_ref.at[here], send_sem.at[0]).wait()
        pltpu.make_async_copy(vec_out_ref.at[here], vec_out_ref.at[here], recv_sem.at[2]).wait()
        pltpu.make_async_copy(updates_ref.at[here], updates_ref.at[here], recv_sem.at[3]).wait()

    @pl.when(is_handler)
    def _():
        finish(SLOTS - 1)
        rest = pl.ds(0, count - 1)
        pltpu.make_async_copy(vec_pieces.at[rest], vec_pieces.at[rest], send_sem.at[2]).wait()
        pltpu.make_async_copy(turned.at[rest], turned.at[rest], send_sem.at[3]).wait()

    @pl.when(jnp.logical_not(is_handler))
    def _():
        finish(SLOTS)


def muon_call(moments, vec_parts):
    count = lax.axis_size("dp") * lax.axis_size("tensor")
    rows = moments.shape[1]
    vmem = pl.BlockSpec(memory_space=pltpu.VMEM)
    low = pltpu.VMEM((D, D), jnp.bfloat16)
    return pl.pallas_call(
        muon_kernel,
        in_specs=[vmem, vmem],
        out_specs=[vmem, vmem],
        out_shape=[
            jax.ShapeDtypeStruct(moments.shape, jnp.bfloat16),
            jax.ShapeDtypeStruct(vec_parts.shape, jnp.float32),
        ],
        scratch_shapes=[
            pltpu.VMEM((count, rows, SLOT), jnp.bfloat16),
            pltpu.VMEM((count, rows, SLOT), jnp.bfloat16),
            pltpu.VMEM((count,) + vec_parts.shape[1:], jnp.float32),
            pltpu.VMEM(vec_parts.shape[1:], jnp.float32),
            pltpu.VMEM((D, D), jnp.float32),
            low,
            low,
            low,
            low,
            low,
            pltpu.VMEM((3, D // 2, D), jnp.bfloat16),
            pltpu.VMEM((3, D // 2, D), jnp.bfloat16),
            pltpu.SemaphoreType.DMA((2,)),
            pltpu.SemaphoreType.DMA((4,)),
            pltpu.SemaphoreType.DMA((4,)),
            pltpu.SemaphoreType.DMA((3,)),
            pltpu.SemaphoreType.DMA((3,)),
        ],
        compiler_params=pltpu.CompilerParams(
            collective_id=1, has_side_effects=True, vmem_limit_bytes=VMEM_LIMIT
        ),
        cost_estimate=pl.CostEstimate(flops=12 * 2 * D**3, bytes_accessed=4 * 1024 * 1024, transcendentals=0),
    )(moments, vec_parts)


def by_slots(rows):
    return jnp.swapaxes(rows.reshape(rows.shape[0], -1, SLOT), 0, 1)


def from_slots(rows):
    return jnp.swapaxes(rows, 0, 1).reshape(rows.shape[1], -1)


def muon_step(
    shards, vector_total, w_qkv, w_out, w_up, w_down, vectors, m_qkv, m_out, m_up, m_down, m_vec
):
    grad_qkv_shard, grad_out_shard, grad_up_shard, grad_down_shard = shards
    moment_qkv = MOMENTUM_DECAY * m_qkv + grad_qkv_shard
    moment_out = MOMENTUM_DECAY * m_out + grad_out_shard
    moment_up = MOMENTUM_DECAY * m_up + grad_up_shard
    moment_down = MOMENTUM_DECAY * m_down + grad_down_shard
    slots = jnp.concatenate(
        [
            narrow(moment_qkv),
            narrow(moment_out).T[None],
            by_slots(narrow(moment_up)),
            by_slots(narrow(moment_down).T),
        ]
    )
    updates, vector_rows = muon_call(slots, vector_total.reshape(SLOTS, 8, 128))
    vector_grad = vector_rows.reshape(12, D)
    wide_factor = math.sqrt(FF / D)
    new_qkv = w_qkv - MATRIX_RATE * updates[0:3].astype(jnp.float32)
    new_out = w_out - MATRIX_RATE * updates[3].T.astype(jnp.float32)
    new_up = w_up - MATRIX_RATE * wide_factor * from_slots(updates[4:8]).astype(jnp.float32)
    new_down = w_down - MATRIX_RATE * wide_factor * from_slots(updates[8:12]).T.astype(jnp.float32)
    moment_vec = MOMENTUM_DECAY * m_vec + vector_grad
    new_vec = vectors - VECTOR_RATE * moment_vec * lax.rsqrt(
        jnp.mean(moment_vec * moment_vec, axis=1, keepdims=True) + SQUARE_EPSILON
    )
    return (
        grad_qkv_shard,
        grad_out_shard,
        grad_up_shard,
        grad_down_shard,
        vector_grad,
        moment_qkv,
        moment_out,
        moment_up,
        moment_down,
        moment_vec,
        new_qkv,
        new_out,
        new_up,
        new_down,
        new_vec,
    )


def neighbours():
    dp_me = lax.axis_index("dp")
    y = lax.axis_index("tensor")
    core = lax.rem(dp_me, 2)
    x = lax.rem(dp_me // 2, 2)
    z = dp_me // 4
    sibling = (dp_me + 1 - 2 * core, y)
    beside = (dp_me + 2 - 4 * x, y)
    across = (dp_me, 1 - y)
    stations = [(lax.rem(dp_me + 4 * hop, 16), y) for hop in (1, 2, 3)]
    return (z, x, core, y), sibling, beside, across, stations


def greet_neighbours(places):
    barrier = pltpu.get_barrier_semaphore()
    for place in places:
        pl.semaphore_signal(barrier, inc=1, device_id=place, device_id_type=MESH_IDS)
    pl.semaphore_wait(barrier, len(places))


SWAP_AT = 2
SPREAD_LAG = 1


class Spread:
    def __init__(self, slots_ref, table, local_sem, send_sem, recv_sem):
        self.slots_ref, self.table = slots_ref, table
        self.local_sem, self.send_sem, self.recv_sem = local_sem, send_sem, recv_sem
        (self.z, self.x, self.core, self.y), self.sibling, self.beside, self.across, self.stations = neighbours()

    def remote(self, source, target, stage, slot, place):
        return pltpu.make_async_remote_copy(
            src_ref=source,
            dst_ref=target,
            send_sem=self.send_sem.at[stage, slot],
            recv_sem=self.recv_sem.at[stage, slot],
            device_id=place,
            device_id_type=MESH_IDS,
        )

    def cols(self, slot, part, start=0, size=SLOT):
        _, column, distance, _ = self.table[slot]
        if isinstance(part, int):
            return pl.ds(column + part * distance + start, size)
        return pl.ds(pl.multiple_of(column + part * distance + start, 128), size)

    def own(self, slot):
        here = self.table[slot][0].at[self.z, self.x, self.core, :, self.cols(slot, self.y)]
        return pltpu.make_async_copy(self.slots_ref.at[slot], here, self.local_sem.at[slot])

    def along_z(self, slot):
        here = self.table[slot][0].at[self.z, self.x, self.core, :, self.cols(slot, self.y)]
        return [
            self.remote(self.slots_ref.at[slot], here, hop, slot, place)
            for hop, place in enumerate(self.stations)
        ]

    def second(self, slot):
        whole, _, _, size = self.table[slot]
        copies = []
        if size:
            part = whole.at[:, self.x, self.core, :, self.cols(slot, self.y, 0, size)]
            copies.append(self.remote(part, part, 3, slot, self.beside))
        if size < SLOT:
            part = whole.at[:, self.x, self.core, :, self.cols(slot, self.y, size, SLOT - size)]
            copies.append(self.remote(part, part, 4, slot, self.across))
        return copies

    def third(self, slot):
        whole, _, _, size = self.table[slot]
        copies = []
        if size:
            part = whole.at[:, :, self.core, :, self.cols(slot, self.y, 0, size)]
            copies.append(self.remote(part, part, 5, slot, self.across))
        if size < SLOT:
            for index in (0, 1):
                part = whole.at[:, self.x, self.core, :, self.cols(slot, index, size, SLOT - size)]
                copies.append(self.remote(part, part, 6 + index, slot, self.beside))
        return copies

    def fourth(self, slot):
        whole = self.table[slot][0]
        copies = []
        for index in (0, 1):
            part = whole.at[:, :, self.core, :, self.cols(slot, index)]
            copies.append(self.remote(part, part, 8 + index, slot, self.sibling))
        return copies

    def begin(self):
        for slot in range(len(self.table)):
            self.own(slot).start()
            for copy in self.along_z(slot):
                copy.start()

    def tick(self, index):
        count = len(self.table)
        if index < count:
            self.own(index).wait()
            for copy in self.along_z(index):
                copy.wait_recv()
            for copy in self.second(index):
                copy.start()
        if 0 <= index - SPREAD_LAG < count:
            for copy in self.second(index - SPREAD_LAG):
                copy.wait_recv()
            for copy in self.third(index - SPREAD_LAG):
                copy.start()
        if 0 <= index - 2 * SPREAD_LAG < count:
            for copy in self.third(index - 2 * SPREAD_LAG):
                copy.wait_recv()
            for copy in self.fourth(index - 2 * SPREAD_LAG):
                copy.start()

    def ticks(self):
        return len(self.table) + 2 * SPREAD_LAG

    def finish(self):
        for slot in range(len(self.table)):
            for copy in self.along_z(slot) + self.second(slot) + self.third(slot):
                copy.wait_send()
            for copy in self.fourth(slot):
                copy.wait()


def spread_semaphores(count):
    return [
        pltpu.SemaphoreType.DMA((count,)),
        pltpu.SemaphoreType.DMA((10, count)),
        pltpu.SemaphoreType.DMA((10, count)),
    ]


def first_spread_kernel(slots_ref, tokens_ref, whole_ref, got_ref, local_sem, send_sem, recv_sem, token_sem):
    table = [(whole_ref, index * SLOT, 3 * SLOT, 0) for index in range(3)]
    spread = Spread(slots_ref, table, local_sem, send_sem, recv_sem)
    greet_neighbours([spread.sibling, spread.beside, spread.across] + spread.stations)
    swap = pltpu.make_async_remote_copy(
        src_ref=tokens_ref.at[1 - spread.y],
        dst_ref=got_ref,
        send_sem=token_sem.at[0],
        recv_sem=token_sem.at[1],
        device_id=spread.across,
        device_id_type=MESH_IDS,
    )
    spread.begin()
    for index in range(spread.ticks()):
        spread.tick(index)
        if index == SWAP_AT:
            swap.start()
    spread.finish()
    swap.wait()


def attend_spread_kernel(
    starts_ref,
    slopes_ref,
    normed_ref,
    weights_ref,
    shifts_ref,
    slots_ref,
    cotangent_ref,
    packed_ref,
    ctx_ref,
    exps_ref,
    stat_ref,
    out_ref,
    up_ref,
    down_ref,
    got_ref,
    dist_ref,
    ctx_t,
    local_sem,
    send_sem,
    recv_sem,
    token_sem,
):
    pair = pl.program_id(0)
    table = [(out_ref, 0, SLOT, 0)]
    table += [(up_ref, index * SLOT, 4 * SLOT, HALF_SLOT if index % 2 else 0) for index in range(4)]
    table += [(down_ref, index * SLOT, 4 * SLOT, HALF_SLOT if index % 2 else 0) for index in range(4)]
    spread = Spread(slots_ref, table, local_sem, send_sem, recv_sem)
    swap = pltpu.make_async_remote_copy(
        src_ref=cotangent_ref.at[1 - spread.y],
        dst_ref=got_ref,
        send_sem=token_sem.at[0],
        recv_sem=token_sem.at[1],
        device_id=spread.across,
        device_id_type=MESH_IDS,
    )

    @pl.when(pair == 0)
    def _():
        greet_neighbours([spread.sibling, spread.beside, spread.across] + spread.stations)
        spread.begin()
        layout_grid(starts_ref, dist_ref)

    for index in range(1, PAIRS):

        @pl.when(pair == index)
        def _(index=index):
            spread.tick(index - 1)
            if index == 5:
                swap.start()

    packed = (mul(normed_ref[...], weights_ref[...]) + shifts_ref[...]).astype(jnp.bfloat16)
    packed_ref[...] = packed
    attend_pair(pair, slopes_ref, packed, dist_ref, ctx_ref, exps_ref, stat_ref, ctx_t)

    @pl.when(pair == PAIRS - 1)
    def _():
        for index in range(PAIRS - 1, spread.ticks()):
            spread.tick(index)
        spread.finish()
        swap.wait()


def whole_shape(columns):
    return jax.ShapeDtypeStruct((4, 2, 2, 64, columns), jnp.bfloat16)


def first_spread(slots, tokens):
    anywhere = pl.BlockSpec(memory_space=pl.ANY)
    whole, got = pl.pallas_call(
        first_spread_kernel,
        in_specs=[anywhere] * 2,
        out_specs=[anywhere] * 2,
        out_shape=[whole_shape(3 * D), jax.ShapeDtypeStruct(tokens.shape[1:], tokens.dtype)],
        scratch_shapes=spread_semaphores(3) + [pltpu.SemaphoreType.DMA((2,))],
        compiler_params=pltpu.CompilerParams(collective_id=3, has_side_effects=True),
    )(slots, tokens)
    return whole.reshape(D, 3 * D), got


def attend_spread(starts, slopes, normed, weights, shifts, slots, cotangent):
    anywhere = pl.BlockSpec(memory_space=pl.ANY)
    packed, context, exps, stats, out, up, down, got = pl.pallas_call(
        attend_spread_kernel,
        grid=(PAIRS,),
        in_specs=[
            SCALARS,
            SCALARS,
            pl.BlockSpec((LEN, D), lambda p: (0, 0)),
            PACKED_COLS,
            pl.BlockSpec((1, 3 * PAIR), lambda p: (0, p)),
            anywhere,
            anywhere,
        ],
        out_specs=[PACKED_COLS, PAIR_COLS, PAIR_GRID, PAIR_STAT] + [anywhere] * 4,
        out_shape=[
            jax.ShapeDtypeStruct((LEN, 3 * D), jnp.bfloat16),
            jax.ShapeDtypeStruct((LEN, D), jnp.bfloat16),
            jax.ShapeDtypeStruct((H, LEN, LEN), jnp.bfloat16),
            jax.ShapeDtypeStruct((PAIRS, 2, LEN), jnp.float32),
            whole_shape(D),
            whole_shape(FF),
            whole_shape(FF),
            jax.ShapeDtypeStruct(cotangent.shape[1:], cotangent.dtype),
        ],
        scratch_shapes=[pltpu.VMEM((LEN, LEN), jnp.float32), pltpu.VMEM((PAIR, LEN), jnp.float32)]
        + spread_semaphores(9)
        + [pltpu.SemaphoreType.DMA((2,))],
        compiler_params=pltpu.CompilerParams(
            collective_id=4, has_side_effects=True, vmem_limit_bytes=VMEM_LIMIT
        ),
        cost_estimate=pl.CostEstimate(
            flops=16 * LEN * LEN * D, bytes_accessed=90 * 1024 * 1024, transcendentals=H * LEN * LEN
        ),
    )(starts, slopes, normed, weights, shifts, slots, cotangent)
    wholes = out.reshape(D, D), up.reshape(D, FF), down.reshape(D, FF)
    return packed, context, exps, stats, wholes, got


GROUP_SLOTS = (3, 1, 4, 4)
LAG = 2


def sum_kernel(
    qkv_ref,
    out_ref,
    up_ref,
    down_ref,
    total_ref,
    mine,
    first,
    second_y,
    second_x,
    third,
    fourth,
    load_sem,
    send_sem,
    recv_sem,
):
    (z, x, core, y), sibling, beside, across, stations = neighbours()
    low_cols = pl.ds(0, HALF_SLOT)
    high_cols = pl.ds(HALF_SLOT, HALF_SLOT)

    greet_neighbours([sibling, beside, across] + stations)

    def remote(source, target, stage, slot, place):
        return pltpu.make_async_remote_copy(
            src_ref=source,
            dst_ref=target,
            send_sem=send_sem.at[stage, slot],
            recv_sem=recv_sem.at[stage, slot],
            device_id=place,
            device_id_type=MESH_IDS,
        )

    slot = 0
    for ref, number in zip((qkv_ref, out_ref, up_ref, down_ref), GROUP_SLOTS):
        for index in range(number):
            for part in (0, 1):
                cols = pl.ds((part * number + index) * SLOT, SLOT)
                remote(ref.at[:, :, 1 - core, :, cols], first.at[slot, part], 0, slot, sibling).start()
                pltpu.make_async_copy(
                    ref.at[:, :, core, :, cols], mine.at[slot, part], load_sem.at[slot]
                ).start()
            slot += 1

    def second_copies(slot):
        return (
            remote(first.at[slot, 1 - y, :, :, :, low_cols], second_y.at[slot], 1, slot, across),
            remote(first.at[slot, :, :, 1 - x, :, high_cols], second_x.at[slot], 2, slot, beside),
        )

    def third_copies(slot):
        return (
            remote(second_y.at[slot, :, 1 - x], third.at[slot, :, :, low_cols], 3, slot, beside),
            remote(second_x.at[slot, 1 - y], third.at[slot, :, :, high_cols], 4, slot, across),
        )

    def fourth_copies(slot):
        return [
            remote(third.at[slot, lax.rem(z + hop, 4)], fourth.at[slot, hop - 1], 4 + hop, slot, place)
            for hop, place in zip((1, 2, 3), stations)
        ]

    def landed(ref, stage, slot):
        pltpu.make_async_copy(ref, ref, recv_sem.at[stage, slot]).wait()

    def step(index, carry):
        @pl.when(index < SLOTS)
        def _():
            slot = index
            pltpu.make_async_copy(mine.at[slot], mine.at[slot], load_sem.at[slot]).wait()
            landed(first.at[slot], 0, slot)
            first[slot] = first[slot] + mine[slot]
            for copy in second_copies(slot):
                copy.start()

        @pl.when((index >= LAG) & (index < SLOTS + LAG))
        def _():
            slot = index - LAG
            landed(second_y.at[slot], 1, slot)
            second_y[slot] = second_y[slot] + first[slot, y, :, :, :, :HALF_SLOT]
            landed(second_x.at[slot], 2, slot)
            second_x[slot] = second_x[slot] + first[slot, :, :, x, :, HALF_SLOT:]
            for copy in third_copies(slot):
                copy.start()

        @pl.when((index >= 2 * LAG) & (index < SLOTS + 2 * LAG))
        def _():
            slot = index - 2 * LAG
            landed(third.at[slot, :, :, low_cols], 3, slot)
            landed(third.at[slot, :, :, high_cols], 4, slot)
            third[slot, :, :, :HALF_SLOT] = third[slot, :, :, :HALF_SLOT] + second_y[slot, :, x]
            third[slot, :, :, HALF_SLOT:] = third[slot, :, :, HALF_SLOT:] + second_x[slot, y]
            for copy in fourth_copies(slot):
                copy.start()

        @pl.when(index >= 3 * LAG)
        def _():
            slot = index - 3 * LAG
            total = third[slot, z].astype(jnp.float32)
            for hop in (1, 2, 3):
                landed(fourth.at[slot, hop - 1], 4 + hop, slot)
                total = total + fourth[slot, hop - 1].astype(jnp.float32)
            total_ref[slot] = total

        return carry

    lax.fori_loop(0, SLOTS + 3 * LAG, step, 0)

    def sent(slot, carry):
        pltpu.make_async_copy(mine.at[slot], mine.at[slot], send_sem.at[0, slot]).wait()
        for copy in second_copies(slot) + third_copies(slot) + tuple(fourth_copies(slot)):
            copy.wait_send()
        return carry

    lax.fori_loop(0, SLOTS, sent, 0)


def sum_over_devices(grads):
    rows = 64
    refs = [grad.reshape(4, 2, 2, rows, grad.shape[-1]) for grad in grads]
    part = (SLOTS, 2, 4, 2, rows, SLOT)
    anywhere = pl.BlockSpec(memory_space=pl.ANY)
    return pl.pallas_call(
        sum_kernel,
        in_specs=[anywhere] * 4,
        out_specs=pl.BlockSpec(memory_space=pltpu.VMEM),
        out_shape=jax.ShapeDtypeStruct((SLOTS, rows, SLOT), jnp.float32),
        scratch_shapes=[
            pltpu.VMEM(part, jnp.bfloat16),
            pltpu.VMEM(part, jnp.bfloat16),
            pltpu.VMEM((SLOTS, 4, 2, rows, HALF_SLOT), jnp.bfloat16),
            pltpu.VMEM((SLOTS, 2, 4, rows, HALF_SLOT), jnp.bfloat16),
            pltpu.VMEM((SLOTS, 4, rows, SLOT), jnp.bfloat16),
            pltpu.VMEM((SLOTS, 3, rows, SLOT), jnp.bfloat16),
            pltpu.SemaphoreType.DMA((SLOTS,)),
            pltpu.SemaphoreType.DMA((8, SLOTS)),
            pltpu.SemaphoreType.DMA((8, SLOTS)),
        ],
        compiler_params=pltpu.CompilerParams(
            collective_id=2, has_side_effects=True, vmem_limit_bytes=VMEM_LIMIT
        ),
        cost_estimate=pl.CostEstimate(flops=0, bytes_accessed=300 * 1024 * 1024, transcendentals=0),
    )(*refs)


def narrow(rows):
    return rows.astype(jnp.bfloat16)


def contract(left, right, left_dim, right_dim):
    return lax.dot_general(
        left, right, (((left_dim,), (right_dim,)), ((), ())), preferred_element_type=jnp.float32
    )


def in_order(rank, own, got):
    return jnp.where(rank == 0, jnp.concatenate([own, got]), jnp.concatenate([got, own]))


def swap_halves(mine, rank):
    rows = mine.shape[0] // 2
    kept = lax.dynamic_slice_in_dim(mine, rank * rows, rows, 0)
    sent = lax.dynamic_slice_in_dim(mine, (1 - rank) * rows, rows, 0)
    got = lax.ppermute(sent, "tensor", [(0, 1), (1, 0)])
    return jnp.where(rank == 0, jnp.stack([kept, got]), jnp.stack([got, kept]))


def by_pairs(rows):
    count, height, width = rows.shape
    return jnp.transpose(rows.reshape(count, height, width // PAIR, PAIR), (1, 2, 0, 3)).reshape(height, -1)


def from_pairs(rows):
    height = rows.shape[0]
    return jnp.transpose(rows.reshape(height, -1, 3, PAIR), (2, 0, 1, 3)).reshape(3, height, -1)


def sequence_step(
    tokens,
    cotangent,
    piece_starts,
    w_qkv,
    w_out,
    w_up,
    w_down,
    vectors,
    m_qkv,
    m_out,
    m_up,
    m_down,
    m_vec,
):
    rank = lax.axis_index("tensor")
    slopes = jnp.exp2(-8.0 * jnp.arange(1, H + 1, dtype=jnp.float32) / H)
    starts = lax.dynamic_slice_in_dim(piece_starts[:, 0], rank, 1, 0)[0]
    own_tokens = lax.dynamic_index_in_dim(tokens, rank, 0, keepdims=False)
    own_cotangent = lax.dynamic_index_in_dim(cotangent, rank, 0, keepdims=False)

    full_qkv, other_tokens = first_spread(by_slots(by_pairs(narrow(w_qkv))), tokens)
    token_rows = in_order(rank, own_tokens, other_tokens).astype(jnp.float32)
    normed_one = narrow(layer_norm(token_rows, vectors[0], vectors[1]))
    shifts = by_pairs(jnp.stack([vectors[2], jnp.zeros((D,), jnp.float32), vectors[3]])[:, None])
    later_slots = jnp.concatenate(
        [narrow(w_out).T[None], by_slots(narrow(w_up)), by_slots(narrow(w_down).T)]
    )
    packed, context, exps, stats, wholes, other_cotangent = attend_spread(
        starts, slopes, normed_one, full_qkv, shifts, later_slots, cotangent
    )
    full_out, full_up, full_down = wholes
    cotangent_low = in_order(rank, own_cotangent, other_cotangent)
    cotangent_rows = cotangent_low.astype(jnp.float32)

    middle = token_rows + contract(context, full_out, 1, 1) + vectors[4]
    normed_two = narrow(layer_norm(middle, vectors[5], vectors[6]))
    before = contract(normed_two, full_up, 1, 0) + vectors[7:11].reshape(FF)
    activated = narrow(gelu_tanh(before))
    block_rows = narrow(middle + contract(activated, full_down, 1, 1) + vectors[11])
    output_pair = swap_halves(block_rows, rank)

    grad_down = narrow(contract(cotangent_low, activated, 0, 0))
    gelu_pull = jax.vjp(gelu_tanh, before)[1]
    grad_before = narrow(gelu_pull(contract(cotangent_low, full_down, 1, 0))[0])
    grad_up = narrow(contract(normed_two, grad_before, 0, 0))
    second_pull = jax.vjp(layer_norm, middle, vectors[5], vectors[6])[1]
    middle_from_norm, gain_two_grad, shift_two_grad = second_pull(contract(grad_before, full_up, 1, 1))
    grad_middle = cotangent_rows + middle_from_norm
    grad_middle_low = narrow(grad_middle)
    grad_out = narrow(contract(grad_middle_low, context, 0, 0))
    grad_context = narrow(contract(grad_middle_low, full_out, 1, 0))
    grad_packed = attention_backward(packed, context, grad_context, exps, stats)
    grad_qkv = narrow(contract(normed_one, grad_packed, 0, 0))
    sums = sum_over_devices((grad_qkv, grad_out, grad_up, grad_down))
    first_pull = jax.vjp(layer_norm, token_rows, vectors[0], vectors[1])[1]
    token_from_norm, gain_one_grad, shift_one_grad = first_pull(contract(grad_packed, full_qkv, 1, 1))
    grad_token_rows = grad_middle + token_from_norm
    token_pair = swap_halves(narrow(grad_token_rows), rank).astype(jnp.float32)

    packed_sums = from_pairs(jnp.sum(grad_packed, axis=0, dtype=jnp.float32)[None])[:, 0]
    vector_total = jnp.concatenate(
        [
            jnp.stack(
                [
                    gain_one_grad,
                    shift_one_grad,
                    packed_sums[0],
                    packed_sums[2],
                    jnp.sum(grad_middle, axis=0),
                    gain_two_grad,
                    shift_two_grad,
                ]
            ),
            jnp.sum(grad_before, axis=0, dtype=jnp.float32).reshape(4, D),
            jnp.sum(cotangent_rows, axis=0)[None],
        ]
    )
    shards = (
        from_pairs(from_slots(sums[0:3])),
        sums[3].T,
        from_slots(sums[4:8]),
        from_slots(sums[8:12]).T,
    )
    outputs = muon_step(shards, vector_total, w_qkv, w_out, w_up, w_down, vectors, m_qkv, m_out, m_up, m_down, m_vec)
    return (output_pair, token_pair) + outputs


def solution(mesh):
    in_specs = (
        P(None, ("dp", "tensor"), None),
        P(None, ("dp", "tensor"), None),
        P(None, "dp", None),
        P(None, "dp", "tensor"),
        P("tensor", "dp"),
        P("dp", "tensor"),
        P("tensor", "dp"),
        P(),
        P(None, "dp", "tensor"),
        P("tensor", "dp"),
        P("dp", "tensor"),
        P("tensor", "dp"),
        P(),
    )
    out_specs = (
        P(None, ("dp", "tensor"), None),
        P(None, ("dp", "tensor"), None),
        P(None, "dp", "tensor"),
        P("tensor", "dp"),
        P("dp", "tensor"),
        P("tensor", "dp"),
        P(),
        P(None, "dp", "tensor"),
        P("tensor", "dp"),
        P("dp", "tensor"),
        P("tensor", "dp"),
        P(),
        P(None, "dp", "tensor"),
        P("tensor", "dp"),
        P("dp", "tensor"),
        P("tensor", "dp"),
        P(),
    )
    groups_fit = mesh.shape["tensor"] == MB and mesh.shape["dp"] == 16

    def pick(*arrays):
        if groups_fit and arrays[2].shape[1] == 1:
            return sequence_step(*arrays)
        return on_device(*arrays)

    return jax.shard_map(
        pick, mesh=mesh, in_specs=in_specs, out_specs=out_specs, check_vma=False
    )
```

```python
import math

import jax
import jax.numpy as jnp
from jax import lax
from jax.experimental import pallas as pl
from jax.experimental.pallas import tpu as pltpu
from jax.sharding import PartitionSpec as P

D = 1024
H = 16
HD = 64
FF = 4096
LEN = 1024
PIECE = 256
NPIECE = 2
MB = 2
NS_ITERS = 3


NORM_EPSILON = 1e-05
SQUARE_EPSILON = 1e-06
MASKED_SCORE = -1e30
SCHULZ_FIRST = 3.4445
SCHULZ_SECOND = -4.775
SCHULZ_THIRD = 2.0315
MOMENTUM_DECAY = 0.5
MATRIX_RATE = 0.5
VECTOR_RATE = 0.05


def layer_norm(inputs, gain_row, shift_row):
    average = jnp.mean(inputs, axis=-1, keepdims=True)
    centered = inputs - average
    variance = jnp.mean(centered * centered, axis=-1, keepdims=True)
    return centered * lax.rsqrt(variance + NORM_EPSILON) * gain_row + shift_row


def gelu_tanh(inputs):
    return jax.nn.gelu(inputs, approximate=True)


def score_layout(starts, slopes):
    positions = jnp.arange(LEN, dtype=jnp.int32)
    inside = (positions[None, :] >= starts[:, None]) & (
        positions[None, :] < starts[:, None] + PIECE
    )
    labels = jnp.arange(1, NPIECE + 1, dtype=jnp.int32)
    piece_label = jnp.sum(jnp.where(inside, labels[:, None], 0), axis=0)
    same_piece = (piece_label[:, None] == piece_label[None, :]) & (piece_label[:, None] > 0)
    visible = (positions[None, :] <= positions[:, None]) | same_piece
    distance = jnp.abs(positions[:, None] - positions[None, :]).astype(jnp.float32)
    penalty = -slopes[:, None, None] * distance[None, :, :]
    return (visible, penalty)


def head_scores(query_heads, key_heads, starts, slopes):
    visible, penalty = score_layout(starts, slopes)
    raw_scores = jnp.einsum(
        "qhd,khd->hqk", query_heads, key_heads, preferred_element_type=jnp.float32
    )
    scores = raw_scores * (1.0 / math.sqrt(HD)) + penalty
    return jnp.where(visible[None, :, :], scores, MASKED_SCORE)


def attend_forward(element, slopes):
    query_seq, key_seq, value_seq, starts = element
    heads_here = slopes.shape[0]
    query_heads = query_seq.reshape(LEN, heads_here, HD)
    key_heads = key_seq.reshape(LEN, heads_here, HD)
    value_heads = value_seq.reshape(LEN, heads_here, HD)
    scores = head_scores(query_heads, key_heads, starts, slopes)
    maximum = jnp.max(scores, axis=-1, keepdims=True)
    weights_raw = jnp.exp(scores - maximum)
    denominator = jnp.sum(weights_raw, axis=-1, keepdims=True)
    probabilities = weights_raw / denominator
    context = jnp.einsum(
        "hqk,khd->qhd",
        probabilities.astype(jnp.bfloat16),
        value_heads,
        preferred_element_type=jnp.float32,
    )
    logsum = (maximum + jnp.log(denominator))[..., 0]
    return (context.reshape(LEN, heads_here * HD), logsum)


def attend_backward(element, slopes):
    query_seq, key_seq, value_seq, context_grad, logsum, starts = element
    heads_here = slopes.shape[0]
    query_heads = query_seq.reshape(LEN, heads_here, HD)
    key_heads = key_seq.reshape(LEN, heads_here, HD)
    value_heads = value_seq.reshape(LEN, heads_here, HD)
    grad_heads = context_grad.reshape(LEN, heads_here, HD)
    scores = head_scores(query_heads, key_heads, starts, slopes)
    probabilities = jnp.exp(scores - logsum[..., None])
    grad_probs = jnp.einsum(
        "qhd,khd->hqk", grad_heads, value_heads, preferred_element_type=jnp.float32
    )
    inner_sum = jnp.sum(probabilities * grad_probs, axis=-1, keepdims=True)
    grad_scores = (probabilities * (grad_probs - inner_sum)).astype(jnp.bfloat16)
    scale_factor = 1.0 / math.sqrt(HD)
    grad_query = (
        jnp.einsum("hqk,khd->qhd", grad_scores, key_heads, preferred_element_type=jnp.float32)
        * scale_factor
    )
    grad_key = (
        jnp.einsum("hqk,qhd->khd", grad_scores, query_heads, preferred_element_type=jnp.float32)
        * scale_factor
    )
    grad_value = jnp.einsum(
        "hqk,qhd->khd",
        probabilities.astype(jnp.bfloat16),
        grad_heads,
        preferred_element_type=jnp.float32,
    )
    width_here = heads_here * HD
    return (
        grad_query.astype(jnp.bfloat16).reshape(LEN, width_here),
        grad_key.astype(jnp.bfloat16).reshape(LEN, width_here),
        grad_value.astype(jnp.bfloat16).reshape(LEN, width_here),
    )


def placed(values, offset, length):
    return lax.dynamic_update_slice_in_dim(jnp.zeros((length,), jnp.float32), values, offset, 0)


def accumulate(totals, addend):
    if totals is None:
        return addend
    return tuple((former + latter for former, latter in zip(totals, addend)))


def gram_term(narrow_rows, wide_rows):
    part_narrow = jnp.einsum(
        "mrc,mrd->cmd", narrow_rows, narrow_rows, preferred_element_type=jnp.float32
    )
    part_wide = jnp.einsum("mrc,mrd->cmd", wide_rows, wide_rows, preferred_element_type=jnp.float32)
    return jnp.concatenate([part_narrow, part_wide], axis=1)


def schulz_step(state, gram_matrix):
    turned = jnp.einsum("mrc,cmd->mrd", state, gram_matrix, preferred_element_type=jnp.float32)
    mixed = (SCHULZ_SECOND * state.astype(jnp.float32) + SCHULZ_THIRD * turned).astype(jnp.bfloat16)
    return (
        SCHULZ_FIRST * state.astype(jnp.float32)
        + jnp.einsum("mrc,cmd->mrd", mixed, gram_matrix, preferred_element_type=jnp.float32)
    ).astype(jnp.bfloat16)


def slice_term(source, weights, pattern):
    return jnp.einsum(pattern, source, weights, preferred_element_type=jnp.float32)


def on_device(
    tokens,
    cotangent,
    piece_starts,
    w_qkv,
    w_out,
    w_up,
    w_down,
    vectors,
    m_qkv,
    m_out,
    m_up,
    m_down,
    m_vec,
):
    tensor_count = lax.axis_size("tensor")
    tensor_rank = lax.axis_index("tensor")
    shard_rank = lax.axis_index("dp")
    heads_here = H // tensor_count
    width_here = heads_here * HD
    hidden_here = FF // tensor_count
    rows_here = tokens.shape[1]
    group_rows = rows_here * tensor_count
    seqs_here = piece_starts.shape[1]
    shard_rows = w_qkv.shape[1]
    head_ids = tensor_rank * heads_here + jnp.arange(heads_here, dtype=jnp.int32) + 1
    slopes = jnp.exp2(-8.0 * head_ids.astype(jnp.float32) / H)
    query_shift = lax.dynamic_slice_in_dim(vectors[2], tensor_rank * width_here, width_here, 0)
    value_shift = lax.dynamic_slice_in_dim(vectors[3], tensor_rank * width_here, width_here, 0)
    up_shift = lax.dynamic_slice_in_dim(
        vectors[7:11].reshape(FF), tensor_rank * hidden_here, hidden_here, 0
    )
    low_qkv = w_qkv.astype(jnp.bfloat16)
    low_out = w_out.astype(jnp.bfloat16)
    low_up = w_up.astype(jnp.bfloat16)
    low_down = w_down.astype(jnp.bfloat16)
    outputs_list = []
    input_grads = []
    vector_total = jnp.zeros((12, D), jnp.float32)
    grad_total = None

    def forward_one(element):
        return attend_forward(element, slopes)

    def backward_one(element):
        return attend_backward(element, slopes)

    for batch_index in range(MB):
        full_qkv, full_out, full_up, full_down = (
            lax.all_gather(low_qkv, "dp", axis=1, tiled=True),
            lax.all_gather(low_out, "dp", axis=1, tiled=True),
            lax.all_gather(low_up, "dp", axis=0, tiled=True),
            lax.all_gather(low_down, "dp", axis=1, tiled=True),
        )
        token_rows = tokens[batch_index].astype(jnp.float32)
        cotangent_rows = cotangent[batch_index]
        normed_one = layer_norm(token_rows, vectors[0], vectors[1])
        normed_all, cotangent_all = (
            lax.all_gather(normed_one.astype(jnp.bfloat16), "tensor", axis=0, tiled=True),
            lax.all_gather(cotangent_rows, "tensor", axis=0, tiled=True),
        )
        projected = jnp.einsum(
            "td,cde->cte", normed_all, full_qkv, preferred_element_type=jnp.float32
        )
        query_low = (projected[0] + query_shift).astype(jnp.bfloat16)
        key_low = projected[1].astype(jnp.bfloat16)
        value_low = (projected[2] + value_shift).astype(jnp.bfloat16)
        query_seqs = query_low.reshape(seqs_here, LEN, width_here)
        key_seqs = key_low.reshape(seqs_here, LEN, width_here)
        value_seqs = value_low.reshape(seqs_here, LEN, width_here)
        starts_here = piece_starts[batch_index]
        context_seq, logsum = lax.map(forward_one, (query_seqs, key_seqs, value_seqs, starts_here))
        context_low = context_seq.reshape(group_rows, width_here).astype(jnp.bfloat16)
        attended = lax.psum_scatter(
            slice_term(context_low, full_out, "tc,cd->td").astype(jnp.bfloat16),
            "tensor",
            scatter_dimension=0,
            tiled=True,
        ).astype(jnp.float32)
        middle = token_rows + attended + vectors[4]
        normed_two = layer_norm(middle, vectors[5], vectors[6])
        normed_two_all = lax.all_gather(
            normed_two.astype(jnp.bfloat16), "tensor", axis=0, tiled=True
        )
        before = jnp.dot(normed_two_all, full_up, preferred_element_type=jnp.float32) + up_shift
        activated = gelu_tanh(before).astype(jnp.bfloat16)
        expanded = lax.psum_scatter(
            slice_term(activated, full_down, "tf,fd->td").astype(jnp.bfloat16),
            "tensor",
            scatter_dimension=0,
            tiled=True,
        ).astype(jnp.float32)
        outputs_list.append((middle + expanded + vectors[11]).astype(jnp.bfloat16))
        grad_down = jnp.einsum(
            "tf,td->fd", activated, cotangent_all, preferred_element_type=jnp.float32
        )
        grad_activated = jnp.einsum(
            "td,fd->tf", cotangent_all, full_down, preferred_element_type=jnp.float32
        )
        gelu_pull = jax.vjp(gelu_tanh, before)[1]
        grad_before = gelu_pull(grad_activated)[0].astype(jnp.bfloat16)
        grad_up = jnp.einsum(
            "td,tf->df", normed_two_all, grad_before, preferred_element_type=jnp.float32
        )
        grad_normed_two = lax.psum_scatter(
            slice_term(grad_before, full_up, "tf,df->td").astype(jnp.bfloat16),
            "tensor",
            scatter_dimension=0,
            tiled=True,
        ).astype(jnp.float32)
        second_pull = jax.vjp(layer_norm, middle, vectors[5], vectors[6])[1]
        middle_from_norm, gain_two_grad, shift_two_grad = second_pull(grad_normed_two)
        grad_middle = cotangent_rows.astype(jnp.float32) + middle_from_norm
        grad_middle_all = lax.all_gather(
            grad_middle.astype(jnp.bfloat16), "tensor", axis=0, tiled=True
        )
        grad_out = jnp.einsum(
            "tc,td->cd", context_low, grad_middle_all, preferred_element_type=jnp.float32
        )
        grad_context = jnp.einsum(
            "td,cd->tc", grad_middle_all, full_out, preferred_element_type=jnp.float32
        ).astype(jnp.bfloat16)
        grad_query, grad_key, grad_value = lax.map(
            backward_one,
            (
                query_seqs,
                key_seqs,
                value_seqs,
                grad_context.reshape(seqs_here, LEN, width_here),
                logsum,
                starts_here,
            ),
        )
        grad_stack = jnp.stack(
            [
                grad_query.reshape(group_rows, width_here),
                grad_key.reshape(group_rows, width_here),
                grad_value.reshape(group_rows, width_here),
            ]
        )
        grad_qkv = jnp.einsum(
            "td,cte->cde", normed_all, grad_stack, preferred_element_type=jnp.float32
        )
        grad_normed_one = lax.psum_scatter(
            slice_term(grad_stack, full_qkv, "cte,cde->td").astype(jnp.bfloat16),
            "tensor",
            scatter_dimension=0,
            tiled=True,
        ).astype(jnp.float32)
        first_pull = jax.vjp(layer_norm, token_rows, vectors[0], vectors[1])[1]
        token_from_norm, gain_one_grad, shift_one_grad = first_pull(grad_normed_one)
        input_grads.append(grad_middle + token_from_norm)
        query_bias = jnp.sum(grad_stack[0], axis=0, dtype=jnp.float32)
        value_bias = jnp.sum(grad_stack[2], axis=0, dtype=jnp.float32)
        up_bias = jnp.sum(grad_before, axis=0, dtype=jnp.float32)
        head_rows = jnp.stack(
            [
                gain_one_grad,
                shift_one_grad,
                placed(query_bias, tensor_rank * width_here, D),
                placed(value_bias, tensor_rank * width_here, D),
                jnp.sum(grad_middle, axis=0),
                gain_two_grad,
                shift_two_grad,
            ]
        )
        up_rows = placed(up_bias, tensor_rank * hidden_here, FF).reshape(4, D)
        tail_row = jnp.sum(cotangent_rows, axis=0, dtype=jnp.float32)[None, :]
        vector_total = vector_total + jnp.concatenate([head_rows, up_rows, tail_row], axis=0)
        shard_grads = (
            lax.psum_scatter(
                grad_qkv.astype(jnp.bfloat16), "dp", scatter_dimension=1, tiled=True
            ).astype(jnp.float32),
            lax.psum_scatter(
                grad_out.astype(jnp.bfloat16), "dp", scatter_dimension=1, tiled=True
            ).astype(jnp.float32),
            lax.psum_scatter(
                grad_up.astype(jnp.bfloat16), "dp", scatter_dimension=0, tiled=True
            ).astype(jnp.float32),
            lax.psum_scatter(
                grad_down.astype(jnp.bfloat16), "dp", scatter_dimension=1, tiled=True
            ).astype(jnp.float32),
        )
        grad_total = accumulate(grad_total, shard_grads)
    grad_qkv_shard, grad_out_shard, grad_up_shard, grad_down_shard = grad_total
    moment_qkv = MOMENTUM_DECAY * m_qkv + grad_qkv_shard
    moment_out = MOMENTUM_DECAY * m_out + grad_out_shard
    moment_up = MOMENTUM_DECAY * m_up + grad_up_shard
    moment_down = MOMENTUM_DECAY * m_down + grad_down_shard
    squares = jnp.concatenate(
        [
            jnp.sum(moment_qkv * moment_qkv, axis=(1, 2)),
            jnp.stack(
                [
                    jnp.sum(moment_out * moment_out),
                    jnp.sum(moment_up * moment_up),
                    jnp.sum(moment_down * moment_down),
                ]
            ),
        ]
    )
    vector_grad, square_total = lax.psum((vector_total, squares), ("dp", "tensor"))
    factors = lax.rsqrt(square_total + SQUARE_EPSILON)
    scaled_qkv = (moment_qkv * factors[0:3][:, None, None]).astype(jnp.bfloat16)
    scaled_out = (moment_out * factors[3]).astype(jnp.bfloat16)
    scaled_up = (moment_up * factors[4]).astype(jnp.bfloat16)
    scaled_down = (moment_down * factors[5]).astype(jnp.bfloat16)
    gathered_qkv, gathered_out, gathered_up, gathered_down = (
        lax.all_gather(scaled_qkv, "dp", axis=1, tiled=True),
        lax.all_gather(scaled_out, "dp", axis=1, tiled=True),
        lax.all_gather(scaled_up, "dp", axis=0, tiled=True),
        lax.all_gather(scaled_down, "dp", axis=1, tiled=True),
    )
    offset = shard_rank * shard_rows
    narrow_rows = jnp.concatenate([jnp.swapaxes(gathered_qkv, 1, 2), gathered_out[None]], axis=0)
    wide_rows = jnp.stack([gathered_up.T, gathered_down])
    for sweep_index in range(NS_ITERS):
        gram_share = lax.psum_scatter(
            gram_term(narrow_rows, wide_rows).astype(jnp.bfloat16),
            "tensor",
            scatter_dimension=0,
            tiled=True,
        )
        gram_matrix = lax.all_gather(gram_share, "tensor", axis=0, tiled=True)
        narrow_rows = schulz_step(narrow_rows, gram_matrix[:, 0:4])
        wide_rows = schulz_step(wide_rows, gram_matrix[:, 4:6])
    final_narrow = narrow_rows.astype(jnp.float32)
    final_wide = wide_rows.astype(jnp.float32)
    update_qkv = lax.dynamic_slice_in_dim(
        jnp.swapaxes(final_narrow[0:3], 1, 2), offset, shard_rows, 1
    )
    update_out = lax.dynamic_slice_in_dim(final_narrow[3], offset, shard_rows, 1)
    update_up = lax.dynamic_slice_in_dim(final_wide[0].T, offset, shard_rows, 0)
    update_down = lax.dynamic_slice_in_dim(final_wide[1], offset, shard_rows, 1)
    wide_factor = math.sqrt(FF / D)
    new_qkv = w_qkv - MATRIX_RATE * update_qkv
    new_out = w_out - MATRIX_RATE * update_out
    new_up = w_up - MATRIX_RATE * wide_factor * update_up
    new_down = w_down - MATRIX_RATE * wide_factor * update_down
    moment_vec = MOMENTUM_DECAY * m_vec + vector_grad
    new_vec = vectors - VECTOR_RATE * moment_vec * lax.rsqrt(
        jnp.mean(moment_vec * moment_vec, axis=1, keepdims=True) + SQUARE_EPSILON
    )
    return (
        jnp.stack(outputs_list),
        jnp.stack(input_grads),
        grad_qkv_shard,
        grad_out_shard,
        grad_up_shard,
        grad_down_shard,
        vector_grad,
        moment_qkv,
        moment_out,
        moment_up,
        moment_down,
        moment_vec,
        new_qkv,
        new_out,
        new_up,
        new_down,
        new_vec,
    )


QB = 256
PAIR = 2 * HD
PAIRS = D // PAIR
VMEM_LIMIT = 56 * 1024 * 1024


def layout_grid(starts_ref, dist_ref):
    key_pos = lax.broadcasted_iota(jnp.int32, (LEN, LEN), 0)
    query_pos = lax.broadcasted_iota(jnp.int32, (LEN, LEN), 1)
    gap = query_pos - key_pos
    visible = gap >= 0
    for piece in range(NPIECE):
        start = starts_ref[piece]
        inside_key = (key_pos >= start) & (key_pos < start + PIECE)
        inside_query = (query_pos >= start) & (query_pos < start + PIECE)
        visible = visible | (inside_key & inside_query)
    dist_ref[...] = jnp.where(visible, jnp.abs(gap).astype(jnp.float32), -MASKED_SCORE)


def only_rows(pair, half):
    rows = lax.broadcasted_iota(jnp.int32, pair.shape, 0)
    return jnp.where((rows >= HD) if half else (rows < HD), pair, jnp.zeros_like(pair))


def only_cols(pair, half):
    cols = lax.broadcasted_iota(jnp.int32, pair.shape, 1)
    return jnp.where((cols >= HD) if half else (cols < HD), pair, jnp.zeros_like(pair))


def mul(left, right):
    return jnp.dot(left, right, preferred_element_type=jnp.float32)


def attend_pair(pair, slopes_ref, packed, dist_ref, ctx_ref, exps_ref, stat_ref, ctx_t):
    keys = packed[:, PAIR : 2 * PAIR]
    values_t = packed[:, 2 * PAIR :].T
    queries_t = (packed[:, :PAIR] * (1.0 / math.sqrt(HD))).T
    for half in (0, 1):
        slope = slopes_ref[2 * pair + half]
        queries = only_rows(queries_t, half)
        heads = slice(half * HD, half * HD + HD)
        for block in range(LEN // QB):
            span = min(LEN, QB * block + QB + PIECE)
            cols = slice(block * QB, block * QB + QB)
            scores = mul(keys[:span], queries[:, cols]) - slope * dist_ref[:span, cols]
            top = jnp.max(scores, axis=0, keepdims=True)
            raw = jnp.exp(scores - top)
            inverse = 1.0 / jnp.sum(raw, axis=0, keepdims=True)
            low = raw.astype(jnp.bfloat16)
            exps_ref[half, :span, cols] = low
            ctx_t[heads, cols] = mul(values_t[heads, :span], low) * inverse
            stat_ref[0, half : half + 1, cols] = inverse
    ctx_ref[...] = ctx_t[...].T.astype(jnp.bfloat16)


PACKED_COLS = pl.BlockSpec((LEN, 3 * PAIR), lambda p: (0, p))
PAIR_COLS = pl.BlockSpec((LEN, PAIR), lambda p: (0, p))
PAIR_GRID = pl.BlockSpec((2, LEN, LEN), lambda p: (p, 0, 0))
PAIR_STAT = pl.BlockSpec((1, 2, LEN), lambda p: (p, 0, 0))
SCALARS = pl.BlockSpec(memory_space=pltpu.SMEM)


HIDDEN = 512
CHUNK = 256
HIDDEN_STEPS = FF // HIDDEN
GELU_SLOPE = math.sqrt(2.0 / math.pi)
GELU_CUBE = 0.044715


def dot_last(left, right):
    return lax.dot_general(left, right, (((1,), (1,)), ((), ())), preferred_element_type=jnp.float32)


def gelu_both(rows):
    square = rows * rows
    bent = jnp.tanh(rows * (GELU_SLOPE + GELU_SLOPE * GELU_CUBE * square))
    half = 0.5 + 0.5 * bent
    slope = half + 0.5 * rows * (1.0 - bent * bent) * (GELU_SLOPE + 3.0 * GELU_SLOPE * GELU_CUBE * square)
    return rows * half, slope


def hidden_block(step):
    return (step % 2) * (HIDDEN_STEPS // 2) + step // 2


def mlp_kernel(
    rows_ref,
    cot_ref,
    base_ref,
    bias_ref,
    up_ref,
    down_ref,
    block_ref,
    grad_rows_ref,
    grad_up_ref,
    grad_down_ref,
    bias_sum_ref,
    rows_t,
    cot_t,
    total,
    up_part,
    down_part,
    active,
    grad_before,
    load_sem,
):
    step = pl.program_id(0)

    def loads(at):
        cols = pl.ds(pl.multiple_of(hidden_block(at) * HIDDEN, HIDDEN), HIDDEN)
        place = lax.rem(at, 2)
        return (
            pltpu.make_async_copy(up_ref.at[:, cols], up_part.at[place], load_sem.at[0, place]),
            pltpu.make_async_copy(down_ref.at[:, cols], down_part.at[place], load_sem.at[1, place]),
        )

    @pl.when(step == 0)
    def _():
        for copy in loads(step):
            copy.start()
        rows_t[...] = rows_ref[...].T
        cot_t[...] = cot_ref[...].T
        total[...] = base_ref[...]
        grad_rows_ref[...] = jnp.zeros_like(grad_rows_ref)

    for copy in loads(step):
        copy.wait()

    @pl.when(step < HIDDEN_STEPS - 1)
    def _():
        for copy in loads(step + 1):
            copy.start()

    place = lax.rem(step, 2)
    up = up_part[place]
    down = down_part[place]
    bias = bias_ref[...]
    bias_sum = jnp.zeros((1, HIDDEN), jnp.float32)
    for index in range(LEN // CHUNK):
        here = slice(index * CHUNK, index * CHUNK + CHUNK)
        value, slope = gelu_both(mul(rows_ref[here], up) + bias)
        value = value.astype(jnp.bfloat16)
        grads = (slope * mul(cot_ref[here], down)).astype(jnp.bfloat16)
        active[here] = value
        grad_before[here] = grads
        bias_sum += jnp.sum(grads.astype(jnp.float32), axis=0, keepdims=True)
        total[here] += dot_last(value, down)
        grad_rows_ref[here] += dot_last(grads, up)
    bias_sum_ref[...] = bias_sum
    grad_down_ref[...] = mul(cot_t[...], active[...]).astype(jnp.bfloat16)
    grad_up_ref[...] = mul(rows_t[...], grad_before[...]).astype(jnp.bfloat16)

    @pl.when(step == HIDDEN_STEPS - 1)
    def _():
        block_ref[...] = total[...].astype(jnp.bfloat16)


def mlp_both(rows, cot, base, bias, up, down):
    anywhere = pl.BlockSpec(memory_space=pl.ANY)
    whole = pl.BlockSpec((LEN, D), lambda s: (0, 0))
    hidden = pl.BlockSpec((D, HIDDEN), lambda s: (0, hidden_block(s)))
    hidden_row = pl.BlockSpec((1, HIDDEN), lambda s: (0, hidden_block(s)))
    part = pltpu.VMEM((2, D, HIDDEN), jnp.bfloat16)
    low = jnp.bfloat16
    return pl.pallas_call(
        mlp_kernel,
        grid=(HIDDEN_STEPS,),
        in_specs=[whole, whole, whole, hidden_row, anywhere, anywhere],
        out_specs=[whole, whole, hidden, hidden, hidden_row],
        out_shape=[
            jax.ShapeDtypeStruct((LEN, D), low),
            jax.ShapeDtypeStruct((LEN, D), jnp.float32),
            jax.ShapeDtypeStruct((D, FF), low),
            jax.ShapeDtypeStruct((D, FF), low),
            jax.ShapeDtypeStruct((1, FF), jnp.float32),
        ],
        scratch_shapes=[
            pltpu.VMEM((D, LEN), low),
            pltpu.VMEM((D, LEN), low),
            pltpu.VMEM((LEN, D), jnp.float32),
            part,
            part,
            pltpu.VMEM((LEN, HIDDEN), low),
            pltpu.VMEM((LEN, HIDDEN), low),
            pltpu.SemaphoreType.DMA((2, 2)),
        ],
        compiler_params=pltpu.CompilerParams(vmem_limit_bytes=VMEM_LIMIT),
        cost_estimate=pl.CostEstimate(
            flops=12 * LEN * D * FF, bytes_accessed=60 * 1024 * 1024, transcendentals=LEN * FF
        ),
    )(rows, cot, base, bias, up, down)


SLOTS = 12
SLOT = 512
HALF_SLOT = SLOT // 2
TILE = 256
MESH_IDS = pl.DeviceIdType.MESH


def handler_of(slot):
    wide = slot - 4
    square = slot < 4
    dp_index = jnp.where(square, jnp.where(slot < 2, 2, 12), 4 + 6 * (wide // 4) + wide % 2)
    tensor_index = jnp.where(square, slot % 2, (wide // 2) % 2)
    return dp_index, tensor_index


def muon_kernel(
    moments_ref,
    vec_ref,
    updates_ref,
    vec_out_ref,
    pieces,
    turned,
    vec_pieces,
    vec_sum,
    gram,
    gram_low,
    poly_low,
    half_low,
    chain_low,
    chain_next,
    out_half,
    in_half,
    local_sem,
    send_sem,
    recv_sem,
    half_send,
    half_recv,
):
    groups = lax.axis_size("dp")
    parts = lax.axis_size("tensor")
    count = groups * parts
    dp_me = lax.axis_index("dp")
    t_me = lax.axis_index("tensor")
    me = t_me * groups + dp_me
    is_square = (dp_me == 2) | (dp_me == 12)
    is_up = (dp_me == 4) | (dp_me == 5)
    is_down = (dp_me == 10) | (dp_me == 11)
    is_wide = is_up | is_down
    is_handler = is_square | is_wide
    wide_slot = jnp.where(is_up, 4 + (dp_me - 4), 8 + (dp_me - 10)) + 2 * t_me
    slot_me = jnp.where(is_square, t_me + jnp.where(dp_me == 12, 2, 0), wide_slot)
    slot_me = jnp.where(is_handler, slot_me, 0)

    barrier = pltpu.get_barrier_semaphore()

    def greet(step, carry):
        other = lax.rem(me + step, count)
        pl.semaphore_signal(
            barrier, inc=1, device_id=(lax.rem(other, groups), other // groups), device_id_type=MESH_IDS
        )
        return carry

    lax.fori_loop(1, count, greet, 0)
    pl.semaphore_wait(barrier, count - 1)

    def give(step, carry):
        slot = lax.rem(me + step, SLOTS)
        dp_to, t_to = handler_of(slot)
        away = (dp_to != dp_me) | (t_to != t_me)

        @pl.when(away)
        def _():
            pltpu.make_async_remote_copy(
                src_ref=vec_ref.at[slot],
                dst_ref=vec_pieces.at[me],
                send_sem=send_sem.at[1],
                recv_sem=recv_sem.at[1],
                device_id=(dp_to, t_to),
                device_id_type=MESH_IDS,
            ).start()
            pltpu.make_async_remote_copy(
                src_ref=moments_ref.at[slot],
                dst_ref=pieces.at[me],
                send_sem=send_sem.at[0],
                recv_sem=recv_sem.at[0],
                device_id=(dp_to, t_to),
                device_id_type=MESH_IDS,
            ).start()

        return carry

    lax.fori_loop(0, SLOTS, give, 0)

    def give_back(source, sem, target):
        def one(step, carry):
            other = lax.rem(me + step, count)
            pltpu.make_async_remote_copy(
                src_ref=source.at[other] if source is turned else source,
                dst_ref=target.at[slot_me],
                send_sem=send_sem.at[sem],
                recv_sem=recv_sem.at[sem],
                device_id=(lax.rem(other, groups), other // groups),
                device_id_type=MESH_IDS,
            ).start()
            return carry

        lax.fori_loop(1, count, one, 0)

    @pl.when(is_handler)
    def _():
        own = [
            pltpu.make_async_copy(vec_ref.at[slot_me], vec_pieces.at[me], local_sem.at[0]),
            pltpu.make_async_copy(moments_ref.at[slot_me], pieces.at[me], local_sem.at[1]),
        ]
        for copy in own:
            copy.start()
        for copy in own:
            copy.wait()
        rest = pl.ds(0, count - 1)
        pltpu.make_async_copy(vec_pieces.at[rest], vec_pieces.at[rest], recv_sem.at[1]).wait()
        vec_sum[...] = jnp.sum(vec_pieces[...], axis=0)
        give_back(vec_sum, 2, vec_out_ref)
        own_vec = pltpu.make_async_copy(vec_sum, vec_out_ref.at[slot_me], local_sem.at[0])
        own_vec.start()
        own_vec.wait()
        pltpu.make_async_copy(pieces.at[rest], pieces.at[rest], recv_sem.at[0]).wait()

        rows_of = TILE // 64

        def gram_tile(tile, carry):
            rows = pl.ds(pl.multiple_of(tile * TILE, TILE), TILE)
            total = jnp.zeros((TILE, D), jnp.float32)
            for part in range(parts):
                left = pieces[pl.ds(part * groups + tile * rows_of, rows_of)].reshape(TILE, SLOT)
                right = pieces[part * groups : (part + 1) * groups].reshape(D, SLOT)
                total += lax.dot_general(
                    left, right, (((1,), (1,)), ((), ())), preferred_element_type=jnp.float32
                )
            gram[rows, :] = total
            return carry

        lax.fori_loop(0, D // TILE, gram_tile, 0)

        @pl.when(is_wide)
        def _():
            core = lax.rem(dp_me, 2)
            half = D // 2
            mine = pl.ds(pl.multiple_of(core * half, half), half)
            theirs = pl.ds(pl.multiple_of((1 - core) * half, half), half)
            sibling = (dp_me + 1 - 2 * core, t_me)
            across = (dp_me, 1 - t_me)

            def exchange(stage, place):
                copy = pltpu.make_async_remote_copy(
                    src_ref=out_half.at[stage],
                    dst_ref=in_half.at[stage],
                    send_sem=half_send.at[stage],
                    recv_sem=half_recv.at[stage],
                    device_id=place,
                    device_id_type=MESH_IDS,
                )
                copy.start()
                copy.wait()

            out_half[0] = gram[theirs, :].astype(jnp.bfloat16)
            exchange(0, sibling)
            out_half[1] = (gram[mine, :] + in_half[0].astype(jnp.float32)).astype(jnp.bfloat16)
            exchange(1, across)
            total = out_half[1].astype(jnp.float32) + in_half[1].astype(jnp.float32)
            out_half[2] = total.astype(jnp.bfloat16)
            exchange(2, sibling)
            gram[mine, :] = out_half[2].astype(jnp.float32)
            gram[theirs, :] = in_half[2].astype(jnp.float32)

        def trace_tile(tile, total):
            rows = pl.ds(pl.multiple_of(tile * TILE, TILE), TILE)
            row_ids = lax.broadcasted_iota(jnp.int32, (TILE, D), 0) + tile * TILE
            col_ids = lax.broadcasted_iota(jnp.int32, (TILE, D), 1)
            diagonal = jnp.where(row_ids == col_ids, gram[rows, :], 0.0)
            return total + jnp.sum(jnp.sum(diagonal, axis=0, keepdims=True), axis=1, keepdims=True)

        square_total = lax.fori_loop(0, D // TILE, trace_tile, jnp.zeros((1, 1), jnp.float32))
        factor = lax.rsqrt(square_total + SQUARE_EPSILON)
        gram_low[...] = (gram[...] * (factor * factor)).astype(jnp.bfloat16)

        first, second, third = SCHULZ_FIRST, SCHULZ_SECOND, SCHULZ_THIRD

        def tiles(body):
            def one(tile, carry):
                body(pl.ds(pl.multiple_of(tile * TILE, TILE), TILE))
                return carry

            lax.fori_loop(0, D // TILE, one, 0)

        chain = chain_low
        other = chain_next
        for sweep in range(NS_ITERS):
            target = chain if sweep == 0 else poly_low

            def poly(rows):
                square = mul(gram_low[rows, :], gram_low[...])
                grown = (second / first) * gram_low[rows, :].astype(jnp.float32) + (third / first) * square
                target[rows, :] = grown.astype(jnp.bfloat16)

            tiles(poly)
            if sweep > 0:

                def join(rows, chain=chain, other=other):
                    total = chain[rows, :].astype(jnp.float32) + poly_low[rows, :].astype(jnp.float32)
                    other[rows, :] = (total + mul(chain[rows, :], poly_low[...])).astype(jnp.bfloat16)

                tiles(join)
                chain, other = other, chain
            if sweep < NS_ITERS - 1:

                def half(rows):
                    grown = gram_low[rows, :].astype(jnp.float32) + mul(gram_low[rows, :], target[...])
                    half_low[rows, :] = grown.astype(jnp.bfloat16)

                def full(rows):
                    grown = half_low[rows, :].astype(jnp.float32) + mul(half_low[rows, :], target[...])
                    gram_low[rows, :] = (grown * (first * first)).astype(jnp.bfloat16)

                tiles(half)
                tiles(full)

        scale = factor * (first**NS_ITERS)

        def turn_tile(tile, carry):
            rows = pl.ds(pl.multiple_of(tile * TILE, TILE), TILE)
            for part in range(parts):
                at = pl.ds(part * groups + tile * rows_of, rows_of)
                whole = pieces[part * groups : (part + 1) * groups].reshape(D, SLOT)
                kept = pieces[at].reshape(TILE, SLOT).astype(jnp.float32)
                fresh = (kept + mul(chain[rows, :], whole)) * scale
                turned[at] = fresh.astype(jnp.bfloat16).reshape(rows_of, 64, SLOT)
            return carry

        lax.fori_loop(0, D // TILE, turn_tile, 0)
        give_back(turned, 3, updates_ref)
        own_turned = pltpu.make_async_copy(turned.at[me], updates_ref.at[slot_me], local_sem.at[1])
        own_turned.start()
        own_turned.wait()

    def finish(length):
        here = pl.ds(0, length)
        pltpu.make_async_copy(vec_ref.at[here], vec_ref.at[here], send_sem.at[1]).wait()
        pltpu.make_async_copy(moments_ref.at[here], moments_ref.at[here], send_sem.at[0]).wait()
        pltpu.make_async_copy(vec_out_ref.at[here], vec_out_ref.at[here], recv_sem.at[2]).wait()
        pltpu.make_async_copy(updates_ref.at[here], updates_ref.at[here], recv_sem.at[3]).wait()

    @pl.when(is_handler)
    def _():
        finish(SLOTS - 1)
        rest = pl.ds(0, count - 1)
        pltpu.make_async_copy(vec_pieces.at[rest], vec_pieces.at[rest], send_sem.at[2]).wait()
        pltpu.make_async_copy(turned.at[rest], turned.at[rest], send_sem.at[3]).wait()

    @pl.when(jnp.logical_not(is_handler))
    def _():
        finish(SLOTS)


def muon_call(moments, vec_parts):
    count = lax.axis_size("dp") * lax.axis_size("tensor")
    rows = moments.shape[1]
    vmem = pl.BlockSpec(memory_space=pltpu.VMEM)
    low = pltpu.VMEM((D, D), jnp.bfloat16)
    return pl.pallas_call(
        muon_kernel,
        in_specs=[vmem, vmem],
        out_specs=[vmem, vmem],
        out_shape=[
            jax.ShapeDtypeStruct(moments.shape, jnp.bfloat16),
            jax.ShapeDtypeStruct(vec_parts.shape, jnp.float32),
        ],
        scratch_shapes=[
            pltpu.VMEM((count, rows, SLOT), jnp.bfloat16),
            pltpu.VMEM((count, rows, SLOT), jnp.bfloat16),
            pltpu.VMEM((count,) + vec_parts.shape[1:], jnp.float32),
            pltpu.VMEM(vec_parts.shape[1:], jnp.float32),
            pltpu.VMEM((D, D), jnp.float32),
            low,
            low,
            low,
            low,
            low,
            pltpu.VMEM((3, D // 2, D), jnp.bfloat16),
            pltpu.VMEM((3, D // 2, D), jnp.bfloat16),
            pltpu.SemaphoreType.DMA((2,)),
            pltpu.SemaphoreType.DMA((4,)),
            pltpu.SemaphoreType.DMA((4,)),
            pltpu.SemaphoreType.DMA((3,)),
            pltpu.SemaphoreType.DMA((3,)),
        ],
        compiler_params=pltpu.CompilerParams(
            collective_id=1, has_side_effects=True, vmem_limit_bytes=VMEM_LIMIT
        ),
        cost_estimate=pl.CostEstimate(flops=12 * 2 * D**3, bytes_accessed=4 * 1024 * 1024, transcendentals=0),
    )(moments, vec_parts)


def by_slots(rows):
    return jnp.swapaxes(rows.reshape(rows.shape[0], -1, SLOT), 0, 1)


def from_slots(rows):
    return jnp.swapaxes(rows, 0, 1).reshape(rows.shape[1], -1)


def muon_step(
    shards, vector_total, w_qkv, w_out, w_up, w_down, vectors, m_qkv, m_out, m_up, m_down, m_vec
):
    grad_qkv_shard, grad_out_shard, grad_up_shard, grad_down_shard = shards
    moment_qkv = MOMENTUM_DECAY * m_qkv + grad_qkv_shard
    moment_out = MOMENTUM_DECAY * m_out + grad_out_shard
    moment_up = MOMENTUM_DECAY * m_up + grad_up_shard
    moment_down = MOMENTUM_DECAY * m_down + grad_down_shard
    slots = jnp.concatenate(
        [
            narrow(moment_qkv),
            narrow(moment_out).T[None],
            by_slots(narrow(moment_up)),
            by_slots(narrow(moment_down).T),
        ]
    )
    updates, vector_rows = muon_call(slots, vector_total.reshape(SLOTS, 8, 128))
    vector_grad = vector_rows.reshape(12, D)
    wide_factor = math.sqrt(FF / D)
    new_qkv = w_qkv - MATRIX_RATE * updates[0:3].astype(jnp.float32)
    new_out = w_out - MATRIX_RATE * updates[3].T.astype(jnp.float32)
    new_up = w_up - MATRIX_RATE * wide_factor * from_slots(updates[4:8]).astype(jnp.float32)
    new_down = w_down - MATRIX_RATE * wide_factor * from_slots(updates[8:12]).T.astype(jnp.float32)
    moment_vec = MOMENTUM_DECAY * m_vec + vector_grad
    new_vec = vectors - VECTOR_RATE * moment_vec * lax.rsqrt(
        jnp.mean(moment_vec * moment_vec, axis=1, keepdims=True) + SQUARE_EPSILON
    )
    return (
        grad_qkv_shard,
        grad_out_shard,
        grad_up_shard,
        grad_down_shard,
        vector_grad,
        moment_qkv,
        moment_out,
        moment_up,
        moment_down,
        moment_vec,
        new_qkv,
        new_out,
        new_up,
        new_down,
        new_vec,
    )


def neighbours():
    dp_me = lax.axis_index("dp")
    y = lax.axis_index("tensor")
    core = lax.rem(dp_me, 2)
    x = lax.rem(dp_me // 2, 2)
    z = dp_me // 4
    sibling = (dp_me + 1 - 2 * core, y)
    beside = (dp_me + 2 - 4 * x, y)
    across = (dp_me, 1 - y)
    stations = [(lax.rem(dp_me + 4 * hop, 16), y) for hop in (1, 2, 3)]
    return (z, x, core, y), sibling, beside, across, stations


def greet_neighbours(places):
    barrier = pltpu.get_barrier_semaphore()
    for place in places:
        pl.semaphore_signal(barrier, inc=1, device_id=place, device_id_type=MESH_IDS)
    pl.semaphore_wait(barrier, len(places))


SWAP_AT = 2
SPREAD_LAG = 1


class Spread:
    def __init__(self, slots_ref, table, local_sem, send_sem, recv_sem):
        self.slots_ref, self.table = slots_ref, table
        self.local_sem, self.send_sem, self.recv_sem = local_sem, send_sem, recv_sem
        (self.z, self.x, self.core, self.y), self.sibling, self.beside, self.across, self.stations = neighbours()

    def remote(self, source, target, stage, slot, place):
        return pltpu.make_async_remote_copy(
            src_ref=source,
            dst_ref=target,
            send_sem=self.send_sem.at[stage, slot],
            recv_sem=self.recv_sem.at[stage, slot],
            device_id=place,
            device_id_type=MESH_IDS,
        )

    def cols(self, slot, part, start=0, size=SLOT):
        _, column, distance, _ = self.table[slot]
        if isinstance(part, int):
            return pl.ds(column + part * distance + start, size)
        return pl.ds(pl.multiple_of(column + part * distance + start, 128), size)

    def own(self, slot):
        here = self.table[slot][0].at[self.z, self.x, self.core, :, self.cols(slot, self.y)]
        return pltpu.make_async_copy(self.slots_ref.at[slot], here, self.local_sem.at[slot])

    def along_z(self, slot):
        here = self.table[slot][0].at[self.z, self.x, self.core, :, self.cols(slot, self.y)]
        return [
            self.remote(self.slots_ref.at[slot], here, hop, slot, place)
            for hop, place in enumerate(self.stations)
        ]

    def second(self, slot):
        whole, _, _, size = self.table[slot]
        copies = []
        if size:
            part = whole.at[:, self.x, self.core, :, self.cols(slot, self.y, 0, size)]
            copies.append(self.remote(part, part, 3, slot, self.beside))
        if size < SLOT:
            part = whole.at[:, self.x, self.core, :, self.cols(slot, self.y, size, SLOT - size)]
            copies.append(self.remote(part, part, 4, slot, self.across))
        return copies

    def third(self, slot):
        whole, _, _, size = self.table[slot]
        copies = []
        if size:
            part = whole.at[:, :, self.core, :, self.cols(slot, self.y, 0, size)]
            copies.append(self.remote(part, part, 5, slot, self.across))
        if size < SLOT:
            for index in (0, 1):
                part = whole.at[:, self.x, self.core, :, self.cols(slot, index, size, SLOT - size)]
                copies.append(self.remote(part, part, 6 + index, slot, self.beside))
        return copies

    def fourth(self, slot):
        whole = self.table[slot][0]
        copies = []
        for index in (0, 1):
            part = whole.at[:, :, self.core, :, self.cols(slot, index)]
            copies.append(self.remote(part, part, 8 + index, slot, self.sibling))
        return copies

    def begin(self):
        for slot in range(len(self.table)):
            self.own(slot).start()
            for copy in self.along_z(slot):
                copy.start()

    def tick(self, index):
        count = len(self.table)
        if index < count:
            self.own(index).wait()
            for copy in self.along_z(index):
                copy.wait_recv()
            for copy in self.second(index):
                copy.start()
        if 0 <= index - SPREAD_LAG < count:
            for copy in self.second(index - SPREAD_LAG):
                copy.wait_recv()
            for copy in self.third(index - SPREAD_LAG):
                copy.start()
        if 0 <= index - 2 * SPREAD_LAG < count:
            for copy in self.third(index - 2 * SPREAD_LAG):
                copy.wait_recv()
            for copy in self.fourth(index - 2 * SPREAD_LAG):
                copy.start()

    def ticks(self):
        return len(self.table) + 2 * SPREAD_LAG

    def finish(self):
        for slot in range(len(self.table)):
            for copy in self.along_z(slot) + self.second(slot) + self.third(slot):
                copy.wait_send()
            for copy in self.fourth(slot):
                copy.wait()


def spread_semaphores(count):
    return [
        pltpu.SemaphoreType.DMA((count,)),
        pltpu.SemaphoreType.DMA((10, count)),
        pltpu.SemaphoreType.DMA((10, count)),
    ]


def first_spread_kernel(slots_ref, tokens_ref, whole_ref, got_ref, local_sem, send_sem, recv_sem, token_sem):
    table = [(whole_ref, index * SLOT, 3 * SLOT, 0) for index in range(3)]
    spread = Spread(slots_ref, table, local_sem, send_sem, recv_sem)
    greet_neighbours([spread.sibling, spread.beside, spread.across] + spread.stations)
    swap = pltpu.make_async_remote_copy(
        src_ref=tokens_ref.at[1 - spread.y],
        dst_ref=got_ref,
        send_sem=token_sem.at[0],
        recv_sem=token_sem.at[1],
        device_id=spread.across,
        device_id_type=MESH_IDS,
    )
    spread.begin()
    for index in range(spread.ticks()):
        spread.tick(index)
        if index == SWAP_AT:
            swap.start()
    spread.finish()
    swap.wait()


def attend_spread_kernel(
    starts_ref,
    slopes_ref,
    normed_ref,
    weights_ref,
    shifts_ref,
    slots_ref,
    cotangent_ref,
    packed_ref,
    ctx_ref,
    exps_ref,
    stat_ref,
    normed_t_ref,
    out_ref,
    up_ref,
    down_ref,
    got_ref,
    dist_ref,
    ctx_t,
    local_sem,
    send_sem,
    recv_sem,
    token_sem,
):
    pair = pl.program_id(0)
    table = [(out_ref, 0, SLOT, 0)]
    table += [(up_ref, index * SLOT, 4 * SLOT, HALF_SLOT if index % 2 else 0) for index in range(4)]
    table += [(down_ref, index * SLOT, 4 * SLOT, HALF_SLOT if index % 2 else 0) for index in range(4)]
    spread = Spread(slots_ref, table, local_sem, send_sem, recv_sem)
    swap = pltpu.make_async_remote_copy(
        src_ref=cotangent_ref.at[1 - spread.y],
        dst_ref=got_ref,
        send_sem=token_sem.at[0],
        recv_sem=token_sem.at[1],
        device_id=spread.across,
        device_id_type=MESH_IDS,
    )

    @pl.when(pair == 0)
    def _():
        greet_neighbours([spread.sibling, spread.beside, spread.across] + spread.stations)
        spread.begin()
        normed_t_ref[...] = normed_ref[...].T
        layout_grid(starts_ref, dist_ref)

    for index in range(1, PAIRS):

        @pl.when(pair == index)
        def _(index=index):
            spread.tick(index - 1)
            if index == 5:
                swap.start()

    packed = (mul(normed_ref[...], weights_ref[...]) + shifts_ref[...]).astype(jnp.bfloat16)
    packed_ref[...] = packed
    attend_pair(pair, slopes_ref, packed, dist_ref, ctx_ref, exps_ref, stat_ref, ctx_t)

    @pl.when(pair == PAIRS - 1)
    def _():
        for index in range(PAIRS - 1, spread.ticks()):
            spread.tick(index)
        spread.finish()
        swap.wait()


def whole_shape(columns):
    return jax.ShapeDtypeStruct((4, 2, 2, 64, columns), jnp.bfloat16)


def first_spread(slots, tokens):
    anywhere = pl.BlockSpec(memory_space=pl.ANY)
    whole, got = pl.pallas_call(
        first_spread_kernel,
        in_specs=[anywhere] * 2,
        out_specs=[anywhere] * 2,
        out_shape=[whole_shape(3 * D), jax.ShapeDtypeStruct(tokens.shape[1:], tokens.dtype)],
        scratch_shapes=spread_semaphores(3) + [pltpu.SemaphoreType.DMA((2,))],
        compiler_params=pltpu.CompilerParams(collective_id=3, has_side_effects=True),
    )(slots, tokens)
    return whole.reshape(D, 3 * D), got


def attend_spread(starts, slopes, normed, weights, shifts, slots, cotangent):
    anywhere = pl.BlockSpec(memory_space=pl.ANY)
    packed, context, exps, stats, normed_t, out, up, down, got = pl.pallas_call(
        attend_spread_kernel,
        grid=(PAIRS,),
        in_specs=[
            SCALARS,
            SCALARS,
            pl.BlockSpec((LEN, D), lambda p: (0, 0)),
            PACKED_COLS,
            pl.BlockSpec((1, 3 * PAIR), lambda p: (0, p)),
            anywhere,
            anywhere,
        ],
        out_specs=[PACKED_COLS, PAIR_COLS, PAIR_GRID, PAIR_STAT, pl.BlockSpec((D, LEN), lambda p: (0, 0))]
        + [anywhere] * 4,
        out_shape=[
            jax.ShapeDtypeStruct((LEN, 3 * D), jnp.bfloat16),
            jax.ShapeDtypeStruct((LEN, D), jnp.bfloat16),
            jax.ShapeDtypeStruct((H, LEN, LEN), jnp.bfloat16),
            jax.ShapeDtypeStruct((PAIRS, 2, LEN), jnp.float32),
            jax.ShapeDtypeStruct((D, LEN), jnp.bfloat16),
            whole_shape(D),
            whole_shape(FF),
            whole_shape(FF),
            jax.ShapeDtypeStruct(cotangent.shape[1:], cotangent.dtype),
        ],
        scratch_shapes=[pltpu.VMEM((LEN, LEN), jnp.float32), pltpu.VMEM((PAIR, LEN), jnp.float32)]
        + spread_semaphores(9)
        + [pltpu.SemaphoreType.DMA((2,))],
        compiler_params=pltpu.CompilerParams(
            collective_id=4, has_side_effects=True, vmem_limit_bytes=VMEM_LIMIT
        ),
        cost_estimate=pl.CostEstimate(
            flops=16 * LEN * LEN * D, bytes_accessed=90 * 1024 * 1024, transcendentals=H * LEN * LEN
        ),
    )(starts, slopes, normed, weights, shifts, slots, cotangent)
    wholes = out.reshape(D, D), up.reshape(D, FF), down.reshape(D, FF)
    return packed, context, exps, stats, normed_t, wholes, got


LAG = 2
ORDER = (4, 8, 5, 9, 6, 10, 7, 11, 3, 0, 1, 2)
READY = 9
RING = 4


def attend_bwd_half(half, scale, values, keys_t, parts, exps, sums):
    half_t, half_rows, half_queries, inner = parts
    dq_t, dk_sum, dv_sum = sums
    heads = slice(half * HD, half * HD + HD)
    for block in range(LEN // QB):
        span = min(LEN, QB * block + QB + PIECE)
        cols = slice(block * QB, block * QB + QB)
        weights = exps[:span, cols]
        grad_probs = mul(values[:span], half_t[:, cols])
        grad_scores = (weights.astype(jnp.float32) * (grad_probs - inner[:, cols])).astype(jnp.bfloat16)
        dv_sum[:span, :] += mul(weights, half_rows[cols])
        dk_sum[:span, :] += mul(grad_scores, half_queries[cols])
        dq_t[heads, cols] = mul(keys_t[heads, :span], grad_scores) * scale


def attend_sum_kernel(
    packed_ref,
    ctx_ref,
    grad_ref,
    stat_ref,
    weights_ref,
    normed_t_ref,
    exps_ref,
    up_ref,
    down_ref,
    out_ref,
    total_ref,
    grad_normed_ref,
    packed_sum_ref,
    exps,
    dq_t,
    dk_sum,
    dv_sum,
    grad_qkv,
    mine,
    first,
    second_y,
    second_x,
    third,
    fourth,
    exps_sem,
    load_sem,
    send_sem,
    recv_sem,
):
    pair = pl.program_id(0)
    (z, x, core, y), sibling, beside, across, stations = neighbours()
    low_cols = pl.ds(0, HALF_SLOT)
    high_cols = pl.ds(HALF_SLOT, HALF_SLOT)

    def remote(source, target, stage, slot, place):
        return pltpu.make_async_remote_copy(
            src_ref=source,
            dst_ref=target,
            send_sem=send_sem.at[stage, slot],
            recv_sem=recv_sem.at[stage, slot],
            device_id=place,
            device_id_type=MESH_IDS,
        )

    def source(slot, part):
        kind = ORDER[slot]
        if kind < 3:
            ref, column = grad_qkv, (part * 3 + kind) * SLOT
        elif kind == 3:
            ref, column = out_ref, part * SLOT
        else:
            ref = up_ref if kind < 8 else down_ref
            column = (part * 4 + kind % 4) * SLOT
        return ref, pl.ds(column, SLOT)

    def load(slot, part):
        ref, cols = source(slot, part)
        place = slot % RING
        return pltpu.make_async_copy(ref.at[:, :, core, :, cols], mine.at[place, part], load_sem.at[place])

    def send_first(slot):
        for part in (0, 1):
            ref, cols = source(slot, part)
            remote(ref.at[:, :, 1 - core, :, cols], first.at[slot, part], 0, slot, sibling).start()

    def second_copies(slot):
        return (
            remote(first.at[slot, 1 - y, :, :, :, low_cols], second_y.at[slot], 1, slot, across),
            remote(first.at[slot, :, :, 1 - x, :, high_cols], second_x.at[slot], 2, slot, beside),
        )

    def third_copies(slot):
        return (
            remote(second_y.at[slot, :, 1 - x], third.at[slot, :, :, low_cols], 3, slot, beside),
            remote(second_x.at[slot, 1 - y], third.at[slot, :, :, high_cols], 4, slot, across),
        )

    def fourth_copies(slot):
        return tuple(
            remote(third.at[slot, lax.rem(z + hop, 4)], fourth.at[slot, hop - 1], 4 + hop, slot, place)
            for hop, place in zip((1, 2, 3), stations)
        )

    def landed(ref, stage, slot):
        pltpu.make_async_copy(ref, ref, recv_sem.at[stage, slot]).wait()

    def tick(index):
        for slot in range(SLOTS):

            @pl.when(index == slot)
            def _(slot=slot):
                landed(first.at[slot], 0, slot)
                if slot < READY:
                    place = slot % RING
                    pltpu.make_async_copy(mine.at[place], mine.at[place], load_sem.at[place]).wait()
                    first[slot] = first[slot] + mine[place]
                    if slot + RING < READY:
                        for part in (0, 1):
                            load(slot + RING, part).start()
                else:
                    for part in (0, 1):
                        _, cols = source(slot, part)
                        first[slot, part] = first[slot, part] + grad_qkv[:, :, core, :, cols]
                for copy in second_copies(slot):
                    copy.start()

        @pl.when((index >= LAG) & (index < SLOTS + LAG))
        def _():
            slot = index - LAG
            landed(second_y.at[slot], 1, slot)
            second_y[slot] = second_y[slot] + first[slot, y, :, :, :, :HALF_SLOT]
            landed(second_x.at[slot], 2, slot)
            second_x[slot] = second_x[slot] + first[slot, :, :, x, :, HALF_SLOT:]
            for copy in third_copies(slot):
                copy.start()

        @pl.when((index >= 2 * LAG) & (index < SLOTS + 2 * LAG))
        def _():
            slot = index - 2 * LAG
            landed(third.at[slot, :, :, low_cols], 3, slot)
            landed(third.at[slot, :, :, high_cols], 4, slot)
            third[slot, :, :, :HALF_SLOT] = third[slot, :, :, :HALF_SLOT] + second_y[slot, :, x]
            third[slot, :, :, HALF_SLOT:] = third[slot, :, :, HALF_SLOT:] + second_x[slot, y]
            for copy in fourth_copies(slot):
                copy.start()

        @pl.when(index >= 3 * LAG)
        def _():
            slot = index - 3 * LAG
            total = third[slot, z].astype(jnp.float32)
            for hop in (1, 2, 3):
                landed(fourth.at[slot, hop - 1], 4 + hop, slot)
                total = total + fourth[slot, hop - 1].astype(jnp.float32)
            total_ref[slot] = total

    def exps_load(head, half):
        return pltpu.make_async_copy(exps_ref.at[head], exps.at[half], exps_sem.at[half])

    @pl.when(pair == 0)
    def _():
        for half in (0, 1):
            exps_load(half, half).start()
        for slot in range(RING):
            for part in (0, 1):
                load(slot, part).start()
        greet_neighbours([sibling, beside, across] + stations)
        for slot in range(READY):
            send_first(slot)
        grad_normed_ref[...] = jnp.zeros_like(grad_normed_ref)

    scale = 1.0 / math.sqrt(HD)
    queries = packed_ref[:, :PAIR]
    keys_t = packed_ref[:, PAIR : 2 * PAIR].T
    values = packed_ref[:, 2 * PAIR :]
    grads_t = grad_ref[...].T.astype(jnp.float32)
    context_t = ctx_ref[...].T.astype(jnp.float32)
    scaled = []
    inner_rows = []
    for half in (0, 1):
        heads = slice(half * HD, half * HD + HD)
        scaled.append(grads_t[heads] * stat_ref[0, half : half + 1, :])
        inner_rows.append(jnp.sum(scaled[half] * context_t[heads], axis=0, keepdims=True))
    scaled_t = jnp.concatenate(scaled, axis=0).astype(jnp.bfloat16)
    scaled_rows = scaled_t.T
    dk_sum[...] = jnp.zeros_like(dk_sum)
    dv_sum[...] = jnp.zeros_like(dv_sum)
    for half in (0, 1):
        exps_load(2 * pair + half, half).wait()
        parts = (
            only_rows(scaled_t, half),
            only_cols(scaled_rows, half),
            only_cols(queries, half),
            inner_rows[half],
        )
        attend_bwd_half(half, scale, values, keys_t, parts, exps.at[half], (dq_t, dk_sum, dv_sum))

        @pl.when(pair < PAIRS - 1)
        def _(half=half):
            exps_load(2 * pair + 2 + half, half).start()

        if half == 0:
            tick(pair)
    grads = jnp.concatenate([dq_t[...].T, dk_sum[...] * scale, dv_sum[...]], axis=1).astype(jnp.bfloat16)
    packed_sum_ref[...] = jnp.sum(grads.astype(jnp.float32), axis=0, keepdims=True)
    cols = pl.ds(pl.multiple_of(pair * (3 * PAIR), PAIR), 3 * PAIR)
    grad_weights = mul(normed_t_ref[...], grads).astype(jnp.bfloat16)
    grad_qkv[:, :, :, :, cols] = grad_weights.reshape(4, 2, 2, 64, 3 * PAIR)
    grad_normed_ref[...] += dot_last(grads, weights_ref[...])

    @pl.when(pair == PAIRS - 1)
    def _():
        for slot in range(READY, SLOTS):
            send_first(slot)

        def late(index, carry):
            tick(index)
            return carry

        lax.fori_loop(PAIRS, SLOTS + 3 * LAG, late, 0)

        def sent(slot, carry):
            pltpu.make_async_copy(first.at[slot], first.at[slot], send_sem.at[0, slot]).wait()
            for copy in second_copies(slot) + third_copies(slot) + fourth_copies(slot):
                copy.wait_send()
            return carry

        lax.fori_loop(0, SLOTS, sent, 0)


def attend_sum(packed, context, grad_context, stats, weights, normed_t, exps, grad_up, grad_down, grad_out):
    anywhere = pl.BlockSpec(memory_space=pl.ANY)
    rows = 64
    low = jnp.bfloat16
    once = pl.Buffered(1)
    tall = pl.BlockSpec((LEN, D), lambda p: (0, 0), pipeline_mode=once)
    split = [grad.reshape(4, 2, 2, rows, grad.shape[-1]) for grad in (grad_up, grad_down, grad_out)]
    return pl.pallas_call(
        attend_sum_kernel,
        grid=(PAIRS,),
        in_specs=[PACKED_COLS, PAIR_COLS, PAIR_COLS, PAIR_STAT, PACKED_COLS, tall] + [anywhere] * 4,
        out_specs=[
            pl.BlockSpec((SLOTS, rows, SLOT), lambda p: (0, 0, 0), pipeline_mode=once),
            tall,
            pl.BlockSpec((1, 3 * PAIR), lambda p: (0, p)),
        ],
        out_shape=[
            jax.ShapeDtypeStruct((SLOTS, rows, SLOT), jnp.float32),
            jax.ShapeDtypeStruct((LEN, D), jnp.float32),
            jax.ShapeDtypeStruct((1, 3 * D), jnp.float32),
        ],
        scratch_shapes=[
            pltpu.VMEM((2, LEN, LEN), low),
            pltpu.VMEM((PAIR, LEN), jnp.float32),
            pltpu.VMEM((LEN, PAIR), jnp.float32),
            pltpu.VMEM((LEN, PAIR), jnp.float32),
            pltpu.VMEM((4, 2, 2, rows, 3 * D), low),
            pltpu.VMEM((RING, 2, 4, 2, rows, SLOT), low),
            pltpu.VMEM((SLOTS, 2, 4, 2, rows, SLOT), low),
            pltpu.VMEM((SLOTS, 4, 2, rows, HALF_SLOT), low),
            pltpu.VMEM((SLOTS, 2, 4, rows, HALF_SLOT), low),
            pltpu.VMEM((SLOTS, 4, rows, SLOT), low),
            pltpu.VMEM((SLOTS, 3, rows, SLOT), low),
            pltpu.SemaphoreType.DMA((2,)),
            pltpu.SemaphoreType.DMA((RING,)),
            pltpu.SemaphoreType.DMA((8, SLOTS)),
            pltpu.SemaphoreType.DMA((8, SLOTS)),
        ],
        compiler_params=pltpu.CompilerParams(
            collective_id=2, has_side_effects=True, vmem_limit_bytes=62 * 1024 * 1024
        ),
        cost_estimate=pl.CostEstimate(
            flops=44 * LEN * LEN * D, bytes_accessed=400 * 1024 * 1024, transcendentals=0
        ),
    )(packed, context, grad_context, stats, weights, normed_t, exps, *split)


def narrow(rows):
    return rows.astype(jnp.bfloat16)


def contract(left, right, left_dim, right_dim):
    return lax.dot_general(
        left, right, (((left_dim,), (right_dim,)), ((), ())), preferred_element_type=jnp.float32
    )


def in_order(rank, own, got):
    return jnp.where(rank == 0, jnp.concatenate([own, got]), jnp.concatenate([got, own]))


def swap_halves(mine, rank):
    rows = mine.shape[0] // 2
    kept = lax.dynamic_slice_in_dim(mine, rank * rows, rows, 0)
    sent = lax.dynamic_slice_in_dim(mine, (1 - rank) * rows, rows, 0)
    got = lax.ppermute(sent, "tensor", [(0, 1), (1, 0)])
    return jnp.where(rank == 0, jnp.stack([kept, got]), jnp.stack([got, kept]))


def by_pairs(rows):
    count, height, width = rows.shape
    return jnp.transpose(rows.reshape(count, height, width // PAIR, PAIR), (1, 2, 0, 3)).reshape(height, -1)


def from_pairs(rows):
    height = rows.shape[0]
    return jnp.transpose(rows.reshape(height, -1, 3, PAIR), (2, 0, 1, 3)).reshape(3, height, -1)


def sequence_step(
    tokens,
    cotangent,
    piece_starts,
    w_qkv,
    w_out,
    w_up,
    w_down,
    vectors,
    m_qkv,
    m_out,
    m_up,
    m_down,
    m_vec,
):
    rank = lax.axis_index("tensor")
    slopes = jnp.exp2(-8.0 * jnp.arange(1, H + 1, dtype=jnp.float32) / H)
    starts = lax.dynamic_slice_in_dim(piece_starts[:, 0], rank, 1, 0)[0]
    own_tokens = lax.dynamic_index_in_dim(tokens, rank, 0, keepdims=False)
    own_cotangent = lax.dynamic_index_in_dim(cotangent, rank, 0, keepdims=False)

    full_qkv, other_tokens = first_spread(by_slots(by_pairs(narrow(w_qkv))), tokens)
    token_rows = in_order(rank, own_tokens, other_tokens).astype(jnp.float32)
    normed_one = narrow(layer_norm(token_rows, vectors[0], vectors[1]))
    shifts = by_pairs(jnp.stack([vectors[2], jnp.zeros((D,), jnp.float32), vectors[3]])[:, None])
    later_slots = jnp.concatenate(
        [narrow(w_out).T[None], by_slots(narrow(w_up)), by_slots(narrow(w_down).T)]
    )
    packed, context, exps, stats, normed_t, wholes, other_cotangent = attend_spread(
        starts, slopes, normed_one, full_qkv, shifts, later_slots, cotangent
    )
    full_out, full_up, full_down = wholes
    cotangent_low = in_order(rank, own_cotangent, other_cotangent)
    cotangent_rows = cotangent_low.astype(jnp.float32)

    middle = token_rows + contract(context, full_out, 1, 1) + vectors[4]
    normed_two = narrow(layer_norm(middle, vectors[5], vectors[6]))
    block_rows, grad_normed_two, grad_up, grad_down, up_bias = mlp_both(
        normed_two, cotangent_low, middle + vectors[11], vectors[7:11].reshape(1, FF), full_up, full_down
    )
    output_pair = swap_halves(block_rows, rank)
    second_pull = jax.vjp(layer_norm, middle, vectors[5], vectors[6])[1]
    middle_from_norm, gain_two_grad, shift_two_grad = second_pull(grad_normed_two)
    grad_middle = cotangent_rows + middle_from_norm
    grad_middle_low = narrow(grad_middle)
    grad_out = narrow(contract(grad_middle_low, context, 0, 0))
    grad_context = narrow(contract(grad_middle_low, full_out, 1, 0))
    sums, grad_normed_one, packed_grads = attend_sum(
        packed, context, grad_context, stats, full_qkv, normed_t, exps, grad_up, grad_down, grad_out
    )
    first_pull = jax.vjp(layer_norm, token_rows, vectors[0], vectors[1])[1]
    token_from_norm, gain_one_grad, shift_one_grad = first_pull(grad_normed_one)
    grad_token_rows = grad_middle + token_from_norm
    token_pair = swap_halves(narrow(grad_token_rows), rank).astype(jnp.float32)

    packed_sums = from_pairs(packed_grads)[:, 0]
    vector_total = jnp.concatenate(
        [
            jnp.stack(
                [
                    gain_one_grad,
                    shift_one_grad,
                    packed_sums[0],
                    packed_sums[2],
                    jnp.sum(grad_middle, axis=0),
                    gain_two_grad,
                    shift_two_grad,
                ]
            ),
            up_bias.reshape(4, D),
            jnp.sum(cotangent_rows, axis=0)[None],
        ]
    )
    shards = (
        from_pairs(from_slots(sums[9:12])),
        sums[8].T,
        from_slots(sums[0:8:2]),
        from_slots(sums[1:8:2]).T,
    )
    outputs = muon_step(shards, vector_total, w_qkv, w_out, w_up, w_down, vectors, m_qkv, m_out, m_up, m_down, m_vec)
    return (output_pair, token_pair) + outputs


def solution(mesh):
    in_specs = (
        P(None, ("dp", "tensor"), None),
        P(None, ("dp", "tensor"), None),
        P(None, "dp", None),
        P(None, "dp", "tensor"),
        P("tensor", "dp"),
        P("dp", "tensor"),
        P("tensor", "dp"),
        P(),
        P(None, "dp", "tensor"),
        P("tensor", "dp"),
        P("dp", "tensor"),
        P("tensor", "dp"),
        P(),
    )
    out_specs = (
        P(None, ("dp", "tensor"), None),
        P(None, ("dp", "tensor"), None),
        P(None, "dp", "tensor"),
        P("tensor", "dp"),
        P("dp", "tensor"),
        P("tensor", "dp"),
        P(),
        P(None, "dp", "tensor"),
        P("tensor", "dp"),
        P("dp", "tensor"),
        P("tensor", "dp"),
        P(),
        P(None, "dp", "tensor"),
        P("tensor", "dp"),
        P("dp", "tensor"),
        P("tensor", "dp"),
        P(),
    )
    groups_fit = mesh.shape["tensor"] == MB and mesh.shape["dp"] == 16

    def pick(*arrays):
        if groups_fit and arrays[2].shape[1] == 1:
            return sequence_step(*arrays)
        return on_device(*arrays)

    return jax.shard_map(
        pick, mesh=mesh, in_specs=in_specs, out_specs=out_specs, check_vma=False
    )
```

```python
import math

import jax
import jax.numpy as jnp
from jax import lax
from jax.experimental import pallas as pl
from jax.experimental.pallas import tpu as pltpu
from jax.sharding import PartitionSpec as P

D = 1024
H = 16
HD = 64
FF = 4096
LEN = 1024
PIECE = 256
NPIECE = 2
MB = 2
NS_ITERS = 3


NORM_EPSILON = 1e-05
SQUARE_EPSILON = 1e-06
MASKED_SCORE = -1e30
SCHULZ_FIRST = 3.4445
SCHULZ_SECOND = -4.775
SCHULZ_THIRD = 2.0315
MOMENTUM_DECAY = 0.5
MATRIX_RATE = 0.5
VECTOR_RATE = 0.05


def layer_norm(inputs, gain_row, shift_row):
    average = jnp.mean(inputs, axis=-1, keepdims=True)
    centered = inputs - average
    variance = jnp.mean(centered * centered, axis=-1, keepdims=True)
    return centered * lax.rsqrt(variance + NORM_EPSILON) * gain_row + shift_row


def gelu_tanh(inputs):
    return jax.nn.gelu(inputs, approximate=True)


def score_layout(starts, slopes):
    positions = jnp.arange(LEN, dtype=jnp.int32)
    inside = (positions[None, :] >= starts[:, None]) & (
        positions[None, :] < starts[:, None] + PIECE
    )
    labels = jnp.arange(1, NPIECE + 1, dtype=jnp.int32)
    piece_label = jnp.sum(jnp.where(inside, labels[:, None], 0), axis=0)
    same_piece = (piece_label[:, None] == piece_label[None, :]) & (piece_label[:, None] > 0)
    visible = (positions[None, :] <= positions[:, None]) | same_piece
    distance = jnp.abs(positions[:, None] - positions[None, :]).astype(jnp.float32)
    penalty = -slopes[:, None, None] * distance[None, :, :]
    return (visible, penalty)


def head_scores(query_heads, key_heads, starts, slopes):
    visible, penalty = score_layout(starts, slopes)
    raw_scores = jnp.einsum(
        "qhd,khd->hqk", query_heads, key_heads, preferred_element_type=jnp.float32
    )
    scores = raw_scores * (1.0 / math.sqrt(HD)) + penalty
    return jnp.where(visible[None, :, :], scores, MASKED_SCORE)


def attend_forward(element, slopes):
    query_seq, key_seq, value_seq, starts = element
    heads_here = slopes.shape[0]
    query_heads = query_seq.reshape(LEN, heads_here, HD)
    key_heads = key_seq.reshape(LEN, heads_here, HD)
    value_heads = value_seq.reshape(LEN, heads_here, HD)
    scores = head_scores(query_heads, key_heads, starts, slopes)
    maximum = jnp.max(scores, axis=-1, keepdims=True)
    weights_raw = jnp.exp(scores - maximum)
    denominator = jnp.sum(weights_raw, axis=-1, keepdims=True)
    probabilities = weights_raw / denominator
    context = jnp.einsum(
        "hqk,khd->qhd",
        probabilities.astype(jnp.bfloat16),
        value_heads,
        preferred_element_type=jnp.float32,
    )
    logsum = (maximum + jnp.log(denominator))[..., 0]
    return (context.reshape(LEN, heads_here * HD), logsum)


def attend_backward(element, slopes):
    query_seq, key_seq, value_seq, context_grad, logsum, starts = element
    heads_here = slopes.shape[0]
    query_heads = query_seq.reshape(LEN, heads_here, HD)
    key_heads = key_seq.reshape(LEN, heads_here, HD)
    value_heads = value_seq.reshape(LEN, heads_here, HD)
    grad_heads = context_grad.reshape(LEN, heads_here, HD)
    scores = head_scores(query_heads, key_heads, starts, slopes)
    probabilities = jnp.exp(scores - logsum[..., None])
    grad_probs = jnp.einsum(
        "qhd,khd->hqk", grad_heads, value_heads, preferred_element_type=jnp.float32
    )
    inner_sum = jnp.sum(probabilities * grad_probs, axis=-1, keepdims=True)
    grad_scores = (probabilities * (grad_probs - inner_sum)).astype(jnp.bfloat16)
    scale_factor = 1.0 / math.sqrt(HD)
    grad_query = (
        jnp.einsum("hqk,khd->qhd", grad_scores, key_heads, preferred_element_type=jnp.float32)
        * scale_factor
    )
    grad_key = (
        jnp.einsum("hqk,qhd->khd", grad_scores, query_heads, preferred_element_type=jnp.float32)
        * scale_factor
    )
    grad_value = jnp.einsum(
        "hqk,qhd->khd",
        probabilities.astype(jnp.bfloat16),
        grad_heads,
        preferred_element_type=jnp.float32,
    )
    width_here = heads_here * HD
    return (
        grad_query.astype(jnp.bfloat16).reshape(LEN, width_here),
        grad_key.astype(jnp.bfloat16).reshape(LEN, width_here),
        grad_value.astype(jnp.bfloat16).reshape(LEN, width_here),
    )


def placed(values, offset, length):
    return lax.dynamic_update_slice_in_dim(jnp.zeros((length,), jnp.float32), values, offset, 0)


def accumulate(totals, addend):
    if totals is None:
        return addend
    return tuple((former + latter for former, latter in zip(totals, addend)))


def gram_term(narrow_rows, wide_rows):
    part_narrow = jnp.einsum(
        "mrc,mrd->cmd", narrow_rows, narrow_rows, preferred_element_type=jnp.float32
    )
    part_wide = jnp.einsum("mrc,mrd->cmd", wide_rows, wide_rows, preferred_element_type=jnp.float32)
    return jnp.concatenate([part_narrow, part_wide], axis=1)


def schulz_step(state, gram_matrix):
    turned = jnp.einsum("mrc,cmd->mrd", state, gram_matrix, preferred_element_type=jnp.float32)
    mixed = (SCHULZ_SECOND * state.astype(jnp.float32) + SCHULZ_THIRD * turned).astype(jnp.bfloat16)
    return (
        SCHULZ_FIRST * state.astype(jnp.float32)
        + jnp.einsum("mrc,cmd->mrd", mixed, gram_matrix, preferred_element_type=jnp.float32)
    ).astype(jnp.bfloat16)


def slice_term(source, weights, pattern):
    return jnp.einsum(pattern, source, weights, preferred_element_type=jnp.float32)


def on_device(
    tokens,
    cotangent,
    piece_starts,
    w_qkv,
    w_out,
    w_up,
    w_down,
    vectors,
    m_qkv,
    m_out,
    m_up,
    m_down,
    m_vec,
):
    tensor_count = lax.axis_size("tensor")
    tensor_rank = lax.axis_index("tensor")
    shard_rank = lax.axis_index("dp")
    heads_here = H // tensor_count
    width_here = heads_here * HD
    hidden_here = FF // tensor_count
    rows_here = tokens.shape[1]
    group_rows = rows_here * tensor_count
    seqs_here = piece_starts.shape[1]
    shard_rows = w_qkv.shape[1]
    head_ids = tensor_rank * heads_here + jnp.arange(heads_here, dtype=jnp.int32) + 1
    slopes = jnp.exp2(-8.0 * head_ids.astype(jnp.float32) / H)
    query_shift = lax.dynamic_slice_in_dim(vectors[2], tensor_rank * width_here, width_here, 0)
    value_shift = lax.dynamic_slice_in_dim(vectors[3], tensor_rank * width_here, width_here, 0)
    up_shift = lax.dynamic_slice_in_dim(
        vectors[7:11].reshape(FF), tensor_rank * hidden_here, hidden_here, 0
    )
    low_qkv = w_qkv.astype(jnp.bfloat16)
    low_out = w_out.astype(jnp.bfloat16)
    low_up = w_up.astype(jnp.bfloat16)
    low_down = w_down.astype(jnp.bfloat16)
    outputs_list = []
    input_grads = []
    vector_total = jnp.zeros((12, D), jnp.float32)
    grad_total = None

    def forward_one(element):
        return attend_forward(element, slopes)

    def backward_one(element):
        return attend_backward(element, slopes)

    for batch_index in range(MB):
        full_qkv, full_out, full_up, full_down = (
            lax.all_gather(low_qkv, "dp", axis=1, tiled=True),
            lax.all_gather(low_out, "dp", axis=1, tiled=True),
            lax.all_gather(low_up, "dp", axis=0, tiled=True),
            lax.all_gather(low_down, "dp", axis=1, tiled=True),
        )
        token_rows = tokens[batch_index].astype(jnp.float32)
        cotangent_rows = cotangent[batch_index]
        normed_one = layer_norm(token_rows, vectors[0], vectors[1])
        normed_all, cotangent_all = (
            lax.all_gather(normed_one.astype(jnp.bfloat16), "tensor", axis=0, tiled=True),
            lax.all_gather(cotangent_rows, "tensor", axis=0, tiled=True),
        )
        projected = jnp.einsum(
            "td,cde->cte", normed_all, full_qkv, preferred_element_type=jnp.float32
        )
        query_low = (projected[0] + query_shift).astype(jnp.bfloat16)
        key_low = projected[1].astype(jnp.bfloat16)
        value_low = (projected[2] + value_shift).astype(jnp.bfloat16)
        query_seqs = query_low.reshape(seqs_here, LEN, width_here)
        key_seqs = key_low.reshape(seqs_here, LEN, width_here)
        value_seqs = value_low.reshape(seqs_here, LEN, width_here)
        starts_here = piece_starts[batch_index]
        context_seq, logsum = lax.map(forward_one, (query_seqs, key_seqs, value_seqs, starts_here))
        context_low = context_seq.reshape(group_rows, width_here).astype(jnp.bfloat16)
        attended = lax.psum_scatter(
            slice_term(context_low, full_out, "tc,cd->td").astype(jnp.bfloat16),
            "tensor",
            scatter_dimension=0,
            tiled=True,
        ).astype(jnp.float32)
        middle = token_rows + attended + vectors[4]
        normed_two = layer_norm(middle, vectors[5], vectors[6])
        normed_two_all = lax.all_gather(
            normed_two.astype(jnp.bfloat16), "tensor", axis=0, tiled=True
        )
        before = jnp.dot(normed_two_all, full_up, preferred_element_type=jnp.float32) + up_shift
        activated = gelu_tanh(before).astype(jnp.bfloat16)
        expanded = lax.psum_scatter(
            slice_term(activated, full_down, "tf,fd->td").astype(jnp.bfloat16),
            "tensor",
            scatter_dimension=0,
            tiled=True,
        ).astype(jnp.float32)
        outputs_list.append((middle + expanded + vectors[11]).astype(jnp.bfloat16))
        grad_down = jnp.einsum(
            "tf,td->fd", activated, cotangent_all, preferred_element_type=jnp.float32
        )
        grad_activated = jnp.einsum(
            "td,fd->tf", cotangent_all, full_down, preferred_element_type=jnp.float32
        )
        gelu_pull = jax.vjp(gelu_tanh, before)[1]
        grad_before = gelu_pull(grad_activated)[0].astype(jnp.bfloat16)
        grad_up = jnp.einsum(
            "td,tf->df", normed_two_all, grad_before, preferred_element_type=jnp.float32
        )
        grad_normed_two = lax.psum_scatter(
            slice_term(grad_before, full_up, "tf,df->td").astype(jnp.bfloat16),
            "tensor",
            scatter_dimension=0,
            tiled=True,
        ).astype(jnp.float32)
        second_pull = jax.vjp(layer_norm, middle, vectors[5], vectors[6])[1]
        middle_from_norm, gain_two_grad, shift_two_grad = second_pull(grad_normed_two)
        grad_middle = cotangent_rows.astype(jnp.float32) + middle_from_norm
        grad_middle_all = lax.all_gather(
            grad_middle.astype(jnp.bfloat16), "tensor", axis=0, tiled=True
        )
        grad_out = jnp.einsum(
            "tc,td->cd", context_low, grad_middle_all, preferred_element_type=jnp.float32
        )
        grad_context = jnp.einsum(
            "td,cd->tc", grad_middle_all, full_out, preferred_element_type=jnp.float32
        ).astype(jnp.bfloat16)
        grad_query, grad_key, grad_value = lax.map(
            backward_one,
            (
                query_seqs,
                key_seqs,
                value_seqs,
                grad_context.reshape(seqs_here, LEN, width_here),
                logsum,
                starts_here,
            ),
        )
        grad_stack = jnp.stack(
            [
                grad_query.reshape(group_rows, width_here),
                grad_key.reshape(group_rows, width_here),
                grad_value.reshape(group_rows, width_here),
            ]
        )
        grad_qkv = jnp.einsum(
            "td,cte->cde", normed_all, grad_stack, preferred_element_type=jnp.float32
        )
        grad_normed_one = lax.psum_scatter(
            slice_term(grad_stack, full_qkv, "cte,cde->td").astype(jnp.bfloat16),
            "tensor",
            scatter_dimension=0,
            tiled=True,
        ).astype(jnp.float32)
        first_pull = jax.vjp(layer_norm, token_rows, vectors[0], vectors[1])[1]
        token_from_norm, gain_one_grad, shift_one_grad = first_pull(grad_normed_one)
        input_grads.append(grad_middle + token_from_norm)
        query_bias = jnp.sum(grad_stack[0], axis=0, dtype=jnp.float32)
        value_bias = jnp.sum(grad_stack[2], axis=0, dtype=jnp.float32)
        up_bias = jnp.sum(grad_before, axis=0, dtype=jnp.float32)
        head_rows = jnp.stack(
            [
                gain_one_grad,
                shift_one_grad,
                placed(query_bias, tensor_rank * width_here, D),
                placed(value_bias, tensor_rank * width_here, D),
                jnp.sum(grad_middle, axis=0),
                gain_two_grad,
                shift_two_grad,
            ]
        )
        up_rows = placed(up_bias, tensor_rank * hidden_here, FF).reshape(4, D)
        tail_row = jnp.sum(cotangent_rows, axis=0, dtype=jnp.float32)[None, :]
        vector_total = vector_total + jnp.concatenate([head_rows, up_rows, tail_row], axis=0)
        shard_grads = (
            lax.psum_scatter(
                grad_qkv.astype(jnp.bfloat16), "dp", scatter_dimension=1, tiled=True
            ).astype(jnp.float32),
            lax.psum_scatter(
                grad_out.astype(jnp.bfloat16), "dp", scatter_dimension=1, tiled=True
            ).astype(jnp.float32),
            lax.psum_scatter(
                grad_up.astype(jnp.bfloat16), "dp", scatter_dimension=0, tiled=True
            ).astype(jnp.float32),
            lax.psum_scatter(
                grad_down.astype(jnp.bfloat16), "dp", scatter_dimension=1, tiled=True
            ).astype(jnp.float32),
        )
        grad_total = accumulate(grad_total, shard_grads)
    grad_qkv_shard, grad_out_shard, grad_up_shard, grad_down_shard = grad_total
    moment_qkv = MOMENTUM_DECAY * m_qkv + grad_qkv_shard
    moment_out = MOMENTUM_DECAY * m_out + grad_out_shard
    moment_up = MOMENTUM_DECAY * m_up + grad_up_shard
    moment_down = MOMENTUM_DECAY * m_down + grad_down_shard
    squares = jnp.concatenate(
        [
            jnp.sum(moment_qkv * moment_qkv, axis=(1, 2)),
            jnp.stack(
                [
                    jnp.sum(moment_out * moment_out),
                    jnp.sum(moment_up * moment_up),
                    jnp.sum(moment_down * moment_down),
                ]
            ),
        ]
    )
    vector_grad, square_total = lax.psum((vector_total, squares), ("dp", "tensor"))
    factors = lax.rsqrt(square_total + SQUARE_EPSILON)
    scaled_qkv = (moment_qkv * factors[0:3][:, None, None]).astype(jnp.bfloat16)
    scaled_out = (moment_out * factors[3]).astype(jnp.bfloat16)
    scaled_up = (moment_up * factors[4]).astype(jnp.bfloat16)
    scaled_down = (moment_down * factors[5]).astype(jnp.bfloat16)
    gathered_qkv, gathered_out, gathered_up, gathered_down = (
        lax.all_gather(scaled_qkv, "dp", axis=1, tiled=True),
        lax.all_gather(scaled_out, "dp", axis=1, tiled=True),
        lax.all_gather(scaled_up, "dp", axis=0, tiled=True),
        lax.all_gather(scaled_down, "dp", axis=1, tiled=True),
    )
    offset = shard_rank * shard_rows
    narrow_rows = jnp.concatenate([jnp.swapaxes(gathered_qkv, 1, 2), gathered_out[None]], axis=0)
    wide_rows = jnp.stack([gathered_up.T, gathered_down])
    for sweep_index in range(NS_ITERS):
        gram_share = lax.psum_scatter(
            gram_term(narrow_rows, wide_rows).astype(jnp.bfloat16),
            "tensor",
            scatter_dimension=0,
            tiled=True,
        )
        gram_matrix = lax.all_gather(gram_share, "tensor", axis=0, tiled=True)
        narrow_rows = schulz_step(narrow_rows, gram_matrix[:, 0:4])
        wide_rows = schulz_step(wide_rows, gram_matrix[:, 4:6])
    final_narrow = narrow_rows.astype(jnp.float32)
    final_wide = wide_rows.astype(jnp.float32)
    update_qkv = lax.dynamic_slice_in_dim(
        jnp.swapaxes(final_narrow[0:3], 1, 2), offset, shard_rows, 1
    )
    update_out = lax.dynamic_slice_in_dim(final_narrow[3], offset, shard_rows, 1)
    update_up = lax.dynamic_slice_in_dim(final_wide[0].T, offset, shard_rows, 0)
    update_down = lax.dynamic_slice_in_dim(final_wide[1], offset, shard_rows, 1)
    wide_factor = math.sqrt(FF / D)
    new_qkv = w_qkv - MATRIX_RATE * update_qkv
    new_out = w_out - MATRIX_RATE * update_out
    new_up = w_up - MATRIX_RATE * wide_factor * update_up
    new_down = w_down - MATRIX_RATE * wide_factor * update_down
    moment_vec = MOMENTUM_DECAY * m_vec + vector_grad
    new_vec = vectors - VECTOR_RATE * moment_vec * lax.rsqrt(
        jnp.mean(moment_vec * moment_vec, axis=1, keepdims=True) + SQUARE_EPSILON
    )
    return (
        jnp.stack(outputs_list),
        jnp.stack(input_grads),
        grad_qkv_shard,
        grad_out_shard,
        grad_up_shard,
        grad_down_shard,
        vector_grad,
        moment_qkv,
        moment_out,
        moment_up,
        moment_down,
        moment_vec,
        new_qkv,
        new_out,
        new_up,
        new_down,
        new_vec,
    )


QB = 256
PAIR = 2 * HD
PAIRS = D // PAIR
VMEM_LIMIT = 56 * 1024 * 1024


def layout_grid(starts_ref, dist_ref):
    key_pos = lax.broadcasted_iota(jnp.int32, (LEN, LEN), 0)
    query_pos = lax.broadcasted_iota(jnp.int32, (LEN, LEN), 1)
    gap = query_pos - key_pos
    visible = gap >= 0
    for piece in range(NPIECE):
        start = starts_ref[piece]
        inside_key = (key_pos >= start) & (key_pos < start + PIECE)
        inside_query = (query_pos >= start) & (query_pos < start + PIECE)
        visible = visible | (inside_key & inside_query)
    dist_ref[...] = jnp.where(visible, jnp.abs(gap).astype(jnp.float32), -MASKED_SCORE)


def only_rows(pair, half):
    rows = lax.broadcasted_iota(jnp.int32, pair.shape, 0)
    return jnp.where((rows >= HD) if half else (rows < HD), pair, jnp.zeros_like(pair))


def only_cols(pair, half):
    cols = lax.broadcasted_iota(jnp.int32, pair.shape, 1)
    return jnp.where((cols >= HD) if half else (cols < HD), pair, jnp.zeros_like(pair))


def mul(left, right):
    return jnp.dot(left, right, preferred_element_type=jnp.float32)


def attend_pair(pair, slopes_ref, packed, dist_ref, ctx_ref, exps_ref, stat_ref, ctx_t, between):
    keys = packed[:, PAIR : 2 * PAIR]
    values_t = packed[:, 2 * PAIR :].T
    queries_t = (packed[:, :PAIR] * (1.0 / math.sqrt(HD))).T
    for half in (0, 1):
        slope = slopes_ref[2 * pair + half]
        queries = only_rows(queries_t, half)
        heads = slice(half * HD, half * HD + HD)
        for block in range(LEN // QB):
            span = min(LEN, QB * block + QB + PIECE)
            cols = slice(block * QB, block * QB + QB)
            scores = mul(keys[:span], queries[:, cols]) - slope * dist_ref[:span, cols]
            top = jnp.max(scores, axis=0, keepdims=True)
            raw = jnp.exp(scores - top)
            inverse = 1.0 / jnp.sum(raw, axis=0, keepdims=True)
            low = raw.astype(jnp.bfloat16)
            exps_ref[half, :span, cols] = low
            ctx_t[heads, cols] = mul(values_t[heads, :span], low) * inverse
            stat_ref[0, half : half + 1, cols] = inverse
        if half == 0:
            between()
    ctx_ref[...] = ctx_t[...].T.astype(jnp.bfloat16)


PACKED_COLS = pl.BlockSpec((LEN, 3 * PAIR), lambda p: (0, p))
PAIR_COLS = pl.BlockSpec((LEN, PAIR), lambda p: (0, p))
PAIR_GRID = pl.BlockSpec((2, LEN, LEN), lambda p: (p, 0, 0))
PAIR_STAT = pl.BlockSpec((1, 2, LEN), lambda p: (p, 0, 0))
SCALARS = pl.BlockSpec(memory_space=pltpu.SMEM)


SLOTS = 12
SLOT = 512
HALF_SLOT = SLOT // 2
TILE = 256
GRAM_TILES = 5
MESH_IDS = pl.DeviceIdType.MESH


def handler_of(slot):
    wide = slot - 4
    square = slot < 4
    dp_index = jnp.where(square, jnp.where(slot < 2, 2, 12), 4 + 6 * (wide // 4) + wide % 2)
    tensor_index = jnp.where(square, slot % 2, (wide // 2) % 2)
    return dp_index, tensor_index


def muon_kernel(
    moments_ref,
    vec_ref,
    updates_ref,
    vec_out_ref,
    pieces,
    turned,
    vec_pieces,
    vec_sum,
    gram,
    gram_low,
    poly_low,
    half_low,
    chain_low,
    chain_next,
    out_half,
    in_half,
    local_sem,
    send_sem,
    recv_sem,
    half_send,
    half_recv,
):
    groups = lax.axis_size("dp")
    parts = lax.axis_size("tensor")
    count = groups * parts
    dp_me = lax.axis_index("dp")
    t_me = lax.axis_index("tensor")
    me = t_me * groups + dp_me
    is_square = (dp_me == 2) | (dp_me == 12)
    is_up = (dp_me == 4) | (dp_me == 5)
    is_down = (dp_me == 10) | (dp_me == 11)
    is_wide = is_up | is_down
    is_handler = is_square | is_wide
    wide_slot = jnp.where(is_up, 4 + (dp_me - 4), 8 + (dp_me - 10)) + 2 * t_me
    slot_me = jnp.where(is_square, t_me + jnp.where(dp_me == 12, 2, 0), wide_slot)
    slot_me = jnp.where(is_handler, slot_me, 0)

    barrier = pltpu.get_barrier_semaphore()

    def greet(step, carry):
        other = lax.rem(me + step, count)
        pl.semaphore_signal(
            barrier, inc=1, device_id=(lax.rem(other, groups), other // groups), device_id_type=MESH_IDS
        )
        return carry

    lax.fori_loop(1, count, greet, 0)
    pl.semaphore_wait(barrier, count - 1)

    def give(step, carry):
        slot = lax.rem(me + step, SLOTS)
        dp_to, t_to = handler_of(slot)
        away = (dp_to != dp_me) | (t_to != t_me)

        @pl.when(away)
        def _():
            pltpu.make_async_remote_copy(
                src_ref=vec_ref.at[slot],
                dst_ref=vec_pieces.at[me],
                send_sem=send_sem.at[1],
                recv_sem=recv_sem.at[1],
                device_id=(dp_to, t_to),
                device_id_type=MESH_IDS,
            ).start()
            pltpu.make_async_remote_copy(
                src_ref=moments_ref.at[slot],
                dst_ref=pieces.at[me],
                send_sem=send_sem.at[0],
                recv_sem=recv_sem.at[0],
                device_id=(dp_to, t_to),
                device_id_type=MESH_IDS,
            ).start()

        return carry

    lax.fori_loop(0, SLOTS, give, 0)

    def give_back(source, sem, target):
        def one(step, carry):
            other = lax.rem(me + step, count)
            pltpu.make_async_remote_copy(
                src_ref=source.at[other] if source is turned else source,
                dst_ref=target.at[slot_me],
                send_sem=send_sem.at[sem],
                recv_sem=recv_sem.at[sem],
                device_id=(lax.rem(other, groups), other // groups),
                device_id_type=MESH_IDS,
            ).start()
            return carry

        lax.fori_loop(1, count, one, 0)

    @pl.when(is_handler)
    def _():
        own = [
            pltpu.make_async_copy(vec_ref.at[slot_me], vec_pieces.at[me], local_sem.at[0]),
            pltpu.make_async_copy(moments_ref.at[slot_me], pieces.at[me], local_sem.at[1]),
        ]
        for copy in own:
            copy.start()
        for copy in own:
            copy.wait()
        rest = pl.ds(0, count - 1)
        pltpu.make_async_copy(vec_pieces.at[rest], vec_pieces.at[rest], recv_sem.at[1]).wait()
        vec_sum[...] = jnp.sum(vec_pieces[...], axis=0)
        give_back(vec_sum, 2, vec_out_ref)
        own_vec = pltpu.make_async_copy(vec_sum, vec_out_ref.at[slot_me], local_sem.at[0])
        own_vec.start()
        own_vec.wait()
        pltpu.make_async_copy(pieces.at[rest], pieces.at[rest], recv_sem.at[0]).wait()

        rows_of = TILE // 64

        def gram_tile(tile, carry):
            rows = pl.ds(pl.multiple_of(tile * TILE, TILE), TILE)
            total = jnp.zeros((TILE, D), jnp.float32)
            for part in range(parts):
                left = pieces[pl.ds(part * groups + tile * rows_of, rows_of)].reshape(TILE, SLOT)
                right = pieces[part * groups : (part + 1) * groups].reshape(D, SLOT)
                total += lax.dot_general(
                    left, right, (((1,), (1,)), ((), ())), preferred_element_type=jnp.float32
                )
            gram[rows, :] = total
            return carry

        lax.fori_loop(0, D // TILE, gram_tile, 0)

        @pl.when(is_wide)
        def _():
            core = lax.rem(dp_me, 2)
            sibling = (dp_me + 1 - 2 * core, t_me)
            across = (dp_me, 1 - t_me)

            def tile_at(index, owner):
                if index == 4:
                    row, col = jnp.where(owner == 0, 3, 2), 3
                elif index == 3:
                    row, col = jnp.where(owner == 0, 0, 2), jnp.where(owner == 0, 3, 2)
                else:
                    row, col = owner, owner + index
                return (
                    pl.ds(pl.multiple_of(row * TILE, TILE), TILE),
                    pl.ds(pl.multiple_of(col * TILE, TILE), TILE),
                )

            def exchange(stage, index, place):
                return pltpu.make_async_remote_copy(
                    src_ref=out_half.at[stage, index],
                    dst_ref=in_half.at[stage, index],
                    send_sem=half_send.at[stage, index],
                    recv_sem=half_recv.at[stage, index],
                    device_id=place,
                    device_id_type=MESH_IDS,
                )

            for index in range(GRAM_TILES):
                out_half[0, index] = gram[tile_at(index, 1 - core)].astype(jnp.bfloat16)
                exchange(0, index, sibling).start()
            for index in range(GRAM_TILES):
                exchange(0, index, sibling).wait_recv()
                total = gram[tile_at(index, core)] + in_half[0, index].astype(jnp.float32)
                out_half[1, index] = total.astype(jnp.bfloat16)
                exchange(1, index, across).start()
            for index in range(GRAM_TILES):
                exchange(1, index, across).wait_recv()
                total = out_half[1, index].astype(jnp.float32) + in_half[1, index].astype(jnp.float32)
                out_half[2, index] = total.astype(jnp.bfloat16)
                exchange(2, index, sibling).start()
                rows, cols = tile_at(index, core)
                gram[cols, rows] = out_half[2, index].astype(jnp.float32).T
                gram[rows, cols] = out_half[2, index].astype(jnp.float32)
            for index in range(GRAM_TILES):
                exchange(2, index, sibling).wait_recv()
                rows, cols = tile_at(index, 1 - core)
                gram[cols, rows] = in_half[2, index].astype(jnp.float32).T
                gram[rows, cols] = in_half[2, index].astype(jnp.float32)
            for index in range(GRAM_TILES):
                exchange(0, index, sibling).wait_send()
                exchange(1, index, across).wait_send()
                exchange(2, index, sibling).wait_send()

        def trace_tile(tile, total):
            rows = pl.ds(pl.multiple_of(tile * TILE, TILE), TILE)
            row_ids = lax.broadcasted_iota(jnp.int32, (TILE, D), 0) + tile * TILE
            col_ids = lax.broadcasted_iota(jnp.int32, (TILE, D), 1)
            diagonal = jnp.where(row_ids == col_ids, gram[rows, :], 0.0)
            return total + jnp.sum(jnp.sum(diagonal, axis=0, keepdims=True), axis=1, keepdims=True)

        square_total = lax.fori_loop(0, D // TILE, trace_tile, jnp.zeros((1, 1), jnp.float32))
        factor = lax.rsqrt(square_total + SQUARE_EPSILON)
        gram_low[...] = (gram[...] * (factor * factor)).astype(jnp.bfloat16)

        first, second, third = SCHULZ_FIRST, SCHULZ_SECOND, SCHULZ_THIRD

        def tiles(body):
            def one(tile, carry):
                body(pl.ds(pl.multiple_of(tile * TILE, TILE), TILE))
                return carry

            lax.fori_loop(0, D // TILE, one, 0)

        chain = chain_low
        other = chain_next
        for sweep in range(NS_ITERS):
            target = chain if sweep == 0 else poly_low

            def poly(rows):
                square = mul(gram_low[rows, :], gram_low[...])
                grown = (second / first) * gram_low[rows, :].astype(jnp.float32) + (third / first) * square
                target[rows, :] = grown.astype(jnp.bfloat16)

            tiles(poly)
            if sweep > 0:

                def join(rows, chain=chain, other=other):
                    total = chain[rows, :].astype(jnp.float32) + poly_low[rows, :].astype(jnp.float32)
                    other[rows, :] = (total + mul(chain[rows, :], poly_low[...])).astype(jnp.bfloat16)

                tiles(join)
                chain, other = other, chain
            if sweep < NS_ITERS - 1:

                def half(rows):
                    grown = gram_low[rows, :].astype(jnp.float32) + mul(gram_low[rows, :], target[...])
                    half_low[rows, :] = grown.astype(jnp.bfloat16)

                def full(rows):
                    grown = half_low[rows, :].astype(jnp.float32) + mul(half_low[rows, :], target[...])
                    gram_low[rows, :] = (grown * (first * first)).astype(jnp.bfloat16)

                tiles(half)
                tiles(full)

        scale = factor * (first**NS_ITERS)

        def turn_tile(tile, carry):
            rows = pl.ds(pl.multiple_of(tile * TILE, TILE), TILE)
            for part in range(parts):
                at = pl.ds(part * groups + tile * rows_of, rows_of)
                whole = pieces[part * groups : (part + 1) * groups].reshape(D, SLOT)
                kept = pieces[at].reshape(TILE, SLOT).astype(jnp.float32)
                fresh = (kept + mul(chain[rows, :], whole)) * scale
                turned[at] = fresh.astype(jnp.bfloat16).reshape(rows_of, 64, SLOT)
            return carry

        lax.fori_loop(0, D // TILE, turn_tile, 0)
        give_back(turned, 3, updates_ref)
        own_turned = pltpu.make_async_copy(turned.at[me], updates_ref.at[slot_me], local_sem.at[1])
        own_turned.start()
        own_turned.wait()

    def finish(length):
        here = pl.ds(0, length)
        pltpu.make_async_copy(vec_ref.at[here], vec_ref.at[here], send_sem.at[1]).wait()
        pltpu.make_async_copy(moments_ref.at[here], moments_ref.at[here], send_sem.at[0]).wait()
        pltpu.make_async_copy(vec_out_ref.at[here], vec_out_ref.at[here], recv_sem.at[2]).wait()
        pltpu.make_async_copy(updates_ref.at[here], updates_ref.at[here], recv_sem.at[3]).wait()

    @pl.when(is_handler)
    def _():
        finish(SLOTS - 1)
        rest = pl.ds(0, count - 1)
        pltpu.make_async_copy(vec_pieces.at[rest], vec_pieces.at[rest], send_sem.at[2]).wait()
        pltpu.make_async_copy(turned.at[rest], turned.at[rest], send_sem.at[3]).wait()

    @pl.when(jnp.logical_not(is_handler))
    def _():
        finish(SLOTS)


def muon_call(moments, vec_parts):
    count = lax.axis_size("dp") * lax.axis_size("tensor")
    rows = moments.shape[1]
    vmem = pl.BlockSpec(memory_space=pltpu.VMEM)
    low = pltpu.VMEM((D, D), jnp.bfloat16)
    return pl.pallas_call(
        muon_kernel,
        in_specs=[vmem, vmem],
        out_specs=[vmem, vmem],
        out_shape=[
            jax.ShapeDtypeStruct(moments.shape, jnp.bfloat16),
            jax.ShapeDtypeStruct(vec_parts.shape, jnp.float32),
        ],
        scratch_shapes=[
            pltpu.VMEM((count, rows, SLOT), jnp.bfloat16),
            pltpu.VMEM((count, rows, SLOT), jnp.bfloat16),
            pltpu.VMEM((count,) + vec_parts.shape[1:], jnp.float32),
            pltpu.VMEM(vec_parts.shape[1:], jnp.float32),
            pltpu.VMEM((D, D), jnp.float32),
            low,
            low,
            low,
            low,
            low,
            pltpu.VMEM((3, GRAM_TILES, TILE, TILE), jnp.bfloat16),
            pltpu.VMEM((3, GRAM_TILES, TILE, TILE), jnp.bfloat16),
            pltpu.SemaphoreType.DMA((2,)),
            pltpu.SemaphoreType.DMA((4,)),
            pltpu.SemaphoreType.DMA((4,)),
            pltpu.SemaphoreType.DMA((3, GRAM_TILES)),
            pltpu.SemaphoreType.DMA((3, GRAM_TILES)),
        ],
        compiler_params=pltpu.CompilerParams(
            collective_id=1, has_side_effects=True, vmem_limit_bytes=VMEM_LIMIT
        ),
        cost_estimate=pl.CostEstimate(flops=12 * 2 * D**3, bytes_accessed=4 * 1024 * 1024, transcendentals=0),
    )(moments, vec_parts)


def by_slots(rows):
    return jnp.swapaxes(rows.reshape(rows.shape[0], -1, SLOT), 0, 1)


def from_slots(rows):
    return jnp.swapaxes(rows, 0, 1).reshape(rows.shape[1], -1)


def muon_step(
    shards, vector_total, w_qkv, w_out, w_up, w_down, vectors, m_qkv, m_out, m_up, m_down, m_vec
):
    grad_qkv_shard, grad_out_shard, grad_up_shard, grad_down_shard = shards
    moment_qkv = MOMENTUM_DECAY * m_qkv + grad_qkv_shard
    moment_out = MOMENTUM_DECAY * m_out + grad_out_shard
    moment_up = MOMENTUM_DECAY * m_up + grad_up_shard
    moment_down = MOMENTUM_DECAY * m_down + grad_down_shard
    slots = jnp.concatenate(
        [
            narrow(moment_qkv),
            narrow(moment_out).T[None],
            by_slots(narrow(moment_up)),
            by_slots(narrow(moment_down).T),
        ]
    )
    updates, vector_rows = muon_call(slots, vector_total.reshape(SLOTS, 8, 128))
    vector_grad = vector_rows.reshape(12, D)
    wide_factor = math.sqrt(FF / D)
    new_qkv = w_qkv - MATRIX_RATE * updates[0:3].astype(jnp.float32)
    new_out = w_out - MATRIX_RATE * updates[3].T.astype(jnp.float32)
    new_up = w_up - MATRIX_RATE * wide_factor * from_slots(updates[4:8]).astype(jnp.float32)
    new_down = w_down - MATRIX_RATE * wide_factor * from_slots(updates[8:12]).T.astype(jnp.float32)
    moment_vec = MOMENTUM_DECAY * m_vec + vector_grad
    new_vec = vectors - VECTOR_RATE * moment_vec * lax.rsqrt(
        jnp.mean(moment_vec * moment_vec, axis=1, keepdims=True) + SQUARE_EPSILON
    )
    return (
        grad_qkv_shard,
        grad_out_shard,
        grad_up_shard,
        grad_down_shard,
        vector_grad,
        moment_qkv,
        moment_out,
        moment_up,
        moment_down,
        moment_vec,
        new_qkv,
        new_out,
        new_up,
        new_down,
        new_vec,
    )


def neighbours():
    dp_me = lax.axis_index("dp")
    y = lax.axis_index("tensor")
    core = lax.rem(dp_me, 2)
    x = lax.rem(dp_me // 2, 2)
    z = dp_me // 4
    sibling = (dp_me + 1 - 2 * core, y)
    beside = (dp_me + 2 - 4 * x, y)
    across = (dp_me, 1 - y)
    stations = [(lax.rem(dp_me + 4 * hop, 16), y) for hop in (1, 2, 3)]
    return (z, x, core, y), sibling, beside, across, stations


def greet_neighbours(places):
    barrier = pltpu.get_barrier_semaphore()
    for place in places:
        pl.semaphore_signal(barrier, inc=1, device_id=place, device_id_type=MESH_IDS)
    pl.semaphore_wait(barrier, len(places))


SWAP_AT = 2
EARLY = 2
AHEAD = 2
SPREAD_LAG = 1


class Spread:
    def __init__(self, slots_ref, table, local_sem, send_sem, recv_sem):
        self.slots_ref, self.table = slots_ref, table
        self.local_sem, self.send_sem, self.recv_sem = local_sem, send_sem, recv_sem
        (self.z, self.x, self.core, self.y), self.sibling, self.beside, self.across, self.stations = neighbours()

    def remote(self, source, target, stage, slot, place):
        return pltpu.make_async_remote_copy(
            src_ref=source,
            dst_ref=target,
            send_sem=self.send_sem.at[stage, slot],
            recv_sem=self.recv_sem.at[stage, slot],
            device_id=place,
            device_id_type=MESH_IDS,
        )

    def own(self, slot):
        here = self.table[slot][0](self.y, 0, SLOT).at[self.z, self.x, self.core]
        return pltpu.make_async_copy(self.slots_ref.at[slot], here, self.local_sem.at[slot])

    def along_z(self, slot):
        here = self.table[slot][0](self.y, 0, SLOT).at[self.z, self.x, self.core]
        return [
            self.remote(self.slots_ref.at[slot], here, hop, slot, place)
            for hop, place in enumerate(self.stations)
        ]

    def second(self, slot):
        view, size = self.table[slot]
        copies = []
        if size:
            part = view(self.y, 0, size).at[:, self.x, self.core]
            copies.append(self.remote(part, part, 3, slot, self.beside))
        if size < SLOT:
            part = view(self.y, size, SLOT - size).at[:, self.x, self.core]
            copies.append(self.remote(part, part, 4, slot, self.across))
        return copies

    def third(self, slot):
        view, size = self.table[slot]
        copies = []
        if size:
            part = view(self.y, 0, size).at[:, :, self.core]
            copies.append(self.remote(part, part, 5, slot, self.across))
        if size < SLOT:
            for index in (0, 1):
                part = view(index, size, SLOT - size).at[:, self.x, self.core]
                copies.append(self.remote(part, part, 6 + index, slot, self.beside))
        return copies

    def fourth(self, slot):
        view, _ = self.table[slot]
        copies = []
        for index in (0, 1):
            part = view(index, 0, SLOT).at[:, :, self.core]
            copies.append(self.remote(part, part, 8 + index, slot, self.sibling))
        return copies

    def launch(self, slot):
        if slot < len(self.table):
            self.own(slot).start()
            for copy in self.along_z(slot):
                copy.start()

    def begin(self):
        for slot in range(AHEAD):
            self.launch(slot)

    def tick(self, index):
        count = len(self.table)
        self.launch(index + AHEAD)
        if index < count:
            self.own(index).wait()
            for copy in self.along_z(index):
                copy.wait_recv()
            for copy in self.second(index):
                copy.start()
        if 0 <= index - SPREAD_LAG < count:
            for copy in self.second(index - SPREAD_LAG):
                copy.wait_recv()
            for copy in self.third(index - SPREAD_LAG):
                copy.start()
        if 0 <= index - 2 * SPREAD_LAG < count:
            for copy in self.third(index - 2 * SPREAD_LAG):
                copy.wait_recv()
            for copy in self.fourth(index - 2 * SPREAD_LAG):
                copy.start()

    def ticks(self):
        return len(self.table) + 2 * SPREAD_LAG

    def arrived(self, slot):
        for copy in self.fourth(slot):
            copy.wait_recv()

    def sent(self):
        for slot in range(len(self.table)):
            for copy in self.along_z(slot) + self.second(slot) + self.third(slot) + self.fourth(slot):
                copy.wait_send()

    def finish(self):
        for slot in range(len(self.table)):
            self.arrived(slot)
        self.sent()


def column_view(ref, column, distance):
    def view(part, start, size):
        first = column + part * distance + start
        if not isinstance(part, int):
            first = pl.multiple_of(first, 128)
        return ref.at[:, :, :, :, pl.ds(first, size)]

    return view


def place_view(ref, place):
    def view(part, start, size):
        return ref.at[place + part, :, :, :, :, pl.ds(start, size)]

    return view


def spread_semaphores(count):
    return [
        pltpu.SemaphoreType.DMA((count,)),
        pltpu.SemaphoreType.DMA((10, count)),
        pltpu.SemaphoreType.DMA((10, count)),
    ]


def first_spread_kernel(slots_ref, tokens_ref, whole_ref, got_ref, local_sem, send_sem, recv_sem, token_sem):
    table = [(column_view(whole_ref, index * SLOT, 3 * SLOT), 0) for index in range(3)]
    spread = Spread(slots_ref, table, local_sem, send_sem, recv_sem)
    greet_neighbours([spread.sibling, spread.beside, spread.across] + spread.stations)
    swap = pltpu.make_async_remote_copy(
        src_ref=tokens_ref.at[1 - spread.y],
        dst_ref=got_ref,
        send_sem=token_sem.at[0],
        recv_sem=token_sem.at[1],
        device_id=spread.across,
        device_id_type=MESH_IDS,
    )
    spread.begin()
    for index in range(spread.ticks()):
        spread.tick(index)
        if index == SWAP_AT:
            swap.start()
    spread.finish()
    swap.wait()


def attend_spread_kernel(
    starts_ref,
    slopes_ref,
    normed_ref,
    weights_ref,
    shifts_ref,
    slots_ref,
    cotangent_ref,
    packed_ref,
    ctx_ref,
    exps_ref,
    stat_ref,
    normed_t_ref,
    out_ref,
    up_ref,
    down_ref,
    got_ref,
    dist_ref,
    ctx_t,
    local_sem,
    send_sem,
    recv_sem,
    token_sem,
):
    pair = pl.program_id(0)
    table = [(column_view(out_ref, 0, SLOT), HALF_SLOT)]
    for index in range(EARLY):
        over_x = HALF_SLOT if index == EARLY - 1 else 0
        table += [(column_view(ref, index * SLOT, EARLY * SLOT), over_x) for ref in (up_ref, down_ref)]
    spread = Spread(slots_ref, table, local_sem, send_sem, recv_sem)
    swap = pltpu.make_async_remote_copy(
        src_ref=cotangent_ref.at[1 - spread.y],
        dst_ref=got_ref,
        send_sem=token_sem.at[0],
        recv_sem=token_sem.at[1],
        device_id=spread.across,
        device_id_type=MESH_IDS,
    )

    @pl.when(pair == 0)
    def _():
        greet_neighbours([spread.sibling, spread.beside, spread.across] + spread.stations)
        spread.begin()
        normed_t_ref[...] = normed_ref[...].T
        layout_grid(starts_ref, dist_ref)

    def between():
        for index in range(spread.ticks()):

            @pl.when(pair == index)
            def _(index=index):
                spread.tick(index)
                if index == len(table) - 1:
                    swap.start()

    packed = (mul(normed_ref[...], weights_ref[...]) + shifts_ref[...]).astype(jnp.bfloat16)
    packed_ref[...] = packed
    attend_pair(pair, slopes_ref, packed, dist_ref, ctx_ref, exps_ref, stat_ref, ctx_t, between)

    @pl.when(pair == PAIRS - 1)
    def _():
        spread.finish()
        swap.wait()


def whole_shape(columns):
    return jax.ShapeDtypeStruct((4, 2, 2, 64, columns), jnp.bfloat16)


def first_spread(slots, tokens):
    anywhere = pl.BlockSpec(memory_space=pl.ANY)
    whole, got = pl.pallas_call(
        first_spread_kernel,
        in_specs=[anywhere] * 2,
        out_specs=[anywhere] * 2,
        out_shape=[whole_shape(3 * D), jax.ShapeDtypeStruct(tokens.shape[1:], tokens.dtype)],
        scratch_shapes=spread_semaphores(3) + [pltpu.SemaphoreType.DMA((2,))],
        compiler_params=pltpu.CompilerParams(collective_id=3, has_side_effects=True),
    )(slots, tokens)
    return whole.reshape(D, 3 * D), got


def attend_spread(starts, slopes, normed, weights, shifts, slots, cotangent):
    anywhere = pl.BlockSpec(memory_space=pl.ANY)
    packed, context, exps, stats, normed_t, out, up, down, got = pl.pallas_call(
        attend_spread_kernel,
        grid=(PAIRS,),
        in_specs=[
            SCALARS,
            SCALARS,
            pl.BlockSpec((LEN, D), lambda p: (0, 0)),
            PACKED_COLS,
            pl.BlockSpec((1, 3 * PAIR), lambda p: (0, p)),
            anywhere,
            anywhere,
        ],
        out_specs=[PACKED_COLS, PAIR_COLS, PAIR_GRID, PAIR_STAT, pl.BlockSpec((D, LEN), lambda p: (0, 0))]
        + [anywhere] * 4,
        out_shape=[
            jax.ShapeDtypeStruct((LEN, 3 * D), jnp.bfloat16),
            jax.ShapeDtypeStruct((LEN, D), jnp.bfloat16),
            jax.ShapeDtypeStruct((H, LEN, LEN), jnp.bfloat16),
            jax.ShapeDtypeStruct((PAIRS, 2, LEN), jnp.float32),
            jax.ShapeDtypeStruct((D, LEN), jnp.bfloat16),
            whole_shape(D),
            whole_shape(2 * EARLY * SLOT),
            whole_shape(2 * EARLY * SLOT),
            jax.ShapeDtypeStruct(cotangent.shape[1:], cotangent.dtype),
        ],
        scratch_shapes=[pltpu.VMEM((LEN, LEN), jnp.float32), pltpu.VMEM((PAIR, LEN), jnp.float32)]
        + spread_semaphores(1 + 2 * EARLY)
        + [pltpu.SemaphoreType.DMA((2,))],
        compiler_params=pltpu.CompilerParams(
            collective_id=4, has_side_effects=True, vmem_limit_bytes=VMEM_LIMIT
        ),
        cost_estimate=pl.CostEstimate(
            flops=16 * LEN * LEN * D, bytes_accessed=90 * 1024 * 1024, transcendentals=H * LEN * LEN
        ),
    )(starts, slopes, normed, weights, shifts, slots, cotangent)
    wholes = out.reshape(D, D), up.reshape(D, -1), down.reshape(D, -1)
    return packed, context, exps, stats, normed_t, wholes, got


class Summing:
    def __init__(self, sources, add_own, buffers, total_ref, sems, lag, ready=0, hold=0):
        self.sources, self.add_own, self.total_ref, self.lag = sources, add_own, total_ref, lag
        self.ready, self.hold = ready, hold
        self.first, self.second_y, self.second_x, self.third, self.fourth = buffers
        self.send_sem, self.recv_sem = sems
        (self.z, self.x, self.core, self.y), self.sibling, self.beside, self.across, self.stations = neighbours()
        self.low_cols = pl.ds(0, HALF_SLOT)
        self.high_cols = pl.ds(HALF_SLOT, HALF_SLOT)

    def count(self):
        return len(self.sources)

    def remote(self, source, target, stage, slot, place):
        return pltpu.make_async_remote_copy(
            src_ref=source,
            dst_ref=target,
            send_sem=self.send_sem.at[stage, slot],
            recv_sem=self.recv_sem.at[stage, slot],
            device_id=place,
            device_id_type=MESH_IDS,
        )

    def landed(self, ref, stage, slot):
        pltpu.make_async_copy(ref, ref, self.recv_sem.at[stage, slot]).wait()

    def send_first(self, slot):
        for part in (0, 1):
            source = self.sources[slot](part).at[:, :, 1 - self.core]
            self.remote(source, self.first.at[slot, part], 0, slot, self.sibling).start()

    def second_copies(self, slot):
        for_y = self.first.at[slot, 1 - self.y, :, :, :, self.low_cols]
        for_x = self.first.at[slot, :, :, 1 - self.x, :, self.high_cols]
        return (
            self.remote(for_y, self.second_y.at[slot], 1, slot, self.across),
            self.remote(for_x, self.second_x.at[slot], 2, slot, self.beside),
        )

    def third_copies(self, slot):
        for_x = self.second_y.at[slot, :, 1 - self.x]
        for_y = self.second_x.at[slot, 1 - self.y]
        return (
            self.remote(for_x, self.third.at[slot, :, :, self.low_cols], 3, slot, self.beside),
            self.remote(for_y, self.third.at[slot, :, :, self.high_cols], 4, slot, self.across),
        )

    def fourth_copies(self, slot):
        return tuple(
            self.remote(
                self.third.at[slot, lax.rem(self.z + hop, 4)], self.fourth.at[slot, hop - 1], 4 + hop, slot, place
            )
            for hop, place in zip((1, 2, 3), self.stations)
        )

    def stage_one(self, slot):
        self.landed(self.first.at[slot], 0, slot)
        self.add_own(slot)
        for copy in self.second_copies(slot):
            copy.start()

    def stage_two(self, slot):
        first, second_y, second_x = self.first, self.second_y, self.second_x
        self.landed(second_y.at[slot], 1, slot)
        second_y[slot] = second_y[slot] + first[slot, self.y, :, :, :, :HALF_SLOT]
        self.landed(second_x.at[slot], 2, slot)
        second_x[slot] = second_x[slot] + first[slot, :, :, self.x, :, HALF_SLOT:]
        for copy in self.third_copies(slot):
            copy.start()

    def stage_three(self, slot):
        third = self.third
        self.landed(third.at[slot, :, :, self.low_cols], 3, slot)
        self.landed(third.at[slot, :, :, self.high_cols], 4, slot)
        third[slot, :, :, :HALF_SLOT] = third[slot, :, :, :HALF_SLOT] + self.second_y[slot, :, self.x]
        third[slot, :, :, HALF_SLOT:] = third[slot, :, :, HALF_SLOT:] + self.second_x[slot, self.y]
        for copy in self.fourth_copies(slot):
            copy.start()

    def stage_four(self, slot):
        total = self.third[slot, self.z].astype(jnp.float32)
        for hop in (1, 2, 3):
            self.landed(self.fourth.at[slot, hop - 1], 4 + hop, slot)
            total = total + self.fourth[slot, hop - 1].astype(jnp.float32)
        self.total_ref[slot] = total

    def ticks(self):
        return self.count() + self.hold + 3 * self.lag

    def tick(self, index):
        for slot in range(self.count()):
            entry = slot + (self.hold if slot >= self.ready else 0)
            pl.when(index == entry)(lambda slot=slot: self.stage_one(slot))
        for number, stage in enumerate((self.stage_two, self.stage_three, self.stage_four)):
            entry = index - (number + 1) * self.lag
            slot = jnp.where(entry < self.ready, entry, entry - self.hold)
            late = (entry >= self.ready + self.hold) & (slot < self.count())
            early = (entry >= 0) & (entry < self.ready)
            pl.when(early | late)(lambda stage=stage, slot=slot: stage(slot))

    def fixed_tick(self, index):
        for number, stage in enumerate((self.stage_one, self.stage_two, self.stage_three, self.stage_four)):
            slot = index - number * self.lag
            if 0 <= slot < self.count():
                stage(slot)

    def sent(self):
        def one(slot, carry):
            pltpu.make_async_copy(self.first.at[slot], self.first.at[slot], self.send_sem.at[0, slot]).wait()
            for copy in self.second_copies(slot) + self.third_copies(slot) + self.fourth_copies(slot):
                copy.wait_send()
            return carry

        lax.fori_loop(0, self.count(), one, 0)


def summing_buffers(count):
    rows, low = 64, jnp.bfloat16
    return [
        pltpu.VMEM((count, 2, 4, 2, rows, SLOT), low),
        pltpu.VMEM((count, 4, 2, rows, HALF_SLOT), low),
        pltpu.VMEM((count, 2, 4, rows, HALF_SLOT), low),
        pltpu.VMEM((count, 4, rows, SLOT), low),
        pltpu.VMEM((count, 3, rows, SLOT), low),
        pltpu.SemaphoreType.DMA((8, count)),
        pltpu.SemaphoreType.DMA((8, count)),
    ]


HIDDEN = 512
CHUNK = 256
HIDDEN_STEPS = FF // HIDDEN
GELU_SLOPE = math.sqrt(2.0 / math.pi)
GELU_CUBE = 0.044715


def dot_last(left, right):
    return lax.dot_general(left, right, (((1,), (1,)), ((), ())), preferred_element_type=jnp.float32)


def gelu_both(rows):
    square = rows * rows
    bent = jnp.tanh(rows * (GELU_SLOPE + GELU_SLOPE * GELU_CUBE * square))
    half = 0.5 + 0.5 * bent
    slope = half + 0.5 * rows * (1.0 - bent * bent) * (GELU_SLOPE + 3.0 * GELU_SLOPE * GELU_CUBE * square)
    return rows * half, slope


def hidden_block(step):
    return (step % 2) * (HIDDEN_STEPS // 2) + step // 2


def mlp_kernel(
    rows_ref,
    cot_ref,
    base_ref,
    bias_ref,
    up_ref,
    down_ref,
    slots_ref,
    block_ref,
    grad_rows_ref,
    grad_up_ref,
    grad_down_ref,
    bias_sum_ref,
    total_ref,
    rows_t,
    cot_t,
    total,
    up_part,
    down_part,
    active,
    grad_before,
    grad_early,
    first,
    second_y,
    second_x,
    third,
    fourth,
    sum_send,
    sum_recv,
    local_sem,
    spread_send,
    spread_recv,
    load_sem,
):
    step = pl.program_id(0)
    early_steps = 2 * EARLY
    table = []
    for index in range(HIDDEN_STEPS // 2 - EARLY):
        table += [(place_view(ref, 2 + 2 * index), HALF_SLOT) for ref in (up_part, down_part)]
    spread = Spread(slots_ref, table, local_sem, spread_send, spread_recv)

    def early_block(slot, part):
        return grad_early.at[slot % 2, 2 * (slot // 2) + part]

    def add_own(slot):
        for part in (0, 1):
            first[slot, part] = first[slot, part] + grad_early[slot % 2, 2 * (slot // 2) + part, :, :, summing.core]

    sources = [lambda part, slot=slot: early_block(slot, part) for slot in range(2 * EARLY)]
    buffers = (first, second_y, second_x, third, fourth)
    summing = Summing(sources, add_own, buffers, total_ref, (sum_send, sum_recv), 1)

    def loads(at):
        column = lax.rem(at, 2) * EARLY + at // 2
        cols = pl.ds(pl.multiple_of(column * HIDDEN, HIDDEN), HIDDEN)
        place = lax.rem(at, 2)
        return (
            pltpu.make_async_copy(up_ref.at[:, :, :, :, cols], up_part.at[place], load_sem.at[0, place]),
            pltpu.make_async_copy(down_ref.at[:, :, :, :, cols], down_part.at[place], load_sem.at[1, place]),
        )

    @pl.when(step == 0)
    def _():
        for copy in loads(step):
            copy.start()
        greet_neighbours([spread.sibling, spread.beside, spread.across] + spread.stations)
        spread.begin()
        rows_t[...] = rows_ref[...].T
        cot_t[...] = cot_ref[...].T
        total[...] = base_ref[...]
        grad_rows_ref[...] = jnp.zeros_like(grad_rows_ref)

    @pl.when(step < early_steps)
    def _():
        for copy in loads(step):
            copy.wait()

    @pl.when(step < early_steps - 1)
    def _():
        for copy in loads(step + 1):
            copy.start()

    for index in range(HIDDEN_STEPS // 2 - EARLY):

        @pl.when(step == early_steps + 2 * index)
        def _(index=index):
            spread.arrived(2 * index)
            spread.arrived(2 * index + 1)

    place = jnp.where(step < early_steps, lax.rem(step, 2), step - early_steps + 2)
    up = up_part[place].reshape(D, HIDDEN)
    down = down_part[place].reshape(D, HIDDEN)
    bias = bias_ref[...]
    bias_sum = jnp.zeros((1, HIDDEN), jnp.float32)
    for index in range(LEN // CHUNK):
        here = slice(index * CHUNK, index * CHUNK + CHUNK)
        value, slope = gelu_both(mul(rows_ref[here], up) + bias)
        value = value.astype(jnp.bfloat16)
        grads = (slope * mul(cot_ref[here], down)).astype(jnp.bfloat16)
        active[here] = value
        grad_before[here] = grads
        bias_sum += jnp.sum(grads.astype(jnp.float32), axis=0, keepdims=True)
        total[here] += dot_last(value, down)
        grad_rows_ref[here] += dot_last(grads, up)
        if index == LEN // CHUNK // 2 - 1:
            for number in range(spread.ticks()):
                pl.when(step == number)(lambda number=number: spread.tick(number))
    bias_sum_ref[...] = bias_sum
    grad_down = mul(cot_t[...], active[...]).astype(jnp.bfloat16)
    grad_up = mul(rows_t[...], grad_before[...]).astype(jnp.bfloat16)

    @pl.when(step < early_steps)
    def _():
        grad_early[0, step] = grad_up.reshape(grad_early.shape[2:])
        grad_early[1, step] = grad_down.reshape(grad_early.shape[2:])

    @pl.when(step >= early_steps)
    def _():
        grad_up_ref[...] = grad_up
        grad_down_ref[...] = grad_down

    for number in range(HIDDEN_STEPS):

        @pl.when(step == number)
        def _(number=number):
            if number < early_steps and number % 2:
                summing.send_first(number - 1)
                summing.send_first(number)
            if number >= 2:
                summing.fixed_tick(number - 2)

    @pl.when(step == HIDDEN_STEPS - 1)
    def _():
        block_ref[...] = total[...].astype(jnp.bfloat16)
        for number in range(HIDDEN_STEPS - 2, summing.ticks()):
            summing.fixed_tick(number)
        summing.sent()
        spread.sent()


def late_block(step):
    late = HIDDEN_STEPS // 2 - EARLY
    return jnp.where(step < 2 * EARLY, 0, (step % 2) * late + step // 2 - EARLY)


def mlp_both(rows, cot, base, bias, up, down, slots):
    anywhere = pl.BlockSpec(memory_space=pl.ANY)
    once = pl.Buffered(1)
    whole = pl.BlockSpec((LEN, D), lambda s: (0, 0), pipeline_mode=once)
    hidden = pl.BlockSpec((D, HIDDEN), lambda s: (0, late_block(s)))
    hidden_row = pl.BlockSpec((1, HIDDEN), lambda s: (0, hidden_block(s)))
    low = jnp.bfloat16
    late = HIDDEN_STEPS // 2 - EARLY
    part = pltpu.VMEM((2 + 2 * late, 4, 2, 2, 64, HIDDEN), low)
    split = [weights.reshape(4, 2, 2, 64, -1) for weights in (up, down)]
    return pl.pallas_call(
        mlp_kernel,
        grid=(HIDDEN_STEPS,),
        in_specs=[whole, whole, whole, hidden_row, anywhere, anywhere, anywhere],
        out_specs=[
            whole,
            whole,
            hidden,
            hidden,
            hidden_row,
            pl.BlockSpec((2 * EARLY, 64, SLOT), lambda s: (0, 0, 0), pipeline_mode=once),
        ],
        out_shape=[
            jax.ShapeDtypeStruct((LEN, D), low),
            jax.ShapeDtypeStruct((LEN, D), jnp.float32),
            jax.ShapeDtypeStruct((D, 2 * late * HIDDEN), low),
            jax.ShapeDtypeStruct((D, 2 * late * HIDDEN), low),
            jax.ShapeDtypeStruct((1, FF), jnp.float32),
            jax.ShapeDtypeStruct((2 * EARLY, 64, SLOT), jnp.float32),
        ],
        scratch_shapes=[
            pltpu.VMEM((D, LEN), low),
            pltpu.VMEM((D, LEN), low),
            pltpu.VMEM((LEN, D), jnp.float32),
            part,
            part,
            pltpu.VMEM((LEN, HIDDEN), low),
            pltpu.VMEM((LEN, HIDDEN), low),
            pltpu.VMEM((2, 2 * EARLY, 4, 2, 2, 64, HIDDEN), low),
            *summing_buffers(2 * EARLY),
            *spread_semaphores(2 * late),
            pltpu.SemaphoreType.DMA((2, 2)),
        ],
        compiler_params=pltpu.CompilerParams(
            collective_id=5, has_side_effects=True, vmem_limit_bytes=62 * 1024 * 1024
        ),
        cost_estimate=pl.CostEstimate(
            flops=12 * LEN * D * FF, bytes_accessed=60 * 1024 * 1024, transcendentals=LEN * FF
        ),
    )(rows, cot, base, bias, *split, slots)


LAG = 2
READY = 5
LATE_SLOTS = 8
RING = 4


def block_view(ref, column):
    return ref.at[:, :, :, :, pl.ds(column, SLOT)]


def attend_bwd_half(half, scale, values, keys_t, parts, exps, sums):
    half_t, half_rows, half_queries, inner = parts
    dq_t, dk_sum, dv_sum = sums
    heads = slice(half * HD, half * HD + HD)
    for block in range(LEN // QB):
        span = min(LEN, QB * block + QB + PIECE)
        cols = slice(block * QB, block * QB + QB)
        weights = exps[:span, cols]
        grad_probs = mul(values[:span], half_t[:, cols])
        grad_scores = (weights.astype(jnp.float32) * (grad_probs - inner[:, cols])).astype(jnp.bfloat16)
        dv_sum[:span, :] += mul(weights, half_rows[cols])
        dk_sum[:span, :] += mul(grad_scores, half_queries[cols])
        dq_t[heads, cols] = mul(keys_t[heads, :span], grad_scores) * scale


def attend_sum_kernel(
    packed_ref,
    ctx_ref,
    grad_ref,
    stat_ref,
    weights_ref,
    normed_t_ref,
    exps_ref,
    up_ref,
    down_ref,
    out_ref,
    total_ref,
    grad_normed_ref,
    packed_sum_ref,
    exps,
    dq_t,
    dk_sum,
    dv_sum,
    grad_qkv,
    mine,
    first,
    second_y,
    second_x,
    third,
    fourth,
    send_sem,
    recv_sem,
    exps_sem,
    load_sem,
):
    pair = pl.program_id(0)
    width = up_ref.shape[-1] // 2
    sources = []
    for index in range(width // SLOT):
        for ref in (up_ref, down_ref):
            sources.append(lambda part, ref=ref, index=index: block_view(ref, part * width + index * SLOT))
    sources.append(lambda part: block_view(out_ref, part * SLOT))
    for index in range(3):
        sources.append(lambda part, index=index: block_view(grad_qkv, (part * 3 + index) * SLOT))

    def load(slot, part):
        block = sources[slot](part).at[:, :, summing.core]
        return pltpu.make_async_copy(block, mine.at[slot % RING, part], load_sem.at[slot % RING])

    def add_own(slot):
        if slot < READY:
            place = slot % RING
            pltpu.make_async_copy(mine.at[place], mine.at[place], load_sem.at[place]).wait()
            first[slot] = first[slot] + mine[place]
            if slot + RING < READY:
                for part in (0, 1):
                    load(slot + RING, part).start()
        else:
            for part in (0, 1):
                cols = pl.ds((part * 3 + slot - READY) * SLOT, SLOT)
                first[slot, part] = first[slot, part] + grad_qkv[:, :, summing.core, :, cols]

    buffers = (first, second_y, second_x, third, fourth)
    summing = Summing(sources, add_own, buffers, total_ref, (send_sem, recv_sem), LAG, READY, 1)

    def exps_load(head, half):
        return pltpu.make_async_copy(exps_ref.at[head], exps.at[half], exps_sem.at[half])

    @pl.when(pair == 0)
    def _():
        for half in (0, 1):
            exps_load(half, half).start()
        for slot in range(RING):
            for part in (0, 1):
                load(slot, part).start()
        greet_neighbours([summing.sibling, summing.beside, summing.across] + summing.stations)
        for slot in range(READY):
            summing.send_first(slot)
        grad_normed_ref[...] = jnp.zeros_like(grad_normed_ref)

    scale = 1.0 / math.sqrt(HD)
    queries = packed_ref[:, :PAIR]
    keys_t = packed_ref[:, PAIR : 2 * PAIR].T
    values = packed_ref[:, 2 * PAIR :]
    grads_t = grad_ref[...].T.astype(jnp.float32)
    context_t = ctx_ref[...].T.astype(jnp.float32)
    scaled = []
    inner_rows = []
    for half in (0, 1):
        heads = slice(half * HD, half * HD + HD)
        scaled.append(grads_t[heads] * stat_ref[0, half : half + 1, :])
        inner_rows.append(jnp.sum(scaled[half] * context_t[heads], axis=0, keepdims=True))
    scaled_t = jnp.concatenate(scaled, axis=0).astype(jnp.bfloat16)
    scaled_rows = scaled_t.T
    dk_sum[...] = jnp.zeros_like(dk_sum)
    dv_sum[...] = jnp.zeros_like(dv_sum)
    for half in (0, 1):
        exps_load(2 * pair + half, half).wait()
        parts = (
            only_rows(scaled_t, half),
            only_cols(scaled_rows, half),
            only_cols(queries, half),
            inner_rows[half],
        )
        attend_bwd_half(half, scale, values, keys_t, parts, exps.at[half], (dq_t, dk_sum, dv_sum))

        @pl.when(pair < PAIRS - 1)
        def _(half=half):
            exps_load(2 * pair + 2 + half, half).start()

        if half == 0:
            summing.tick(pair)
    grads = jnp.concatenate([dq_t[...].T, dk_sum[...] * scale, dv_sum[...]], axis=1).astype(jnp.bfloat16)
    packed_sum_ref[...] = jnp.sum(grads.astype(jnp.float32), axis=0, keepdims=True)
    cols = pl.ds(pl.multiple_of(pair * (3 * PAIR), PAIR), 3 * PAIR)
    grad_weights = mul(normed_t_ref[...], grads).astype(jnp.bfloat16)
    grad_qkv[:, :, :, :, cols] = grad_weights.reshape(4, 2, 2, 64, 3 * PAIR)
    grad_normed_ref[...] += dot_last(grads, weights_ref[...])

    for slot in range(READY, LATE_SLOTS):
        pl.when(pair == PAIRS - LATE_SLOTS + slot)(lambda slot=slot: summing.send_first(slot))

    @pl.when(pair == PAIRS - 1)
    def _():
        def late(index, carry):
            summing.tick(index)
            return carry

        lax.fori_loop(PAIRS, summing.ticks(), late, 0)
        summing.sent()


def attend_sum(packed, context, grad_context, stats, weights, normed_t, exps, grad_up, grad_down, grad_out):
    anywhere = pl.BlockSpec(memory_space=pl.ANY)
    rows = 64
    low = jnp.bfloat16
    once = pl.Buffered(1)
    tall = pl.BlockSpec((LEN, D), lambda p: (0, 0), pipeline_mode=once)
    split = [grad.reshape(4, 2, 2, rows, grad.shape[-1]) for grad in (grad_up, grad_down, grad_out)]
    return pl.pallas_call(
        attend_sum_kernel,
        grid=(PAIRS,),
        in_specs=[PACKED_COLS, PAIR_COLS, PAIR_COLS, PAIR_STAT, PACKED_COLS, tall] + [anywhere] * 4,
        out_specs=[
            pl.BlockSpec((LATE_SLOTS, rows, SLOT), lambda p: (0, 0, 0), pipeline_mode=once),
            tall,
            pl.BlockSpec((1, 3 * PAIR), lambda p: (0, p)),
        ],
        out_shape=[
            jax.ShapeDtypeStruct((LATE_SLOTS, rows, SLOT), jnp.float32),
            jax.ShapeDtypeStruct((LEN, D), jnp.float32),
            jax.ShapeDtypeStruct((1, 3 * D), jnp.float32),
        ],
        scratch_shapes=[
            pltpu.VMEM((2, LEN, LEN), low),
            pltpu.VMEM((PAIR, LEN), jnp.float32),
            pltpu.VMEM((LEN, PAIR), jnp.float32),
            pltpu.VMEM((LEN, PAIR), jnp.float32),
            pltpu.VMEM((4, 2, 2, rows, 3 * D), low),
            pltpu.VMEM((RING, 2, 4, 2, rows, SLOT), low),
            *summing_buffers(LATE_SLOTS),
            pltpu.SemaphoreType.DMA((2,)),
            pltpu.SemaphoreType.DMA((RING,)),
        ],
        compiler_params=pltpu.CompilerParams(
            collective_id=2, has_side_effects=True, vmem_limit_bytes=62 * 1024 * 1024
        ),
        cost_estimate=pl.CostEstimate(
            flops=44 * LEN * LEN * D, bytes_accessed=400 * 1024 * 1024, transcendentals=0
        ),
    )(packed, context, grad_context, stats, weights, normed_t, exps, *split)


ROWS = 256


def norm_pull(rows, grads, gain):
    centered = rows - jnp.mean(rows, axis=-1, keepdims=True)
    inverse = lax.rsqrt(jnp.mean(centered * centered, axis=-1, keepdims=True) + NORM_EPSILON)
    normed = centered * inverse
    scaled = grads * gain
    along = jnp.mean(scaled * normed, axis=-1, keepdims=True)
    pulled = inverse * (scaled - jnp.mean(scaled, axis=-1, keepdims=True) - normed * along)
    gain_sum = jnp.sum(grads * normed, axis=0, keepdims=True)
    return pulled, gain_sum, jnp.sum(grads, axis=0, keepdims=True)


def add_rows(sums_ref, rows):
    for index, row in enumerate(rows):
        sums_ref[index : index + 1, :] += row


def middle_kernel(
    middle_ref, grad_ref, cot_ref, ctx_ref, gain_ref, weights_ref, grad_middle_ref, grad_ctx_ref, grad_out_ref, sums_ref, total
):
    step = pl.program_id(0)

    @pl.when(step == 0)
    def _():
        sums_ref[...] = jnp.zeros_like(sums_ref)
        total[...] = jnp.zeros_like(total)

    cot = cot_ref[...].astype(jnp.float32)
    pulled, gain_sum, shift_sum = norm_pull(middle_ref[...], grad_ref[...], gain_ref[...])
    grads = cot + pulled
    low = grads.astype(jnp.bfloat16)
    grad_middle_ref[...] = grads
    grad_ctx_ref[...] = mul(low, weights_ref[...]).astype(jnp.bfloat16)
    total[...] += mul(low.T, ctx_ref[...])
    grad_sum = jnp.sum(grads, axis=0, keepdims=True)
    add_rows(sums_ref, (gain_sum, shift_sum, grad_sum, jnp.sum(cot, axis=0, keepdims=True)))

    @pl.when(step == LEN // ROWS - 1)
    def _():
        grad_out_ref[...] = total[...].astype(jnp.bfloat16)


def middle_backward(middle, grad_rows, cot, context, gain, weights):
    rows = pl.BlockSpec((ROWS, D), lambda s: (s, 0))
    whole = pl.BlockSpec((D, D), lambda s: (0, 0), pipeline_mode=pl.Buffered(1))
    row = pl.BlockSpec((1, D), lambda s: (0, 0))
    sums = pl.BlockSpec((8, D), lambda s: (0, 0))
    return pl.pallas_call(
        middle_kernel,
        grid=(LEN // ROWS,),
        in_specs=[rows, rows, rows, rows, row, whole],
        out_specs=[rows, rows, whole, sums],
        out_shape=[
            jax.ShapeDtypeStruct((LEN, D), jnp.float32),
            jax.ShapeDtypeStruct((LEN, D), jnp.bfloat16),
            jax.ShapeDtypeStruct((D, D), jnp.bfloat16),
            jax.ShapeDtypeStruct((8, D), jnp.float32),
        ],
        scratch_shapes=[pltpu.VMEM((D, D), jnp.float32)],
        compiler_params=pltpu.CompilerParams(vmem_limit_bytes=VMEM_LIMIT),
        cost_estimate=pl.CostEstimate(flops=4 * LEN * D * D, bytes_accessed=24 * 1024 * 1024, transcendentals=0),
    )(middle, grad_rows, cot, context, gain, weights)


def token_kernel(rows_ref, grad_ref, grad_middle_ref, gain_ref, out_ref, sums_ref):
    @pl.when(pl.program_id(0) == 0)
    def _():
        sums_ref[...] = jnp.zeros_like(sums_ref)

    pulled, gain_sum, shift_sum = norm_pull(rows_ref[...].astype(jnp.float32), grad_ref[...], gain_ref[...])
    out_ref[...] = (grad_middle_ref[...] + pulled).astype(jnp.bfloat16)
    add_rows(sums_ref, (gain_sum, shift_sum))


def token_backward(rows_low, grad_rows, grad_middle, gain):
    rows = pl.BlockSpec((ROWS, D), lambda s: (s, 0))
    row = pl.BlockSpec((1, D), lambda s: (0, 0))
    sums = pl.BlockSpec((8, D), lambda s: (0, 0))
    return pl.pallas_call(
        token_kernel,
        grid=(LEN // ROWS,),
        in_specs=[rows, rows, rows, row],
        out_specs=[rows, sums],
        out_shape=[jax.ShapeDtypeStruct((LEN, D), jnp.bfloat16), jax.ShapeDtypeStruct((8, D), jnp.float32)],
        compiler_params=pltpu.CompilerParams(vmem_limit_bytes=VMEM_LIMIT),
        cost_estimate=pl.CostEstimate(flops=0, bytes_accessed=12 * 1024 * 1024, transcendentals=0),
    )(rows_low, grad_rows, grad_middle, gain)


def narrow(rows):
    return rows.astype(jnp.bfloat16)


def contract(left, right, left_dim, right_dim):
    return lax.dot_general(
        left, right, (((left_dim,), (right_dim,)), ((), ())), preferred_element_type=jnp.float32
    )


def in_order(rank, own, got):
    return jnp.where(rank == 0, jnp.concatenate([own, got]), jnp.concatenate([got, own]))


def swap_halves(mine, rank):
    rows = mine.shape[0] // 2
    kept = lax.dynamic_slice_in_dim(mine, rank * rows, rows, 0)
    sent = lax.dynamic_slice_in_dim(mine, (1 - rank) * rows, rows, 0)
    got = lax.ppermute(sent, "tensor", [(0, 1), (1, 0)])
    return jnp.where(rank == 0, jnp.stack([kept, got]), jnp.stack([got, kept]))


def by_pairs(rows):
    count, height, width = rows.shape
    return jnp.transpose(rows.reshape(count, height, width // PAIR, PAIR), (1, 2, 0, 3)).reshape(height, -1)


def from_pairs(rows):
    height = rows.shape[0]
    return jnp.transpose(rows.reshape(height, -1, 3, PAIR), (2, 0, 1, 3)).reshape(3, height, -1)


def sequence_step(
    tokens,
    cotangent,
    piece_starts,
    w_qkv,
    w_out,
    w_up,
    w_down,
    vectors,
    m_qkv,
    m_out,
    m_up,
    m_down,
    m_vec,
):
    rank = lax.axis_index("tensor")
    slopes = jnp.exp2(-8.0 * jnp.arange(1, H + 1, dtype=jnp.float32) / H)
    starts = lax.dynamic_slice_in_dim(piece_starts[:, 0], rank, 1, 0)[0]
    own_tokens = lax.dynamic_index_in_dim(tokens, rank, 0, keepdims=False)
    own_cotangent = lax.dynamic_index_in_dim(cotangent, rank, 0, keepdims=False)

    full_qkv, other_tokens = first_spread(by_slots(by_pairs(narrow(w_qkv))), tokens)
    token_low = in_order(rank, own_tokens, other_tokens)
    token_rows = token_low.astype(jnp.float32)
    normed_one = narrow(layer_norm(token_rows, vectors[0], vectors[1]))
    shifts = by_pairs(jnp.stack([vectors[2], jnp.zeros((D,), jnp.float32), vectors[3]])[:, None])
    up_slots = by_slots(narrow(w_up))
    down_slots = by_slots(narrow(w_down).T)
    in_turn = jnp.stack([up_slots, down_slots], axis=1).reshape(2 * up_slots.shape[0], *up_slots.shape[1:])
    later_slots = jnp.concatenate([narrow(w_out).T[None], in_turn[: 2 * EARLY]])
    packed, context, exps, stats, normed_t, wholes, other_cotangent = attend_spread(
        starts, slopes, normed_one, full_qkv, shifts, later_slots, cotangent
    )
    full_out, full_up, full_down = wholes
    cotangent_low = in_order(rank, own_cotangent, other_cotangent)

    middle = token_rows + contract(context, full_out, 1, 1) + vectors[4]
    normed_two = narrow(layer_norm(middle, vectors[5], vectors[6]))
    block_rows, grad_normed_two, grad_up, grad_down, up_bias, early_sums = mlp_both(
        normed_two,
        cotangent_low,
        middle + vectors[11],
        vectors[7:11].reshape(1, FF),
        full_up,
        full_down,
        in_turn[2 * EARLY :],
    )
    output_pair = swap_halves(block_rows, rank)
    grad_middle, grad_context, grad_out, middle_sums = middle_backward(
        middle, grad_normed_two, cotangent_low, context, vectors[5:6], full_out
    )
    sums, grad_normed_one, packed_grads = attend_sum(
        packed, context, grad_context, stats, full_qkv, normed_t, exps, grad_up, grad_down, grad_out
    )
    grad_token_low, token_sums = token_backward(token_low, grad_normed_one, grad_middle, vectors[0:1])
    token_pair = swap_halves(grad_token_low, rank).astype(jnp.float32)

    packed_sums = from_pairs(packed_grads)[:, 0]
    vector_total = jnp.concatenate(
        [
            token_sums[0:2],
            packed_sums[0:1],
            packed_sums[2:3],
            middle_sums[2:3],
            middle_sums[0:2],
            up_bias.reshape(4, D),
            middle_sums[3:4],
        ]
    )
    shards = (
        from_pairs(from_slots(sums[5:8])),
        sums[4].T,
        from_slots(jnp.concatenate([early_sums[0::2], sums[0:4:2]])),
        from_slots(jnp.concatenate([early_sums[1::2], sums[1:4:2]])).T,
    )
    outputs = muon_step(shards, vector_total, w_qkv, w_out, w_up, w_down, vectors, m_qkv, m_out, m_up, m_down, m_vec)
    return (output_pair, token_pair) + outputs


def solution(mesh):
    in_specs = (
        P(None, ("dp", "tensor"), None),
        P(None, ("dp", "tensor"), None),
        P(None, "dp", None),
        P(None, "dp", "tensor"),
        P("tensor", "dp"),
        P("dp", "tensor"),
        P("tensor", "dp"),
        P(),
        P(None, "dp", "tensor"),
        P("tensor", "dp"),
        P("dp", "tensor"),
        P("tensor", "dp"),
        P(),
    )
    out_specs = (
        P(None, ("dp", "tensor"), None),
        P(None, ("dp", "tensor"), None),
        P(None, "dp", "tensor"),
        P("tensor", "dp"),
        P("dp", "tensor"),
        P("tensor", "dp"),
        P(),
        P(None, "dp", "tensor"),
        P("tensor", "dp"),
        P("dp", "tensor"),
        P("tensor", "dp"),
        P(),
        P(None, "dp", "tensor"),
        P("tensor", "dp"),
        P("dp", "tensor"),
        P("tensor", "dp"),
        P(),
    )
    groups_fit = mesh.shape["tensor"] == MB and mesh.shape["dp"] == 16

    def pick(*arrays):
        if groups_fit and arrays[2].shape[1] == 1:
            return sequence_step(*arrays)
        return on_device(*arrays)

    return jax.shard_map(
        pick, mesh=mesh, in_specs=in_specs, out_specs=out_specs, check_vma=False
    )
```

```python
import math

import jax
import jax.numpy as jnp
from jax import lax
from jax.experimental import pallas as pl
from jax.experimental.pallas import tpu as pltpu
from jax.sharding import PartitionSpec as P

D = 1024
H = 16
HD = 64
FF = 4096
LEN = 1024
PIECE = 256
NPIECE = 2
MB = 2
NS_ITERS = 3


NORM_EPSILON = 1e-05
SQUARE_EPSILON = 1e-06
MASKED_SCORE = -1e30
SCHULZ_FIRST = 3.4445
SCHULZ_SECOND = -4.775
SCHULZ_THIRD = 2.0315
MOMENTUM_DECAY = 0.5
MATRIX_RATE = 0.5
VECTOR_RATE = 0.05


def layer_norm(inputs, gain_row, shift_row):
    average = jnp.mean(inputs, axis=-1, keepdims=True)
    centered = inputs - average
    variance = jnp.mean(centered * centered, axis=-1, keepdims=True)
    return centered * lax.rsqrt(variance + NORM_EPSILON) * gain_row + shift_row


def gelu_tanh(inputs):
    return jax.nn.gelu(inputs, approximate=True)


def score_layout(starts, slopes):
    positions = jnp.arange(LEN, dtype=jnp.int32)
    inside = (positions[None, :] >= starts[:, None]) & (
        positions[None, :] < starts[:, None] + PIECE
    )
    labels = jnp.arange(1, NPIECE + 1, dtype=jnp.int32)
    piece_label = jnp.sum(jnp.where(inside, labels[:, None], 0), axis=0)
    same_piece = (piece_label[:, None] == piece_label[None, :]) & (piece_label[:, None] > 0)
    visible = (positions[None, :] <= positions[:, None]) | same_piece
    distance = jnp.abs(positions[:, None] - positions[None, :]).astype(jnp.float32)
    penalty = -slopes[:, None, None] * distance[None, :, :]
    return (visible, penalty)


def head_scores(query_heads, key_heads, starts, slopes):
    visible, penalty = score_layout(starts, slopes)
    raw_scores = jnp.einsum(
        "qhd,khd->hqk", query_heads, key_heads, preferred_element_type=jnp.float32
    )
    scores = raw_scores * (1.0 / math.sqrt(HD)) + penalty
    return jnp.where(visible[None, :, :], scores, MASKED_SCORE)


def attend_forward(element, slopes):
    query_seq, key_seq, value_seq, starts = element
    heads_here = slopes.shape[0]
    query_heads = query_seq.reshape(LEN, heads_here, HD)
    key_heads = key_seq.reshape(LEN, heads_here, HD)
    value_heads = value_seq.reshape(LEN, heads_here, HD)
    scores = head_scores(query_heads, key_heads, starts, slopes)
    maximum = jnp.max(scores, axis=-1, keepdims=True)
    weights_raw = jnp.exp(scores - maximum)
    denominator = jnp.sum(weights_raw, axis=-1, keepdims=True)
    probabilities = weights_raw / denominator
    context = jnp.einsum(
        "hqk,khd->qhd",
        probabilities.astype(jnp.bfloat16),
        value_heads,
        preferred_element_type=jnp.float32,
    )
    logsum = (maximum + jnp.log(denominator))[..., 0]
    return (context.reshape(LEN, heads_here * HD), logsum)


def attend_backward(element, slopes):
    query_seq, key_seq, value_seq, context_grad, logsum, starts = element
    heads_here = slopes.shape[0]
    query_heads = query_seq.reshape(LEN, heads_here, HD)
    key_heads = key_seq.reshape(LEN, heads_here, HD)
    value_heads = value_seq.reshape(LEN, heads_here, HD)
    grad_heads = context_grad.reshape(LEN, heads_here, HD)
    scores = head_scores(query_heads, key_heads, starts, slopes)
    probabilities = jnp.exp(scores - logsum[..., None])
    grad_probs = jnp.einsum(
        "qhd,khd->hqk", grad_heads, value_heads, preferred_element_type=jnp.float32
    )
    inner_sum = jnp.sum(probabilities * grad_probs, axis=-1, keepdims=True)
    grad_scores = (probabilities * (grad_probs - inner_sum)).astype(jnp.bfloat16)
    scale_factor = 1.0 / math.sqrt(HD)
    grad_query = (
        jnp.einsum("hqk,khd->qhd", grad_scores, key_heads, preferred_element_type=jnp.float32)
        * scale_factor
    )
    grad_key = (
        jnp.einsum("hqk,qhd->khd", grad_scores, query_heads, preferred_element_type=jnp.float32)
        * scale_factor
    )
    grad_value = jnp.einsum(
        "hqk,qhd->khd",
        probabilities.astype(jnp.bfloat16),
        grad_heads,
        preferred_element_type=jnp.float32,
    )
    width_here = heads_here * HD
    return (
        grad_query.astype(jnp.bfloat16).reshape(LEN, width_here),
        grad_key.astype(jnp.bfloat16).reshape(LEN, width_here),
        grad_value.astype(jnp.bfloat16).reshape(LEN, width_here),
    )


def placed(values, offset, length):
    return lax.dynamic_update_slice_in_dim(jnp.zeros((length,), jnp.float32), values, offset, 0)


def accumulate(totals, addend):
    if totals is None:
        return addend
    return tuple((former + latter for former, latter in zip(totals, addend)))


def gram_term(narrow_rows, wide_rows):
    part_narrow = jnp.einsum(
        "mrc,mrd->cmd", narrow_rows, narrow_rows, preferred_element_type=jnp.float32
    )
    part_wide = jnp.einsum("mrc,mrd->cmd", wide_rows, wide_rows, preferred_element_type=jnp.float32)
    return jnp.concatenate([part_narrow, part_wide], axis=1)


def schulz_step(state, gram_matrix):
    turned = jnp.einsum("mrc,cmd->mrd", state, gram_matrix, preferred_element_type=jnp.float32)
    mixed = (SCHULZ_SECOND * state.astype(jnp.float32) + SCHULZ_THIRD * turned).astype(jnp.bfloat16)
    return (
        SCHULZ_FIRST * state.astype(jnp.float32)
        + jnp.einsum("mrc,cmd->mrd", mixed, gram_matrix, preferred_element_type=jnp.float32)
    ).astype(jnp.bfloat16)


def slice_term(source, weights, pattern):
    return jnp.einsum(pattern, source, weights, preferred_element_type=jnp.float32)


def on_device(
    tokens,
    cotangent,
    piece_starts,
    w_qkv,
    w_out,
    w_up,
    w_down,
    vectors,
    m_qkv,
    m_out,
    m_up,
    m_down,
    m_vec,
):
    tensor_count = lax.axis_size("tensor")
    tensor_rank = lax.axis_index("tensor")
    shard_rank = lax.axis_index("dp")
    heads_here = H // tensor_count
    width_here = heads_here * HD
    hidden_here = FF // tensor_count
    rows_here = tokens.shape[1]
    group_rows = rows_here * tensor_count
    seqs_here = piece_starts.shape[1]
    shard_rows = w_qkv.shape[1]
    head_ids = tensor_rank * heads_here + jnp.arange(heads_here, dtype=jnp.int32) + 1
    slopes = jnp.exp2(-8.0 * head_ids.astype(jnp.float32) / H)
    query_shift = lax.dynamic_slice_in_dim(vectors[2], tensor_rank * width_here, width_here, 0)
    value_shift = lax.dynamic_slice_in_dim(vectors[3], tensor_rank * width_here, width_here, 0)
    up_shift = lax.dynamic_slice_in_dim(
        vectors[7:11].reshape(FF), tensor_rank * hidden_here, hidden_here, 0
    )
    low_qkv = w_qkv.astype(jnp.bfloat16)
    low_out = w_out.astype(jnp.bfloat16)
    low_up = w_up.astype(jnp.bfloat16)
    low_down = w_down.astype(jnp.bfloat16)
    outputs_list = []
    input_grads = []
    vector_total = jnp.zeros((12, D), jnp.float32)
    grad_total = None

    def forward_one(element):
        return attend_forward(element, slopes)

    def backward_one(element):
        return attend_backward(element, slopes)

    for batch_index in range(MB):
        full_qkv, full_out, full_up, full_down = (
            lax.all_gather(low_qkv, "dp", axis=1, tiled=True),
            lax.all_gather(low_out, "dp", axis=1, tiled=True),
            lax.all_gather(low_up, "dp", axis=0, tiled=True),
            lax.all_gather(low_down, "dp", axis=1, tiled=True),
        )
        token_rows = tokens[batch_index].astype(jnp.float32)
        cotangent_rows = cotangent[batch_index]
        normed_one = layer_norm(token_rows, vectors[0], vectors[1])
        normed_all, cotangent_all = (
            lax.all_gather(normed_one.astype(jnp.bfloat16), "tensor", axis=0, tiled=True),
            lax.all_gather(cotangent_rows, "tensor", axis=0, tiled=True),
        )
        projected = jnp.einsum(
            "td,cde->cte", normed_all, full_qkv, preferred_element_type=jnp.float32
        )
        query_low = (projected[0] + query_shift).astype(jnp.bfloat16)
        key_low = projected[1].astype(jnp.bfloat16)
        value_low = (projected[2] + value_shift).astype(jnp.bfloat16)
        query_seqs = query_low.reshape(seqs_here, LEN, width_here)
        key_seqs = key_low.reshape(seqs_here, LEN, width_here)
        value_seqs = value_low.reshape(seqs_here, LEN, width_here)
        starts_here = piece_starts[batch_index]
        context_seq, logsum = lax.map(forward_one, (query_seqs, key_seqs, value_seqs, starts_here))
        context_low = context_seq.reshape(group_rows, width_here).astype(jnp.bfloat16)
        attended = lax.psum_scatter(
            slice_term(context_low, full_out, "tc,cd->td").astype(jnp.bfloat16),
            "tensor",
            scatter_dimension=0,
            tiled=True,
        ).astype(jnp.float32)
        middle = token_rows + attended + vectors[4]
        normed_two = layer_norm(middle, vectors[5], vectors[6])
        normed_two_all = lax.all_gather(
            normed_two.astype(jnp.bfloat16), "tensor", axis=0, tiled=True
        )
        before = jnp.dot(normed_two_all, full_up, preferred_element_type=jnp.float32) + up_shift
        activated = gelu_tanh(before).astype(jnp.bfloat16)
        expanded = lax.psum_scatter(
            slice_term(activated, full_down, "tf,fd->td").astype(jnp.bfloat16),
            "tensor",
            scatter_dimension=0,
            tiled=True,
        ).astype(jnp.float32)
        outputs_list.append((middle + expanded + vectors[11]).astype(jnp.bfloat16))
        grad_down = jnp.einsum(
            "tf,td->fd", activated, cotangent_all, preferred_element_type=jnp.float32
        )
        grad_activated = jnp.einsum(
            "td,fd->tf", cotangent_all, full_down, preferred_element_type=jnp.float32
        )
        gelu_pull = jax.vjp(gelu_tanh, before)[1]
        grad_before = gelu_pull(grad_activated)[0].astype(jnp.bfloat16)
        grad_up = jnp.einsum(
            "td,tf->df", normed_two_all, grad_before, preferred_element_type=jnp.float32
        )
        grad_normed_two = lax.psum_scatter(
            slice_term(grad_before, full_up, "tf,df->td").astype(jnp.bfloat16),
            "tensor",
            scatter_dimension=0,
            tiled=True,
        ).astype(jnp.float32)
        second_pull = jax.vjp(layer_norm, middle, vectors[5], vectors[6])[1]
        middle_from_norm, gain_two_grad, shift_two_grad = second_pull(grad_normed_two)
        grad_middle = cotangent_rows.astype(jnp.float32) + middle_from_norm
        grad_middle_all = lax.all_gather(
            grad_middle.astype(jnp.bfloat16), "tensor", axis=0, tiled=True
        )
        grad_out = jnp.einsum(
            "tc,td->cd", context_low, grad_middle_all, preferred_element_type=jnp.float32
        )
        grad_context = jnp.einsum(
            "td,cd->tc", grad_middle_all, full_out, preferred_element_type=jnp.float32
        ).astype(jnp.bfloat16)
        grad_query, grad_key, grad_value = lax.map(
            backward_one,
            (
                query_seqs,
                key_seqs,
                value_seqs,
                grad_context.reshape(seqs_here, LEN, width_here),
                logsum,
                starts_here,
            ),
        )
        grad_stack = jnp.stack(
            [
                grad_query.reshape(group_rows, width_here),
                grad_key.reshape(group_rows, width_here),
                grad_value.reshape(group_rows, width_here),
            ]
        )
        grad_qkv = jnp.einsum(
            "td,cte->cde", normed_all, grad_stack, preferred_element_type=jnp.float32
        )
        grad_normed_one = lax.psum_scatter(
            slice_term(grad_stack, full_qkv, "cte,cde->td").astype(jnp.bfloat16),
            "tensor",
            scatter_dimension=0,
            tiled=True,
        ).astype(jnp.float32)
        first_pull = jax.vjp(layer_norm, token_rows, vectors[0], vectors[1])[1]
        token_from_norm, gain_one_grad, shift_one_grad = first_pull(grad_normed_one)
        input_grads.append(grad_middle + token_from_norm)
        query_bias = jnp.sum(grad_stack[0], axis=0, dtype=jnp.float32)
        value_bias = jnp.sum(grad_stack[2], axis=0, dtype=jnp.float32)
        up_bias = jnp.sum(grad_before, axis=0, dtype=jnp.float32)
        head_rows = jnp.stack(
            [
                gain_one_grad,
                shift_one_grad,
                placed(query_bias, tensor_rank * width_here, D),
                placed(value_bias, tensor_rank * width_here, D),
                jnp.sum(grad_middle, axis=0),
                gain_two_grad,
                shift_two_grad,
            ]
        )
        up_rows = placed(up_bias, tensor_rank * hidden_here, FF).reshape(4, D)
        tail_row = jnp.sum(cotangent_rows, axis=0, dtype=jnp.float32)[None, :]
        vector_total = vector_total + jnp.concatenate([head_rows, up_rows, tail_row], axis=0)
        shard_grads = (
            lax.psum_scatter(
                grad_qkv.astype(jnp.bfloat16), "dp", scatter_dimension=1, tiled=True
            ).astype(jnp.float32),
            lax.psum_scatter(
                grad_out.astype(jnp.bfloat16), "dp", scatter_dimension=1, tiled=True
            ).astype(jnp.float32),
            lax.psum_scatter(
                grad_up.astype(jnp.bfloat16), "dp", scatter_dimension=0, tiled=True
            ).astype(jnp.float32),
            lax.psum_scatter(
                grad_down.astype(jnp.bfloat16), "dp", scatter_dimension=1, tiled=True
            ).astype(jnp.float32),
        )
        grad_total = accumulate(grad_total, shard_grads)
    grad_qkv_shard, grad_out_shard, grad_up_shard, grad_down_shard = grad_total
    moment_qkv = MOMENTUM_DECAY * m_qkv + grad_qkv_shard
    moment_out = MOMENTUM_DECAY * m_out + grad_out_shard
    moment_up = MOMENTUM_DECAY * m_up + grad_up_shard
    moment_down = MOMENTUM_DECAY * m_down + grad_down_shard
    squares = jnp.concatenate(
        [
            jnp.sum(moment_qkv * moment_qkv, axis=(1, 2)),
            jnp.stack(
                [
                    jnp.sum(moment_out * moment_out),
                    jnp.sum(moment_up * moment_up),
                    jnp.sum(moment_down * moment_down),
                ]
            ),
        ]
    )
    vector_grad, square_total = lax.psum((vector_total, squares), ("dp", "tensor"))
    factors = lax.rsqrt(square_total + SQUARE_EPSILON)
    scaled_qkv = (moment_qkv * factors[0:3][:, None, None]).astype(jnp.bfloat16)
    scaled_out = (moment_out * factors[3]).astype(jnp.bfloat16)
    scaled_up = (moment_up * factors[4]).astype(jnp.bfloat16)
    scaled_down = (moment_down * factors[5]).astype(jnp.bfloat16)
    gathered_qkv, gathered_out, gathered_up, gathered_down = (
        lax.all_gather(scaled_qkv, "dp", axis=1, tiled=True),
        lax.all_gather(scaled_out, "dp", axis=1, tiled=True),
        lax.all_gather(scaled_up, "dp", axis=0, tiled=True),
        lax.all_gather(scaled_down, "dp", axis=1, tiled=True),
    )
    offset = shard_rank * shard_rows
    narrow_rows = jnp.concatenate([jnp.swapaxes(gathered_qkv, 1, 2), gathered_out[None]], axis=0)
    wide_rows = jnp.stack([gathered_up.T, gathered_down])
    for sweep_index in range(NS_ITERS):
        gram_share = lax.psum_scatter(
            gram_term(narrow_rows, wide_rows).astype(jnp.bfloat16),
            "tensor",
            scatter_dimension=0,
            tiled=True,
        )
        gram_matrix = lax.all_gather(gram_share, "tensor", axis=0, tiled=True)
        narrow_rows = schulz_step(narrow_rows, gram_matrix[:, 0:4])
        wide_rows = schulz_step(wide_rows, gram_matrix[:, 4:6])
    final_narrow = narrow_rows.astype(jnp.float32)
    final_wide = wide_rows.astype(jnp.float32)
    update_qkv = lax.dynamic_slice_in_dim(
        jnp.swapaxes(final_narrow[0:3], 1, 2), offset, shard_rows, 1
    )
    update_out = lax.dynamic_slice_in_dim(final_narrow[3], offset, shard_rows, 1)
    update_up = lax.dynamic_slice_in_dim(final_wide[0].T, offset, shard_rows, 0)
    update_down = lax.dynamic_slice_in_dim(final_wide[1], offset, shard_rows, 1)
    wide_factor = math.sqrt(FF / D)
    new_qkv = w_qkv - MATRIX_RATE * update_qkv
    new_out = w_out - MATRIX_RATE * update_out
    new_up = w_up - MATRIX_RATE * wide_factor * update_up
    new_down = w_down - MATRIX_RATE * wide_factor * update_down
    moment_vec = MOMENTUM_DECAY * m_vec + vector_grad
    new_vec = vectors - VECTOR_RATE * moment_vec * lax.rsqrt(
        jnp.mean(moment_vec * moment_vec, axis=1, keepdims=True) + SQUARE_EPSILON
    )
    return (
        jnp.stack(outputs_list),
        jnp.stack(input_grads),
        grad_qkv_shard,
        grad_out_shard,
        grad_up_shard,
        grad_down_shard,
        vector_grad,
        moment_qkv,
        moment_out,
        moment_up,
        moment_down,
        moment_vec,
        new_qkv,
        new_out,
        new_up,
        new_down,
        new_vec,
    )


QB = 256
PAIR = 2 * HD
PAIRS = D // PAIR
VMEM_LIMIT = 56 * 1024 * 1024


def layout_grid(starts_ref, dist_ref):
    key_pos = lax.broadcasted_iota(jnp.int32, (LEN, LEN), 0)
    query_pos = lax.broadcasted_iota(jnp.int32, (LEN, LEN), 1)
    gap = query_pos - key_pos
    visible = gap >= 0
    for piece in range(NPIECE):
        start = starts_ref[piece]
        inside_key = (key_pos >= start) & (key_pos < start + PIECE)
        inside_query = (query_pos >= start) & (query_pos < start + PIECE)
        visible = visible | (inside_key & inside_query)
    dist_ref[...] = jnp.where(visible, jnp.abs(gap).astype(jnp.float32), -MASKED_SCORE)


def only_rows(pair, half):
    rows = lax.broadcasted_iota(jnp.int32, pair.shape, 0)
    return jnp.where((rows >= HD) if half else (rows < HD), pair, jnp.zeros_like(pair))


def only_cols(pair, half):
    cols = lax.broadcasted_iota(jnp.int32, pair.shape, 1)
    return jnp.where((cols >= HD) if half else (cols < HD), pair, jnp.zeros_like(pair))


def mul(left, right):
    return jnp.dot(left, right, preferred_element_type=jnp.float32)


def attend_pair(pair, slopes_ref, packed, dist_ref, ctx_ref, exps_ref, stat_ref, ctx_t, between):
    keys = packed[:, PAIR : 2 * PAIR]
    values_t = packed[:, 2 * PAIR :].T
    queries_t = (packed[:, :PAIR] * (1.0 / math.sqrt(HD))).T
    for half in (0, 1):
        slope = slopes_ref[2 * pair + half]
        queries = only_rows(queries_t, half)
        heads = slice(half * HD, half * HD + HD)
        for block in range(LEN // QB):
            span = min(LEN, QB * block + QB + PIECE)
            cols = slice(block * QB, block * QB + QB)
            scores = mul(keys[:span], queries[:, cols]) - slope * dist_ref[:span, cols]
            top = jnp.max(scores, axis=0, keepdims=True)
            raw = jnp.exp(scores - top)
            inverse = 1.0 / jnp.sum(raw, axis=0, keepdims=True)
            low = raw.astype(jnp.bfloat16)
            exps_ref[half, :span, cols] = low
            ctx_t[heads, cols] = mul(values_t[heads, :span], low) * inverse
            stat_ref[0, half : half + 1, cols] = inverse
        if half == 0:
            between()
    ctx_ref[...] = ctx_t[...].T.astype(jnp.bfloat16)


PACKED_COLS = pl.BlockSpec((LEN, 3 * PAIR), lambda p: (0, p))
PAIR_COLS = pl.BlockSpec((LEN, PAIR), lambda p: (0, p))
PAIR_GRID = pl.BlockSpec((2, LEN, LEN), lambda p: (p, 0, 0))
PAIR_STAT = pl.BlockSpec((1, 2, LEN), lambda p: (p, 0, 0))
SCALARS = pl.BlockSpec(memory_space=pltpu.SMEM)


SLOTS = 12
SLOT = 512
HALF_SLOT = SLOT // 2
TILE = 256
GRAM_TILES = 5
MESH_IDS = pl.DeviceIdType.MESH


def handler_of(slot):
    wide = slot - 4
    square = slot < 4
    dp_index = jnp.where(square, jnp.where(slot < 2, 2, 12), 4 + 6 * (wide // 4) + wide % 2)
    tensor_index = jnp.where(square, slot % 2, (wide // 2) % 2)
    return dp_index, tensor_index


def muon_kernel(
    moments_ref,
    vec_ref,
    block_ref,
    token_ref,
    updates_ref,
    vec_out_ref,
    block_pair_ref,
    token_pair_ref,
    pieces,
    turned,
    vec_pieces,
    vec_sum,
    gram,
    gram_low,
    poly_low,
    half_low,
    chain_low,
    chain_next,
    out_half,
    in_half,
    local_sem,
    send_sem,
    recv_sem,
    half_send,
    half_recv,
    swap_sem,
):
    groups = lax.axis_size("dp")
    parts = lax.axis_size("tensor")
    count = groups * parts
    dp_me = lax.axis_index("dp")
    t_me = lax.axis_index("tensor")
    me = t_me * groups + dp_me
    is_square = (dp_me == 2) | (dp_me == 12)
    is_up = (dp_me == 4) | (dp_me == 5)
    is_down = (dp_me == 10) | (dp_me == 11)
    is_wide = is_up | is_down
    is_handler = is_square | is_wide
    wide_slot = jnp.where(is_up, 4 + (dp_me - 4), 8 + (dp_me - 10)) + 2 * t_me
    slot_me = jnp.where(is_square, t_me + jnp.where(dp_me == 12, 2, 0), wide_slot)
    slot_me = jnp.where(is_handler, slot_me, 0)

    barrier = pltpu.get_barrier_semaphore()

    def greet(step, carry):
        other = lax.rem(me + step, count)
        pl.semaphore_signal(
            barrier, inc=1, device_id=(lax.rem(other, groups), other // groups), device_id_type=MESH_IDS
        )
        return carry

    lax.fori_loop(1, count, greet, 0)
    pl.semaphore_wait(barrier, count - 1)

    def give(step, carry):
        slot = lax.rem(me + step, SLOTS)
        dp_to, t_to = handler_of(slot)
        away = (dp_to != dp_me) | (t_to != t_me)

        @pl.when(away)
        def _():
            pltpu.make_async_remote_copy(
                src_ref=vec_ref.at[slot],
                dst_ref=vec_pieces.at[me],
                send_sem=send_sem.at[1],
                recv_sem=recv_sem.at[1],
                device_id=(dp_to, t_to),
                device_id_type=MESH_IDS,
            ).start()
            pltpu.make_async_remote_copy(
                src_ref=moments_ref.at[slot],
                dst_ref=pieces.at[me],
                send_sem=send_sem.at[0],
                recv_sem=recv_sem.at[0],
                device_id=(dp_to, t_to),
                device_id_type=MESH_IDS,
            ).start()

        return carry

    lax.fori_loop(0, SLOTS, give, 0)

    rows = block_ref.shape[0] // 2
    kept_rows = pl.ds(pl.multiple_of(t_me * rows, rows), rows)
    sent_rows = pl.ds(pl.multiple_of((1 - t_me) * rows, rows), rows)
    kept = []
    swaps = []
    for index, (whole, pair) in enumerate(((block_ref, block_pair_ref), (token_ref, token_pair_ref))):
        kept.append(pltpu.make_async_copy(whole.at[kept_rows], pair.at[t_me], swap_sem.at[2, index]))
        swaps.append(
            pltpu.make_async_remote_copy(
                src_ref=whole.at[sent_rows],
                dst_ref=pair.at[t_me],
                send_sem=swap_sem.at[0, index],
                recv_sem=swap_sem.at[1, index],
                device_id=(dp_me, 1 - t_me),
                device_id_type=MESH_IDS,
            )
        )

    @pl.when(jnp.logical_not(is_wide))
    def _():
        for copy in kept + swaps:
            copy.start()

    def give_back(source, sem, target):
        def one(step, carry):
            other = lax.rem(me + step, count)
            pltpu.make_async_remote_copy(
                src_ref=source.at[other] if source is turned else source,
                dst_ref=target.at[slot_me],
                send_sem=send_sem.at[sem],
                recv_sem=recv_sem.at[sem],
                device_id=(lax.rem(other, groups), other // groups),
                device_id_type=MESH_IDS,
            ).start()
            return carry

        lax.fori_loop(1, count, one, 0)

    @pl.when(is_handler)
    def _():
        own = [
            pltpu.make_async_copy(vec_ref.at[slot_me], vec_pieces.at[me], local_sem.at[0]),
            pltpu.make_async_copy(moments_ref.at[slot_me], pieces.at[me], local_sem.at[1]),
        ]
        for copy in own:
            copy.start()
        for copy in own:
            copy.wait()
        rest = pl.ds(0, count - 1)
        pltpu.make_async_copy(vec_pieces.at[rest], vec_pieces.at[rest], recv_sem.at[1]).wait()
        vec_sum[...] = jnp.sum(vec_pieces[...], axis=0)
        give_back(vec_sum, 2, vec_out_ref)
        own_vec = pltpu.make_async_copy(vec_sum, vec_out_ref.at[slot_me], local_sem.at[0])
        own_vec.start()
        own_vec.wait()
        pltpu.make_async_copy(pieces.at[rest], pieces.at[rest], recv_sem.at[0]).wait()

        rows_of = TILE // 64

        def gram_tile(tile, carry):
            rows = pl.ds(pl.multiple_of(tile * TILE, TILE), TILE)
            total = jnp.zeros((TILE, D), jnp.float32)
            for part in range(parts):
                left = pieces[pl.ds(part * groups + tile * rows_of, rows_of)].reshape(TILE, SLOT)
                right = pieces[part * groups : (part + 1) * groups].reshape(D, SLOT)
                total += lax.dot_general(
                    left, right, (((1,), (1,)), ((), ())), preferred_element_type=jnp.float32
                )
            gram[rows, :] = total
            return carry

        lax.fori_loop(0, D // TILE, gram_tile, 0)

        @pl.when(is_wide)
        def _():
            core = lax.rem(dp_me, 2)
            sibling = (dp_me + 1 - 2 * core, t_me)
            across = (dp_me, 1 - t_me)

            def tile_at(index, owner):
                if index == 4:
                    row, col = jnp.where(owner == 0, 3, 2), 3
                elif index == 3:
                    row, col = jnp.where(owner == 0, 0, 2), jnp.where(owner == 0, 3, 2)
                else:
                    row, col = owner, owner + index
                return (
                    pl.ds(pl.multiple_of(row * TILE, TILE), TILE),
                    pl.ds(pl.multiple_of(col * TILE, TILE), TILE),
                )

            def exchange(stage, index, place):
                return pltpu.make_async_remote_copy(
                    src_ref=out_half.at[stage, index],
                    dst_ref=in_half.at[stage, index],
                    send_sem=half_send.at[stage, index],
                    recv_sem=half_recv.at[stage, index],
                    device_id=place,
                    device_id_type=MESH_IDS,
                )

            for index in range(GRAM_TILES):
                out_half[0, index] = gram[tile_at(index, 1 - core)].astype(jnp.bfloat16)
                exchange(0, index, sibling).start()
            for index in range(GRAM_TILES):
                exchange(0, index, sibling).wait_recv()
                total = gram[tile_at(index, core)] + in_half[0, index].astype(jnp.float32)
                out_half[1, index] = total.astype(jnp.bfloat16)
                exchange(1, index, across).start()
            for index in range(GRAM_TILES):
                exchange(1, index, across).wait_recv()
                total = out_half[1, index].astype(jnp.float32) + in_half[1, index].astype(jnp.float32)
                out_half[2, index] = total.astype(jnp.bfloat16)
                exchange(2, index, sibling).start()
                rows, cols = tile_at(index, core)
                gram[cols, rows] = out_half[2, index].astype(jnp.float32).T
                gram[rows, cols] = out_half[2, index].astype(jnp.float32)
            for index in range(GRAM_TILES):
                exchange(2, index, sibling).wait_recv()
                rows, cols = tile_at(index, 1 - core)
                gram[cols, rows] = in_half[2, index].astype(jnp.float32).T
                gram[rows, cols] = in_half[2, index].astype(jnp.float32)
            for index in range(GRAM_TILES):
                exchange(0, index, sibling).wait_send()
                exchange(1, index, across).wait_send()
                exchange(2, index, sibling).wait_send()
            for copy in kept + swaps:
                copy.start()

        def trace_tile(tile, total):
            rows = pl.ds(pl.multiple_of(tile * TILE, TILE), TILE)
            row_ids = lax.broadcasted_iota(jnp.int32, (TILE, D), 0) + tile * TILE
            col_ids = lax.broadcasted_iota(jnp.int32, (TILE, D), 1)
            diagonal = jnp.where(row_ids == col_ids, gram[rows, :], 0.0)
            return total + jnp.sum(jnp.sum(diagonal, axis=0, keepdims=True), axis=1, keepdims=True)

        square_total = lax.fori_loop(0, D // TILE, trace_tile, jnp.zeros((1, 1), jnp.float32))
        factor = lax.rsqrt(square_total + SQUARE_EPSILON)
        gram_low[...] = (gram[...] * (factor * factor)).astype(jnp.bfloat16)

        first, second, third = SCHULZ_FIRST, SCHULZ_SECOND, SCHULZ_THIRD

        def tiles(body):
            def one(tile, carry):
                body(pl.ds(pl.multiple_of(tile * TILE, TILE), TILE))
                return carry

            lax.fori_loop(0, D // TILE, one, 0)

        chain = chain_low
        other = chain_next
        for sweep in range(NS_ITERS):
            target = chain if sweep == 0 else poly_low

            def poly(rows):
                square = mul(gram_low[rows, :], gram_low[...])
                grown = (second / first) * gram_low[rows, :].astype(jnp.float32) + (third / first) * square
                target[rows, :] = grown.astype(jnp.bfloat16)

            tiles(poly)
            if sweep > 0:

                def join(rows, chain=chain, other=other):
                    total = chain[rows, :].astype(jnp.float32) + poly_low[rows, :].astype(jnp.float32)
                    other[rows, :] = (total + mul(chain[rows, :], poly_low[...])).astype(jnp.bfloat16)

                tiles(join)
                chain, other = other, chain
            if sweep < NS_ITERS - 1:

                def half(rows):
                    grown = gram_low[rows, :].astype(jnp.float32) + mul(gram_low[rows, :], target[...])
                    half_low[rows, :] = grown.astype(jnp.bfloat16)

                def full(rows):
                    grown = half_low[rows, :].astype(jnp.float32) + mul(half_low[rows, :], target[...])
                    gram_low[rows, :] = (grown * (first * first)).astype(jnp.bfloat16)

                tiles(half)
                tiles(full)

        scale = factor * (first**NS_ITERS)

        def turn_tile(tile, carry):
            rows = pl.ds(pl.multiple_of(tile * TILE, TILE), TILE)
            for part in range(parts):
                at = pl.ds(part * groups + tile * rows_of, rows_of)
                whole = pieces[part * groups : (part + 1) * groups].reshape(D, SLOT)
                kept = pieces[at].reshape(TILE, SLOT).astype(jnp.float32)
                fresh = (kept + mul(chain[rows, :], whole)) * scale
                turned[at] = fresh.astype(jnp.bfloat16).reshape(rows_of, 64, SLOT)
            return carry

        lax.fori_loop(0, D // TILE, turn_tile, 0)
        give_back(turned, 3, updates_ref)
        own_turned = pltpu.make_async_copy(turned.at[me], updates_ref.at[slot_me], local_sem.at[1])
        own_turned.start()
        own_turned.wait()

    def finish(length):
        here = pl.ds(0, length)
        pltpu.make_async_copy(vec_ref.at[here], vec_ref.at[here], send_sem.at[1]).wait()
        pltpu.make_async_copy(moments_ref.at[here], moments_ref.at[here], send_sem.at[0]).wait()
        pltpu.make_async_copy(vec_out_ref.at[here], vec_out_ref.at[here], recv_sem.at[2]).wait()
        pltpu.make_async_copy(updates_ref.at[here], updates_ref.at[here], recv_sem.at[3]).wait()

    @pl.when(is_handler)
    def _():
        finish(SLOTS - 1)
        rest = pl.ds(0, count - 1)
        pltpu.make_async_copy(vec_pieces.at[rest], vec_pieces.at[rest], send_sem.at[2]).wait()
        pltpu.make_async_copy(turned.at[rest], turned.at[rest], send_sem.at[3]).wait()

    @pl.when(jnp.logical_not(is_handler))
    def _():
        finish(SLOTS)

    for copy in kept + swaps:
        copy.wait()


def muon_call(moments, vec_parts, block_rows, token_grads):
    count = lax.axis_size("dp") * lax.axis_size("tensor")
    rows = moments.shape[1]
    vmem = pl.BlockSpec(memory_space=pltpu.VMEM)
    anywhere = pl.BlockSpec(memory_space=pl.ANY)
    pair = jax.ShapeDtypeStruct((2, LEN // 2, D), jnp.bfloat16)
    low = pltpu.VMEM((D, D), jnp.bfloat16)
    return pl.pallas_call(
        muon_kernel,
        in_specs=[vmem, vmem, anywhere, anywhere],
        out_specs=[vmem, vmem, anywhere, anywhere],
        out_shape=[
            jax.ShapeDtypeStruct(moments.shape, jnp.bfloat16),
            jax.ShapeDtypeStruct(vec_parts.shape, jnp.float32),
            pair,
            pair,
        ],
        scratch_shapes=[
            pltpu.VMEM((count, rows, SLOT), jnp.bfloat16),
            pltpu.VMEM((count, rows, SLOT), jnp.bfloat16),
            pltpu.VMEM((count,) + vec_parts.shape[1:], jnp.float32),
            pltpu.VMEM(vec_parts.shape[1:], jnp.float32),
            pltpu.VMEM((D, D), jnp.float32),
            low,
            low,
            low,
            low,
            low,
            pltpu.VMEM((3, GRAM_TILES, TILE, TILE), jnp.bfloat16),
            pltpu.VMEM((3, GRAM_TILES, TILE, TILE), jnp.bfloat16),
            pltpu.SemaphoreType.DMA((2,)),
            pltpu.SemaphoreType.DMA((4,)),
            pltpu.SemaphoreType.DMA((4,)),
            pltpu.SemaphoreType.DMA((3, GRAM_TILES)),
            pltpu.SemaphoreType.DMA((3, GRAM_TILES)),
            pltpu.SemaphoreType.DMA((3, 2)),
        ],
        compiler_params=pltpu.CompilerParams(
            collective_id=1, has_side_effects=True, vmem_limit_bytes=VMEM_LIMIT
        ),
        cost_estimate=pl.CostEstimate(flops=12 * 2 * D**3, bytes_accessed=4 * 1024 * 1024, transcendentals=0),
    )(moments, vec_parts, block_rows, token_grads)


def neighbours():
    dp_me = lax.axis_index("dp")
    y = lax.axis_index("tensor")
    core = lax.rem(dp_me, 2)
    x = lax.rem(dp_me // 2, 2)
    z = dp_me // 4
    sibling = (dp_me + 1 - 2 * core, y)
    beside = (dp_me + 2 - 4 * x, y)
    across = (dp_me, 1 - y)
    stations = [(lax.rem(dp_me + 4 * hop, 16), y) for hop in (1, 2, 3)]
    return (z, x, core, y), sibling, beside, across, stations


def greet_neighbours(places):
    barrier = pltpu.get_barrier_semaphore()
    for place in places:
        pl.semaphore_signal(barrier, inc=1, device_id=place, device_id_type=MESH_IDS)
    pl.semaphore_wait(barrier, len(places))


SWAP_AT = 2
EARLY = 2
AHEAD = 2
SPREAD_LAG = 1


class Spread:
    def __init__(self, slots_ref, table, local_sem, send_sem, recv_sem):
        self.slots_ref, self.table = slots_ref, table
        self.local_sem, self.send_sem, self.recv_sem = local_sem, send_sem, recv_sem
        (self.z, self.x, self.core, self.y), self.sibling, self.beside, self.across, self.stations = neighbours()

    def remote(self, source, target, stage, slot, place):
        return pltpu.make_async_remote_copy(
            src_ref=source,
            dst_ref=target,
            send_sem=self.send_sem.at[stage, slot],
            recv_sem=self.recv_sem.at[stage, slot],
            device_id=place,
            device_id_type=MESH_IDS,
        )

    def own(self, slot):
        here = self.table[slot][0](self.y, 0, SLOT).at[self.z, self.x, self.core]
        return pltpu.make_async_copy(self.slots_ref.at[slot], here, self.local_sem.at[slot])

    def along_z(self, slot):
        here = self.table[slot][0](self.y, 0, SLOT).at[self.z, self.x, self.core]
        return [
            self.remote(self.slots_ref.at[slot], here, hop, slot, place)
            for hop, place in enumerate(self.stations)
        ]

    def second(self, slot):
        view, size = self.table[slot]
        copies = []
        if size:
            part = view(self.y, 0, size).at[:, self.x, self.core]
            copies.append(self.remote(part, part, 3, slot, self.beside))
        if size < SLOT:
            part = view(self.y, size, SLOT - size).at[:, self.x, self.core]
            copies.append(self.remote(part, part, 4, slot, self.across))
        return copies

    def third(self, slot):
        view, size = self.table[slot]
        copies = []
        if size:
            part = view(self.y, 0, size).at[:, :, self.core]
            copies.append(self.remote(part, part, 5, slot, self.across))
        if size < SLOT:
            for index in (0, 1):
                part = view(index, size, SLOT - size).at[:, self.x, self.core]
                copies.append(self.remote(part, part, 6 + index, slot, self.beside))
        return copies

    def fourth(self, slot):
        view, _ = self.table[slot]
        copies = []
        for index in (0, 1):
            part = view(index, 0, SLOT).at[:, :, self.core]
            copies.append(self.remote(part, part, 8 + index, slot, self.sibling))
        return copies

    def launch(self, slot):
        if slot < len(self.table):
            self.own(slot).start()
            for copy in self.along_z(slot):
                copy.start()

    def begin(self):
        for slot in range(AHEAD):
            self.launch(slot)

    def tick(self, index):
        count = len(self.table)
        self.launch(index + AHEAD)
        if index < count:
            self.own(index).wait()
            for copy in self.along_z(index):
                copy.wait_recv()
            for copy in self.second(index):
                copy.start()
        if 0 <= index - SPREAD_LAG < count:
            for copy in self.second(index - SPREAD_LAG):
                copy.wait_recv()
            for copy in self.third(index - SPREAD_LAG):
                copy.start()
        if 0 <= index - 2 * SPREAD_LAG < count:
            for copy in self.third(index - 2 * SPREAD_LAG):
                copy.wait_recv()
            for copy in self.fourth(index - 2 * SPREAD_LAG):
                copy.start()

    def ticks(self):
        return len(self.table) + 2 * SPREAD_LAG

    def arrived(self, slot):
        for copy in self.fourth(slot):
            copy.wait_recv()

    def sent(self):
        for slot in range(len(self.table)):
            for copy in self.along_z(slot) + self.second(slot) + self.third(slot) + self.fourth(slot):
                copy.wait_send()

    def finish(self):
        for slot in range(len(self.table)):
            self.arrived(slot)
        self.sent()


def column_view(ref, column, distance):
    def view(part, start, size):
        first = column + part * distance + start
        if not isinstance(part, int):
            first = pl.multiple_of(first, 128)
        return ref.at[:, :, :, :, pl.ds(first, size)]

    return view


def place_view(ref, place):
    def view(part, start, size):
        return ref.at[place + part, :, :, :, :, pl.ds(start, size)]

    return view


def spread_semaphores(count):
    return [
        pltpu.SemaphoreType.DMA((count,)),
        pltpu.SemaphoreType.DMA((10, count)),
        pltpu.SemaphoreType.DMA((10, count)),
    ]


def first_spread_kernel(slots_ref, tokens_ref, whole_ref, got_ref, local_sem, send_sem, recv_sem, token_sem):
    table = [(column_view(whole_ref, index * SLOT, 3 * SLOT), 0) for index in range(3)]
    spread = Spread(slots_ref, table, local_sem, send_sem, recv_sem)
    greet_neighbours([spread.sibling, spread.beside, spread.across] + spread.stations)
    swap = pltpu.make_async_remote_copy(
        src_ref=tokens_ref.at[1 - spread.y],
        dst_ref=got_ref,
        send_sem=token_sem.at[0],
        recv_sem=token_sem.at[1],
        device_id=spread.across,
        device_id_type=MESH_IDS,
    )
    spread.begin()
    for index in range(spread.ticks()):
        spread.tick(index)
        if index == SWAP_AT:
            swap.start()
    spread.finish()
    swap.wait()


def attend_spread_kernel(
    starts_ref,
    slopes_ref,
    normed_ref,
    weights_ref,
    shifts_ref,
    slots_ref,
    cotangent_ref,
    packed_ref,
    ctx_ref,
    exps_ref,
    stat_ref,
    normed_t_ref,
    out_ref,
    up_ref,
    down_ref,
    got_ref,
    dist_ref,
    ctx_t,
    local_sem,
    send_sem,
    recv_sem,
    token_sem,
):
    pair = pl.program_id(0)
    table = [(column_view(out_ref, 0, SLOT), HALF_SLOT)]
    for index in range(EARLY):
        over_x = HALF_SLOT if index == EARLY - 1 else 0
        table += [(column_view(ref, index * SLOT, EARLY * SLOT), over_x) for ref in (up_ref, down_ref)]
    spread = Spread(slots_ref, table, local_sem, send_sem, recv_sem)
    swap = pltpu.make_async_remote_copy(
        src_ref=cotangent_ref.at[1 - spread.y],
        dst_ref=got_ref,
        send_sem=token_sem.at[0],
        recv_sem=token_sem.at[1],
        device_id=spread.across,
        device_id_type=MESH_IDS,
    )

    @pl.when(pair == 0)
    def _():
        greet_neighbours([spread.sibling, spread.beside, spread.across] + spread.stations)
        spread.begin()
        normed_t_ref[...] = normed_ref[...].T
        layout_grid(starts_ref, dist_ref)

    def between():
        for index in range(spread.ticks()):

            @pl.when(pair == index)
            def _(index=index):
                spread.tick(index)
                if index == len(table) - 1:
                    swap.start()

    packed = (mul(normed_ref[...], weights_ref[...]) + shifts_ref[...]).astype(jnp.bfloat16)
    packed_ref[...] = packed
    attend_pair(pair, slopes_ref, packed, dist_ref, ctx_ref, exps_ref, stat_ref, ctx_t, between)

    @pl.when(pair == PAIRS - 1)
    def _():
        spread.finish()
        swap.wait()


def whole_shape(columns):
    return jax.ShapeDtypeStruct((4, 2, 2, 64, columns), jnp.bfloat16)


def first_spread(slots, tokens):
    anywhere = pl.BlockSpec(memory_space=pl.ANY)
    whole, got = pl.pallas_call(
        first_spread_kernel,
        in_specs=[anywhere] * 2,
        out_specs=[anywhere] * 2,
        out_shape=[whole_shape(3 * D), jax.ShapeDtypeStruct(tokens.shape[1:], tokens.dtype)],
        scratch_shapes=spread_semaphores(3) + [pltpu.SemaphoreType.DMA((2,))],
        compiler_params=pltpu.CompilerParams(collective_id=3, has_side_effects=True),
    )(slots, tokens)
    return whole.reshape(D, 3 * D), got


def attend_spread(starts, slopes, normed, weights, shifts, slots, cotangent):
    anywhere = pl.BlockSpec(memory_space=pl.ANY)
    packed, context, exps, stats, normed_t, out, up, down, got = pl.pallas_call(
        attend_spread_kernel,
        grid=(PAIRS,),
        in_specs=[
            SCALARS,
            SCALARS,
            pl.BlockSpec((LEN, D), lambda p: (0, 0)),
            PACKED_COLS,
            pl.BlockSpec((1, 3 * PAIR), lambda p: (0, p)),
            anywhere,
            anywhere,
        ],
        out_specs=[PACKED_COLS, PAIR_COLS, PAIR_GRID, PAIR_STAT, pl.BlockSpec((D, LEN), lambda p: (0, 0))]
        + [anywhere] * 4,
        out_shape=[
            jax.ShapeDtypeStruct((LEN, 3 * D), jnp.bfloat16),
            jax.ShapeDtypeStruct((LEN, D), jnp.bfloat16),
            jax.ShapeDtypeStruct((H, LEN, LEN), jnp.bfloat16),
            jax.ShapeDtypeStruct((PAIRS, 2, LEN), jnp.float32),
            jax.ShapeDtypeStruct((D, LEN), jnp.bfloat16),
            whole_shape(D),
            whole_shape(2 * EARLY * SLOT),
            whole_shape(2 * EARLY * SLOT),
            jax.ShapeDtypeStruct(cotangent.shape[1:], cotangent.dtype),
        ],
        scratch_shapes=[pltpu.VMEM((LEN, LEN), jnp.float32), pltpu.VMEM((PAIR, LEN), jnp.float32)]
        + spread_semaphores(1 + 2 * EARLY)
        + [pltpu.SemaphoreType.DMA((2,))],
        compiler_params=pltpu.CompilerParams(
            collective_id=4, has_side_effects=True, vmem_limit_bytes=VMEM_LIMIT
        ),
        cost_estimate=pl.CostEstimate(
            flops=16 * LEN * LEN * D, bytes_accessed=90 * 1024 * 1024, transcendentals=H * LEN * LEN
        ),
    )(starts, slopes, normed, weights, shifts, slots, cotangent)
    wholes = out.reshape(D, D), up.reshape(D, -1), down.reshape(D, -1)
    return packed, context, exps, stats, normed_t, wholes, got


class Summing:
    def __init__(self, sources, add_own, buffers, total_ref, sems, lag, ready=0, hold=0):
        self.sources, self.add_own, self.total_ref, self.lag = sources, add_own, total_ref, lag
        self.ready, self.hold = ready, hold
        self.first, self.second_y, self.second_x, self.third, self.fourth = buffers
        self.send_sem, self.recv_sem = sems
        (self.z, self.x, self.core, self.y), self.sibling, self.beside, self.across, self.stations = neighbours()
        self.low_cols = pl.ds(0, HALF_SLOT)
        self.high_cols = pl.ds(HALF_SLOT, HALF_SLOT)

    def count(self):
        return len(self.sources)

    def remote(self, source, target, stage, slot, place):
        return pltpu.make_async_remote_copy(
            src_ref=source,
            dst_ref=target,
            send_sem=self.send_sem.at[stage, slot],
            recv_sem=self.recv_sem.at[stage, slot],
            device_id=place,
            device_id_type=MESH_IDS,
        )

    def landed(self, ref, stage, slot):
        pltpu.make_async_copy(ref, ref, self.recv_sem.at[stage, slot]).wait()

    def send_first(self, slot):
        for part in (0, 1):
            source = self.sources[slot](part).at[:, :, 1 - self.core]
            self.remote(source, self.first.at[slot, part], 0, slot, self.sibling).start()

    def second_copies(self, slot):
        for_y = self.first.at[slot, 1 - self.y, :, :, :, self.low_cols]
        for_x = self.first.at[slot, :, :, 1 - self.x, :, self.high_cols]
        return (
            self.remote(for_y, self.second_y.at[slot], 1, slot, self.across),
            self.remote(for_x, self.second_x.at[slot], 2, slot, self.beside),
        )

    def third_copies(self, slot):
        for_x = self.second_y.at[slot, :, 1 - self.x]
        for_y = self.second_x.at[slot, 1 - self.y]
        return (
            self.remote(for_x, self.third.at[slot, :, :, self.low_cols], 3, slot, self.beside),
            self.remote(for_y, self.third.at[slot, :, :, self.high_cols], 4, slot, self.across),
        )

    def fourth_copies(self, slot):
        return tuple(
            self.remote(
                self.third.at[slot, lax.rem(self.z + hop, 4)], self.fourth.at[slot, hop - 1], 4 + hop, slot, place
            )
            for hop, place in zip((1, 2, 3), self.stations)
        )

    def stage_one(self, slot):
        self.landed(self.first.at[slot], 0, slot)
        self.add_own(slot)
        for copy in self.second_copies(slot):
            copy.start()

    def stage_two(self, slot):
        first, second_y, second_x = self.first, self.second_y, self.second_x
        self.landed(second_y.at[slot], 1, slot)
        second_y[slot] = second_y[slot] + first[slot, self.y, :, :, :, :HALF_SLOT]
        self.landed(second_x.at[slot], 2, slot)
        second_x[slot] = second_x[slot] + first[slot, :, :, self.x, :, HALF_SLOT:]
        for copy in self.third_copies(slot):
            copy.start()

    def stage_three(self, slot):
        third = self.third
        self.landed(third.at[slot, :, :, self.low_cols], 3, slot)
        self.landed(third.at[slot, :, :, self.high_cols], 4, slot)
        third[slot, :, :, :HALF_SLOT] = third[slot, :, :, :HALF_SLOT] + self.second_y[slot, :, self.x]
        third[slot, :, :, HALF_SLOT:] = third[slot, :, :, HALF_SLOT:] + self.second_x[slot, self.y]
        for copy in self.fourth_copies(slot):
            copy.start()

    def stage_four(self, slot):
        total = self.third[slot, self.z].astype(jnp.float32)
        for hop in (1, 2, 3):
            self.landed(self.fourth.at[slot, hop - 1], 4 + hop, slot)
            total = total + self.fourth[slot, hop - 1].astype(jnp.float32)
        self.total_ref[slot] = total

    def ticks(self):
        return self.count() + self.hold + 3 * self.lag

    def tick(self, index):
        for slot in range(self.count()):
            entry = slot + (self.hold if slot >= self.ready else 0)
            pl.when(index == entry)(lambda slot=slot: self.stage_one(slot))
        for number, stage in enumerate((self.stage_two, self.stage_three, self.stage_four)):
            entry = index - (number + 1) * self.lag
            slot = jnp.where(entry < self.ready, entry, entry - self.hold)
            late = (entry >= self.ready + self.hold) & (slot < self.count())
            early = (entry >= 0) & (entry < self.ready)
            pl.when(early | late)(lambda stage=stage, slot=slot: stage(slot))

    def fixed_tick(self, index):
        for number, stage in enumerate((self.stage_one, self.stage_two, self.stage_three, self.stage_four)):
            slot = index - number * self.lag
            if 0 <= slot < self.count():
                stage(slot)

    def sent(self):
        def one(slot, carry):
            pltpu.make_async_copy(self.first.at[slot], self.first.at[slot], self.send_sem.at[0, slot]).wait()
            for copy in self.second_copies(slot) + self.third_copies(slot) + self.fourth_copies(slot):
                copy.wait_send()
            return carry

        lax.fori_loop(0, self.count(), one, 0)


def summing_buffers(count):
    rows, low = 64, jnp.bfloat16
    return [
        pltpu.VMEM((count, 2, 4, 2, rows, SLOT), low),
        pltpu.VMEM((count, 4, 2, rows, HALF_SLOT), low),
        pltpu.VMEM((count, 2, 4, rows, HALF_SLOT), low),
        pltpu.VMEM((count, 4, rows, SLOT), low),
        pltpu.VMEM((count, 3, rows, SLOT), low),
        pltpu.SemaphoreType.DMA((8, count)),
        pltpu.SemaphoreType.DMA((8, count)),
    ]


HIDDEN = 512
CHUNK = 256
HIDDEN_STEPS = FF // HIDDEN
GELU_SLOPE = math.sqrt(2.0 / math.pi)
GELU_CUBE = 0.044715


def dot_last(left, right):
    return lax.dot_general(left, right, (((1,), (1,)), ((), ())), preferred_element_type=jnp.float32)


def gelu_both(rows):
    square = rows * rows
    bent = jnp.tanh(rows * (GELU_SLOPE + GELU_SLOPE * GELU_CUBE * square))
    half = 0.5 + 0.5 * bent
    slope = half + 0.5 * rows * (1.0 - bent * bent) * (GELU_SLOPE + 3.0 * GELU_SLOPE * GELU_CUBE * square)
    return rows * half, slope


def hidden_block(step):
    return (step % 2) * (HIDDEN_STEPS // 2) + step // 2


def mlp_kernel(
    rows_ref,
    cot_ref,
    base_ref,
    bias_ref,
    up_ref,
    down_ref,
    slots_ref,
    block_ref,
    grad_rows_ref,
    grad_up_ref,
    grad_down_ref,
    bias_sum_ref,
    total_ref,
    rows_t,
    cot_t,
    total,
    up_part,
    down_part,
    active,
    grad_before,
    grad_early,
    first,
    second_y,
    second_x,
    third,
    fourth,
    sum_send,
    sum_recv,
    local_sem,
    spread_send,
    spread_recv,
    load_sem,
):
    step = pl.program_id(0)
    early_steps = 2 * EARLY
    table = []
    for index in range(HIDDEN_STEPS // 2 - EARLY):
        table += [(place_view(ref, 2 + 2 * index), HALF_SLOT) for ref in (up_part, down_part)]
    spread = Spread(slots_ref, table, local_sem, spread_send, spread_recv)

    def early_block(slot, part):
        return grad_early.at[slot % 2, 2 * (slot // 2) + part]

    def add_own(slot):
        for part in (0, 1):
            first[slot, part] = first[slot, part] + grad_early[slot % 2, 2 * (slot // 2) + part, :, :, summing.core]

    sources = [lambda part, slot=slot: early_block(slot, part) for slot in range(2 * EARLY)]
    buffers = (first, second_y, second_x, third, fourth)
    summing = Summing(sources, add_own, buffers, total_ref, (sum_send, sum_recv), 1)

    def loads(at):
        column = lax.rem(at, 2) * EARLY + at // 2
        cols = pl.ds(pl.multiple_of(column * HIDDEN, HIDDEN), HIDDEN)
        place = lax.rem(at, 2)
        return (
            pltpu.make_async_copy(up_ref.at[:, :, :, :, cols], up_part.at[place], load_sem.at[0, place]),
            pltpu.make_async_copy(down_ref.at[:, :, :, :, cols], down_part.at[place], load_sem.at[1, place]),
        )

    @pl.when(step == 0)
    def _():
        for copy in loads(step):
            copy.start()
        greet_neighbours([spread.sibling, spread.beside, spread.across] + spread.stations)
        spread.begin()
        rows_t[...] = rows_ref[...].T
        cot_t[...] = cot_ref[...].T
        total[...] = base_ref[...]
        grad_rows_ref[...] = jnp.zeros_like(grad_rows_ref)

    @pl.when(step < early_steps)
    def _():
        for copy in loads(step):
            copy.wait()

    @pl.when(step < early_steps - 1)
    def _():
        for copy in loads(step + 1):
            copy.start()

    for index in range(HIDDEN_STEPS // 2 - EARLY):

        @pl.when(step == early_steps + 2 * index)
        def _(index=index):
            spread.arrived(2 * index)
            spread.arrived(2 * index + 1)

    place = jnp.where(step < early_steps, lax.rem(step, 2), step - early_steps + 2)
    up = up_part[place].reshape(D, HIDDEN)
    down = down_part[place].reshape(D, HIDDEN)
    bias = bias_ref[...]
    bias_sum = jnp.zeros((1, HIDDEN), jnp.float32)
    for index in range(LEN // CHUNK):
        here = slice(index * CHUNK, index * CHUNK + CHUNK)
        value, slope = gelu_both(mul(rows_ref[here], up) + bias)
        value = value.astype(jnp.bfloat16)
        grads = (slope * mul(cot_ref[here], down)).astype(jnp.bfloat16)
        active[here] = value
        grad_before[here] = grads
        bias_sum += jnp.sum(grads.astype(jnp.float32), axis=0, keepdims=True)
        total[here] += dot_last(value, down)
        grad_rows_ref[here] += dot_last(grads, up)
        if index == LEN // CHUNK // 2 - 1:
            for number in range(spread.ticks()):
                pl.when(step == number)(lambda number=number: spread.tick(number))
    bias_sum_ref[...] = bias_sum
    grad_down = mul(cot_t[...], active[...]).astype(jnp.bfloat16)
    grad_up = mul(rows_t[...], grad_before[...]).astype(jnp.bfloat16)

    @pl.when(step < early_steps)
    def _():
        grad_early[0, step] = grad_up.reshape(grad_early.shape[2:])
        grad_early[1, step] = grad_down.reshape(grad_early.shape[2:])

    @pl.when(step >= early_steps)
    def _():
        grad_up_ref[...] = grad_up
        grad_down_ref[...] = grad_down

    for number in range(HIDDEN_STEPS):

        @pl.when(step == number)
        def _(number=number):
            if number < early_steps and number % 2:
                summing.send_first(number - 1)
                summing.send_first(number)
            if number >= 2:
                summing.fixed_tick(number - 2)

    @pl.when(step == HIDDEN_STEPS - 1)
    def _():
        block_ref[...] = total[...].astype(jnp.bfloat16)
        for number in range(HIDDEN_STEPS - 2, summing.ticks()):
            summing.fixed_tick(number)
        summing.sent()
        spread.sent()


def late_block(step):
    late = HIDDEN_STEPS // 2 - EARLY
    return jnp.where(step < 2 * EARLY, 0, (step % 2) * late + step // 2 - EARLY)


def mlp_both(rows, cot, base, bias, up, down, slots):
    anywhere = pl.BlockSpec(memory_space=pl.ANY)
    once = pl.Buffered(1)
    whole = pl.BlockSpec((LEN, D), lambda s: (0, 0), pipeline_mode=once)
    hidden = pl.BlockSpec((D, HIDDEN), lambda s: (0, late_block(s)))
    hidden_row = pl.BlockSpec((1, HIDDEN), lambda s: (0, hidden_block(s)))
    low = jnp.bfloat16
    late = HIDDEN_STEPS // 2 - EARLY
    part = pltpu.VMEM((2 + 2 * late, 4, 2, 2, 64, HIDDEN), low)
    split = [weights.reshape(4, 2, 2, 64, -1) for weights in (up, down)]
    return pl.pallas_call(
        mlp_kernel,
        grid=(HIDDEN_STEPS,),
        in_specs=[whole, whole, whole, hidden_row, anywhere, anywhere, anywhere],
        out_specs=[
            whole,
            whole,
            hidden,
            hidden,
            hidden_row,
            pl.BlockSpec((2 * EARLY, 64, SLOT), lambda s: (0, 0, 0), pipeline_mode=once),
        ],
        out_shape=[
            jax.ShapeDtypeStruct((LEN, D), low),
            jax.ShapeDtypeStruct((LEN, D), jnp.float32),
            jax.ShapeDtypeStruct((D, 2 * late * HIDDEN), low),
            jax.ShapeDtypeStruct((D, 2 * late * HIDDEN), low),
            jax.ShapeDtypeStruct((1, FF), jnp.float32),
            jax.ShapeDtypeStruct((2 * EARLY, 64, SLOT), jnp.float32),
        ],
        scratch_shapes=[
            pltpu.VMEM((D, LEN), low),
            pltpu.VMEM((D, LEN), low),
            pltpu.VMEM((LEN, D), jnp.float32),
            part,
            part,
            pltpu.VMEM((LEN, HIDDEN), low),
            pltpu.VMEM((LEN, HIDDEN), low),
            pltpu.VMEM((2, 2 * EARLY, 4, 2, 2, 64, HIDDEN), low),
            *summing_buffers(2 * EARLY),
            *spread_semaphores(2 * late),
            pltpu.SemaphoreType.DMA((2, 2)),
        ],
        compiler_params=pltpu.CompilerParams(
            collective_id=5, has_side_effects=True, vmem_limit_bytes=62 * 1024 * 1024
        ),
        cost_estimate=pl.CostEstimate(
            flops=12 * LEN * D * FF, bytes_accessed=60 * 1024 * 1024, transcendentals=LEN * FF
        ),
    )(rows, cot, base, bias, *split, slots)


LAG = 2
READY = 5
LATE_SLOTS = 8
RING = 4


def block_view(ref, column):
    return ref.at[:, :, :, :, pl.ds(column, SLOT)]


def attend_bwd_half(half, scale, values, keys_t, parts, exps, sums):
    half_t, half_rows, half_queries, inner = parts
    dq_t, dk_sum, dv_sum = sums
    heads = slice(half * HD, half * HD + HD)
    for block in range(LEN // QB):
        span = min(LEN, QB * block + QB + PIECE)
        cols = slice(block * QB, block * QB + QB)
        weights = exps[:span, cols]
        grad_probs = mul(values[:span], half_t[:, cols])
        grad_scores = (weights.astype(jnp.float32) * (grad_probs - inner[:, cols])).astype(jnp.bfloat16)
        dv_sum[:span, :] += mul(weights, half_rows[cols])
        dk_sum[:span, :] += mul(grad_scores, half_queries[cols])
        dq_t[heads, cols] = mul(keys_t[heads, :span], grad_scores) * scale


def attend_sum_kernel(
    packed_ref,
    ctx_ref,
    grad_ref,
    stat_ref,
    weights_ref,
    normed_t_ref,
    exps_ref,
    up_ref,
    down_ref,
    out_ref,
    total_ref,
    grad_normed_ref,
    packed_sum_ref,
    exps,
    dq_t,
    dk_sum,
    dv_sum,
    grad_qkv,
    mine,
    first,
    second_y,
    second_x,
    third,
    fourth,
    send_sem,
    recv_sem,
    exps_sem,
    load_sem,
):
    pair = pl.program_id(0)
    width = up_ref.shape[-1] // 2
    sources = []
    for index in range(width // SLOT):
        for ref in (up_ref, down_ref):
            sources.append(lambda part, ref=ref, index=index: block_view(ref, part * width + index * SLOT))
    sources.append(lambda part: block_view(out_ref, part * SLOT))
    for index in range(3):
        sources.append(lambda part, index=index: block_view(grad_qkv, (part * 3 + index) * SLOT))

    def load(slot, part):
        block = sources[slot](part).at[:, :, summing.core]
        return pltpu.make_async_copy(block, mine.at[slot % RING, part], load_sem.at[slot % RING])

    def add_own(slot):
        if slot < READY:
            place = slot % RING
            pltpu.make_async_copy(mine.at[place], mine.at[place], load_sem.at[place]).wait()
            first[slot] = first[slot] + mine[place]
            if slot + RING < READY:
                for part in (0, 1):
                    load(slot + RING, part).start()
        else:
            for part in (0, 1):
                cols = pl.ds((part * 3 + slot - READY) * SLOT, SLOT)
                first[slot, part] = first[slot, part] + grad_qkv[:, :, summing.core, :, cols]

    buffers = (first, second_y, second_x, third, fourth)
    summing = Summing(sources, add_own, buffers, total_ref, (send_sem, recv_sem), LAG, READY, 1)

    def exps_load(head, half):
        return pltpu.make_async_copy(exps_ref.at[head], exps.at[half], exps_sem.at[half])

    @pl.when(pair == 0)
    def _():
        for half in (0, 1):
            exps_load(half, half).start()
        for slot in range(RING):
            for part in (0, 1):
                load(slot, part).start()
        greet_neighbours([summing.sibling, summing.beside, summing.across] + summing.stations)
        for slot in range(READY):
            summing.send_first(slot)
        grad_normed_ref[...] = jnp.zeros_like(grad_normed_ref)

    scale = 1.0 / math.sqrt(HD)
    queries = packed_ref[:, :PAIR]
    keys_t = packed_ref[:, PAIR : 2 * PAIR].T
    values = packed_ref[:, 2 * PAIR :]
    grads_t = grad_ref[...].T.astype(jnp.float32)
    context_t = ctx_ref[...].T.astype(jnp.float32)
    scaled = []
    inner_rows = []
    for half in (0, 1):
        heads = slice(half * HD, half * HD + HD)
        scaled.append(grads_t[heads] * stat_ref[0, half : half + 1, :])
        inner_rows.append(jnp.sum(scaled[half] * context_t[heads], axis=0, keepdims=True))
    scaled_t = jnp.concatenate(scaled, axis=0).astype(jnp.bfloat16)
    scaled_rows = scaled_t.T
    dk_sum[...] = jnp.zeros_like(dk_sum)
    dv_sum[...] = jnp.zeros_like(dv_sum)
    for half in (0, 1):
        exps_load(2 * pair + half, half).wait()
        parts = (
            only_rows(scaled_t, half),
            only_cols(scaled_rows, half),
            only_cols(queries, half),
            inner_rows[half],
        )
        attend_bwd_half(half, scale, values, keys_t, parts, exps.at[half], (dq_t, dk_sum, dv_sum))

        @pl.when(pair < PAIRS - 1)
        def _(half=half):
            exps_load(2 * pair + 2 + half, half).start()

        if half == 0:
            summing.tick(pair)
    grads = jnp.concatenate([dq_t[...].T, dk_sum[...] * scale, dv_sum[...]], axis=1).astype(jnp.bfloat16)
    packed_sum_ref[...] = jnp.sum(grads.astype(jnp.float32), axis=0, keepdims=True)
    cols = pl.ds(pl.multiple_of(pair * (3 * PAIR), PAIR), 3 * PAIR)
    grad_weights = mul(normed_t_ref[...], grads).astype(jnp.bfloat16)
    grad_qkv[:, :, :, :, cols] = grad_weights.reshape(4, 2, 2, 64, 3 * PAIR)
    grad_normed_ref[...] += dot_last(grads, weights_ref[...])

    for slot in range(READY, LATE_SLOTS):
        pl.when(pair == PAIRS - LATE_SLOTS + slot)(lambda slot=slot: summing.send_first(slot))

    @pl.when(pair == PAIRS - 1)
    def _():
        def late(index, carry):
            summing.tick(index)
            return carry

        lax.fori_loop(PAIRS, summing.ticks(), late, 0)
        summing.sent()


def attend_sum(packed, context, grad_context, stats, weights, normed_t, exps, grad_up, grad_down, grad_out):
    anywhere = pl.BlockSpec(memory_space=pl.ANY)
    rows = 64
    low = jnp.bfloat16
    once = pl.Buffered(1)
    tall = pl.BlockSpec((LEN, D), lambda p: (0, 0), pipeline_mode=once)
    split = [grad.reshape(4, 2, 2, rows, grad.shape[-1]) for grad in (grad_up, grad_down, grad_out)]
    return pl.pallas_call(
        attend_sum_kernel,
        grid=(PAIRS,),
        in_specs=[PACKED_COLS, PAIR_COLS, PAIR_COLS, PAIR_STAT, PACKED_COLS, tall] + [anywhere] * 4,
        out_specs=[
            pl.BlockSpec((LATE_SLOTS, rows, SLOT), lambda p: (0, 0, 0), pipeline_mode=once),
            tall,
            pl.BlockSpec((1, 3 * PAIR), lambda p: (0, p)),
        ],
        out_shape=[
            jax.ShapeDtypeStruct((LATE_SLOTS, rows, SLOT), jnp.float32),
            jax.ShapeDtypeStruct((LEN, D), jnp.float32),
            jax.ShapeDtypeStruct((1, 3 * D), jnp.float32),
        ],
        scratch_shapes=[
            pltpu.VMEM((2, LEN, LEN), low),
            pltpu.VMEM((PAIR, LEN), jnp.float32),
            pltpu.VMEM((LEN, PAIR), jnp.float32),
            pltpu.VMEM((LEN, PAIR), jnp.float32),
            pltpu.VMEM((4, 2, 2, rows, 3 * D), low),
            pltpu.VMEM((RING, 2, 4, 2, rows, SLOT), low),
            *summing_buffers(LATE_SLOTS),
            pltpu.SemaphoreType.DMA((2,)),
            pltpu.SemaphoreType.DMA((RING,)),
        ],
        compiler_params=pltpu.CompilerParams(
            collective_id=2, has_side_effects=True, vmem_limit_bytes=62 * 1024 * 1024
        ),
        cost_estimate=pl.CostEstimate(
            flops=44 * LEN * LEN * D, bytes_accessed=400 * 1024 * 1024, transcendentals=0
        ),
    )(packed, context, grad_context, stats, weights, normed_t, exps, *split)


ROWS = 256


def norm_pull(rows, grads, gain):
    centered = rows - jnp.mean(rows, axis=-1, keepdims=True)
    inverse = lax.rsqrt(jnp.mean(centered * centered, axis=-1, keepdims=True) + NORM_EPSILON)
    normed = centered * inverse
    scaled = grads * gain
    along = jnp.mean(scaled * normed, axis=-1, keepdims=True)
    pulled = inverse * (scaled - jnp.mean(scaled, axis=-1, keepdims=True) - normed * along)
    gain_sum = jnp.sum(grads * normed, axis=0, keepdims=True)
    return pulled, gain_sum, jnp.sum(grads, axis=0, keepdims=True)


def add_rows(sums_ref, rows):
    for index, row in enumerate(rows):
        sums_ref[index : index + 1, :] += row


def middle_kernel(
    middle_ref, grad_ref, cot_ref, ctx_ref, gain_ref, weights_ref, grad_middle_ref, grad_ctx_ref, grad_out_ref, sums_ref, low_t
):
    step = pl.program_id(0)

    @pl.when(step == 0)
    def _():
        sums_ref[...] = jnp.zeros_like(sums_ref)

    cot = cot_ref[...].astype(jnp.float32)
    pulled, gain_sum, shift_sum = norm_pull(middle_ref[...], grad_ref[...], gain_ref[...])
    grads = cot + pulled
    low = grads.astype(jnp.bfloat16)
    grad_middle_ref[...] = grads
    grad_ctx_ref[...] = mul(low, weights_ref[...]).astype(jnp.bfloat16)
    low_t[:, pl.ds(pl.multiple_of(step * ROWS, ROWS), ROWS)] = low.T
    grad_sum = jnp.sum(grads, axis=0, keepdims=True)
    add_rows(sums_ref, (gain_sum, shift_sum, grad_sum, jnp.sum(cot, axis=0, keepdims=True)))

    @pl.when(step == LEN // ROWS - 1)
    def _():
        grad_out_ref[...] = mul(low_t[...], ctx_ref[...]).astype(jnp.bfloat16)


def middle_backward(middle, grad_rows, cot, context, gain, weights):
    rows = pl.BlockSpec((ROWS, D), lambda s: (s, 0))
    whole = pl.BlockSpec((D, D), lambda s: (0, 0), pipeline_mode=pl.Buffered(1))
    row = pl.BlockSpec((1, D), lambda s: (0, 0))
    sums = pl.BlockSpec((8, D), lambda s: (0, 0))
    return pl.pallas_call(
        middle_kernel,
        grid=(LEN // ROWS,),
        in_specs=[rows, rows, rows, whole, row, whole],
        out_specs=[rows, rows, whole, sums],
        out_shape=[
            jax.ShapeDtypeStruct((LEN, D), jnp.float32),
            jax.ShapeDtypeStruct((LEN, D), jnp.bfloat16),
            jax.ShapeDtypeStruct((D, D), jnp.bfloat16),
            jax.ShapeDtypeStruct((8, D), jnp.float32),
        ],
        scratch_shapes=[pltpu.VMEM((D, LEN), jnp.bfloat16)],
        compiler_params=pltpu.CompilerParams(vmem_limit_bytes=VMEM_LIMIT),
        cost_estimate=pl.CostEstimate(flops=4 * LEN * D * D, bytes_accessed=24 * 1024 * 1024, transcendentals=0),
    )(middle, grad_rows, cot, context, gain, weights)


def token_kernel(rows_ref, grad_ref, grad_middle_ref, gain_ref, out_ref, sums_ref):
    @pl.when(pl.program_id(0) == 0)
    def _():
        sums_ref[...] = jnp.zeros_like(sums_ref)

    pulled, gain_sum, shift_sum = norm_pull(rows_ref[...].astype(jnp.float32), grad_ref[...], gain_ref[...])
    out_ref[...] = (grad_middle_ref[...] + pulled).astype(jnp.bfloat16)
    add_rows(sums_ref, (gain_sum, shift_sum))


def token_backward(rows_low, grad_rows, grad_middle, gain):
    rows = pl.BlockSpec((ROWS, D), lambda s: (s, 0))
    row = pl.BlockSpec((1, D), lambda s: (0, 0))
    sums = pl.BlockSpec((8, D), lambda s: (0, 0))
    return pl.pallas_call(
        token_kernel,
        grid=(LEN // ROWS,),
        in_specs=[rows, rows, rows, row],
        out_specs=[rows, sums],
        out_shape=[jax.ShapeDtypeStruct((LEN, D), jnp.bfloat16), jax.ShapeDtypeStruct((8, D), jnp.float32)],
        compiler_params=pltpu.CompilerParams(vmem_limit_bytes=VMEM_LIMIT),
        cost_estimate=pl.CostEstimate(flops=0, bytes_accessed=12 * 1024 * 1024, transcendentals=0),
    )(rows_low, grad_rows, grad_middle, gain)


def slot_rows(early_ref, late_ref, slot):
    index, kind = slot % 4, slot // 4
    if index < EARLY:
        return early_ref[2 * index + kind]
    return late_ref[2 * (index - EARLY) + kind]


def moment_kernel(
    early_ref,
    late_ref,
    m_qkv_ref,
    m_out_ref,
    m_up_ref,
    m_down_ref,
    g_qkv_ref,
    g_out_ref,
    g_up_ref,
    g_down_ref,
    n_qkv_ref,
    n_out_ref,
    n_up_ref,
    n_down_ref,
    slots_ref,
):
    first_packed = LATE_SLOTS - 3
    for pair in range(SLOT // PAIR):
        for part in range(3):
            column = (pair * 3 + part) * PAIR
            source = late_ref[first_packed + column // SLOT, :, column % SLOT : column % SLOT + PAIR]
            g_qkv_ref[part, :, pair * PAIR : (pair + 1) * PAIR] = source
    for part in range(3):
        moment = MOMENTUM_DECAY * m_qkv_ref[part] + g_qkv_ref[part]
        n_qkv_ref[part] = moment
        slots_ref[part] = moment.astype(jnp.bfloat16)
    grads = late_ref[first_packed - 1]
    g_out_ref[...] = grads
    moment = MOMENTUM_DECAY * m_out_ref[...] + grads
    n_out_ref[...] = moment
    slots_ref[3] = moment.astype(jnp.bfloat16)
    for kind, refs in enumerate(((m_up_ref, g_up_ref, n_up_ref), (m_down_ref, g_down_ref, n_down_ref))):
        old_ref, grads_ref, new_ref = refs
        for index in range(4):
            here = slice(index * SLOT, (index + 1) * SLOT)
            grads = slot_rows(early_ref, late_ref, 4 * kind + index)
            grads_ref[:, here] = grads
            moment = MOMENTUM_DECAY * old_ref[:, here] + grads
            new_ref[:, here] = moment
            slots_ref[4 + 4 * kind + index] = moment.astype(jnp.bfloat16)


def update_kernel(
    updates_ref,
    vec_sum_ref,
    w_qkv_ref,
    w_out_ref,
    w_up_ref,
    w_down_ref,
    vectors_ref,
    m_vec_ref,
    o_qkv_ref,
    o_out_ref,
    o_up_ref,
    o_down_ref,
    g_vec_ref,
    n_vec_ref,
    o_vec_ref,
):
    wide_rate = MATRIX_RATE * math.sqrt(FF / D)
    for part in range(3):
        o_qkv_ref[part] = w_qkv_ref[part] - MATRIX_RATE * updates_ref[part].astype(jnp.float32)
    o_out_ref[...] = w_out_ref[...] - MATRIX_RATE * updates_ref[3].astype(jnp.float32)
    for index in range(4):
        here = slice(index * SLOT, (index + 1) * SLOT)
        o_up_ref[:, here] = w_up_ref[:, here] - wide_rate * updates_ref[4 + index].astype(jnp.float32)
        o_down_ref[:, here] = w_down_ref[:, here] - wide_rate * updates_ref[8 + index].astype(jnp.float32)
    grads = vec_sum_ref[...]
    moment = MOMENTUM_DECAY * m_vec_ref[...] + grads
    square = jnp.mean(moment * moment, axis=1, keepdims=True)
    g_vec_ref[...] = grads
    n_vec_ref[...] = moment
    o_vec_ref[...] = vectors_ref[...] - VECTOR_RATE * moment * lax.rsqrt(square + SQUARE_EPSILON)


def like(arrays):
    return [jax.ShapeDtypeStruct(array.shape, jnp.float32) for array in arrays]


def features_first(arrays):
    qkv, out, up, down = arrays
    return qkv, out.T, up, down.T


def muon_step(early, late, vector_total, block_rows, token_grads, weights, vectors, momenta, m_vec):
    limit = pltpu.CompilerParams(vmem_limit_bytes=VMEM_LIMIT)
    weights, momenta = features_first(weights), features_first(momenta)
    slots_shape = jax.ShapeDtypeStruct((SLOTS,) + late.shape[1:], jnp.bfloat16)
    *stored, slots = pl.pallas_call(
        moment_kernel, out_shape=like(momenta) + like(momenta) + [slots_shape], compiler_params=limit
    )(early, late, *momenta)
    updates, vector_rows, output_pair, token_pair = muon_call(
        slots, vector_total.reshape(SLOTS, 8, 128), block_rows, token_grads
    )
    fresh = pl.pallas_call(
        update_kernel, out_shape=like(weights) + like([vectors] * 3), compiler_params=limit
    )(updates, vector_rows.reshape(12, D), *weights, vectors, m_vec)
    vector_grad, moment_vec, new_vec = fresh[4:]
    grads, moments, new = features_first(stored[:4]), features_first(stored[4:]), features_first(fresh[:4])
    return (output_pair, token_pair.astype(jnp.float32), *grads, vector_grad, *moments, moment_vec, *new, new_vec)


def by_slots(rows):
    return jnp.swapaxes(rows.reshape(rows.shape[0], -1, SLOT), 0, 1)


def narrow(rows):
    return rows.astype(jnp.bfloat16)


def contract(left, right, left_dim, right_dim):
    return lax.dot_general(
        left, right, (((left_dim,), (right_dim,)), ((), ())), preferred_element_type=jnp.float32
    )


def in_order(rank, own, got):
    return jnp.where(rank == 0, jnp.concatenate([own, got]), jnp.concatenate([got, own]))


def by_pairs(rows):
    count, height, width = rows.shape
    return jnp.transpose(rows.reshape(count, height, width // PAIR, PAIR), (1, 2, 0, 3)).reshape(height, -1)


def from_pairs(rows):
    height = rows.shape[0]
    return jnp.transpose(rows.reshape(height, -1, 3, PAIR), (2, 0, 1, 3)).reshape(3, height, -1)


def sequence_step(
    tokens,
    cotangent,
    piece_starts,
    w_qkv,
    w_out,
    w_up,
    w_down,
    vectors,
    m_qkv,
    m_out,
    m_up,
    m_down,
    m_vec,
):
    rank = lax.axis_index("tensor")
    slopes = jnp.exp2(-8.0 * jnp.arange(1, H + 1, dtype=jnp.float32) / H)
    starts = lax.dynamic_slice_in_dim(piece_starts[:, 0], rank, 1, 0)[0]
    own_tokens = lax.dynamic_index_in_dim(tokens, rank, 0, keepdims=False)
    own_cotangent = lax.dynamic_index_in_dim(cotangent, rank, 0, keepdims=False)

    full_qkv, other_tokens = first_spread(by_slots(by_pairs(narrow(w_qkv))), tokens)
    token_low = in_order(rank, own_tokens, other_tokens)
    token_rows = token_low.astype(jnp.float32)
    normed_one = narrow(layer_norm(token_rows, vectors[0], vectors[1]))
    shifts = by_pairs(jnp.stack([vectors[2], jnp.zeros((D,), jnp.float32), vectors[3]])[:, None])
    up_slots = by_slots(narrow(w_up))
    down_slots = by_slots(narrow(w_down).T)
    in_turn = jnp.stack([up_slots, down_slots], axis=1).reshape(2 * up_slots.shape[0], *up_slots.shape[1:])
    later_slots = jnp.concatenate([narrow(w_out).T[None], in_turn[: 2 * EARLY]])
    packed, context, exps, stats, normed_t, wholes, other_cotangent = attend_spread(
        starts, slopes, normed_one, full_qkv, shifts, later_slots, cotangent
    )
    full_out, full_up, full_down = wholes
    cotangent_low = in_order(rank, own_cotangent, other_cotangent)

    middle = token_rows + contract(context, full_out, 1, 1) + vectors[4]
    normed_two = narrow(layer_norm(middle, vectors[5], vectors[6]))
    block_rows, grad_normed_two, grad_up, grad_down, up_bias, early_sums = mlp_both(
        normed_two,
        cotangent_low,
        middle + vectors[11],
        vectors[7:11].reshape(1, FF),
        full_up,
        full_down,
        in_turn[2 * EARLY :],
    )
    grad_middle, grad_context, grad_out, middle_sums = middle_backward(
        middle, grad_normed_two, cotangent_low, context, vectors[5:6], full_out
    )
    sums, grad_normed_one, packed_grads = attend_sum(
        packed, context, grad_context, stats, full_qkv, normed_t, exps, grad_up, grad_down, grad_out
    )
    grad_token_low, token_sums = token_backward(token_low, grad_normed_one, grad_middle, vectors[0:1])
    packed_sums = from_pairs(packed_grads)[:, 0]
    vector_total = jnp.concatenate(
        [
            token_sums[0:2],
            packed_sums[0:1],
            packed_sums[2:3],
            middle_sums[2:3],
            middle_sums[0:2],
            up_bias.reshape(4, D),
            middle_sums[3:4],
        ]
    )
    weights = (w_qkv, w_out, w_up, w_down)
    momenta = (m_qkv, m_out, m_up, m_down)
    return muon_step(
        early_sums, sums, vector_total, block_rows, grad_token_low, weights, vectors, momenta, m_vec
    )


def solution(mesh):
    in_specs = (
        P(None, ("dp", "tensor"), None),
        P(None, ("dp", "tensor"), None),
        P(None, "dp", None),
        P(None, "dp", "tensor"),
        P("tensor", "dp"),
        P("dp", "tensor"),
        P("tensor", "dp"),
        P(),
        P(None, "dp", "tensor"),
        P("tensor", "dp"),
        P("dp", "tensor"),
        P("tensor", "dp"),
        P(),
    )
    out_specs = (
        P(None, ("dp", "tensor"), None),
        P(None, ("dp", "tensor"), None),
        P(None, "dp", "tensor"),
        P("tensor", "dp"),
        P("dp", "tensor"),
        P("tensor", "dp"),
        P(),
        P(None, "dp", "tensor"),
        P("tensor", "dp"),
        P("dp", "tensor"),
        P("tensor", "dp"),
        P(),
        P(None, "dp", "tensor"),
        P("tensor", "dp"),
        P("dp", "tensor"),
        P("tensor", "dp"),
        P(),
    )
    groups_fit = mesh.shape["tensor"] == MB and mesh.shape["dp"] == 16

    def pick(*arrays):
        if groups_fit and arrays[2].shape[1] == 1:
            return sequence_step(*arrays)
        return on_device(*arrays)

    return jax.shard_map(
        pick, mesh=mesh, in_specs=in_specs, out_specs=out_specs, check_vma=False
    )
```

```python
import math

import jax
import jax.numpy as jnp
from jax import lax
from jax.experimental import pallas as pl
from jax.experimental.pallas import tpu as pltpu
from jax.sharding import PartitionSpec as P

D = 1024
H = 16
HD = 64
FF = 4096
LEN = 1024
PIECE = 256
NPIECE = 2
MB = 2
NS_ITERS = 3


NORM_EPSILON = 1e-05
SQUARE_EPSILON = 1e-06
MASKED_SCORE = -1e30
SCHULZ_FIRST = 3.4445
SCHULZ_SECOND = -4.775
SCHULZ_THIRD = 2.0315
MOMENTUM_DECAY = 0.5
MATRIX_RATE = 0.5
VECTOR_RATE = 0.05


def layer_norm(inputs, gain_row, shift_row):
    average = jnp.mean(inputs, axis=-1, keepdims=True)
    centered = inputs - average
    variance = jnp.mean(centered * centered, axis=-1, keepdims=True)
    return centered * lax.rsqrt(variance + NORM_EPSILON) * gain_row + shift_row


def gelu_tanh(inputs):
    return jax.nn.gelu(inputs, approximate=True)


def score_layout(starts, slopes):
    positions = jnp.arange(LEN, dtype=jnp.int32)
    inside = (positions[None, :] >= starts[:, None]) & (
        positions[None, :] < starts[:, None] + PIECE
    )
    labels = jnp.arange(1, NPIECE + 1, dtype=jnp.int32)
    piece_label = jnp.sum(jnp.where(inside, labels[:, None], 0), axis=0)
    same_piece = (piece_label[:, None] == piece_label[None, :]) & (piece_label[:, None] > 0)
    visible = (positions[None, :] <= positions[:, None]) | same_piece
    distance = jnp.abs(positions[:, None] - positions[None, :]).astype(jnp.float32)
    penalty = -slopes[:, None, None] * distance[None, :, :]
    return (visible, penalty)


def head_scores(query_heads, key_heads, starts, slopes):
    visible, penalty = score_layout(starts, slopes)
    raw_scores = jnp.einsum(
        "qhd,khd->hqk", query_heads, key_heads, preferred_element_type=jnp.float32
    )
    scores = raw_scores * (1.0 / math.sqrt(HD)) + penalty
    return jnp.where(visible[None, :, :], scores, MASKED_SCORE)


def attend_forward(element, slopes):
    query_seq, key_seq, value_seq, starts = element
    heads_here = slopes.shape[0]
    query_heads = query_seq.reshape(LEN, heads_here, HD)
    key_heads = key_seq.reshape(LEN, heads_here, HD)
    value_heads = value_seq.reshape(LEN, heads_here, HD)
    scores = head_scores(query_heads, key_heads, starts, slopes)
    maximum = jnp.max(scores, axis=-1, keepdims=True)
    weights_raw = jnp.exp(scores - maximum)
    denominator = jnp.sum(weights_raw, axis=-1, keepdims=True)
    probabilities = weights_raw / denominator
    context = jnp.einsum(
        "hqk,khd->qhd",
        probabilities.astype(jnp.bfloat16),
        value_heads,
        preferred_element_type=jnp.float32,
    )
    logsum = (maximum + jnp.log(denominator))[..., 0]
    return (context.reshape(LEN, heads_here * HD), logsum)


def attend_backward(element, slopes):
    query_seq, key_seq, value_seq, context_grad, logsum, starts = element
    heads_here = slopes.shape[0]
    query_heads = query_seq.reshape(LEN, heads_here, HD)
    key_heads = key_seq.reshape(LEN, heads_here, HD)
    value_heads = value_seq.reshape(LEN, heads_here, HD)
    grad_heads = context_grad.reshape(LEN, heads_here, HD)
    scores = head_scores(query_heads, key_heads, starts, slopes)
    probabilities = jnp.exp(scores - logsum[..., None])
    grad_probs = jnp.einsum(
        "qhd,khd->hqk", grad_heads, value_heads, preferred_element_type=jnp.float32
    )
    inner_sum = jnp.sum(probabilities * grad_probs, axis=-1, keepdims=True)
    grad_scores = (probabilities * (grad_probs - inner_sum)).astype(jnp.bfloat16)
    scale_factor = 1.0 / math.sqrt(HD)
    grad_query = (
        jnp.einsum("hqk,khd->qhd", grad_scores, key_heads, preferred_element_type=jnp.float32)
        * scale_factor
    )
    grad_key = (
        jnp.einsum("hqk,qhd->khd", grad_scores, query_heads, preferred_element_type=jnp.float32)
        * scale_factor
    )
    grad_value = jnp.einsum(
        "hqk,qhd->khd",
        probabilities.astype(jnp.bfloat16),
        grad_heads,
        preferred_element_type=jnp.float32,
    )
    width_here = heads_here * HD
    return (
        grad_query.astype(jnp.bfloat16).reshape(LEN, width_here),
        grad_key.astype(jnp.bfloat16).reshape(LEN, width_here),
        grad_value.astype(jnp.bfloat16).reshape(LEN, width_here),
    )


def placed(values, offset, length):
    return lax.dynamic_update_slice_in_dim(jnp.zeros((length,), jnp.float32), values, offset, 0)


def accumulate(totals, addend):
    if totals is None:
        return addend
    return tuple((former + latter for former, latter in zip(totals, addend)))


def gram_term(narrow_rows, wide_rows):
    part_narrow = jnp.einsum(
        "mrc,mrd->cmd", narrow_rows, narrow_rows, preferred_element_type=jnp.float32
    )
    part_wide = jnp.einsum("mrc,mrd->cmd", wide_rows, wide_rows, preferred_element_type=jnp.float32)
    return jnp.concatenate([part_narrow, part_wide], axis=1)


def schulz_step(state, gram_matrix):
    turned = jnp.einsum("mrc,cmd->mrd", state, gram_matrix, preferred_element_type=jnp.float32)
    mixed = (SCHULZ_SECOND * state.astype(jnp.float32) + SCHULZ_THIRD * turned).astype(jnp.bfloat16)
    return (
        SCHULZ_FIRST * state.astype(jnp.float32)
        + jnp.einsum("mrc,cmd->mrd", mixed, gram_matrix, preferred_element_type=jnp.float32)
    ).astype(jnp.bfloat16)


def slice_term(source, weights, pattern):
    return jnp.einsum(pattern, source, weights, preferred_element_type=jnp.float32)


def on_device(
    tokens,
    cotangent,
    piece_starts,
    w_qkv,
    w_out,
    w_up,
    w_down,
    vectors,
    m_qkv,
    m_out,
    m_up,
    m_down,
    m_vec,
):
    tensor_count = lax.axis_size("tensor")
    tensor_rank = lax.axis_index("tensor")
    shard_rank = lax.axis_index("dp")
    heads_here = H // tensor_count
    width_here = heads_here * HD
    hidden_here = FF // tensor_count
    rows_here = tokens.shape[1]
    group_rows = rows_here * tensor_count
    seqs_here = piece_starts.shape[1]
    shard_rows = w_qkv.shape[1]
    head_ids = tensor_rank * heads_here + jnp.arange(heads_here, dtype=jnp.int32) + 1
    slopes = jnp.exp2(-8.0 * head_ids.astype(jnp.float32) / H)
    query_shift = lax.dynamic_slice_in_dim(vectors[2], tensor_rank * width_here, width_here, 0)
    value_shift = lax.dynamic_slice_in_dim(vectors[3], tensor_rank * width_here, width_here, 0)
    up_shift = lax.dynamic_slice_in_dim(
        vectors[7:11].reshape(FF), tensor_rank * hidden_here, hidden_here, 0
    )
    low_qkv = w_qkv.astype(jnp.bfloat16)
    low_out = w_out.astype(jnp.bfloat16)
    low_up = w_up.astype(jnp.bfloat16)
    low_down = w_down.astype(jnp.bfloat16)
    outputs_list = []
    input_grads = []
    vector_total = jnp.zeros((12, D), jnp.float32)
    grad_total = None

    def forward_one(element):
        return attend_forward(element, slopes)

    def backward_one(element):
        return attend_backward(element, slopes)

    for batch_index in range(MB):
        full_qkv, full_out, full_up, full_down = (
            lax.all_gather(low_qkv, "dp", axis=1, tiled=True),
            lax.all_gather(low_out, "dp", axis=1, tiled=True),
            lax.all_gather(low_up, "dp", axis=0, tiled=True),
            lax.all_gather(low_down, "dp", axis=1, tiled=True),
        )
        token_rows = tokens[batch_index].astype(jnp.float32)
        cotangent_rows = cotangent[batch_index]
        normed_one = layer_norm(token_rows, vectors[0], vectors[1])
        normed_all, cotangent_all = (
            lax.all_gather(normed_one.astype(jnp.bfloat16), "tensor", axis=0, tiled=True),
            lax.all_gather(cotangent_rows, "tensor", axis=0, tiled=True),
        )
        projected = jnp.einsum(
            "td,cde->cte", normed_all, full_qkv, preferred_element_type=jnp.float32
        )
        query_low = (projected[0] + query_shift).astype(jnp.bfloat16)
        key_low = projected[1].astype(jnp.bfloat16)
        value_low = (projected[2] + value_shift).astype(jnp.bfloat16)
        query_seqs = query_low.reshape(seqs_here, LEN, width_here)
        key_seqs = key_low.reshape(seqs_here, LEN, width_here)
        value_seqs = value_low.reshape(seqs_here, LEN, width_here)
        starts_here = piece_starts[batch_index]
        context_seq, logsum = lax.map(forward_one, (query_seqs, key_seqs, value_seqs, starts_here))
        context_low = context_seq.reshape(group_rows, width_here).astype(jnp.bfloat16)
        attended = lax.psum_scatter(
            slice_term(context_low, full_out, "tc,cd->td").astype(jnp.bfloat16),
            "tensor",
            scatter_dimension=0,
            tiled=True,
        ).astype(jnp.float32)
        middle = token_rows + attended + vectors[4]
        normed_two = layer_norm(middle, vectors[5], vectors[6])
        normed_two_all = lax.all_gather(
            normed_two.astype(jnp.bfloat16), "tensor", axis=0, tiled=True
        )
        before = jnp.dot(normed_two_all, full_up, preferred_element_type=jnp.float32) + up_shift
        activated = gelu_tanh(before).astype(jnp.bfloat16)
        expanded = lax.psum_scatter(
            slice_term(activated, full_down, "tf,fd->td").astype(jnp.bfloat16),
            "tensor",
            scatter_dimension=0,
            tiled=True,
        ).astype(jnp.float32)
        outputs_list.append((middle + expanded + vectors[11]).astype(jnp.bfloat16))
        grad_down = jnp.einsum(
            "tf,td->fd", activated, cotangent_all, preferred_element_type=jnp.float32
        )
        grad_activated = jnp.einsum(
            "td,fd->tf", cotangent_all, full_down, preferred_element_type=jnp.float32
        )
        gelu_pull = jax.vjp(gelu_tanh, before)[1]
        grad_before = gelu_pull(grad_activated)[0].astype(jnp.bfloat16)
        grad_up = jnp.einsum(
            "td,tf->df", normed_two_all, grad_before, preferred_element_type=jnp.float32
        )
        grad_normed_two = lax.psum_scatter(
            slice_term(grad_before, full_up, "tf,df->td").astype(jnp.bfloat16),
            "tensor",
            scatter_dimension=0,
            tiled=True,
        ).astype(jnp.float32)
        second_pull = jax.vjp(layer_norm, middle, vectors[5], vectors[6])[1]
        middle_from_norm, gain_two_grad, shift_two_grad = second_pull(grad_normed_two)
        grad_middle = cotangent_rows.astype(jnp.float32) + middle_from_norm
        grad_middle_all = lax.all_gather(
            grad_middle.astype(jnp.bfloat16), "tensor", axis=0, tiled=True
        )
        grad_out = jnp.einsum(
            "tc,td->cd", context_low, grad_middle_all, preferred_element_type=jnp.float32
        )
        grad_context = jnp.einsum(
            "td,cd->tc", grad_middle_all, full_out, preferred_element_type=jnp.float32
        ).astype(jnp.bfloat16)
        grad_query, grad_key, grad_value = lax.map(
            backward_one,
            (
                query_seqs,
                key_seqs,
                value_seqs,
                grad_context.reshape(seqs_here, LEN, width_here),
                logsum,
                starts_here,
            ),
        )
        grad_stack = jnp.stack(
            [
                grad_query.reshape(group_rows, width_here),
                grad_key.reshape(group_rows, width_here),
                grad_value.reshape(group_rows, width_here),
            ]
        )
        grad_qkv = jnp.einsum(
            "td,cte->cde", normed_all, grad_stack, preferred_element_type=jnp.float32
        )
        grad_normed_one = lax.psum_scatter(
            slice_term(grad_stack, full_qkv, "cte,cde->td").astype(jnp.bfloat16),
            "tensor",
            scatter_dimension=0,
            tiled=True,
        ).astype(jnp.float32)
        first_pull = jax.vjp(layer_norm, token_rows, vectors[0], vectors[1])[1]
        token_from_norm, gain_one_grad, shift_one_grad = first_pull(grad_normed_one)
        input_grads.append(grad_middle + token_from_norm)
        query_bias = jnp.sum(grad_stack[0], axis=0, dtype=jnp.float32)
        value_bias = jnp.sum(grad_stack[2], axis=0, dtype=jnp.float32)
        up_bias = jnp.sum(grad_before, axis=0, dtype=jnp.float32)
        head_rows = jnp.stack(
            [
                gain_one_grad,
                shift_one_grad,
                placed(query_bias, tensor_rank * width_here, D),
                placed(value_bias, tensor_rank * width_here, D),
                jnp.sum(grad_middle, axis=0),
                gain_two_grad,
                shift_two_grad,
            ]
        )
        up_rows = placed(up_bias, tensor_rank * hidden_here, FF).reshape(4, D)
        tail_row = jnp.sum(cotangent_rows, axis=0, dtype=jnp.float32)[None, :]
        vector_total = vector_total + jnp.concatenate([head_rows, up_rows, tail_row], axis=0)
        shard_grads = (
            lax.psum_scatter(
                grad_qkv.astype(jnp.bfloat16), "dp", scatter_dimension=1, tiled=True
            ).astype(jnp.float32),
            lax.psum_scatter(
                grad_out.astype(jnp.bfloat16), "dp", scatter_dimension=1, tiled=True
            ).astype(jnp.float32),
            lax.psum_scatter(
                grad_up.astype(jnp.bfloat16), "dp", scatter_dimension=0, tiled=True
            ).astype(jnp.float32),
            lax.psum_scatter(
                grad_down.astype(jnp.bfloat16), "dp", scatter_dimension=1, tiled=True
            ).astype(jnp.float32),
        )
        grad_total = accumulate(grad_total, shard_grads)
    grad_qkv_shard, grad_out_shard, grad_up_shard, grad_down_shard = grad_total
    moment_qkv = MOMENTUM_DECAY * m_qkv + grad_qkv_shard
    moment_out = MOMENTUM_DECAY * m_out + grad_out_shard
    moment_up = MOMENTUM_DECAY * m_up + grad_up_shard
    moment_down = MOMENTUM_DECAY * m_down + grad_down_shard
    squares = jnp.concatenate(
        [
            jnp.sum(moment_qkv * moment_qkv, axis=(1, 2)),
            jnp.stack(
                [
                    jnp.sum(moment_out * moment_out),
                    jnp.sum(moment_up * moment_up),
                    jnp.sum(moment_down * moment_down),
                ]
            ),
        ]
    )
    vector_grad, square_total = lax.psum((vector_total, squares), ("dp", "tensor"))
    factors = lax.rsqrt(square_total + SQUARE_EPSILON)
    scaled_qkv = (moment_qkv * factors[0:3][:, None, None]).astype(jnp.bfloat16)
    scaled_out = (moment_out * factors[3]).astype(jnp.bfloat16)
    scaled_up = (moment_up * factors[4]).astype(jnp.bfloat16)
    scaled_down = (moment_down * factors[5]).astype(jnp.bfloat16)
    gathered_qkv, gathered_out, gathered_up, gathered_down = (
        lax.all_gather(scaled_qkv, "dp", axis=1, tiled=True),
        lax.all_gather(scaled_out, "dp", axis=1, tiled=True),
        lax.all_gather(scaled_up, "dp", axis=0, tiled=True),
        lax.all_gather(scaled_down, "dp", axis=1, tiled=True),
    )
    offset = shard_rank * shard_rows
    narrow_rows = jnp.concatenate([jnp.swapaxes(gathered_qkv, 1, 2), gathered_out[None]], axis=0)
    wide_rows = jnp.stack([gathered_up.T, gathered_down])
    for sweep_index in range(NS_ITERS):
        gram_share = lax.psum_scatter(
            gram_term(narrow_rows, wide_rows).astype(jnp.bfloat16),
            "tensor",
            scatter_dimension=0,
            tiled=True,
        )
        gram_matrix = lax.all_gather(gram_share, "tensor", axis=0, tiled=True)
        narrow_rows = schulz_step(narrow_rows, gram_matrix[:, 0:4])
        wide_rows = schulz_step(wide_rows, gram_matrix[:, 4:6])
    final_narrow = narrow_rows.astype(jnp.float32)
    final_wide = wide_rows.astype(jnp.float32)
    update_qkv = lax.dynamic_slice_in_dim(
        jnp.swapaxes(final_narrow[0:3], 1, 2), offset, shard_rows, 1
    )
    update_out = lax.dynamic_slice_in_dim(final_narrow[3], offset, shard_rows, 1)
    update_up = lax.dynamic_slice_in_dim(final_wide[0].T, offset, shard_rows, 0)
    update_down = lax.dynamic_slice_in_dim(final_wide[1], offset, shard_rows, 1)
    wide_factor = math.sqrt(FF / D)
    new_qkv = w_qkv - MATRIX_RATE * update_qkv
    new_out = w_out - MATRIX_RATE * update_out
    new_up = w_up - MATRIX_RATE * wide_factor * update_up
    new_down = w_down - MATRIX_RATE * wide_factor * update_down
    moment_vec = MOMENTUM_DECAY * m_vec + vector_grad
    new_vec = vectors - VECTOR_RATE * moment_vec * lax.rsqrt(
        jnp.mean(moment_vec * moment_vec, axis=1, keepdims=True) + SQUARE_EPSILON
    )
    return (
        jnp.stack(outputs_list),
        jnp.stack(input_grads),
        grad_qkv_shard,
        grad_out_shard,
        grad_up_shard,
        grad_down_shard,
        vector_grad,
        moment_qkv,
        moment_out,
        moment_up,
        moment_down,
        moment_vec,
        new_qkv,
        new_out,
        new_up,
        new_down,
        new_vec,
    )


QB = 256
PAIR = 2 * HD
PAIRS = D // PAIR
VMEM_LIMIT = 56 * 1024 * 1024


def layout_grid(starts_ref, dist_ref):
    key_pos = lax.broadcasted_iota(jnp.int32, (LEN, LEN), 0)
    query_pos = lax.broadcasted_iota(jnp.int32, (LEN, LEN), 1)
    gap = query_pos - key_pos
    visible = gap >= 0
    for piece in range(NPIECE):
        start = starts_ref[piece]
        inside_key = (key_pos >= start) & (key_pos < start + PIECE)
        inside_query = (query_pos >= start) & (query_pos < start + PIECE)
        visible = visible | (inside_key & inside_query)
    dist_ref[...] = jnp.where(visible, jnp.abs(gap).astype(jnp.float32), -MASKED_SCORE)


def only_rows(pair, half):
    rows = lax.broadcasted_iota(jnp.int32, pair.shape, 0)
    return jnp.where((rows >= HD) if half else (rows < HD), pair, jnp.zeros_like(pair))


def only_cols(pair, half):
    cols = lax.broadcasted_iota(jnp.int32, pair.shape, 1)
    return jnp.where((cols >= HD) if half else (cols < HD), pair, jnp.zeros_like(pair))


def mul(left, right):
    return jnp.dot(left, right, preferred_element_type=jnp.float32)


def attend_pair(pair, slopes_ref, packed, dist_ref, ctx_ref, exps_ref, stat_ref, ctx_t, between):
    keys = packed[:, PAIR : 2 * PAIR]
    values_t = packed[:, 2 * PAIR :].T
    queries_t = (packed[:, :PAIR] * (1.0 / math.sqrt(HD))).T
    for half in (0, 1):
        slope = slopes_ref[2 * pair + half]
        queries = only_rows(queries_t, half)
        heads = slice(half * HD, half * HD + HD)
        for block in range(LEN // QB):
            span = min(LEN, QB * block + QB + PIECE)
            cols = slice(block * QB, block * QB + QB)
            scores = mul(keys[:span], queries[:, cols]) - slope * dist_ref[:span, cols]
            top = jnp.max(scores, axis=0, keepdims=True)
            raw = jnp.exp(scores - top)
            inverse = 1.0 / jnp.sum(raw, axis=0, keepdims=True)
            low = raw.astype(jnp.bfloat16)
            exps_ref[half, :span, cols] = low
            ctx_t[heads, cols] = mul(values_t[heads, :span], low) * inverse
            stat_ref[0, half : half + 1, cols] = inverse
        if half == 0:
            between()
    ctx_ref[...] = ctx_t[...].T.astype(jnp.bfloat16)


PACKED_COLS = pl.BlockSpec((LEN, 3 * PAIR), lambda p: (0, p))
PAIR_COLS = pl.BlockSpec((LEN, PAIR), lambda p: (0, p))
PAIR_GRID = pl.BlockSpec((2, LEN, LEN), lambda p: (p, 0, 0))
PAIR_STAT = pl.BlockSpec((1, 2, LEN), lambda p: (p, 0, 0))
SCALARS = pl.BlockSpec(memory_space=pltpu.SMEM)


HIDDEN = 512
CHUNK = 256
HIDDEN_STEPS = FF // HIDDEN
GELU_SLOPE = math.sqrt(2.0 / math.pi)
GELU_CUBE = 0.044715


def dot_last(left, right):
    return lax.dot_general(left, right, (((1,), (1,)), ((), ())), preferred_element_type=jnp.float32)


def gelu_both(rows):
    square = rows * rows
    bent = jnp.tanh(rows * (GELU_SLOPE + GELU_SLOPE * GELU_CUBE * square))
    half = 0.5 + 0.5 * bent
    slope = half + 0.5 * rows * (1.0 - bent * bent) * (GELU_SLOPE + 3.0 * GELU_SLOPE * GELU_CUBE * square)
    return rows * half, slope


def hidden_block(step):
    return (step % 2) * (HIDDEN_STEPS // 2) + step // 2


def mlp_kernel(
    rows_ref,
    cot_ref,
    base_ref,
    bias_ref,
    up_ref,
    down_ref,
    slots_ref,
    block_ref,
    grad_rows_ref,
    grad_up_ref,
    grad_down_ref,
    bias_sum_ref,
    total_ref,
    rows_t,
    cot_t,
    total,
    up_part,
    down_part,
    active,
    grad_before,
    grad_early,
    first,
    second_y,
    second_x,
    third,
    fourth,
    sum_send,
    sum_recv,
    local_sem,
    spread_send,
    spread_recv,
    load_sem,
):
    step = pl.program_id(0)
    early_steps = 2 * EARLY
    table = []
    for index in range(HIDDEN_STEPS // 2 - EARLY):
        table += [(place_view(ref, 2 + 2 * index), HALF_SLOT) for ref in (up_part, down_part)]
    spread = Spread(slots_ref, table, local_sem, spread_send, spread_recv)

    def early_block(slot, part):
        return grad_early.at[slot % 2, 2 * (slot // 2) + part]

    def add_own(slot):
        for part in (0, 1):
            first[slot, part] = first[slot, part] + grad_early[slot % 2, 2 * (slot // 2) + part, :, :, summing.core]

    sources = [lambda part, slot=slot: early_block(slot, part) for slot in range(2 * EARLY)]
    buffers = (first, second_y, second_x, third, fourth)
    summing = Summing(sources, add_own, buffers, total_ref, (sum_send, sum_recv), 1)

    def loads(at):
        column = lax.rem(at, 2) * EARLY + at // 2
        cols = pl.ds(pl.multiple_of(column * HIDDEN, HIDDEN), HIDDEN)
        place = lax.rem(at, 2)
        return (
            pltpu.make_async_copy(up_ref.at[:, :, :, :, cols], up_part.at[place], load_sem.at[0, place]),
            pltpu.make_async_copy(down_ref.at[:, :, :, :, cols], down_part.at[place], load_sem.at[1, place]),
        )

    @pl.when(step == 0)
    def _():
        for copy in loads(step):
            copy.start()
        greet_neighbours([spread.sibling, spread.beside, spread.across] + spread.stations)
        spread.begin()
        rows_t[...] = rows_ref[...].T
        cot_t[...] = cot_ref[...].T
        total[...] = base_ref[...]
        grad_rows_ref[...] = jnp.zeros_like(grad_rows_ref)

    @pl.when(step < early_steps)
    def _():
        for copy in loads(step):
            copy.wait()

    @pl.when(step < early_steps - 1)
    def _():
        for copy in loads(step + 1):
            copy.start()

    for index in range(HIDDEN_STEPS // 2 - EARLY):

        @pl.when(step == early_steps + 2 * index)
        def _(index=index):
            spread.arrived(2 * index)
            spread.arrived(2 * index + 1)

    place = jnp.where(step < early_steps, lax.rem(step, 2), step - early_steps + 2)
    up = up_part[place].reshape(D, HIDDEN)
    down = down_part[place].reshape(D, HIDDEN)
    bias = bias_ref[...]
    bias_sum = jnp.zeros((1, HIDDEN), jnp.float32)
    for index in range(LEN // CHUNK):
        here = slice(index * CHUNK, index * CHUNK + CHUNK)
        value, slope = gelu_both(mul(rows_ref[here], up) + bias)
        value = value.astype(jnp.bfloat16)
        grads = (slope * mul(cot_ref[here], down)).astype(jnp.bfloat16)
        active[here] = value
        grad_before[here] = grads
        bias_sum += jnp.sum(grads.astype(jnp.float32), axis=0, keepdims=True)
        total[here] += dot_last(value, down)
        grad_rows_ref[here] += dot_last(grads, up)
        if index == LEN // CHUNK // 2 - 1:
            for number in range(spread.ticks()):
                pl.when(step == number)(lambda number=number: spread.tick(number))
    bias_sum_ref[...] = bias_sum

    @pl.when(step < early_steps)
    def _():
        for index, (left, right) in enumerate(((rows_t, grad_before), (cot_t, active))):
            grads = mul(left[...], right[...]).astype(jnp.bfloat16)
            grad_early[index, step] = grads.reshape(grad_early.shape[2:])

    @pl.when(step >= early_steps)
    def _():
        grad_up_ref[...] = mul(rows_t[...], grad_before[...]).astype(jnp.bfloat16)
        grad_down_ref[...] = mul(cot_t[...], active[...]).astype(jnp.bfloat16)

    for number in range(HIDDEN_STEPS):

        @pl.when(step == number)
        def _(number=number):
            if number < early_steps and number % 2:
                summing.send_first(number - 1)
                summing.send_first(number)
            if number >= 2:
                summing.fixed_tick(number - 2)

    @pl.when(step == HIDDEN_STEPS - 1)
    def _():
        block_ref[...] = total[...].astype(jnp.bfloat16)
        for number in range(HIDDEN_STEPS - 2, summing.ticks()):
            summing.fixed_tick(number)
        summing.sent()
        spread.sent()


def late_block(step):
    late = HIDDEN_STEPS // 2 - EARLY
    return jnp.where(step < 2 * EARLY, 0, (step % 2) * late + step // 2 - EARLY)


def mlp_both(rows, cot, base, bias, up, down, slots):
    anywhere = pl.BlockSpec(memory_space=pl.ANY)
    once = pl.Buffered(1)
    whole = pl.BlockSpec((LEN, D), lambda s: (0, 0), pipeline_mode=once)
    hidden = pl.BlockSpec((D, HIDDEN), lambda s: (0, late_block(s)))
    hidden_row = pl.BlockSpec((1, HIDDEN), lambda s: (0, hidden_block(s)))
    low = jnp.bfloat16
    late = HIDDEN_STEPS // 2 - EARLY
    part = pltpu.VMEM((2 + 2 * late, 4, 2, 2, 64, HIDDEN), low)
    split = [weights.reshape(4, 2, 2, 64, -1) for weights in (up, down)]
    return pl.pallas_call(
        mlp_kernel,
        grid=(HIDDEN_STEPS,),
        in_specs=[whole, whole, whole, hidden_row, anywhere, anywhere, anywhere],
        out_specs=[
            whole,
            whole,
            hidden,
            hidden,
            hidden_row,
            pl.BlockSpec((2 * EARLY, 64, SLOT), lambda s: (0, 0, 0), pipeline_mode=once),
        ],
        out_shape=[
            jax.ShapeDtypeStruct((LEN, D), low),
            jax.ShapeDtypeStruct((LEN, D), jnp.float32),
            jax.ShapeDtypeStruct((D, 2 * late * HIDDEN), low),
            jax.ShapeDtypeStruct((D, 2 * late * HIDDEN), low),
            jax.ShapeDtypeStruct((1, FF), jnp.float32),
            jax.ShapeDtypeStruct((2 * EARLY, 64, SLOT), jnp.float32),
        ],
        scratch_shapes=[
            pltpu.VMEM((D, LEN), low),
            pltpu.VMEM((D, LEN), low),
            pltpu.VMEM((LEN, D), jnp.float32),
            part,
            part,
            pltpu.VMEM((LEN, HIDDEN), low),
            pltpu.VMEM((LEN, HIDDEN), low),
            pltpu.VMEM((2, 2 * EARLY, 4, 2, 2, 64, HIDDEN), low),
            *summing_buffers(2 * EARLY),
            *spread_semaphores(2 * late),
            pltpu.SemaphoreType.DMA((2, 2)),
        ],
        compiler_params=pltpu.CompilerParams(
            collective_id=5, has_side_effects=True, vmem_limit_bytes=62 * 1024 * 1024
        ),
        cost_estimate=pl.CostEstimate(
            flops=12 * LEN * D * FF, bytes_accessed=60 * 1024 * 1024, transcendentals=LEN * FF
        ),
    )(rows, cot, base, bias, *split, slots)


SLOTS = 12
SLOT = 512
HALF_SLOT = SLOT // 2
TILE = 256
GRAM_TILES = 5
MESH_IDS = pl.DeviceIdType.MESH


def handler_of(slot):
    wide = slot - 4
    square = slot < 4
    dp_index = jnp.where(square, jnp.where(slot < 2, 2, 12), 4 + 6 * (wide // 4) + wide % 2)
    tensor_index = jnp.where(square, slot % 2, (wide // 2) % 2)
    return dp_index, tensor_index


def muon_kernel(
    moments_ref,
    vec_ref,
    block_ref,
    token_ref,
    updates_ref,
    vec_out_ref,
    block_pair_ref,
    token_pair_ref,
    pieces,
    turned,
    vec_pieces,
    vec_sum,
    gram,
    gram_low,
    poly_low,
    half_low,
    chain_low,
    chain_next,
    out_half,
    in_half,
    local_sem,
    send_sem,
    recv_sem,
    half_send,
    half_recv,
    swap_sem,
):
    groups = lax.axis_size("dp")
    parts = lax.axis_size("tensor")
    count = groups * parts
    dp_me = lax.axis_index("dp")
    t_me = lax.axis_index("tensor")
    me = t_me * groups + dp_me
    is_square = (dp_me == 2) | (dp_me == 12)
    is_up = (dp_me == 4) | (dp_me == 5)
    is_down = (dp_me == 10) | (dp_me == 11)
    is_wide = is_up | is_down
    is_handler = is_square | is_wide
    wide_slot = jnp.where(is_up, 4 + (dp_me - 4), 8 + (dp_me - 10)) + 2 * t_me
    slot_me = jnp.where(is_square, t_me + jnp.where(dp_me == 12, 2, 0), wide_slot)
    slot_me = jnp.where(is_handler, slot_me, 0)

    barrier = pltpu.get_barrier_semaphore()

    def greet(step, carry):
        other = lax.rem(me + step, count)
        pl.semaphore_signal(
            barrier, inc=1, device_id=(lax.rem(other, groups), other // groups), device_id_type=MESH_IDS
        )
        return carry

    lax.fori_loop(1, count, greet, 0)
    pl.semaphore_wait(barrier, count - 1)

    def give(step, carry):
        slot = lax.rem(me + step, SLOTS)
        dp_to, t_to = handler_of(slot)
        away = (dp_to != dp_me) | (t_to != t_me)

        @pl.when(away)
        def _():
            pltpu.make_async_remote_copy(
                src_ref=vec_ref.at[slot],
                dst_ref=vec_pieces.at[me],
                send_sem=send_sem.at[1],
                recv_sem=recv_sem.at[1],
                device_id=(dp_to, t_to),
                device_id_type=MESH_IDS,
            ).start()
            pltpu.make_async_remote_copy(
                src_ref=moments_ref.at[slot],
                dst_ref=pieces.at[me],
                send_sem=send_sem.at[0],
                recv_sem=recv_sem.at[0],
                device_id=(dp_to, t_to),
                device_id_type=MESH_IDS,
            ).start()

        return carry

    lax.fori_loop(0, SLOTS, give, 0)

    rows = block_ref.shape[0] // 2
    kept_rows = pl.ds(pl.multiple_of(t_me * rows, rows), rows)
    sent_rows = pl.ds(pl.multiple_of((1 - t_me) * rows, rows), rows)
    kept = []
    swaps = []
    for index, (whole, pair) in enumerate(((block_ref, block_pair_ref), (token_ref, token_pair_ref))):
        kept.append(pltpu.make_async_copy(whole.at[kept_rows], pair.at[t_me], swap_sem.at[2, index]))
        swaps.append(
            pltpu.make_async_remote_copy(
                src_ref=whole.at[sent_rows],
                dst_ref=pair.at[t_me],
                send_sem=swap_sem.at[0, index],
                recv_sem=swap_sem.at[1, index],
                device_id=(dp_me, 1 - t_me),
                device_id_type=MESH_IDS,
            )
        )

    @pl.when(jnp.logical_not(is_wide))
    def _():
        for copy in kept + swaps:
            copy.start()

    def give_back(source, sem, target):
        def one(step, carry):
            other = lax.rem(me + step, count)
            pltpu.make_async_remote_copy(
                src_ref=source.at[other] if source is turned else source,
                dst_ref=target.at[slot_me],
                send_sem=send_sem.at[sem],
                recv_sem=recv_sem.at[sem],
                device_id=(lax.rem(other, groups), other // groups),
                device_id_type=MESH_IDS,
            ).start()
            return carry

        lax.fori_loop(1, count, one, 0)

    @pl.when(is_handler)
    def _():
        own = [
            pltpu.make_async_copy(vec_ref.at[slot_me], vec_pieces.at[me], local_sem.at[0]),
            pltpu.make_async_copy(moments_ref.at[slot_me], pieces.at[me], local_sem.at[1]),
        ]
        for copy in own:
            copy.start()
        for copy in own:
            copy.wait()
        rest = pl.ds(0, count - 1)
        pltpu.make_async_copy(vec_pieces.at[rest], vec_pieces.at[rest], recv_sem.at[1]).wait()
        vec_sum[...] = jnp.sum(vec_pieces[...], axis=0)
        give_back(vec_sum, 2, vec_out_ref)
        own_vec = pltpu.make_async_copy(vec_sum, vec_out_ref.at[slot_me], local_sem.at[0])
        own_vec.start()
        own_vec.wait()
        pltpu.make_async_copy(pieces.at[rest], pieces.at[rest], recv_sem.at[0]).wait()

        rows_of = TILE // 64

        def gram_tile(tile, carry):
            rows = pl.ds(pl.multiple_of(tile * TILE, TILE), TILE)
            total = jnp.zeros((TILE, D), jnp.float32)
            for part in range(parts):
                left = pieces[pl.ds(part * groups + tile * rows_of, rows_of)].reshape(TILE, SLOT)
                right = pieces[part * groups : (part + 1) * groups].reshape(D, SLOT)
                total += lax.dot_general(
                    left, right, (((1,), (1,)), ((), ())), preferred_element_type=jnp.float32
                )
            gram[rows, :] = total
            return carry

        lax.fori_loop(0, D // TILE, gram_tile, 0)

        @pl.when(is_wide)
        def _():
            core = lax.rem(dp_me, 2)
            sibling = (dp_me + 1 - 2 * core, t_me)
            across = (dp_me, 1 - t_me)

            def tile_at(index, owner):
                if index == 4:
                    row, col = jnp.where(owner == 0, 3, 2), 3
                elif index == 3:
                    row, col = jnp.where(owner == 0, 0, 2), jnp.where(owner == 0, 3, 2)
                else:
                    row, col = owner, owner + index
                return (
                    pl.ds(pl.multiple_of(row * TILE, TILE), TILE),
                    pl.ds(pl.multiple_of(col * TILE, TILE), TILE),
                )

            def exchange(stage, index, place):
                return pltpu.make_async_remote_copy(
                    src_ref=out_half.at[stage, index],
                    dst_ref=in_half.at[stage, index],
                    send_sem=half_send.at[stage, index],
                    recv_sem=half_recv.at[stage, index],
                    device_id=place,
                    device_id_type=MESH_IDS,
                )

            for index in range(GRAM_TILES):
                out_half[0, index] = gram[tile_at(index, 1 - core)].astype(jnp.bfloat16)
                exchange(0, index, sibling).start()
            for index in range(GRAM_TILES):
                exchange(0, index, sibling).wait_recv()
                total = gram[tile_at(index, core)] + in_half[0, index].astype(jnp.float32)
                out_half[1, index] = total.astype(jnp.bfloat16)
                exchange(1, index, across).start()
            for index in range(GRAM_TILES):
                exchange(1, index, across).wait_recv()
                total = out_half[1, index].astype(jnp.float32) + in_half[1, index].astype(jnp.float32)
                out_half[2, index] = total.astype(jnp.bfloat16)
                exchange(2, index, sibling).start()
                rows, cols = tile_at(index, core)
                gram[cols, rows] = out_half[2, index].astype(jnp.float32).T
                gram[rows, cols] = out_half[2, index].astype(jnp.float32)
            for index in range(GRAM_TILES):
                exchange(2, index, sibling).wait_recv()
                rows, cols = tile_at(index, 1 - core)
                gram[cols, rows] = in_half[2, index].astype(jnp.float32).T
                gram[rows, cols] = in_half[2, index].astype(jnp.float32)
            for index in range(GRAM_TILES):
                exchange(0, index, sibling).wait_send()
                exchange(1, index, across).wait_send()
                exchange(2, index, sibling).wait_send()
            for copy in kept + swaps:
                copy.start()

        def trace_tile(tile, total):
            rows = pl.ds(pl.multiple_of(tile * TILE, TILE), TILE)
            row_ids = lax.broadcasted_iota(jnp.int32, (TILE, D), 0) + tile * TILE
            col_ids = lax.broadcasted_iota(jnp.int32, (TILE, D), 1)
            diagonal = jnp.where(row_ids == col_ids, gram[rows, :], 0.0)
            return total + jnp.sum(jnp.sum(diagonal, axis=0, keepdims=True), axis=1, keepdims=True)

        square_total = lax.fori_loop(0, D // TILE, trace_tile, jnp.zeros((1, 1), jnp.float32))
        factor = lax.rsqrt(square_total + SQUARE_EPSILON)
        gram_low[...] = (gram[...] * (factor * factor)).astype(jnp.bfloat16)

        first, second, third = SCHULZ_FIRST, SCHULZ_SECOND, SCHULZ_THIRD

        def tiles(body):
            def one(tile, carry):
                body(pl.ds(pl.multiple_of(tile * TILE, TILE), TILE))
                return carry

            lax.fori_loop(0, D // TILE, one, 0)

        chain = chain_low
        other = chain_next
        for sweep in range(NS_ITERS):
            target = chain if sweep == 0 else poly_low

            def poly(rows):
                square = mul(gram_low[rows, :], gram_low[...])
                grown = (second / first) * gram_low[rows, :].astype(jnp.float32) + (third / first) * square
                target[rows, :] = grown.astype(jnp.bfloat16)

            tiles(poly)
            if sweep > 0:

                def join(rows, chain=chain, other=other):
                    total = chain[rows, :].astype(jnp.float32) + poly_low[rows, :].astype(jnp.float32)
                    other[rows, :] = (total + mul(chain[rows, :], poly_low[...])).astype(jnp.bfloat16)

                tiles(join)
                chain, other = other, chain
            if sweep < NS_ITERS - 1:

                def half(rows):
                    grown = gram_low[rows, :].astype(jnp.float32) + mul(gram_low[rows, :], target[...])
                    half_low[rows, :] = grown.astype(jnp.bfloat16)

                def full(rows):
                    grown = half_low[rows, :].astype(jnp.float32) + mul(half_low[rows, :], target[...])
                    gram_low[rows, :] = (grown * (first * first)).astype(jnp.bfloat16)

                tiles(half)
                tiles(full)

        scale = factor * (first**NS_ITERS)

        def turn_tile(tile, carry):
            rows = pl.ds(pl.multiple_of(tile * TILE, TILE), TILE)
            for part in range(parts):
                at = pl.ds(part * groups + tile * rows_of, rows_of)
                whole = pieces[part * groups : (part + 1) * groups].reshape(D, SLOT)
                kept = pieces[at].reshape(TILE, SLOT).astype(jnp.float32)
                fresh = (kept + mul(chain[rows, :], whole)) * scale
                turned[at] = fresh.astype(jnp.bfloat16).reshape(rows_of, 64, SLOT)
            return carry

        lax.fori_loop(0, D // TILE, turn_tile, 0)
        give_back(turned, 3, updates_ref)
        own_turned = pltpu.make_async_copy(turned.at[me], updates_ref.at[slot_me], local_sem.at[1])
        own_turned.start()
        own_turned.wait()

    def finish(length):
        here = pl.ds(0, length)
        pltpu.make_async_copy(vec_ref.at[here], vec_ref.at[here], send_sem.at[1]).wait()
        pltpu.make_async_copy(moments_ref.at[here], moments_ref.at[here], send_sem.at[0]).wait()
        pltpu.make_async_copy(vec_out_ref.at[here], vec_out_ref.at[here], recv_sem.at[2]).wait()
        pltpu.make_async_copy(updates_ref.at[here], updates_ref.at[here], recv_sem.at[3]).wait()

    @pl.when(is_handler)
    def _():
        finish(SLOTS - 1)
        rest = pl.ds(0, count - 1)
        pltpu.make_async_copy(vec_pieces.at[rest], vec_pieces.at[rest], send_sem.at[2]).wait()
        pltpu.make_async_copy(turned.at[rest], turned.at[rest], send_sem.at[3]).wait()

    @pl.when(jnp.logical_not(is_handler))
    def _():
        finish(SLOTS)

    for copy in kept + swaps:
        copy.wait()


def muon_call(moments, vec_parts, block_rows, token_grads):
    count = lax.axis_size("dp") * lax.axis_size("tensor")
    rows = moments.shape[1]
    vmem = pl.BlockSpec(memory_space=pltpu.VMEM)
    anywhere = pl.BlockSpec(memory_space=pl.ANY)
    pair = jax.ShapeDtypeStruct((2, LEN // 2, D), jnp.bfloat16)
    low = pltpu.VMEM((D, D), jnp.bfloat16)
    return pl.pallas_call(
        muon_kernel,
        in_specs=[vmem, vmem, anywhere, anywhere],
        out_specs=[vmem, vmem, anywhere, anywhere],
        out_shape=[
            jax.ShapeDtypeStruct(moments.shape, jnp.bfloat16),
            jax.ShapeDtypeStruct(vec_parts.shape, jnp.float32),
            pair,
            pair,
        ],
        scratch_shapes=[
            pltpu.VMEM((count, rows, SLOT), jnp.bfloat16),
            pltpu.VMEM((count, rows, SLOT), jnp.bfloat16),
            pltpu.VMEM((count,) + vec_parts.shape[1:], jnp.float32),
            pltpu.VMEM(vec_parts.shape[1:], jnp.float32),
            pltpu.VMEM((D, D), jnp.float32),
            low,
            low,
            low,
            low,
            low,
            pltpu.VMEM((3, GRAM_TILES, TILE, TILE), jnp.bfloat16),
            pltpu.VMEM((3, GRAM_TILES, TILE, TILE), jnp.bfloat16),
            pltpu.SemaphoreType.DMA((2,)),
            pltpu.SemaphoreType.DMA((4,)),
            pltpu.SemaphoreType.DMA((4,)),
            pltpu.SemaphoreType.DMA((3, GRAM_TILES)),
            pltpu.SemaphoreType.DMA((3, GRAM_TILES)),
            pltpu.SemaphoreType.DMA((3, 2)),
        ],
        compiler_params=pltpu.CompilerParams(
            collective_id=1, has_side_effects=True, vmem_limit_bytes=VMEM_LIMIT
        ),
        cost_estimate=pl.CostEstimate(flops=12 * 2 * D**3, bytes_accessed=4 * 1024 * 1024, transcendentals=0),
    )(moments, vec_parts, block_rows, token_grads)


def neighbours():
    dp_me = lax.axis_index("dp")
    y = lax.axis_index("tensor")
    core = lax.rem(dp_me, 2)
    x = lax.rem(dp_me // 2, 2)
    z = dp_me // 4
    sibling = (dp_me + 1 - 2 * core, y)
    beside = (dp_me + 2 - 4 * x, y)
    across = (dp_me, 1 - y)
    stations = [(lax.rem(dp_me + 4 * hop, 16), y) for hop in (1, 2, 3)]
    return (z, x, core, y), sibling, beside, across, stations


def greet_neighbours(places):
    barrier = pltpu.get_barrier_semaphore()
    for place in places:
        pl.semaphore_signal(barrier, inc=1, device_id=place, device_id_type=MESH_IDS)
    pl.semaphore_wait(barrier, len(places))


EARLY = 2
AHEAD = 2


class Spread:
    def __init__(self, slots_ref, table, local_sem, send_sem, recv_sem):
        self.slots_ref, self.table = slots_ref, table
        self.local_sem, self.send_sem, self.recv_sem = local_sem, send_sem, recv_sem
        (self.z, self.x, self.core, self.y), self.sibling, self.beside, self.across, self.stations = neighbours()

    def remote(self, source, target, stage, slot, place):
        return pltpu.make_async_remote_copy(
            src_ref=source,
            dst_ref=target,
            send_sem=self.send_sem.at[stage, slot],
            recv_sem=self.recv_sem.at[stage, slot],
            device_id=place,
            device_id_type=MESH_IDS,
        )

    def own(self, slot):
        here = self.table[slot][0](self.y, 0, SLOT).at[self.z, self.x, self.core]
        return pltpu.make_async_copy(self.slots_ref.at[slot], here, self.local_sem.at[slot])

    def along_z(self, slot):
        here = self.table[slot][0](self.y, 0, SLOT).at[self.z, self.x, self.core]
        return [
            self.remote(self.slots_ref.at[slot], here, hop, slot, place)
            for hop, place in enumerate(self.stations)
        ]

    def second(self, slot):
        view, size = self.table[slot]
        copies = []
        if size:
            part = view(self.y, 0, size).at[:, self.x, self.core]
            copies.append(self.remote(part, part, 3, slot, self.beside))
        if size < SLOT:
            part = view(self.y, size, SLOT - size).at[:, self.x, self.core]
            copies.append(self.remote(part, part, 4, slot, self.across))
        return copies

    def third(self, slot):
        view, size = self.table[slot]
        copies = []
        if size:
            part = view(self.y, 0, size).at[:, :, self.core]
            copies.append(self.remote(part, part, 5, slot, self.across))
        if size < SLOT:
            for index in (0, 1):
                part = view(index, size, SLOT - size).at[:, self.x, self.core]
                copies.append(self.remote(part, part, 6 + index, slot, self.beside))
        return copies

    def fourth(self, slot):
        view, _ = self.table[slot]
        copies = []
        for index in (0, 1):
            part = view(index, 0, SLOT).at[:, :, self.core]
            copies.append(self.remote(part, part, 8 + index, slot, self.sibling))
        return copies

    def launch(self, slot):
        if slot < len(self.table):
            self.own(slot).start()
            for copy in self.along_z(slot):
                copy.start()

    def begin(self):
        for slot in range(AHEAD):
            self.launch(slot)

    def push_second(self, slot):
        self.own(slot).wait()
        for copy in self.along_z(slot):
            copy.wait_recv()
        for copy in self.second(slot):
            copy.start()

    def push_third(self, slot):
        for copy in self.second(slot):
            copy.wait_recv()
        for copy in self.third(slot):
            copy.start()

    def push_fourth(self, slot):
        for copy in self.third(slot):
            copy.wait_recv()
        for copy in self.fourth(slot):
            copy.start()

    def tick(self, index):
        count = len(self.table)
        self.launch(index + AHEAD)
        if index < count:
            self.push_second(index)
        if 0 <= index - 1 < count:
            self.push_third(index - 1)
        if 0 <= index - 2 < count:
            self.push_fourth(index - 2)

    def ticks(self):
        return len(self.table) + 2

    def arrived(self, slot):
        for copy in self.fourth(slot):
            copy.wait_recv()

    def sent(self):
        for slot in range(len(self.table)):
            for copy in self.along_z(slot) + self.second(slot) + self.third(slot) + self.fourth(slot):
                copy.wait_send()


def column_view(ref, column, distance):
    def view(part, start, size):
        first = column + part * distance + start
        if not isinstance(part, int):
            first = pl.multiple_of(first, 128)
        return ref.at[:, :, :, :, pl.ds(first, size)]

    return view


def place_view(ref, place):
    def view(part, start, size):
        return ref.at[place + part, :, :, :, :, pl.ds(start, size)]

    return view


def spread_semaphores(count):
    return [
        pltpu.SemaphoreType.DMA((count,)),
        pltpu.SemaphoreType.DMA((10, count)),
        pltpu.SemaphoreType.DMA((10, count)),
    ]


def pair_of(step):
    return (step % 2) * (PAIRS // 2) + step // 2


def attend_spread_kernel(
    starts_ref,
    slopes_ref,
    norm_ref,
    shifts_ref,
    tokens_ref,
    cotangent_ref,
    slots_ref,
    packed_ref,
    ctx_ref,
    exps_ref,
    stat_ref,
    normed_t_ref,
    rows_ref,
    qkv_ref,
    out_ref,
    up_ref,
    down_ref,
    got_ref,
    dist_ref,
    ctx_t,
    rows,
    normed,
    weights,
    local_sem,
    send_sem,
    recv_sem,
    swap_sem,
    load_sem,
):
    step = pl.program_id(0)
    pair = pair_of(step)
    table = [(column_view(qkv_ref, index * SLOT, 3 * SLOT), SLOT if index == 1 else 0) for index in range(3)]
    table += [(column_view(out_ref, 0, SLOT), 0)]
    for index in range(EARLY):
        for ref, over_x in ((up_ref, 0), (down_ref, HALF_SLOT if index else 0)):
            table += [(column_view(ref, index * SLOT, EARLY * SLOT), over_x)]
    count = len(table)
    spread = Spread(slots_ref, table, local_sem, send_sem, recv_sem)
    half_rows = pl.ds(pl.multiple_of(spread.y * (LEN // 2), LEN // 2), LEN // 2)
    own_rows = pltpu.make_async_copy(tokens_ref.at[spread.y], rows.at[half_rows], load_sem.at[2])

    def swap(source, target, index):
        return pltpu.make_async_remote_copy(
            src_ref=source.at[1 - spread.y],
            dst_ref=target,
            send_sem=swap_sem.at[0, index],
            recv_sem=swap_sem.at[1, index],
            device_id=spread.across,
            device_id_type=MESH_IDS,
        )

    token_swap = swap(tokens_ref, rows.at[half_rows], 0)
    cotangent_swap = swap(cotangent_ref, got_ref, 1)

    def load(at):
        cols = pl.ds(pl.multiple_of(pair_of(at) * (3 * PAIR), PAIR), 3 * PAIR)
        place = lax.rem(at, 2)
        return pltpu.make_async_copy(qkv_ref.at[:, :, :, :, cols], weights.at[place], load_sem.at[place])

    @pl.when(step == 0)
    def _():
        greet_neighbours([spread.sibling, spread.beside, spread.across] + spread.stations)
        own_rows.start()
        for slot in range(3):
            spread.launch(slot)
        spread.push_second(0)
        token_swap.start()
        spread.push_second(1)
        spread.push_third(0)
        spread.push_second(2)
        for slot in range(3, count):
            spread.launch(slot)
        layout_grid(starts_ref, dist_ref)
        spread.push_fourth(0)
        own_rows.wait()
        token_swap.wait_recv()
        spread.push_third(1)
        for index in range(LEN // CHUNK):
            here = slice(index * CHUNK, index * CHUNK + CHUNK)
            block = rows[here].astype(jnp.float32)
            low = layer_norm(block, norm_ref[0:1], norm_ref[1:2]).astype(jnp.bfloat16)
            normed[here] = low
            normed_t_ref[:, here] = low.T
            rows_ref[here] = rows[here]

    for slot in range(3):

        @pl.when(step == 2 * slot)
        def _(slot=slot):
            spread.arrived(slot)

    @pl.when(lax.rem(step, 2) == 0)
    def _():
        load(step).start()

    load(step).wait()

    def between():
        @pl.when(lax.rem(step, 2) == 0)
        def _():
            load(step + 1).start()

        moves = (
            ((), (), 3),
            ((1,), (2,), 4),
            ((), (3,), 5),
            ((2,), (4,), 6),
            ((3,), (5,), 7),
            ((4,), (6,), None),
            ((5,), (7,), None),
            ((6,), (), None),
        )
        for index, (fourth, third, fresh) in enumerate(moves):

            @pl.when(step == index)
            def _(index=index, fourth=fourth, third=third, fresh=fresh):
                for slot in fourth:
                    spread.push_fourth(slot)
                for slot in third:
                    spread.push_third(slot)
                if fresh is not None:
                    spread.push_second(fresh)
                if fresh == count - 1:
                    cotangent_swap.start()

    packed = mul(normed[...], weights[lax.rem(step, 2)].reshape(D, 3 * PAIR)) + shifts_ref[...]
    packed = packed.astype(jnp.bfloat16)
    packed_ref[...] = packed
    attend_pair(pair, slopes_ref, packed, dist_ref, ctx_ref, exps_ref, stat_ref, ctx_t, between)

    @pl.when(step == PAIRS - 1)
    def _():
        spread.push_fourth(count - 1)
        for slot in range(3, count):
            spread.arrived(slot)
        spread.sent()
        token_swap.wait_send()
        cotangent_swap.wait()


def whole_shape(columns):
    return jax.ShapeDtypeStruct((4, 2, 2, 64, columns), jnp.bfloat16)


def attend_spread(starts, slopes, norm_rows, shifts, tokens, cotangent, slots):
    anywhere = pl.BlockSpec(memory_space=pl.ANY)
    whole = pl.BlockSpec((LEN, D), lambda s: (0, 0), pipeline_mode=pl.Buffered(1))
    low = jnp.bfloat16
    packed, context, exps, stats, normed_t, rows, qkv, out, up, down, got = pl.pallas_call(
        attend_spread_kernel,
        grid=(PAIRS,),
        in_specs=[
            SCALARS,
            SCALARS,
            pl.BlockSpec((2, D), lambda s: (0, 0)),
            pl.BlockSpec((1, 3 * PAIR), lambda s: (0, pair_of(s))),
            anywhere,
            anywhere,
            anywhere,
        ],
        out_specs=[
            pl.BlockSpec((LEN, 3 * PAIR), lambda s: (0, pair_of(s))),
            pl.BlockSpec((LEN, PAIR), lambda s: (0, pair_of(s))),
            pl.BlockSpec((2, LEN, LEN), lambda s: (pair_of(s), 0, 0)),
            pl.BlockSpec((1, 2, LEN), lambda s: (pair_of(s), 0, 0)),
            whole,
            whole,
        ]
        + [anywhere] * 5,
        out_shape=[
            jax.ShapeDtypeStruct((LEN, 3 * D), low),
            jax.ShapeDtypeStruct((LEN, D), low),
            jax.ShapeDtypeStruct((H, LEN, LEN), low),
            jax.ShapeDtypeStruct((PAIRS, 2, LEN), jnp.float32),
            jax.ShapeDtypeStruct((D, LEN), low),
            jax.ShapeDtypeStruct((LEN, D), low),
            whole_shape(3 * D),
            whole_shape(D),
            whole_shape(2 * EARLY * SLOT),
            whole_shape(2 * EARLY * SLOT),
            jax.ShapeDtypeStruct(cotangent.shape[1:], low),
        ],
        scratch_shapes=[
            pltpu.VMEM((LEN, LEN), jnp.float32),
            pltpu.VMEM((PAIR, LEN), jnp.float32),
            pltpu.VMEM((LEN, D), low),
            pltpu.VMEM((LEN, D), low),
            pltpu.VMEM((2, 4, 2, 2, 64, 3 * PAIR), low),
        ]
        + spread_semaphores(4 + 2 * EARLY)
        + [pltpu.SemaphoreType.DMA((2, 2)), pltpu.SemaphoreType.DMA((3,))],
        compiler_params=pltpu.CompilerParams(
            collective_id=4, has_side_effects=True, vmem_limit_bytes=VMEM_LIMIT
        ),
        cost_estimate=pl.CostEstimate(
            flops=22 * LEN * LEN * D, bytes_accessed=90 * 1024 * 1024, transcendentals=H * LEN * LEN
        ),
    )(starts, slopes, norm_rows, shifts, tokens, cotangent, slots)
    wholes = [whole.reshape(D, -1) for whole in (qkv, out, up, down)]
    return packed, context, exps, stats, normed_t, rows, wholes, got


class Summing:
    def __init__(self, sources, add_own, buffers, total_ref, sems, lag, ready=0, hold=0):
        self.sources, self.add_own, self.total_ref, self.lag = sources, add_own, total_ref, lag
        self.ready, self.hold = ready, hold
        self.first, self.second_y, self.second_x, self.third, self.fourth = buffers
        self.send_sem, self.recv_sem = sems
        (self.z, self.x, self.core, self.y), self.sibling, self.beside, self.across, self.stations = neighbours()
        self.low_cols = pl.ds(0, HALF_SLOT)
        self.high_cols = pl.ds(HALF_SLOT, HALF_SLOT)

    def count(self):
        return len(self.sources)

    def remote(self, source, target, stage, slot, place):
        return pltpu.make_async_remote_copy(
            src_ref=source,
            dst_ref=target,
            send_sem=self.send_sem.at[stage, slot],
            recv_sem=self.recv_sem.at[stage, slot],
            device_id=place,
            device_id_type=MESH_IDS,
        )

    def landed(self, ref, stage, slot):
        pltpu.make_async_copy(ref, ref, self.recv_sem.at[stage, slot]).wait()

    def send_first(self, slot):
        for part in (0, 1):
            source = self.sources[slot](part).at[:, :, 1 - self.core]
            self.remote(source, self.first.at[slot, part], 0, slot, self.sibling).start()

    def second_copies(self, slot):
        for_y = self.first.at[slot, 1 - self.y, :, :, :, self.low_cols]
        for_x = self.first.at[slot, :, :, 1 - self.x, :, self.high_cols]
        return (
            self.remote(for_y, self.second_y.at[slot], 1, slot, self.across),
            self.remote(for_x, self.second_x.at[slot], 2, slot, self.beside),
        )

    def third_copies(self, slot):
        for_x = self.second_y.at[slot, :, 1 - self.x]
        for_y = self.second_x.at[slot, 1 - self.y]
        return (
            self.remote(for_x, self.third.at[slot, :, :, self.low_cols], 3, slot, self.beside),
            self.remote(for_y, self.third.at[slot, :, :, self.high_cols], 4, slot, self.across),
        )

    def fourth_copies(self, slot):
        return tuple(
            self.remote(
                self.third.at[slot, lax.rem(self.z + hop, 4)], self.fourth.at[slot, hop - 1], 4 + hop, slot, place
            )
            for hop, place in zip((1, 2, 3), self.stations)
        )

    def stage_one(self, slot):
        self.landed(self.first.at[slot], 0, slot)
        self.add_own(slot)
        for copy in self.second_copies(slot):
            copy.start()

    def stage_two(self, slot):
        first, second_y, second_x = self.first, self.second_y, self.second_x
        self.landed(second_y.at[slot], 1, slot)
        second_y[slot] = second_y[slot] + first[slot, self.y, :, :, :, :HALF_SLOT]
        self.landed(second_x.at[slot], 2, slot)
        second_x[slot] = second_x[slot] + first[slot, :, :, self.x, :, HALF_SLOT:]
        for copy in self.third_copies(slot):
            copy.start()

    def stage_three(self, slot):
        third = self.third
        self.landed(third.at[slot, :, :, self.low_cols], 3, slot)
        self.landed(third.at[slot, :, :, self.high_cols], 4, slot)
        third[slot, :, :, :HALF_SLOT] = third[slot, :, :, :HALF_SLOT] + self.second_y[slot, :, self.x]
        third[slot, :, :, HALF_SLOT:] = third[slot, :, :, HALF_SLOT:] + self.second_x[slot, self.y]
        for copy in self.fourth_copies(slot):
            copy.start()

    def stage_four(self, slot):
        total = self.third[slot, self.z].astype(jnp.float32)
        for hop in (1, 2, 3):
            self.landed(self.fourth.at[slot, hop - 1], 4 + hop, slot)
            total = total + self.fourth[slot, hop - 1].astype(jnp.float32)
        self.total_ref[slot] = total

    def ticks(self):
        return self.count() + self.hold + 3 * self.lag

    def tick(self, index):
        for slot in range(self.count()):
            entry = slot + (self.hold if slot >= self.ready else 0)
            pl.when(index == entry)(lambda slot=slot: self.stage_one(slot))
        for number, stage in enumerate((self.stage_two, self.stage_three, self.stage_four)):
            entry = index - (number + 1) * self.lag
            slot = jnp.where(entry < self.ready, entry, entry - self.hold)
            late = (entry >= self.ready + self.hold) & (slot < self.count())
            early = (entry >= 0) & (entry < self.ready)
            pl.when(early | late)(lambda stage=stage, slot=slot: stage(slot))

    def fixed_tick(self, index):
        for number, stage in enumerate((self.stage_one, self.stage_two, self.stage_three, self.stage_four)):
            slot = index - number * self.lag
            if 0 <= slot < self.count():
                stage(slot)

    def sent(self):
        def one(slot, carry):
            pltpu.make_async_copy(self.first.at[slot], self.first.at[slot], self.send_sem.at[0, slot]).wait()
            for copy in self.second_copies(slot) + self.third_copies(slot) + self.fourth_copies(slot):
                copy.wait_send()
            return carry

        lax.fori_loop(0, self.count(), one, 0)


def summing_buffers(count):
    rows, low = 64, jnp.bfloat16
    return [
        pltpu.VMEM((count, 2, 4, 2, rows, SLOT), low),
        pltpu.VMEM((count, 4, 2, rows, HALF_SLOT), low),
        pltpu.VMEM((count, 2, 4, rows, HALF_SLOT), low),
        pltpu.VMEM((count, 4, rows, SLOT), low),
        pltpu.VMEM((count, 3, rows, SLOT), low),
        pltpu.SemaphoreType.DMA((8, count)),
        pltpu.SemaphoreType.DMA((8, count)),
    ]


LAG = 2
READY = 5
LATE_SLOTS = 8
RING = 4


def block_view(ref, column):
    return ref.at[:, :, :, :, pl.ds(column, SLOT)]


def attend_bwd_half(half, scale, values, keys_t, parts, exps, sums):
    half_t, half_rows, half_queries, inner = parts
    dq_t, dk_sum, dv_sum = sums
    heads = slice(half * HD, half * HD + HD)
    for block in range(LEN // QB):
        span = min(LEN, QB * block + QB + PIECE)
        cols = slice(block * QB, block * QB + QB)
        weights = exps[:span, cols]
        grad_probs = mul(values[:span], half_t[:, cols])
        grad_scores = (weights.astype(jnp.float32) * (grad_probs - inner[:, cols])).astype(jnp.bfloat16)
        dv_sum[:span, :] += mul(weights, half_rows[cols])
        dk_sum[:span, :] += mul(grad_scores, half_queries[cols])
        dq_t[heads, cols] = mul(keys_t[heads, :span], grad_scores) * scale


def attend_sum_kernel(
    packed_ref,
    ctx_ref,
    grad_ref,
    stat_ref,
    weights_ref,
    normed_t_ref,
    exps_ref,
    up_ref,
    down_ref,
    out_ref,
    total_ref,
    grad_normed_ref,
    packed_sum_ref,
    exps,
    dq_t,
    dk_sum,
    dv_sum,
    grad_qkv,
    mine,
    first,
    second_y,
    second_x,
    third,
    fourth,
    send_sem,
    recv_sem,
    exps_sem,
    load_sem,
):
    pair = pl.program_id(0)
    width = up_ref.shape[-1] // 2
    sources = []
    for index in range(width // SLOT):
        for ref in (up_ref, down_ref):
            sources.append(lambda part, ref=ref, index=index: block_view(ref, part * width + index * SLOT))
    sources.append(lambda part: block_view(out_ref, part * SLOT))
    for index in range(3):
        sources.append(lambda part, index=index: block_view(grad_qkv, (part * 3 + index) * SLOT))

    def load(slot, part):
        block = sources[slot](part).at[:, :, summing.core]
        return pltpu.make_async_copy(block, mine.at[slot % RING, part], load_sem.at[slot % RING])

    def add_own(slot):
        if slot < READY:
            place = slot % RING
            pltpu.make_async_copy(mine.at[place], mine.at[place], load_sem.at[place]).wait()
            first[slot] = first[slot] + mine[place]
            if slot + RING < READY:
                for part in (0, 1):
                    load(slot + RING, part).start()
        else:
            for part in (0, 1):
                cols = pl.ds((part * 3 + slot - READY) * SLOT, SLOT)
                first[slot, part] = first[slot, part] + grad_qkv[:, :, summing.core, :, cols]

    buffers = (first, second_y, second_x, third, fourth)
    summing = Summing(sources, add_own, buffers, total_ref, (send_sem, recv_sem), LAG, READY, 1)

    def exps_load(head, half):
        return pltpu.make_async_copy(exps_ref.at[head], exps.at[half], exps_sem.at[half])

    @pl.when(pair == 0)
    def _():
        for half in (0, 1):
            exps_load(half, half).start()
        for slot in range(RING):
            for part in (0, 1):
                load(slot, part).start()
        greet_neighbours([summing.sibling, summing.beside, summing.across] + summing.stations)
        for slot in range(READY):
            summing.send_first(slot)
        grad_normed_ref[...] = jnp.zeros_like(grad_normed_ref)

    scale = 1.0 / math.sqrt(HD)
    queries = packed_ref[:, :PAIR]
    keys_t = packed_ref[:, PAIR : 2 * PAIR].T
    values = packed_ref[:, 2 * PAIR :]
    grads_t = grad_ref[...].T.astype(jnp.float32)
    context_t = ctx_ref[...].T.astype(jnp.float32)
    scaled = []
    inner_rows = []
    for half in (0, 1):
        heads = slice(half * HD, half * HD + HD)
        scaled.append(grads_t[heads] * stat_ref[0, half : half + 1, :])
        inner_rows.append(jnp.sum(scaled[half] * context_t[heads], axis=0, keepdims=True))
    scaled_t = jnp.concatenate(scaled, axis=0).astype(jnp.bfloat16)
    scaled_rows = scaled_t.T
    dk_sum[...] = jnp.zeros_like(dk_sum)
    dv_sum[...] = jnp.zeros_like(dv_sum)
    for half in (0, 1):
        exps_load(2 * pair + half, half).wait()
        parts = (
            only_rows(scaled_t, half),
            only_cols(scaled_rows, half),
            only_cols(queries, half),
            inner_rows[half],
        )
        attend_bwd_half(half, scale, values, keys_t, parts, exps.at[half], (dq_t, dk_sum, dv_sum))

        @pl.when(pair < PAIRS - 1)
        def _(half=half):
            exps_load(2 * pair + 2 + half, half).start()

        if half == 0:
            summing.tick(pair)
    grads = jnp.concatenate([dq_t[...].T, dk_sum[...] * scale, dv_sum[...]], axis=1).astype(jnp.bfloat16)
    packed_sum_ref[...] = jnp.sum(grads.astype(jnp.float32), axis=0, keepdims=True)
    cols = pl.ds(pl.multiple_of(pair * (3 * PAIR), PAIR), 3 * PAIR)
    grad_weights = mul(normed_t_ref[...], grads).astype(jnp.bfloat16)
    grad_qkv[:, :, :, :, cols] = grad_weights.reshape(4, 2, 2, 64, 3 * PAIR)
    grad_normed_ref[...] += dot_last(grads, weights_ref[...])

    for slot in range(READY, LATE_SLOTS):
        pl.when(pair == PAIRS - LATE_SLOTS + slot)(lambda slot=slot: summing.send_first(slot))

    @pl.when(pair == PAIRS - 1)
    def _():
        def late(index, carry):
            summing.tick(index)
            return carry

        lax.fori_loop(PAIRS, summing.ticks(), late, 0)
        summing.sent()


def attend_sum(packed, context, grad_context, stats, weights, normed_t, exps, grad_up, grad_down, grad_out):
    anywhere = pl.BlockSpec(memory_space=pl.ANY)
    rows = 64
    low = jnp.bfloat16
    once = pl.Buffered(1)
    tall = pl.BlockSpec((LEN, D), lambda p: (0, 0), pipeline_mode=once)
    split = [grad.reshape(4, 2, 2, rows, grad.shape[-1]) for grad in (grad_up, grad_down, grad_out)]
    return pl.pallas_call(
        attend_sum_kernel,
        grid=(PAIRS,),
        in_specs=[PACKED_COLS, PAIR_COLS, PAIR_COLS, PAIR_STAT, PACKED_COLS, tall] + [anywhere] * 4,
        out_specs=[
            pl.BlockSpec((LATE_SLOTS, rows, SLOT), lambda p: (0, 0, 0), pipeline_mode=once),
            tall,
            pl.BlockSpec((1, 3 * PAIR), lambda p: (0, p)),
        ],
        out_shape=[
            jax.ShapeDtypeStruct((LATE_SLOTS, rows, SLOT), jnp.float32),
            jax.ShapeDtypeStruct((LEN, D), jnp.float32),
            jax.ShapeDtypeStruct((1, 3 * D), jnp.float32),
        ],
        scratch_shapes=[
            pltpu.VMEM((2, LEN, LEN), low),
            pltpu.VMEM((PAIR, LEN), jnp.float32),
            pltpu.VMEM((LEN, PAIR), jnp.float32),
            pltpu.VMEM((LEN, PAIR), jnp.float32),
            pltpu.VMEM((4, 2, 2, rows, 3 * D), low),
            pltpu.VMEM((RING, 2, 4, 2, rows, SLOT), low),
            *summing_buffers(LATE_SLOTS),
            pltpu.SemaphoreType.DMA((2,)),
            pltpu.SemaphoreType.DMA((RING,)),
        ],
        compiler_params=pltpu.CompilerParams(
            collective_id=2, has_side_effects=True, vmem_limit_bytes=62 * 1024 * 1024
        ),
        cost_estimate=pl.CostEstimate(
            flops=44 * LEN * LEN * D, bytes_accessed=400 * 1024 * 1024, transcendentals=0
        ),
    )(packed, context, grad_context, stats, weights, normed_t, exps, *split)


ROWS = 256


def norm_pull(rows, grads, gain):
    centered = rows - jnp.mean(rows, axis=-1, keepdims=True)
    inverse = lax.rsqrt(jnp.mean(centered * centered, axis=-1, keepdims=True) + NORM_EPSILON)
    normed = centered * inverse
    scaled = grads * gain
    along = jnp.mean(scaled * normed, axis=-1, keepdims=True)
    pulled = inverse * (scaled - jnp.mean(scaled, axis=-1, keepdims=True) - normed * along)
    gain_sum = jnp.sum(grads * normed, axis=0, keepdims=True)
    return pulled, gain_sum, jnp.sum(grads, axis=0, keepdims=True)


def add_rows(sums_ref, rows):
    for index, row in enumerate(rows):
        sums_ref[index : index + 1, :] += row


def middle_kernel(
    middle_ref, grad_ref, cot_ref, ctx_ref, gain_ref, weights_ref, grad_middle_ref, grad_ctx_ref, grad_out_ref, sums_ref, low_t
):
    step = pl.program_id(0)

    @pl.when(step == 0)
    def _():
        sums_ref[...] = jnp.zeros_like(sums_ref)

    cot = cot_ref[...].astype(jnp.float32)
    pulled, gain_sum, shift_sum = norm_pull(middle_ref[...], grad_ref[...], gain_ref[...])
    grads = cot + pulled
    low = grads.astype(jnp.bfloat16)
    grad_middle_ref[...] = grads
    grad_ctx_ref[...] = mul(low, weights_ref[...]).astype(jnp.bfloat16)
    low_t[:, pl.ds(pl.multiple_of(step * ROWS, ROWS), ROWS)] = low.T
    grad_sum = jnp.sum(grads, axis=0, keepdims=True)
    add_rows(sums_ref, (gain_sum, shift_sum, grad_sum, jnp.sum(cot, axis=0, keepdims=True)))

    @pl.when(step == LEN // ROWS - 1)
    def _():
        grad_out_ref[...] = mul(low_t[...], ctx_ref[...]).astype(jnp.bfloat16)


def middle_backward(middle, grad_rows, cot, context, gain, weights):
    rows = pl.BlockSpec((ROWS, D), lambda s: (s, 0))
    whole = pl.BlockSpec((D, D), lambda s: (0, 0), pipeline_mode=pl.Buffered(1))
    row = pl.BlockSpec((1, D), lambda s: (0, 0))
    sums = pl.BlockSpec((8, D), lambda s: (0, 0))
    return pl.pallas_call(
        middle_kernel,
        grid=(LEN // ROWS,),
        in_specs=[rows, rows, rows, whole, row, whole],
        out_specs=[rows, rows, whole, sums],
        out_shape=[
            jax.ShapeDtypeStruct((LEN, D), jnp.float32),
            jax.ShapeDtypeStruct((LEN, D), jnp.bfloat16),
            jax.ShapeDtypeStruct((D, D), jnp.bfloat16),
            jax.ShapeDtypeStruct((8, D), jnp.float32),
        ],
        scratch_shapes=[pltpu.VMEM((D, LEN), jnp.bfloat16)],
        compiler_params=pltpu.CompilerParams(vmem_limit_bytes=VMEM_LIMIT),
        cost_estimate=pl.CostEstimate(flops=4 * LEN * D * D, bytes_accessed=24 * 1024 * 1024, transcendentals=0),
    )(middle, grad_rows, cot, context, gain, weights)


def token_kernel(rows_ref, grad_ref, grad_middle_ref, gain_ref, out_ref, sums_ref):
    @pl.when(pl.program_id(0) == 0)
    def _():
        sums_ref[...] = jnp.zeros_like(sums_ref)

    pulled, gain_sum, shift_sum = norm_pull(rows_ref[...].astype(jnp.float32), grad_ref[...], gain_ref[...])
    out_ref[...] = (grad_middle_ref[...] + pulled).astype(jnp.bfloat16)
    add_rows(sums_ref, (gain_sum, shift_sum))


def token_backward(rows_low, grad_rows, grad_middle, gain):
    rows = pl.BlockSpec((ROWS, D), lambda s: (s, 0))
    row = pl.BlockSpec((1, D), lambda s: (0, 0))
    sums = pl.BlockSpec((8, D), lambda s: (0, 0))
    return pl.pallas_call(
        token_kernel,
        grid=(LEN // ROWS,),
        in_specs=[rows, rows, rows, row],
        out_specs=[rows, sums],
        out_shape=[jax.ShapeDtypeStruct((LEN, D), jnp.bfloat16), jax.ShapeDtypeStruct((8, D), jnp.float32)],
        compiler_params=pltpu.CompilerParams(vmem_limit_bytes=VMEM_LIMIT),
        cost_estimate=pl.CostEstimate(flops=0, bytes_accessed=12 * 1024 * 1024, transcendentals=0),
    )(rows_low, grad_rows, grad_middle, gain)


def slot_rows(early_ref, late_ref, slot):
    index, kind = slot % 4, slot // 4
    if index < EARLY:
        return early_ref[2 * index + kind]
    return late_ref[2 * (index - EARLY) + kind]


def moment_kernel(
    early_ref,
    late_ref,
    m_qkv_ref,
    m_out_ref,
    m_up_ref,
    m_down_ref,
    g_qkv_ref,
    g_out_ref,
    g_up_ref,
    g_down_ref,
    n_qkv_ref,
    n_out_ref,
    n_up_ref,
    n_down_ref,
    slots_ref,
):
    first_packed = LATE_SLOTS - 3
    for pair in range(SLOT // PAIR):
        for part in range(3):
            column = (pair * 3 + part) * PAIR
            source = late_ref[first_packed + column // SLOT, :, column % SLOT : column % SLOT + PAIR]
            g_qkv_ref[part, :, pair * PAIR : (pair + 1) * PAIR] = source
    for part in range(3):
        moment = MOMENTUM_DECAY * m_qkv_ref[part] + g_qkv_ref[part]
        n_qkv_ref[part] = moment
        slots_ref[part] = moment.astype(jnp.bfloat16)
    grads = late_ref[first_packed - 1]
    g_out_ref[...] = grads
    moment = MOMENTUM_DECAY * m_out_ref[...] + grads
    n_out_ref[...] = moment
    slots_ref[3] = moment.astype(jnp.bfloat16)
    for kind, refs in enumerate(((m_up_ref, g_up_ref, n_up_ref), (m_down_ref, g_down_ref, n_down_ref))):
        old_ref, grads_ref, new_ref = refs
        for index in range(4):
            here = slice(index * SLOT, (index + 1) * SLOT)
            grads = slot_rows(early_ref, late_ref, 4 * kind + index)
            grads_ref[:, here] = grads
            moment = MOMENTUM_DECAY * old_ref[:, here] + grads
            new_ref[:, here] = moment
            slots_ref[4 + 4 * kind + index] = moment.astype(jnp.bfloat16)


def update_kernel(
    updates_ref,
    vec_sum_ref,
    w_qkv_ref,
    w_out_ref,
    w_up_ref,
    w_down_ref,
    vectors_ref,
    m_vec_ref,
    o_qkv_ref,
    o_out_ref,
    o_up_ref,
    o_down_ref,
    g_vec_ref,
    n_vec_ref,
    o_vec_ref,
):
    wide_rate = MATRIX_RATE * math.sqrt(FF / D)
    for part in range(3):
        o_qkv_ref[part] = w_qkv_ref[part] - MATRIX_RATE * updates_ref[part].astype(jnp.float32)
    o_out_ref[...] = w_out_ref[...] - MATRIX_RATE * updates_ref[3].astype(jnp.float32)
    for index in range(4):
        here = slice(index * SLOT, (index + 1) * SLOT)
        o_up_ref[:, here] = w_up_ref[:, here] - wide_rate * updates_ref[4 + index].astype(jnp.float32)
        o_down_ref[:, here] = w_down_ref[:, here] - wide_rate * updates_ref[8 + index].astype(jnp.float32)
    grads = vec_sum_ref[...]
    moment = MOMENTUM_DECAY * m_vec_ref[...] + grads
    square = jnp.mean(moment * moment, axis=1, keepdims=True)
    g_vec_ref[...] = grads
    n_vec_ref[...] = moment
    o_vec_ref[...] = vectors_ref[...] - VECTOR_RATE * moment * lax.rsqrt(square + SQUARE_EPSILON)


def like(arrays):
    return [jax.ShapeDtypeStruct(array.shape, jnp.float32) for array in arrays]


def features_first(arrays):
    qkv, out, up, down = arrays
    return qkv, out.T, up, down.T


def muon_step(early, late, vector_total, block_rows, token_grads, weights, vectors, momenta, m_vec):
    limit = pltpu.CompilerParams(vmem_limit_bytes=VMEM_LIMIT)
    weights, momenta = features_first(weights), features_first(momenta)
    slots_shape = jax.ShapeDtypeStruct((SLOTS,) + late.shape[1:], jnp.bfloat16)
    *stored, slots = pl.pallas_call(
        moment_kernel, out_shape=like(momenta) + like(momenta) + [slots_shape], compiler_params=limit
    )(early, late, *momenta)
    updates, vector_rows, output_pair, token_pair = muon_call(
        slots, vector_total.reshape(SLOTS, 8, 128), block_rows, token_grads
    )
    fresh = pl.pallas_call(
        update_kernel, out_shape=like(weights) + like([vectors] * 3), compiler_params=limit
    )(updates, vector_rows.reshape(12, D), *weights, vectors, m_vec)
    vector_grad, moment_vec, new_vec = fresh[4:]
    grads, moments, new = features_first(stored[:4]), features_first(stored[4:]), features_first(fresh[:4])
    return (output_pair, token_pair.astype(jnp.float32), *grads, vector_grad, *moments, moment_vec, *new, new_vec)


def by_slots(rows):
    return jnp.swapaxes(rows.reshape(rows.shape[0], -1, SLOT), 0, 1)


def narrow(rows):
    return rows.astype(jnp.bfloat16)


def contract(left, right, left_dim, right_dim):
    return lax.dot_general(
        left, right, (((left_dim,), (right_dim,)), ((), ())), preferred_element_type=jnp.float32
    )


def in_order(rank, own, got):
    return jnp.where(rank == 0, jnp.concatenate([own, got]), jnp.concatenate([got, own]))


def by_pairs(rows):
    count, height, width = rows.shape
    return jnp.transpose(rows.reshape(count, height, width // PAIR, PAIR), (1, 2, 0, 3)).reshape(height, -1)


def from_pairs(rows):
    height = rows.shape[0]
    return jnp.transpose(rows.reshape(height, -1, 3, PAIR), (2, 0, 1, 3)).reshape(3, height, -1)


def sequence_step(
    tokens,
    cotangent,
    piece_starts,
    w_qkv,
    w_out,
    w_up,
    w_down,
    vectors,
    m_qkv,
    m_out,
    m_up,
    m_down,
    m_vec,
):
    rank = lax.axis_index("tensor")
    slopes = jnp.exp2(-8.0 * jnp.arange(1, H + 1, dtype=jnp.float32) / H)
    starts = lax.dynamic_slice_in_dim(piece_starts[:, 0], rank, 1, 0)[0]
    own_cotangent = lax.dynamic_index_in_dim(cotangent, rank, 0, keepdims=False)

    shifts = by_pairs(jnp.stack([vectors[2], jnp.zeros((D,), jnp.float32), vectors[3]])[:, None])
    up_slots = by_slots(narrow(w_up))
    down_slots = by_slots(narrow(w_down).T)
    in_turn = jnp.stack([up_slots, down_slots], axis=1).reshape(2 * up_slots.shape[0], *up_slots.shape[1:])
    slots = jnp.concatenate([by_slots(by_pairs(narrow(w_qkv))), narrow(w_out).T[None], in_turn[: 2 * EARLY]])
    packed, context, exps, stats, normed_t, token_low, wholes, other_cotangent = attend_spread(
        starts, slopes, vectors[0:2], shifts, tokens, cotangent, slots
    )
    full_qkv, full_out, full_up, full_down = wholes
    token_rows = token_low.astype(jnp.float32)
    cotangent_low = in_order(rank, own_cotangent, other_cotangent)

    middle = token_rows + contract(context, full_out, 1, 1) + vectors[4]
    normed_two = narrow(layer_norm(middle, vectors[5], vectors[6]))
    block_rows, grad_normed_two, grad_up, grad_down, up_bias, early_sums = mlp_both(
        normed_two,
        cotangent_low,
        middle + vectors[11],
        vectors[7:11].reshape(1, FF),
        full_up,
        full_down,
        in_turn[2 * EARLY :],
    )
    grad_middle, grad_context, grad_out, middle_sums = middle_backward(
        middle, grad_normed_two, cotangent_low, context, vectors[5:6], full_out
    )
    sums, grad_normed_one, packed_grads = attend_sum(
        packed, context, grad_context, stats, full_qkv, normed_t, exps, grad_up, grad_down, grad_out
    )
    grad_token_low, token_sums = token_backward(token_low, grad_normed_one, grad_middle, vectors[0:1])
    packed_sums = from_pairs(packed_grads)[:, 0]
    vector_total = jnp.concatenate(
        [
            token_sums[0:2],
            packed_sums[0:1],
            packed_sums[2:3],
            middle_sums[2:3],
            middle_sums[0:2],
            up_bias.reshape(4, D),
            middle_sums[3:4],
        ]
    )
    weights = (w_qkv, w_out, w_up, w_down)
    momenta = (m_qkv, m_out, m_up, m_down)
    return muon_step(
        early_sums, sums, vector_total, block_rows, grad_token_low, weights, vectors, momenta, m_vec
    )


def solution(mesh):
    in_specs = (
        P(None, ("dp", "tensor"), None),
        P(None, ("dp", "tensor"), None),
        P(None, "dp", None),
        P(None, "dp", "tensor"),
        P("tensor", "dp"),
        P("dp", "tensor"),
        P("tensor", "dp"),
        P(),
        P(None, "dp", "tensor"),
        P("tensor", "dp"),
        P("dp", "tensor"),
        P("tensor", "dp"),
        P(),
    )
    out_specs = (
        P(None, ("dp", "tensor"), None),
        P(None, ("dp", "tensor"), None),
        P(None, "dp", "tensor"),
        P("tensor", "dp"),
        P("dp", "tensor"),
        P("tensor", "dp"),
        P(),
        P(None, "dp", "tensor"),
        P("tensor", "dp"),
        P("dp", "tensor"),
        P("tensor", "dp"),
        P(),
        P(None, "dp", "tensor"),
        P("tensor", "dp"),
        P("dp", "tensor"),
        P("tensor", "dp"),
        P(),
    )
    groups_fit = mesh.shape["tensor"] == MB and mesh.shape["dp"] == 16

    def pick(*arrays):
        if groups_fit and arrays[2].shape[1] == 1:
            return sequence_step(*arrays)
        return on_device(*arrays)

    return jax.shard_map(
        pick, mesh=mesh, in_specs=in_specs, out_specs=out_specs, check_vma=False
    )
```

```python
import math

import jax
import jax.numpy as jnp
from jax import lax
from jax.experimental import pallas as pl
from jax.experimental.pallas import tpu as pltpu
from jax.sharding import PartitionSpec as P

D = 1024
H = 16
HD = 64
FF = 4096
LEN = 1024
PIECE = 256
NPIECE = 2
MB = 2
NS_ITERS = 3


NORM_EPSILON = 1e-05
SQUARE_EPSILON = 1e-06
MASKED_SCORE = -1e30
SCHULZ_FIRST = 3.4445
SCHULZ_SECOND = -4.775
SCHULZ_THIRD = 2.0315
MOMENTUM_DECAY = 0.5
MATRIX_RATE = 0.5
VECTOR_RATE = 0.05


def layer_norm(inputs, gain_row, shift_row):
    average = jnp.mean(inputs, axis=-1, keepdims=True)
    centered = inputs - average
    variance = jnp.mean(centered * centered, axis=-1, keepdims=True)
    return centered * lax.rsqrt(variance + NORM_EPSILON) * gain_row + shift_row


def gelu_tanh(inputs):
    return jax.nn.gelu(inputs, approximate=True)


def score_layout(starts, slopes):
    positions = jnp.arange(LEN, dtype=jnp.int32)
    inside = (positions[None, :] >= starts[:, None]) & (
        positions[None, :] < starts[:, None] + PIECE
    )
    labels = jnp.arange(1, NPIECE + 1, dtype=jnp.int32)
    piece_label = jnp.sum(jnp.where(inside, labels[:, None], 0), axis=0)
    same_piece = (piece_label[:, None] == piece_label[None, :]) & (piece_label[:, None] > 0)
    visible = (positions[None, :] <= positions[:, None]) | same_piece
    distance = jnp.abs(positions[:, None] - positions[None, :]).astype(jnp.float32)
    penalty = -slopes[:, None, None] * distance[None, :, :]
    return (visible, penalty)


def head_scores(query_heads, key_heads, starts, slopes):
    visible, penalty = score_layout(starts, slopes)
    raw_scores = jnp.einsum(
        "qhd,khd->hqk", query_heads, key_heads, preferred_element_type=jnp.float32
    )
    scores = raw_scores * (1.0 / math.sqrt(HD)) + penalty
    return jnp.where(visible[None, :, :], scores, MASKED_SCORE)


def attend_forward(element, slopes):
    query_seq, key_seq, value_seq, starts = element
    heads_here = slopes.shape[0]
    query_heads = query_seq.reshape(LEN, heads_here, HD)
    key_heads = key_seq.reshape(LEN, heads_here, HD)
    value_heads = value_seq.reshape(LEN, heads_here, HD)
    scores = head_scores(query_heads, key_heads, starts, slopes)
    maximum = jnp.max(scores, axis=-1, keepdims=True)
    weights_raw = jnp.exp(scores - maximum)
    denominator = jnp.sum(weights_raw, axis=-1, keepdims=True)
    probabilities = weights_raw / denominator
    context = jnp.einsum(
        "hqk,khd->qhd",
        probabilities.astype(jnp.bfloat16),
        value_heads,
        preferred_element_type=jnp.float32,
    )
    logsum = (maximum + jnp.log(denominator))[..., 0]
    return (context.reshape(LEN, heads_here * HD), logsum)


def attend_backward(element, slopes):
    query_seq, key_seq, value_seq, context_grad, logsum, starts = element
    heads_here = slopes.shape[0]
    query_heads = query_seq.reshape(LEN, heads_here, HD)
    key_heads = key_seq.reshape(LEN, heads_here, HD)
    value_heads = value_seq.reshape(LEN, heads_here, HD)
    grad_heads = context_grad.reshape(LEN, heads_here, HD)
    scores = head_scores(query_heads, key_heads, starts, slopes)
    probabilities = jnp.exp(scores - logsum[..., None])
    grad_probs = jnp.einsum(
        "qhd,khd->hqk", grad_heads, value_heads, preferred_element_type=jnp.float32
    )
    inner_sum = jnp.sum(probabilities * grad_probs, axis=-1, keepdims=True)
    grad_scores = (probabilities * (grad_probs - inner_sum)).astype(jnp.bfloat16)
    scale_factor = 1.0 / math.sqrt(HD)
    grad_query = (
        jnp.einsum("hqk,khd->qhd", grad_scores, key_heads, preferred_element_type=jnp.float32)
        * scale_factor
    )
    grad_key = (
        jnp.einsum("hqk,qhd->khd", grad_scores, query_heads, preferred_element_type=jnp.float32)
        * scale_factor
    )
    grad_value = jnp.einsum(
        "hqk,qhd->khd",
        probabilities.astype(jnp.bfloat16),
        grad_heads,
        preferred_element_type=jnp.float32,
    )
    width_here = heads_here * HD
    return (
        grad_query.astype(jnp.bfloat16).reshape(LEN, width_here),
        grad_key.astype(jnp.bfloat16).reshape(LEN, width_here),
        grad_value.astype(jnp.bfloat16).reshape(LEN, width_here),
    )


def placed(values, offset, length):
    return lax.dynamic_update_slice_in_dim(jnp.zeros((length,), jnp.float32), values, offset, 0)


def accumulate(totals, addend):
    if totals is None:
        return addend
    return tuple((former + latter for former, latter in zip(totals, addend)))


def gram_term(narrow_rows, wide_rows):
    part_narrow = jnp.einsum(
        "mrc,mrd->cmd", narrow_rows, narrow_rows, preferred_element_type=jnp.float32
    )
    part_wide = jnp.einsum("mrc,mrd->cmd", wide_rows, wide_rows, preferred_element_type=jnp.float32)
    return jnp.concatenate([part_narrow, part_wide], axis=1)


def schulz_step(state, gram_matrix):
    turned = jnp.einsum("mrc,cmd->mrd", state, gram_matrix, preferred_element_type=jnp.float32)
    mixed = (SCHULZ_SECOND * state.astype(jnp.float32) + SCHULZ_THIRD * turned).astype(jnp.bfloat16)
    return (
        SCHULZ_FIRST * state.astype(jnp.float32)
        + jnp.einsum("mrc,cmd->mrd", mixed, gram_matrix, preferred_element_type=jnp.float32)
    ).astype(jnp.bfloat16)


def slice_term(source, weights, pattern):
    return jnp.einsum(pattern, source, weights, preferred_element_type=jnp.float32)


def on_device(
    tokens,
    cotangent,
    piece_starts,
    w_qkv,
    w_out,
    w_up,
    w_down,
    vectors,
    m_qkv,
    m_out,
    m_up,
    m_down,
    m_vec,
):
    tensor_count = lax.axis_size("tensor")
    tensor_rank = lax.axis_index("tensor")
    shard_rank = lax.axis_index("dp")
    heads_here = H // tensor_count
    width_here = heads_here * HD
    hidden_here = FF // tensor_count
    rows_here = tokens.shape[1]
    group_rows = rows_here * tensor_count
    seqs_here = piece_starts.shape[1]
    shard_rows = w_qkv.shape[1]
    head_ids = tensor_rank * heads_here + jnp.arange(heads_here, dtype=jnp.int32) + 1
    slopes = jnp.exp2(-8.0 * head_ids.astype(jnp.float32) / H)
    query_shift = lax.dynamic_slice_in_dim(vectors[2], tensor_rank * width_here, width_here, 0)
    value_shift = lax.dynamic_slice_in_dim(vectors[3], tensor_rank * width_here, width_here, 0)
    up_shift = lax.dynamic_slice_in_dim(
        vectors[7:11].reshape(FF), tensor_rank * hidden_here, hidden_here, 0
    )
    low_qkv = w_qkv.astype(jnp.bfloat16)
    low_out = w_out.astype(jnp.bfloat16)
    low_up = w_up.astype(jnp.bfloat16)
    low_down = w_down.astype(jnp.bfloat16)
    outputs_list = []
    input_grads = []
    vector_total = jnp.zeros((12, D), jnp.float32)
    grad_total = None

    def forward_one(element):
        return attend_forward(element, slopes)

    def backward_one(element):
        return attend_backward(element, slopes)

    for batch_index in range(MB):
        full_qkv, full_out, full_up, full_down = (
            lax.all_gather(low_qkv, "dp", axis=1, tiled=True),
            lax.all_gather(low_out, "dp", axis=1, tiled=True),
            lax.all_gather(low_up, "dp", axis=0, tiled=True),
            lax.all_gather(low_down, "dp", axis=1, tiled=True),
        )
        token_rows = tokens[batch_index].astype(jnp.float32)
        cotangent_rows = cotangent[batch_index]
        normed_one = layer_norm(token_rows, vectors[0], vectors[1])
        normed_all, cotangent_all = (
            lax.all_gather(normed_one.astype(jnp.bfloat16), "tensor", axis=0, tiled=True),
            lax.all_gather(cotangent_rows, "tensor", axis=0, tiled=True),
        )
        projected = jnp.einsum(
            "td,cde->cte", normed_all, full_qkv, preferred_element_type=jnp.float32
        )
        query_low = (projected[0] + query_shift).astype(jnp.bfloat16)
        key_low = projected[1].astype(jnp.bfloat16)
        value_low = (projected[2] + value_shift).astype(jnp.bfloat16)
        query_seqs = query_low.reshape(seqs_here, LEN, width_here)
        key_seqs = key_low.reshape(seqs_here, LEN, width_here)
        value_seqs = value_low.reshape(seqs_here, LEN, width_here)
        starts_here = piece_starts[batch_index]
        context_seq, logsum = lax.map(forward_one, (query_seqs, key_seqs, value_seqs, starts_here))
        context_low = context_seq.reshape(group_rows, width_here).astype(jnp.bfloat16)
        attended = lax.psum_scatter(
            slice_term(context_low, full_out, "tc,cd->td").astype(jnp.bfloat16),
            "tensor",
            scatter_dimension=0,
            tiled=True,
        ).astype(jnp.float32)
        middle = token_rows + attended + vectors[4]
        normed_two = layer_norm(middle, vectors[5], vectors[6])
        normed_two_all = lax.all_gather(
            normed_two.astype(jnp.bfloat16), "tensor", axis=0, tiled=True
        )
        before = jnp.dot(normed_two_all, full_up, preferred_element_type=jnp.float32) + up_shift
        activated = gelu_tanh(before).astype(jnp.bfloat16)
        expanded = lax.psum_scatter(
            slice_term(activated, full_down, "tf,fd->td").astype(jnp.bfloat16),
            "tensor",
            scatter_dimension=0,
            tiled=True,
        ).astype(jnp.float32)
        outputs_list.append((middle + expanded + vectors[11]).astype(jnp.bfloat16))
        grad_down = jnp.einsum(
            "tf,td->fd", activated, cotangent_all, preferred_element_type=jnp.float32
        )
        grad_activated = jnp.einsum(
            "td,fd->tf", cotangent_all, full_down, preferred_element_type=jnp.float32
        )
        gelu_pull = jax.vjp(gelu_tanh, before)[1]
        grad_before = gelu_pull(grad_activated)[0].astype(jnp.bfloat16)
        grad_up = jnp.einsum(
            "td,tf->df", normed_two_all, grad_before, preferred_element_type=jnp.float32
        )
        grad_normed_two = lax.psum_scatter(
            slice_term(grad_before, full_up, "tf,df->td").astype(jnp.bfloat16),
            "tensor",
            scatter_dimension=0,
            tiled=True,
        ).astype(jnp.float32)
        second_pull = jax.vjp(layer_norm, middle, vectors[5], vectors[6])[1]
        middle_from_norm, gain_two_grad, shift_two_grad = second_pull(grad_normed_two)
        grad_middle = cotangent_rows.astype(jnp.float32) + middle_from_norm
        grad_middle_all = lax.all_gather(
            grad_middle.astype(jnp.bfloat16), "tensor", axis=0, tiled=True
        )
        grad_out = jnp.einsum(
            "tc,td->cd", context_low, grad_middle_all, preferred_element_type=jnp.float32
        )
        grad_context = jnp.einsum(
            "td,cd->tc", grad_middle_all, full_out, preferred_element_type=jnp.float32
        ).astype(jnp.bfloat16)
        grad_query, grad_key, grad_value = lax.map(
            backward_one,
            (
                query_seqs,
                key_seqs,
                value_seqs,
                grad_context.reshape(seqs_here, LEN, width_here),
                logsum,
                starts_here,
            ),
        )
        grad_stack = jnp.stack(
            [
                grad_query.reshape(group_rows, width_here),
                grad_key.reshape(group_rows, width_here),
                grad_value.reshape(group_rows, width_here),
            ]
        )
        grad_qkv = jnp.einsum(
            "td,cte->cde", normed_all, grad_stack, preferred_element_type=jnp.float32
        )
        grad_normed_one = lax.psum_scatter(
            slice_term(grad_stack, full_qkv, "cte,cde->td").astype(jnp.bfloat16),
            "tensor",
            scatter_dimension=0,
            tiled=True,
        ).astype(jnp.float32)
        first_pull = jax.vjp(layer_norm, token_rows, vectors[0], vectors[1])[1]
        token_from_norm, gain_one_grad, shift_one_grad = first_pull(grad_normed_one)
        input_grads.append(grad_middle + token_from_norm)
        query_bias = jnp.sum(grad_stack[0], axis=0, dtype=jnp.float32)
        value_bias = jnp.sum(grad_stack[2], axis=0, dtype=jnp.float32)
        up_bias = jnp.sum(grad_before, axis=0, dtype=jnp.float32)
        head_rows = jnp.stack(
            [
                gain_one_grad,
                shift_one_grad,
                placed(query_bias, tensor_rank * width_here, D),
                placed(value_bias, tensor_rank * width_here, D),
                jnp.sum(grad_middle, axis=0),
                gain_two_grad,
                shift_two_grad,
            ]
        )
        up_rows = placed(up_bias, tensor_rank * hidden_here, FF).reshape(4, D)
        tail_row = jnp.sum(cotangent_rows, axis=0, dtype=jnp.float32)[None, :]
        vector_total = vector_total + jnp.concatenate([head_rows, up_rows, tail_row], axis=0)
        shard_grads = (
            lax.psum_scatter(
                grad_qkv.astype(jnp.bfloat16), "dp", scatter_dimension=1, tiled=True
            ).astype(jnp.float32),
            lax.psum_scatter(
                grad_out.astype(jnp.bfloat16), "dp", scatter_dimension=1, tiled=True
            ).astype(jnp.float32),
            lax.psum_scatter(
                grad_up.astype(jnp.bfloat16), "dp", scatter_dimension=0, tiled=True
            ).astype(jnp.float32),
            lax.psum_scatter(
                grad_down.astype(jnp.bfloat16), "dp", scatter_dimension=1, tiled=True
            ).astype(jnp.float32),
        )
        grad_total = accumulate(grad_total, shard_grads)
    grad_qkv_shard, grad_out_shard, grad_up_shard, grad_down_shard = grad_total
    moment_qkv = MOMENTUM_DECAY * m_qkv + grad_qkv_shard
    moment_out = MOMENTUM_DECAY * m_out + grad_out_shard
    moment_up = MOMENTUM_DECAY * m_up + grad_up_shard
    moment_down = MOMENTUM_DECAY * m_down + grad_down_shard
    squares = jnp.concatenate(
        [
            jnp.sum(moment_qkv * moment_qkv, axis=(1, 2)),
            jnp.stack(
                [
                    jnp.sum(moment_out * moment_out),
                    jnp.sum(moment_up * moment_up),
                    jnp.sum(moment_down * moment_down),
                ]
            ),
        ]
    )
    vector_grad, square_total = lax.psum((vector_total, squares), ("dp", "tensor"))
    factors = lax.rsqrt(square_total + SQUARE_EPSILON)
    scaled_qkv = (moment_qkv * factors[0:3][:, None, None]).astype(jnp.bfloat16)
    scaled_out = (moment_out * factors[3]).astype(jnp.bfloat16)
    scaled_up = (moment_up * factors[4]).astype(jnp.bfloat16)
    scaled_down = (moment_down * factors[5]).astype(jnp.bfloat16)
    gathered_qkv, gathered_out, gathered_up, gathered_down = (
        lax.all_gather(scaled_qkv, "dp", axis=1, tiled=True),
        lax.all_gather(scaled_out, "dp", axis=1, tiled=True),
        lax.all_gather(scaled_up, "dp", axis=0, tiled=True),
        lax.all_gather(scaled_down, "dp", axis=1, tiled=True),
    )
    offset = shard_rank * shard_rows
    narrow_rows = jnp.concatenate([jnp.swapaxes(gathered_qkv, 1, 2), gathered_out[None]], axis=0)
    wide_rows = jnp.stack([gathered_up.T, gathered_down])
    for sweep_index in range(NS_ITERS):
        gram_share = lax.psum_scatter(
            gram_term(narrow_rows, wide_rows).astype(jnp.bfloat16),
            "tensor",
            scatter_dimension=0,
            tiled=True,
        )
        gram_matrix = lax.all_gather(gram_share, "tensor", axis=0, tiled=True)
        narrow_rows = schulz_step(narrow_rows, gram_matrix[:, 0:4])
        wide_rows = schulz_step(wide_rows, gram_matrix[:, 4:6])
    final_narrow = narrow_rows.astype(jnp.float32)
    final_wide = wide_rows.astype(jnp.float32)
    update_qkv = lax.dynamic_slice_in_dim(
        jnp.swapaxes(final_narrow[0:3], 1, 2), offset, shard_rows, 1
    )
    update_out = lax.dynamic_slice_in_dim(final_narrow[3], offset, shard_rows, 1)
    update_up = lax.dynamic_slice_in_dim(final_wide[0].T, offset, shard_rows, 0)
    update_down = lax.dynamic_slice_in_dim(final_wide[1], offset, shard_rows, 1)
    wide_factor = math.sqrt(FF / D)
    new_qkv = w_qkv - MATRIX_RATE * update_qkv
    new_out = w_out - MATRIX_RATE * update_out
    new_up = w_up - MATRIX_RATE * wide_factor * update_up
    new_down = w_down - MATRIX_RATE * wide_factor * update_down
    moment_vec = MOMENTUM_DECAY * m_vec + vector_grad
    new_vec = vectors - VECTOR_RATE * moment_vec * lax.rsqrt(
        jnp.mean(moment_vec * moment_vec, axis=1, keepdims=True) + SQUARE_EPSILON
    )
    return (
        jnp.stack(outputs_list),
        jnp.stack(input_grads),
        grad_qkv_shard,
        grad_out_shard,
        grad_up_shard,
        grad_down_shard,
        vector_grad,
        moment_qkv,
        moment_out,
        moment_up,
        moment_down,
        moment_vec,
        new_qkv,
        new_out,
        new_up,
        new_down,
        new_vec,
    )


QB = 256
PAIR = 2 * HD
PAIRS = D // PAIR
VMEM_LIMIT = 56 * 1024 * 1024


def layout_grid(starts_ref, dist_ref):
    key_pos = lax.broadcasted_iota(jnp.int32, (LEN, LEN), 0)
    query_pos = lax.broadcasted_iota(jnp.int32, (LEN, LEN), 1)
    gap = query_pos - key_pos
    visible = gap >= 0
    for piece in range(NPIECE):
        start = starts_ref[piece]
        inside_key = (key_pos >= start) & (key_pos < start + PIECE)
        inside_query = (query_pos >= start) & (query_pos < start + PIECE)
        visible = visible | (inside_key & inside_query)
    dist_ref[...] = jnp.where(visible, jnp.abs(gap).astype(jnp.float32), -MASKED_SCORE)


def only_rows(pair, half):
    rows = lax.broadcasted_iota(jnp.int32, pair.shape, 0)
    return jnp.where((rows >= HD) if half else (rows < HD), pair, jnp.zeros_like(pair))


def only_cols(pair, half):
    cols = lax.broadcasted_iota(jnp.int32, pair.shape, 1)
    return jnp.where((cols >= HD) if half else (cols < HD), pair, jnp.zeros_like(pair))


def mul(left, right):
    return jnp.dot(left, right, preferred_element_type=jnp.float32)


def attend_pair(pair, slopes_ref, packed, dist_ref, ctx_ref, exps_ref, stat_ref, ctx_t, between):
    keys = packed[:, PAIR : 2 * PAIR]
    values_t = packed[:, 2 * PAIR :].T
    queries_t = (packed[:, :PAIR] * (1.0 / math.sqrt(HD))).T
    for half in (0, 1):
        slope = slopes_ref[2 * pair + half]
        queries = only_rows(queries_t, half)
        heads = slice(half * HD, half * HD + HD)
        for block in range(LEN // QB):
            span = min(LEN, QB * block + QB + PIECE)
            cols = slice(block * QB, block * QB + QB)
            scores = mul(keys[:span], queries[:, cols]) - slope * dist_ref[:span, cols]
            top = jnp.max(scores, axis=0, keepdims=True)
            raw = jnp.exp(scores - top)
            inverse = 1.0 / jnp.sum(raw, axis=0, keepdims=True)
            low = raw.astype(jnp.bfloat16)
            exps_ref[half, :span, cols] = low
            ctx_t[heads, cols] = mul(values_t[heads, :span], low) * inverse
            stat_ref[0, half : half + 1, cols] = inverse
        if half == 0:
            between()
    ctx_ref[...] = ctx_t[...].T.astype(jnp.bfloat16)


PACKED_COLS = pl.BlockSpec((LEN, 3 * PAIR), lambda p: (0, p))
PAIR_COLS = pl.BlockSpec((LEN, PAIR), lambda p: (0, p))
PAIR_GRID = pl.BlockSpec((2, LEN, LEN), lambda p: (p, 0, 0))
PAIR_STAT = pl.BlockSpec((1, 2, LEN), lambda p: (p, 0, 0))
SCALARS = pl.BlockSpec(memory_space=pltpu.SMEM)


HIDDEN = 512
CHUNK = 256
HIDDEN_STEPS = FF // HIDDEN
GELU_SLOPE = math.sqrt(2.0 / math.pi)
GELU_CUBE = 0.044715


def dot_last(left, right):
    return lax.dot_general(left, right, (((1,), (1,)), ((), ())), preferred_element_type=jnp.float32)


def gelu_both(rows):
    square = rows * rows
    bent = jnp.tanh(rows * (GELU_SLOPE + GELU_SLOPE * GELU_CUBE * square))
    half = 0.5 + 0.5 * bent
    slope = half + 0.5 * rows * (1.0 - bent * bent) * (GELU_SLOPE + 3.0 * GELU_SLOPE * GELU_CUBE * square)
    return rows * half, slope


def hidden_block(step):
    return (step % 2) * (HIDDEN_STEPS // 2) + step // 2


def mlp_kernel(
    rows_ref,
    cot_ref,
    base_ref,
    last_ref,
    bias_ref,
    up_ref,
    down_ref,
    slots_ref,
    block_ref,
    grad_rows_ref,
    grad_up_ref,
    grad_down_ref,
    bias_sum_ref,
    total_ref,
    rows_t,
    cot_t,
    total,
    up_part,
    down_part,
    active,
    grad_before,
    grad_early,
    first,
    second_y,
    second_x,
    third,
    fourth,
    sum_send,
    sum_recv,
    local_sem,
    spread_send,
    spread_recv,
    load_sem,
):
    step = pl.program_id(0)
    early_steps = 2 * EARLY
    table = []
    for index in range(HIDDEN_STEPS // 2 - EARLY):
        table += [(place_view(ref, 2 + 2 * index), HALF_SLOT) for ref in (up_part, down_part)]
    spread = Spread(slots_ref, table, local_sem, spread_send, spread_recv)

    def early_block(slot, part):
        return grad_early.at[slot % 2, 2 * (slot // 2) + part]

    def add_own(slot):
        for part in (0, 1):
            first[slot, part] = first[slot, part] + grad_early[slot % 2, 2 * (slot // 2) + part, :, :, summing.core]

    sources = [lambda part, slot=slot: early_block(slot, part) for slot in range(2 * EARLY)]
    buffers = (first, second_y, second_x, third, fourth)
    summing = Summing(sources, add_own, buffers, total_ref, (sum_send, sum_recv), 1)

    def loads(at):
        column = lax.rem(at, 2) * EARLY + at // 2
        cols = pl.ds(pl.multiple_of(column * HIDDEN, HIDDEN), HIDDEN)
        place = lax.rem(at, 2)
        return (
            pltpu.make_async_copy(up_ref.at[:, :, :, :, cols], up_part.at[place], load_sem.at[0, place]),
            pltpu.make_async_copy(down_ref.at[:, :, :, :, cols], down_part.at[place], load_sem.at[1, place]),
        )

    def sum_moves(moment):
        stages = (summing.stage_one, summing.stage_two, summing.stage_three, summing.stage_four)
        for slot in range(summing.count()):
            entry = 4 * (slot // 2 + 1) + slot % 2
            for number, stage in enumerate(stages):
                if moment == entry + 2 * number:
                    stage(slot)

    @pl.when(step == 0)
    def _():
        for copy in loads(step):
            copy.start()
        greet_neighbours([spread.sibling, spread.beside, spread.across] + spread.stations)
        spread.begin()
        rows_t[...] = rows_ref[...].T
        cot_t[...] = cot_ref[...].T
        total[...] = base_ref[...] + last_ref[...]
        grad_rows_ref[...] = jnp.zeros_like(grad_rows_ref)

    @pl.when(step < early_steps)
    def _():
        for copy in loads(step):
            copy.wait()

    @pl.when(step < early_steps - 1)
    def _():
        for copy in loads(step + 1):
            copy.start()

    for index in range(HIDDEN_STEPS // 2 - EARLY):

        @pl.when(step == early_steps + 2 * index)
        def _(index=index):
            spread.arrived(2 * index)
            spread.arrived(2 * index + 1)

    place = jnp.where(step < early_steps, lax.rem(step, 2), step - early_steps + 2)
    up = up_part[place].reshape(D, HIDDEN)
    down = down_part[place].reshape(D, HIDDEN)
    bias = bias_ref[...]
    bias_sum = jnp.zeros((1, HIDDEN), jnp.float32)
    for index in range(LEN // CHUNK):
        here = slice(index * CHUNK, index * CHUNK + CHUNK)
        value, slope = gelu_both(mul(rows_ref[here], up) + bias)
        value = value.astype(jnp.bfloat16)
        grads = (slope * mul(cot_ref[here], down)).astype(jnp.bfloat16)
        active[here] = value
        grad_before[here] = grads
        bias_sum += jnp.sum(grads.astype(jnp.float32), axis=0, keepdims=True)
        total[here] += dot_last(value, down)
        grad_rows_ref[here] += dot_last(grads, up)
        if index == LEN // CHUNK // 2 - 1:
            for number in range(spread.ticks()):
                pl.when(step == number)(lambda number=number: spread.tick(number))
            for number in range(HIDDEN_STEPS):
                pl.when(step == number)(lambda number=number: sum_moves(2 * number))
    bias_sum_ref[...] = bias_sum

    @pl.when(step < early_steps)
    def _():
        for index, (left, right) in enumerate(((rows_t, grad_before), (cot_t, active))):
            grads = mul(left[...], right[...]).astype(jnp.bfloat16)
            grad_early[index, step] = grads.reshape(grad_early.shape[2:])

    @pl.when(step >= early_steps)
    def _():
        grad_up_ref[...] = mul(rows_t[...], grad_before[...]).astype(jnp.bfloat16)
        grad_down_ref[...] = mul(cot_t[...], active[...]).astype(jnp.bfloat16)

    for number in range(HIDDEN_STEPS):

        @pl.when(step == number)
        def _(number=number):
            if number < early_steps and number % 2:
                summing.send_first(number - 1)
                summing.send_first(number)
            sum_moves(2 * number + 1)

    @pl.when(step == HIDDEN_STEPS - 1)
    def _():
        block_ref[...] = total[...].astype(jnp.bfloat16)
        summing.sent()
        spread.sent()


def late_block(step):
    late = HIDDEN_STEPS // 2 - EARLY
    return jnp.where(step < 2 * EARLY, 0, (step % 2) * late + step // 2 - EARLY)


def mlp_both(rows, cot, base, last, bias, up, down, slots):
    anywhere = pl.BlockSpec(memory_space=pl.ANY)
    once = pl.Buffered(1)
    whole = pl.BlockSpec((LEN, D), lambda s: (0, 0), pipeline_mode=once)
    hidden = pl.BlockSpec((D, HIDDEN), lambda s: (0, late_block(s)))
    hidden_row = pl.BlockSpec((1, HIDDEN), lambda s: (0, hidden_block(s)))
    low = jnp.bfloat16
    late = HIDDEN_STEPS // 2 - EARLY
    part = pltpu.VMEM((2 + 2 * late, 4, 2, 2, 64, HIDDEN), low)
    split = [weights.reshape(4, 2, 2, 64, -1) for weights in (up, down)]
    return pl.pallas_call(
        mlp_kernel,
        grid=(HIDDEN_STEPS,),
        in_specs=[whole, whole, whole, pl.BlockSpec((1, D), lambda s: (0, 0)), hidden_row, anywhere, anywhere, anywhere],
        out_specs=[
            whole,
            whole,
            hidden,
            hidden,
            hidden_row,
            pl.BlockSpec((2 * EARLY, 64, SLOT), lambda s: (0, 0, 0), pipeline_mode=once),
        ],
        out_shape=[
            jax.ShapeDtypeStruct((LEN, D), low),
            jax.ShapeDtypeStruct((LEN, D), jnp.float32),
            jax.ShapeDtypeStruct((D, 2 * late * HIDDEN), low),
            jax.ShapeDtypeStruct((D, 2 * late * HIDDEN), low),
            jax.ShapeDtypeStruct((1, FF), jnp.float32),
            jax.ShapeDtypeStruct((2 * EARLY, 64, SLOT), jnp.float32),
        ],
        scratch_shapes=[
            pltpu.VMEM((D, LEN), low),
            pltpu.VMEM((D, LEN), low),
            pltpu.VMEM((LEN, D), jnp.float32),
            part,
            part,
            pltpu.VMEM((LEN, HIDDEN), low),
            pltpu.VMEM((LEN, HIDDEN), low),
            pltpu.VMEM((2, 2 * EARLY, 4, 2, 2, 64, HIDDEN), low),
            *summing_buffers(2 * EARLY),
            *spread_semaphores(2 * late),
            pltpu.SemaphoreType.DMA((2, 2)),
        ],
        compiler_params=pltpu.CompilerParams(
            collective_id=5, has_side_effects=True, vmem_limit_bytes=62 * 1024 * 1024
        ),
        cost_estimate=pl.CostEstimate(
            flops=12 * LEN * D * FF, bytes_accessed=60 * 1024 * 1024, transcendentals=LEN * FF
        ),
    )(rows, cot, base, last, bias, *split, slots)


SLOTS = 12
SLOT = 512
HALF_SLOT = SLOT // 2
TILE = 256
GRAM_TILES = 5
MESH_IDS = pl.DeviceIdType.MESH


def handler_of(slot):
    wide = slot - 4
    square = slot < 4
    dp_index = jnp.where(square, jnp.where(slot < 2, 2, 12), 4 + 6 * (wide // 4) + wide % 2)
    tensor_index = jnp.where(square, slot % 2, (wide // 2) % 2)
    return dp_index, tensor_index


def muon_kernel(
    moments_ref,
    vec_ref,
    block_ref,
    token_ref,
    updates_ref,
    vec_out_ref,
    block_pair_ref,
    token_pair_ref,
    pieces,
    turned,
    vec_pieces,
    vec_sum,
    gram,
    gram_low,
    poly_low,
    half_low,
    chain_low,
    chain_next,
    out_half,
    in_half,
    local_sem,
    send_sem,
    recv_sem,
    half_send,
    half_recv,
    swap_sem,
):
    groups = lax.axis_size("dp")
    parts = lax.axis_size("tensor")
    count = groups * parts
    dp_me = lax.axis_index("dp")
    t_me = lax.axis_index("tensor")
    me = t_me * groups + dp_me
    is_square = (dp_me == 2) | (dp_me == 12)
    is_up = (dp_me == 4) | (dp_me == 5)
    is_down = (dp_me == 10) | (dp_me == 11)
    is_wide = is_up | is_down
    is_handler = is_square | is_wide
    wide_slot = jnp.where(is_up, 4 + (dp_me - 4), 8 + (dp_me - 10)) + 2 * t_me
    slot_me = jnp.where(is_square, t_me + jnp.where(dp_me == 12, 2, 0), wide_slot)
    slot_me = jnp.where(is_handler, slot_me, 0)

    barrier = pltpu.get_barrier_semaphore()

    def greet(step, carry):
        other = lax.rem(me + step, count)
        pl.semaphore_signal(
            barrier, inc=1, device_id=(lax.rem(other, groups), other // groups), device_id_type=MESH_IDS
        )
        return carry

    lax.fori_loop(1, count, greet, 0)
    pl.semaphore_wait(barrier, count - 1)

    def give(step, carry):
        slot = lax.rem(me + step, SLOTS)
        dp_to, t_to = handler_of(slot)
        away = (dp_to != dp_me) | (t_to != t_me)

        @pl.when(away)
        def _():
            pltpu.make_async_remote_copy(
                src_ref=vec_ref.at[slot],
                dst_ref=vec_pieces.at[me],
                send_sem=send_sem.at[1],
                recv_sem=recv_sem.at[1],
                device_id=(dp_to, t_to),
                device_id_type=MESH_IDS,
            ).start()
            pltpu.make_async_remote_copy(
                src_ref=moments_ref.at[slot],
                dst_ref=pieces.at[me],
                send_sem=send_sem.at[0],
                recv_sem=recv_sem.at[0],
                device_id=(dp_to, t_to),
                device_id_type=MESH_IDS,
            ).start()

        return carry

    lax.fori_loop(0, SLOTS, give, 0)

    rows = block_ref.shape[0] // 2
    kept_rows = pl.ds(pl.multiple_of(t_me * rows, rows), rows)
    sent_rows = pl.ds(pl.multiple_of((1 - t_me) * rows, rows), rows)
    kept = []
    swaps = []
    for index, (whole, pair) in enumerate(((block_ref, block_pair_ref), (token_ref, token_pair_ref))):
        kept.append(pltpu.make_async_copy(whole.at[kept_rows], pair.at[t_me], swap_sem.at[2, index]))
        swaps.append(
            pltpu.make_async_remote_copy(
                src_ref=whole.at[sent_rows],
                dst_ref=pair.at[t_me],
                send_sem=swap_sem.at[0, index],
                recv_sem=swap_sem.at[1, index],
                device_id=(dp_me, 1 - t_me),
                device_id_type=MESH_IDS,
            )
        )

    for copy in kept:
        copy.start()

    @pl.when(jnp.logical_not(is_wide))
    def _():
        for copy in swaps:
            copy.start()

    def give_back(source, sem, target):
        def one(step, carry):
            other = lax.rem(me + step, count)
            pltpu.make_async_remote_copy(
                src_ref=source.at[other] if source is turned else source,
                dst_ref=target.at[slot_me],
                send_sem=send_sem.at[sem],
                recv_sem=recv_sem.at[sem],
                device_id=(lax.rem(other, groups), other // groups),
                device_id_type=MESH_IDS,
            ).start()
            return carry

        lax.fori_loop(1, count, one, 0)

    @pl.when(is_handler)
    def _():
        own = [
            pltpu.make_async_copy(vec_ref.at[slot_me], vec_pieces.at[me], local_sem.at[0]),
            pltpu.make_async_copy(moments_ref.at[slot_me], pieces.at[me], local_sem.at[1]),
        ]
        for copy in own:
            copy.start()
        for copy in own:
            copy.wait()
        rest = pl.ds(0, count - 1)
        pltpu.make_async_copy(vec_pieces.at[rest], vec_pieces.at[rest], recv_sem.at[1]).wait()
        vec_sum[...] = jnp.sum(vec_pieces[...], axis=0)
        give_back(vec_sum, 2, vec_out_ref)
        own_vec = pltpu.make_async_copy(vec_sum, vec_out_ref.at[slot_me], local_sem.at[0])
        own_vec.start()
        own_vec.wait()
        pltpu.make_async_copy(pieces.at[rest], pieces.at[rest], recv_sem.at[0]).wait()

        rows_of = TILE // 64

        def gram_tile(tile, carry):
            rows = pl.ds(pl.multiple_of(tile * TILE, TILE), TILE)
            total = jnp.zeros((TILE, D), jnp.float32)
            for part in range(parts):
                left = pieces[pl.ds(part * groups + tile * rows_of, rows_of)].reshape(TILE, SLOT)
                right = pieces[part * groups : (part + 1) * groups].reshape(D, SLOT)
                total += lax.dot_general(
                    left, right, (((1,), (1,)), ((), ())), preferred_element_type=jnp.float32
                )
            gram[rows, :] = total
            return carry

        lax.fori_loop(0, D // TILE, gram_tile, 0)

        @pl.when(is_wide)
        def _():
            core = lax.rem(dp_me, 2)
            sibling = (dp_me + 1 - 2 * core, t_me)
            across = (dp_me, 1 - t_me)

            def tile_at(index, owner):
                if index == 4:
                    row, col = jnp.where(owner == 0, 3, 2), 3
                elif index == 3:
                    row, col = jnp.where(owner == 0, 0, 2), jnp.where(owner == 0, 3, 2)
                else:
                    row, col = owner, owner + index
                return (
                    pl.ds(pl.multiple_of(row * TILE, TILE), TILE),
                    pl.ds(pl.multiple_of(col * TILE, TILE), TILE),
                )

            def exchange(stage, index, place):
                return pltpu.make_async_remote_copy(
                    src_ref=out_half.at[stage, index],
                    dst_ref=in_half.at[stage, index],
                    send_sem=half_send.at[stage, index],
                    recv_sem=half_recv.at[stage, index],
                    device_id=place,
                    device_id_type=MESH_IDS,
                )

            for index in range(GRAM_TILES):
                out_half[0, index] = gram[tile_at(index, 1 - core)].astype(jnp.bfloat16)
                exchange(0, index, sibling).start()
            for index in range(GRAM_TILES):
                exchange(0, index, sibling).wait_recv()
                total = gram[tile_at(index, core)] + in_half[0, index].astype(jnp.float32)
                out_half[1, index] = total.astype(jnp.bfloat16)
                exchange(1, index, across).start()
            for index in range(GRAM_TILES):
                exchange(1, index, across).wait_recv()
                total = out_half[1, index].astype(jnp.float32) + in_half[1, index].astype(jnp.float32)
                out_half[2, index] = total.astype(jnp.bfloat16)
                exchange(2, index, sibling).start()
                rows, cols = tile_at(index, core)
                gram[cols, rows] = out_half[2, index].astype(jnp.float32).T
                gram[rows, cols] = out_half[2, index].astype(jnp.float32)
            for index in range(GRAM_TILES):
                exchange(2, index, sibling).wait_recv()
                rows, cols = tile_at(index, 1 - core)
                gram[cols, rows] = in_half[2, index].astype(jnp.float32).T
                gram[rows, cols] = in_half[2, index].astype(jnp.float32)
            for index in range(GRAM_TILES):
                exchange(0, index, sibling).wait_send()
                exchange(1, index, across).wait_send()
                exchange(2, index, sibling).wait_send()
            for copy in swaps:
                copy.start()

        def trace_tile(tile, total):
            rows = pl.ds(pl.multiple_of(tile * TILE, TILE), TILE)
            row_ids = lax.broadcasted_iota(jnp.int32, (TILE, D), 0) + tile * TILE
            col_ids = lax.broadcasted_iota(jnp.int32, (TILE, D), 1)
            diagonal = jnp.where(row_ids == col_ids, gram[rows, :], 0.0)
            return total + jnp.sum(jnp.sum(diagonal, axis=0, keepdims=True), axis=1, keepdims=True)

        square_total = lax.fori_loop(0, D // TILE, trace_tile, jnp.zeros((1, 1), jnp.float32))
        factor = lax.rsqrt(square_total + SQUARE_EPSILON)
        gram_low[...] = (gram[...] * (factor * factor)).astype(jnp.bfloat16)

        first, second, third = SCHULZ_FIRST, SCHULZ_SECOND, SCHULZ_THIRD

        def tiles(body):
            def one(tile, carry):
                body(pl.ds(pl.multiple_of(tile * TILE, TILE), TILE))
                return carry

            lax.fori_loop(0, D // TILE, one, 0)

        chain = chain_low
        other = chain_next
        for sweep in range(NS_ITERS):
            target = chain if sweep == 0 else poly_low

            def poly(rows):
                square = mul(gram_low[rows, :], gram_low[...])
                grown = (second / first) * gram_low[rows, :].astype(jnp.float32) + (third / first) * square
                target[rows, :] = grown.astype(jnp.bfloat16)

            tiles(poly)
            if sweep > 0:

                def join(rows, chain=chain, other=other):
                    total = chain[rows, :].astype(jnp.float32) + poly_low[rows, :].astype(jnp.float32)
                    other[rows, :] = (total + mul(chain[rows, :], poly_low[...])).astype(jnp.bfloat16)

                tiles(join)
                chain, other = other, chain
            if sweep < NS_ITERS - 1:

                def half(rows):
                    grown = gram_low[rows, :].astype(jnp.float32) + mul(gram_low[rows, :], target[...])
                    half_low[rows, :] = grown.astype(jnp.bfloat16)

                def full(rows):
                    grown = half_low[rows, :].astype(jnp.float32) + mul(half_low[rows, :], target[...])
                    gram_low[rows, :] = (grown * (first * first)).astype(jnp.bfloat16)

                tiles(half)
                tiles(full)

        scale = factor * (first**NS_ITERS)

        def turn_tile(tile, carry):
            rows = pl.ds(pl.multiple_of(tile * TILE, TILE), TILE)
            for part in range(parts):
                at = pl.ds(part * groups + tile * rows_of, rows_of)
                whole = pieces[part * groups : (part + 1) * groups].reshape(D, SLOT)
                kept = pieces[at].reshape(TILE, SLOT).astype(jnp.float32)
                fresh = (kept + mul(chain[rows, :], whole)) * scale
                turned[at] = fresh.astype(jnp.bfloat16).reshape(rows_of, 64, SLOT)
            return carry

        lax.fori_loop(0, D // TILE, turn_tile, 0)
        give_back(turned, 3, updates_ref)
        own_turned = pltpu.make_async_copy(turned.at[me], updates_ref.at[slot_me], local_sem.at[1])
        own_turned.start()
        own_turned.wait()

    def finish(length):
        here = pl.ds(0, length)
        pltpu.make_async_copy(vec_ref.at[here], vec_ref.at[here], send_sem.at[1]).wait()
        pltpu.make_async_copy(moments_ref.at[here], moments_ref.at[here], send_sem.at[0]).wait()
        pltpu.make_async_copy(vec_out_ref.at[here], vec_out_ref.at[here], recv_sem.at[2]).wait()
        pltpu.make_async_copy(updates_ref.at[here], updates_ref.at[here], recv_sem.at[3]).wait()

    @pl.when(is_handler)
    def _():
        finish(SLOTS - 1)
        rest = pl.ds(0, count - 1)
        pltpu.make_async_copy(vec_pieces.at[rest], vec_pieces.at[rest], send_sem.at[2]).wait()
        pltpu.make_async_copy(turned.at[rest], turned.at[rest], send_sem.at[3]).wait()

    @pl.when(jnp.logical_not(is_handler))
    def _():
        finish(SLOTS)

    for copy in kept + swaps:
        copy.wait()


def muon_call(moments, vec_parts, block_rows, token_grads):
    count = lax.axis_size("dp") * lax.axis_size("tensor")
    rows = moments.shape[1]
    vmem = pl.BlockSpec(memory_space=pltpu.VMEM)
    anywhere = pl.BlockSpec(memory_space=pl.ANY)
    pair = jax.ShapeDtypeStruct((2, LEN // 2, D), jnp.bfloat16)
    low = pltpu.VMEM((D, D), jnp.bfloat16)
    return pl.pallas_call(
        muon_kernel,
        in_specs=[vmem, vmem, anywhere, anywhere],
        out_specs=[vmem, vmem, anywhere, anywhere],
        out_shape=[
            jax.ShapeDtypeStruct(moments.shape, jnp.bfloat16),
            jax.ShapeDtypeStruct(vec_parts.shape, jnp.float32),
            pair,
            pair,
        ],
        scratch_shapes=[
            pltpu.VMEM((count, rows, SLOT), jnp.bfloat16),
            pltpu.VMEM((count, rows, SLOT), jnp.bfloat16),
            pltpu.VMEM((count,) + vec_parts.shape[1:], jnp.float32),
            pltpu.VMEM(vec_parts.shape[1:], jnp.float32),
            pltpu.VMEM((D, D), jnp.float32),
            low,
            low,
            low,
            low,
            low,
            pltpu.VMEM((3, GRAM_TILES, TILE, TILE), jnp.bfloat16),
            pltpu.VMEM((3, GRAM_TILES, TILE, TILE), jnp.bfloat16),
            pltpu.SemaphoreType.DMA((2,)),
            pltpu.SemaphoreType.DMA((4,)),
            pltpu.SemaphoreType.DMA((4,)),
            pltpu.SemaphoreType.DMA((3, GRAM_TILES)),
            pltpu.SemaphoreType.DMA((3, GRAM_TILES)),
            pltpu.SemaphoreType.DMA((3, 2)),
        ],
        compiler_params=pltpu.CompilerParams(
            collective_id=1, has_side_effects=True, vmem_limit_bytes=VMEM_LIMIT
        ),
        cost_estimate=pl.CostEstimate(flops=12 * 2 * D**3, bytes_accessed=4 * 1024 * 1024, transcendentals=0),
    )(moments, vec_parts, block_rows, token_grads)


def neighbours():
    dp_me = lax.axis_index("dp")
    y = lax.axis_index("tensor")
    core = lax.rem(dp_me, 2)
    x = lax.rem(dp_me // 2, 2)
    z = dp_me // 4
    sibling = (dp_me + 1 - 2 * core, y)
    beside = (dp_me + 2 - 4 * x, y)
    across = (dp_me, 1 - y)
    stations = [(lax.rem(dp_me + 4 * hop, 16), y) for hop in (1, 2, 3)]
    return (z, x, core, y), sibling, beside, across, stations


def greet_neighbours(places):
    barrier = pltpu.get_barrier_semaphore()
    for place in places:
        pl.semaphore_signal(barrier, inc=1, device_id=place, device_id_type=MESH_IDS)
    pl.semaphore_wait(barrier, len(places))


EARLY = 2
AHEAD = 2


class Spread:
    def __init__(self, slots_ref, table, local_sem, send_sem, recv_sem):
        self.slots_ref, self.table = slots_ref, table
        self.local_sem, self.send_sem, self.recv_sem = local_sem, send_sem, recv_sem
        (self.z, self.x, self.core, self.y), self.sibling, self.beside, self.across, self.stations = neighbours()

    def remote(self, source, target, stage, slot, place):
        return pltpu.make_async_remote_copy(
            src_ref=source,
            dst_ref=target,
            send_sem=self.send_sem.at[stage, slot],
            recv_sem=self.recv_sem.at[stage, slot],
            device_id=place,
            device_id_type=MESH_IDS,
        )

    def own(self, slot):
        here = self.table[slot][0](self.y, 0, SLOT).at[self.z, self.x, self.core]
        return pltpu.make_async_copy(self.slots_ref.at[slot], here, self.local_sem.at[slot])

    def along_z(self, slot):
        here = self.table[slot][0](self.y, 0, SLOT).at[self.z, self.x, self.core]
        return [
            self.remote(self.slots_ref.at[slot], here, hop, slot, place)
            for hop, place in enumerate(self.stations)
        ]

    def second(self, slot):
        view, size = self.table[slot]
        copies = []
        if size:
            part = view(self.y, 0, size).at[:, self.x, self.core]
            copies.append(self.remote(part, part, 3, slot, self.beside))
        if size < SLOT:
            part = view(self.y, size, SLOT - size).at[:, self.x, self.core]
            copies.append(self.remote(part, part, 4, slot, self.across))
        return copies

    def third(self, slot):
        view, size = self.table[slot]
        copies = []
        if size:
            part = view(self.y, 0, size).at[:, :, self.core]
            copies.append(self.remote(part, part, 5, slot, self.across))
        if size < SLOT:
            for index in (0, 1):
                part = view(index, size, SLOT - size).at[:, self.x, self.core]
                copies.append(self.remote(part, part, 6 + index, slot, self.beside))
        return copies

    def fourth(self, slot):
        view, _ = self.table[slot]
        copies = []
        for index in (0, 1):
            part = view(index, 0, SLOT).at[:, :, self.core]
            copies.append(self.remote(part, part, 8 + index, slot, self.sibling))
        return copies

    def launch(self, slot):
        if slot < len(self.table):
            self.own(slot).start()
            for copy in self.along_z(slot):
                copy.start()

    def begin(self):
        for slot in range(AHEAD):
            self.launch(slot)

    def push_second(self, slot):
        self.own(slot).wait()
        for copy in self.along_z(slot):
            copy.wait_recv()
        for copy in self.second(slot):
            copy.start()

    def push_third(self, slot):
        for copy in self.second(slot):
            copy.wait_recv()
        for copy in self.third(slot):
            copy.start()

    def push_fourth(self, slot):
        for copy in self.third(slot):
            copy.wait_recv()
        for copy in self.fourth(slot):
            copy.start()

    def tick(self, index):
        count = len(self.table)
        self.launch(index + AHEAD)
        if index < count:
            self.push_second(index)
        if 0 <= index - 1 < count:
            self.push_third(index - 1)
        if 0 <= index - 2 < count:
            self.push_fourth(index - 2)

    def ticks(self):
        return len(self.table) + 2

    def arrived(self, slot):
        for copy in self.fourth(slot):
            copy.wait_recv()

    def sent(self):
        for slot in range(len(self.table)):
            for copy in self.along_z(slot) + self.second(slot) + self.third(slot) + self.fourth(slot):
                copy.wait_send()


def column_view(ref, column, distance):
    def view(part, start, size):
        first = column + part * distance + start
        if not isinstance(part, int):
            first = pl.multiple_of(first, 128)
        return ref.at[:, :, :, :, pl.ds(first, size)]

    return view


def place_view(ref, place):
    def view(part, start, size):
        return ref.at[place + part, :, :, :, :, pl.ds(start, size)]

    return view


def spread_semaphores(count):
    return [
        pltpu.SemaphoreType.DMA((count,)),
        pltpu.SemaphoreType.DMA((10, count)),
        pltpu.SemaphoreType.DMA((10, count)),
    ]


def pair_of(step):
    return (step % 2) * (PAIRS // 2) + step // 2


def attend_spread_kernel(
    starts_ref,
    slopes_ref,
    norm_ref,
    middle_rows_ref,
    shifts_ref,
    tokens_ref,
    cotangent_ref,
    slots_ref,
    packed_ref,
    ctx_ref,
    exps_ref,
    stat_ref,
    normed_t_ref,
    rows_ref,
    middle_ref,
    normed_two_ref,
    qkv_ref,
    out_ref,
    up_ref,
    down_ref,
    cot_ref,
    dist_ref,
    ctx_t,
    ctx_all,
    out_weights,
    rows,
    normed,
    weights,
    local_sem,
    send_sem,
    recv_sem,
    swap_sem,
    load_sem,
):
    step = pl.program_id(0)
    pair = pair_of(step)
    table = [(column_view(qkv_ref, index * SLOT, 3 * SLOT), SLOT if index == 1 else 0) for index in range(3)]
    table += [(column_view(out_ref, 0, SLOT), 0)]
    for index in range(EARLY):
        for ref, over_x in ((up_ref, 0), (down_ref, HALF_SLOT if index else 0)):
            table += [(column_view(ref, index * SLOT, EARLY * SLOT), over_x)]
    count = len(table)
    spread = Spread(slots_ref, table, local_sem, send_sem, recv_sem)
    half_rows = pl.ds(pl.multiple_of(spread.y * (LEN // 2), LEN // 2), LEN // 2)
    own_rows = pltpu.make_async_copy(tokens_ref.at[spread.y], rows.at[half_rows], load_sem.at[2])

    def swap(source, target, index):
        return pltpu.make_async_remote_copy(
            src_ref=source.at[1 - spread.y],
            dst_ref=target,
            send_sem=swap_sem.at[0, index],
            recv_sem=swap_sem.at[1, index],
            device_id=spread.across,
            device_id_type=MESH_IDS,
        )

    token_swap = swap(tokens_ref, rows.at[half_rows], 0)
    cotangent_swap = swap(cotangent_ref, cot_ref.at[half_rows], 1)
    own_cotangent = pltpu.make_async_copy(cotangent_ref.at[spread.y], cot_ref.at[half_rows], load_sem.at[3])
    out_load = pltpu.make_async_copy(out_ref, out_weights, load_sem.at[4])

    def load(at):
        cols = pl.ds(pl.multiple_of(pair_of(at) * (3 * PAIR), PAIR), 3 * PAIR)
        place = lax.rem(at, 2)
        return pltpu.make_async_copy(qkv_ref.at[:, :, :, :, cols], weights.at[place], load_sem.at[place])

    @pl.when(step == 0)
    def _():
        greet_neighbours([spread.sibling, spread.beside, spread.across] + spread.stations)
        own_rows.start()
        for slot in range(3):
            spread.launch(slot)
        spread.push_second(0)
        token_swap.start()
        spread.push_second(1)
        spread.push_third(0)
        spread.push_second(2)
        for slot in range(3, count):
            spread.launch(slot)
        layout_grid(starts_ref, dist_ref)
        spread.push_fourth(0)
        own_rows.wait()
        token_swap.wait_recv()
        spread.push_third(1)
        for index in range(LEN // CHUNK):
            here = slice(index * CHUNK, index * CHUNK + CHUNK)
            block = rows[here].astype(jnp.float32)
            low = layer_norm(block, norm_ref[0:1], norm_ref[1:2]).astype(jnp.bfloat16)
            normed[here] = low
            normed_t_ref[:, here] = low.T
            rows_ref[here] = rows[here]
        own_cotangent.start()

    for slot in range(3):

        @pl.when(step == 2 * slot)
        def _(slot=slot):
            spread.arrived(slot)

    @pl.when(lax.rem(step, 2) == 0)
    def _():
        load(step).start()

    load(step).wait()

    def between():
        @pl.when(lax.rem(step, 2) == 0)
        def _():
            load(step + 1).start()

        moves = (
            ((), (), 3),
            ((1,), (2,), 4),
            ((), (3,), 5),
            ((2,), (4,), 6),
            ((3,), (5,), 7),
            ((4,), (6,), None),
            ((5,), (7,), None),
            ((6,), (), None),
        )
        for index, (fourth, third, fresh) in enumerate(moves):

            @pl.when(step == index)
            def _(index=index, fourth=fourth, third=third, fresh=fresh):
                for slot in fourth:
                    spread.push_fourth(slot)
                for slot in third:
                    spread.push_third(slot)
                if fresh is not None:
                    spread.push_second(fresh)
                if fresh == count - 1:
                    cotangent_swap.start()

    packed = mul(normed[...], weights[lax.rem(step, 2)].reshape(D, 3 * PAIR)) + shifts_ref[...]
    packed = packed.astype(jnp.bfloat16)
    packed_ref[...] = packed
    @pl.when(step == PAIRS - 1)
    def _():
        spread.arrived(3)
        out_load.start()

    attend_pair(pair, slopes_ref, packed, dist_ref, ctx_ref, exps_ref, stat_ref, ctx_t, between)
    ctx_all[:, pl.ds(pl.multiple_of(pair * PAIR, PAIR), PAIR)] = ctx_ref[...]

    @pl.when(step == PAIRS - 1)
    def _():
        out_load.wait()
        for index in range(LEN // CHUNK):
            here = slice(index * CHUNK, index * CHUNK + CHUNK)
            attended = dot_last(ctx_all[here], out_weights[...].reshape(D, D))
            middle = rows[here].astype(jnp.float32) + attended + middle_rows_ref[0:1]
            middle_ref[here] = middle
            normed_two = layer_norm(middle, middle_rows_ref[1:2], middle_rows_ref[2:3])
            normed_two_ref[here] = normed_two.astype(jnp.bfloat16)
            if index == LEN // CHUNK // 2 - 1:
                spread.push_fourth(count - 1)
        for slot in range(4, count):
            spread.arrived(slot)
        spread.sent()
        token_swap.wait_send()
        cotangent_swap.wait()
        own_cotangent.wait()


def whole_shape(columns):
    return jax.ShapeDtypeStruct((4, 2, 2, 64, columns), jnp.bfloat16)


def attend_spread(starts, slopes, norm_rows, middle_rows, shifts, tokens, cotangent, slots):
    anywhere = pl.BlockSpec(memory_space=pl.ANY)
    whole = pl.BlockSpec((LEN, D), lambda s: (0, 0), pipeline_mode=pl.Buffered(1))
    low = jnp.bfloat16
    *local, qkv, out, up, down, cotangent_rows = pl.pallas_call(
        attend_spread_kernel,
        grid=(PAIRS,),
        in_specs=[
            SCALARS,
            SCALARS,
            pl.BlockSpec((2, D), lambda s: (0, 0)),
            pl.BlockSpec((3, D), lambda s: (0, 0)),
            pl.BlockSpec((1, 3 * PAIR), lambda s: (0, pair_of(s))),
            anywhere,
            anywhere,
            anywhere,
        ],
        out_specs=[
            pl.BlockSpec((LEN, 3 * PAIR), lambda s: (0, pair_of(s))),
            pl.BlockSpec((LEN, PAIR), lambda s: (0, pair_of(s))),
            pl.BlockSpec((2, LEN, LEN), lambda s: (pair_of(s), 0, 0)),
            pl.BlockSpec((1, 2, LEN), lambda s: (pair_of(s), 0, 0)),
            whole,
            whole,
            whole,
            whole,
        ]
        + [anywhere] * 5,
        out_shape=[
            jax.ShapeDtypeStruct((LEN, 3 * D), low),
            jax.ShapeDtypeStruct((LEN, D), low),
            jax.ShapeDtypeStruct((H, LEN, LEN), low),
            jax.ShapeDtypeStruct((PAIRS, 2, LEN), jnp.float32),
            jax.ShapeDtypeStruct((D, LEN), low),
            jax.ShapeDtypeStruct((LEN, D), low),
            jax.ShapeDtypeStruct((LEN, D), jnp.float32),
            jax.ShapeDtypeStruct((LEN, D), low),
            whole_shape(3 * D),
            whole_shape(D),
            whole_shape(2 * EARLY * SLOT),
            whole_shape(2 * EARLY * SLOT),
            jax.ShapeDtypeStruct((LEN, D), low),
        ],
        scratch_shapes=[
            pltpu.VMEM((LEN, LEN), jnp.float32),
            pltpu.VMEM((PAIR, LEN), jnp.float32),
            pltpu.VMEM((LEN, D), low),
            pltpu.VMEM((4, 2, 2, 64, D), low),
            pltpu.VMEM((LEN, D), low),
            pltpu.VMEM((LEN, D), low),
            pltpu.VMEM((2, 4, 2, 2, 64, 3 * PAIR), low),
        ]
        + spread_semaphores(4 + 2 * EARLY)
        + [pltpu.SemaphoreType.DMA((2, 2)), pltpu.SemaphoreType.DMA((5,))],
        compiler_params=pltpu.CompilerParams(
            collective_id=4, has_side_effects=True, vmem_limit_bytes=VMEM_LIMIT
        ),
        cost_estimate=pl.CostEstimate(
            flops=22 * LEN * LEN * D, bytes_accessed=90 * 1024 * 1024, transcendentals=H * LEN * LEN
        ),
    )(starts, slopes, norm_rows, middle_rows, shifts, tokens, cotangent, slots)
    wholes = [whole.reshape(D, -1) for whole in (qkv, out, up, down)]
    return *local, wholes, cotangent_rows


class Summing:
    def __init__(self, sources, add_own, buffers, total_ref, sems, lag, ready=0, hold=0):
        self.sources, self.add_own, self.total_ref, self.lag = sources, add_own, total_ref, lag
        self.ready, self.hold = ready, hold
        self.first, self.second_y, self.second_x, self.third, self.fourth = buffers
        self.send_sem, self.recv_sem = sems
        (self.z, self.x, self.core, self.y), self.sibling, self.beside, self.across, self.stations = neighbours()
        self.low_cols = pl.ds(0, HALF_SLOT)
        self.high_cols = pl.ds(HALF_SLOT, HALF_SLOT)

    def count(self):
        return len(self.sources)

    def remote(self, source, target, stage, slot, place):
        return pltpu.make_async_remote_copy(
            src_ref=source,
            dst_ref=target,
            send_sem=self.send_sem.at[stage, slot],
            recv_sem=self.recv_sem.at[stage, slot],
            device_id=place,
            device_id_type=MESH_IDS,
        )

    def landed(self, ref, stage, slot):
        pltpu.make_async_copy(ref, ref, self.recv_sem.at[stage, slot]).wait()

    def send_first(self, slot):
        for part in (0, 1):
            source = self.sources[slot](part).at[:, :, 1 - self.core]
            self.remote(source, self.first.at[slot, part], 0, slot, self.sibling).start()

    def second_copies(self, slot):
        for_y = self.first.at[slot, 1 - self.y, :, :, :, self.low_cols]
        for_x = self.first.at[slot, :, :, 1 - self.x, :, self.high_cols]
        return (
            self.remote(for_y, self.second_y.at[slot], 1, slot, self.across),
            self.remote(for_x, self.second_x.at[slot], 2, slot, self.beside),
        )

    def third_copies(self, slot):
        for_x = self.second_y.at[slot, :, 1 - self.x]
        for_y = self.second_x.at[slot, 1 - self.y]
        return (
            self.remote(for_x, self.third.at[slot, :, :, self.low_cols], 3, slot, self.beside),
            self.remote(for_y, self.third.at[slot, :, :, self.high_cols], 4, slot, self.across),
        )

    def fourth_copies(self, slot):
        return tuple(
            self.remote(
                self.third.at[slot, lax.rem(self.z + hop, 4)], self.fourth.at[slot, hop - 1], 4 + hop, slot, place
            )
            for hop, place in zip((1, 2, 3), self.stations)
        )

    def stage_one(self, slot):
        self.landed(self.first.at[slot], 0, slot)
        self.add_own(slot)
        for copy in self.second_copies(slot):
            copy.start()

    def stage_two(self, slot):
        first, second_y, second_x = self.first, self.second_y, self.second_x
        self.landed(second_y.at[slot], 1, slot)
        second_y[slot] = second_y[slot] + first[slot, self.y, :, :, :, :HALF_SLOT]
        self.landed(second_x.at[slot], 2, slot)
        second_x[slot] = second_x[slot] + first[slot, :, :, self.x, :, HALF_SLOT:]
        for copy in self.third_copies(slot):
            copy.start()

    def stage_three(self, slot):
        third = self.third
        self.landed(third.at[slot, :, :, self.low_cols], 3, slot)
        self.landed(third.at[slot, :, :, self.high_cols], 4, slot)
        third[slot, :, :, :HALF_SLOT] = third[slot, :, :, :HALF_SLOT] + self.second_y[slot, :, self.x]
        third[slot, :, :, HALF_SLOT:] = third[slot, :, :, HALF_SLOT:] + self.second_x[slot, self.y]
        for copy in self.fourth_copies(slot):
            copy.start()

    def stage_four(self, slot):
        total = self.third[slot, self.z].astype(jnp.float32)
        for hop in (1, 2, 3):
            self.landed(self.fourth.at[slot, hop - 1], 4 + hop, slot)
            total = total + self.fourth[slot, hop - 1].astype(jnp.float32)
        self.total_ref[slot] = total

    def ticks(self):
        return self.count() + self.hold + 3 * self.lag

    def tick(self, index):
        for slot in range(self.count()):
            entry = slot + (self.hold if slot >= self.ready else 0)
            pl.when(index == entry)(lambda slot=slot: self.stage_one(slot))
        for number, stage in enumerate((self.stage_two, self.stage_three, self.stage_four)):
            entry = index - (number + 1) * self.lag
            slot = jnp.where(entry < self.ready, entry, entry - self.hold)
            late = (entry >= self.ready + self.hold) & (slot < self.count())
            early = (entry >= 0) & (entry < self.ready)
            pl.when(early | late)(lambda stage=stage, slot=slot: stage(slot))

    def sent(self):
        def one(slot, carry):
            pltpu.make_async_copy(self.first.at[slot], self.first.at[slot], self.send_sem.at[0, slot]).wait()
            for copy in self.second_copies(slot) + self.third_copies(slot) + self.fourth_copies(slot):
                copy.wait_send()
            return carry

        lax.fori_loop(0, self.count(), one, 0)


def summing_buffers(count):
    rows, low = 64, jnp.bfloat16
    return [
        pltpu.VMEM((count, 2, 4, 2, rows, SLOT), low),
        pltpu.VMEM((count, 4, 2, rows, HALF_SLOT), low),
        pltpu.VMEM((count, 2, 4, rows, HALF_SLOT), low),
        pltpu.VMEM((count, 4, rows, SLOT), low),
        pltpu.VMEM((count, 3, rows, SLOT), low),
        pltpu.SemaphoreType.DMA((8, count)),
        pltpu.SemaphoreType.DMA((8, count)),
    ]


LAG = 2
READY = 5
LATE_SLOTS = 8
RING = 4


def block_view(ref, column):
    return ref.at[:, :, :, :, pl.ds(column, SLOT)]


def attend_bwd_half(half, scale, values, keys_t, parts, exps, sums):
    half_t, half_rows, half_queries, inner = parts
    dq_t, dk_sum, dv_sum = sums
    heads = slice(half * HD, half * HD + HD)
    for block in range(LEN // QB):
        span = min(LEN, QB * block + QB + PIECE)
        cols = slice(block * QB, block * QB + QB)
        weights = exps[:span, cols]
        grad_probs = mul(values[:span], half_t[:, cols])
        grad_scores = (weights.astype(jnp.float32) * (grad_probs - inner[:, cols])).astype(jnp.bfloat16)
        dv_sum[:span, :] += mul(weights, half_rows[cols])
        dk_sum[:span, :] += mul(grad_scores, half_queries[cols])
        dq_t[heads, cols] = mul(keys_t[heads, :span], grad_scores) * scale


def attend_sum_kernel(
    packed_ref,
    ctx_ref,
    grad_ref,
    stat_ref,
    weights_ref,
    normed_t_ref,
    rows_ref,
    grad_middle_ref,
    gain_ref,
    exps_ref,
    up_ref,
    down_ref,
    out_ref,
    total_ref,
    token_grad_ref,
    sums_ref,
    packed_sum_ref,
    grad_normed,
    exps,
    dq_t,
    dk_sum,
    dv_sum,
    grad_qkv,
    mine,
    first,
    second_y,
    second_x,
    third,
    fourth,
    send_sem,
    recv_sem,
    exps_sem,
    load_sem,
):
    pair = pl.program_id(0)
    width = up_ref.shape[-1] // 2
    sources = []
    for index in range(width // SLOT):
        for ref in (up_ref, down_ref):
            sources.append(lambda part, ref=ref, index=index: block_view(ref, part * width + index * SLOT))
    sources.append(lambda part: block_view(out_ref, part * SLOT))
    for index in range(3):
        sources.append(lambda part, index=index: block_view(grad_qkv, (part * 3 + index) * SLOT))

    def load(slot, part):
        block = sources[slot](part).at[:, :, summing.core]
        return pltpu.make_async_copy(block, mine.at[slot % RING, part], load_sem.at[slot % RING])

    def add_own(slot):
        if slot < READY:
            place = slot % RING
            pltpu.make_async_copy(mine.at[place], mine.at[place], load_sem.at[place]).wait()
            first[slot] = first[slot] + mine[place]
            if slot + RING < READY:
                for part in (0, 1):
                    load(slot + RING, part).start()
        else:
            for part in (0, 1):
                cols = pl.ds((part * 3 + slot - READY) * SLOT, SLOT)
                first[slot, part] = first[slot, part] + grad_qkv[:, :, summing.core, :, cols]

    buffers = (first, second_y, second_x, third, fourth)
    summing = Summing(sources, add_own, buffers, total_ref, (send_sem, recv_sem), LAG, READY, 1)

    def exps_load(head, half):
        return pltpu.make_async_copy(exps_ref.at[head], exps.at[half], exps_sem.at[half])

    @pl.when(pair == 0)
    def _():
        for half in (0, 1):
            exps_load(half, half).start()
        for slot in range(RING):
            for part in (0, 1):
                load(slot, part).start()
        greet_neighbours([summing.sibling, summing.beside, summing.across] + summing.stations)
        for slot in range(READY):
            summing.send_first(slot)
        grad_normed[...] = jnp.zeros_like(grad_normed)
        sums_ref[...] = jnp.zeros_like(sums_ref)

    scale = 1.0 / math.sqrt(HD)
    queries = packed_ref[:, :PAIR]
    keys_t = packed_ref[:, PAIR : 2 * PAIR].T
    values = packed_ref[:, 2 * PAIR :]
    grads_t = grad_ref[...].T.astype(jnp.float32)
    context_t = ctx_ref[...].T.astype(jnp.float32)
    scaled = []
    inner_rows = []
    for half in (0, 1):
        heads = slice(half * HD, half * HD + HD)
        scaled.append(grads_t[heads] * stat_ref[0, half : half + 1, :])
        inner_rows.append(jnp.sum(scaled[half] * context_t[heads], axis=0, keepdims=True))
    scaled_t = jnp.concatenate(scaled, axis=0).astype(jnp.bfloat16)
    scaled_rows = scaled_t.T
    dk_sum[...] = jnp.zeros_like(dk_sum)
    dv_sum[...] = jnp.zeros_like(dv_sum)
    for half in (0, 1):
        exps_load(2 * pair + half, half).wait()
        parts = (
            only_rows(scaled_t, half),
            only_cols(scaled_rows, half),
            only_cols(queries, half),
            inner_rows[half],
        )
        attend_bwd_half(half, scale, values, keys_t, parts, exps.at[half], (dq_t, dk_sum, dv_sum))

        @pl.when(pair < PAIRS - 1)
        def _(half=half):
            exps_load(2 * pair + 2 + half, half).start()

        if half == 0:
            summing.tick(pair)
    grads = jnp.concatenate([dq_t[...].T, dk_sum[...] * scale, dv_sum[...]], axis=1).astype(jnp.bfloat16)
    packed_sum_ref[...] = jnp.sum(grads.astype(jnp.float32), axis=0, keepdims=True)
    cols = pl.ds(pl.multiple_of(pair * (3 * PAIR), PAIR), 3 * PAIR)
    grad_weights = mul(normed_t_ref[...], grads).astype(jnp.bfloat16)
    grad_qkv[:, :, :, :, cols] = grad_weights.reshape(4, 2, 2, 64, 3 * PAIR)
    grad_normed[...] += dot_last(grads, weights_ref[...])

    for slot in range(READY, LATE_SLOTS):
        pl.when(pair == PAIRS - LATE_SLOTS + slot)(lambda slot=slot: summing.send_first(slot))

    @pl.when(pair == PAIRS - 1)
    def _():
        def late(index, carry):
            summing.tick(index)
            chunk = index - PAIRS

            @pl.when(chunk < LEN // ROWS)
            def _():
                here = pl.ds(pl.multiple_of(chunk * ROWS, ROWS), ROWS)
                block = rows_ref[here, :].astype(jnp.float32)
                pulled, gain_sum, shift_sum = norm_pull(block, grad_normed[here, :], gain_ref[...])
                token_grad_ref[here, :] = (grad_middle_ref[here, :] + pulled).astype(jnp.bfloat16)
                add_rows(sums_ref, (gain_sum, shift_sum))

            return carry

        lax.fori_loop(PAIRS, summing.ticks(), late, 0)
        summing.sent()


def attend_sum(
    packed, context, grad_context, stats, weights, normed_t, rows_low, grad_middle, gain, exps, grad_up, grad_down, grad_out
):
    anywhere = pl.BlockSpec(memory_space=pl.ANY)
    rows = 64
    low = jnp.bfloat16
    once = pl.Buffered(1)
    tall = pl.BlockSpec((LEN, D), lambda p: (0, 0), pipeline_mode=once)
    split = [grad.reshape(4, 2, 2, rows, grad.shape[-1]) for grad in (grad_up, grad_down, grad_out)]
    return pl.pallas_call(
        attend_sum_kernel,
        grid=(PAIRS,),
        in_specs=[PACKED_COLS, PAIR_COLS, PAIR_COLS, PAIR_STAT, PACKED_COLS, tall, tall, tall]
        + [pl.BlockSpec((1, D), lambda p: (0, 0))]
        + [anywhere] * 4,
        out_specs=[
            pl.BlockSpec((LATE_SLOTS, rows, SLOT), lambda p: (0, 0, 0), pipeline_mode=once),
            tall,
            pl.BlockSpec((8, D), lambda p: (0, 0)),
            pl.BlockSpec((1, 3 * PAIR), lambda p: (0, p)),
        ],
        out_shape=[
            jax.ShapeDtypeStruct((LATE_SLOTS, rows, SLOT), jnp.float32),
            jax.ShapeDtypeStruct((LEN, D), low),
            jax.ShapeDtypeStruct((8, D), jnp.float32),
            jax.ShapeDtypeStruct((1, 3 * D), jnp.float32),
        ],
        scratch_shapes=[
            pltpu.VMEM((LEN, D), jnp.float32),
            pltpu.VMEM((2, LEN, LEN), low),
            pltpu.VMEM((PAIR, LEN), jnp.float32),
            pltpu.VMEM((LEN, PAIR), jnp.float32),
            pltpu.VMEM((LEN, PAIR), jnp.float32),
            pltpu.VMEM((4, 2, 2, rows, 3 * D), low),
            pltpu.VMEM((RING, 2, 4, 2, rows, SLOT), low),
            *summing_buffers(LATE_SLOTS),
            pltpu.SemaphoreType.DMA((2,)),
            pltpu.SemaphoreType.DMA((RING,)),
        ],
        compiler_params=pltpu.CompilerParams(
            collective_id=2, has_side_effects=True, vmem_limit_bytes=62 * 1024 * 1024
        ),
        cost_estimate=pl.CostEstimate(
            flops=44 * LEN * LEN * D, bytes_accessed=400 * 1024 * 1024, transcendentals=0
        ),
    )(packed, context, grad_context, stats, weights, normed_t, rows_low, grad_middle, gain, exps, *split)


ROWS = 256


def norm_pull(rows, grads, gain):
    centered = rows - jnp.mean(rows, axis=-1, keepdims=True)
    inverse = lax.rsqrt(jnp.mean(centered * centered, axis=-1, keepdims=True) + NORM_EPSILON)
    normed = centered * inverse
    scaled = grads * gain
    along = jnp.mean(scaled * normed, axis=-1, keepdims=True)
    pulled = inverse * (scaled - jnp.mean(scaled, axis=-1, keepdims=True) - normed * along)
    gain_sum = jnp.sum(grads * normed, axis=0, keepdims=True)
    return pulled, gain_sum, jnp.sum(grads, axis=0, keepdims=True)


def add_rows(sums_ref, rows):
    for index, row in enumerate(rows):
        sums_ref[index : index + 1, :] += row


def middle_kernel(
    middle_ref, grad_ref, cot_ref, ctx_ref, gain_ref, weights_ref, grad_middle_ref, grad_ctx_ref, grad_out_ref, sums_ref, low_t
):
    step = pl.program_id(0)

    @pl.when(step == 0)
    def _():
        sums_ref[...] = jnp.zeros_like(sums_ref)

    cot = cot_ref[...].astype(jnp.float32)
    pulled, gain_sum, shift_sum = norm_pull(middle_ref[...], grad_ref[...], gain_ref[...])
    grads = cot + pulled
    low = grads.astype(jnp.bfloat16)
    grad_middle_ref[...] = grads
    grad_ctx_ref[...] = mul(low, weights_ref[...]).astype(jnp.bfloat16)
    low_t[:, pl.ds(pl.multiple_of(step * ROWS, ROWS), ROWS)] = low.T
    grad_sum = jnp.sum(grads, axis=0, keepdims=True)
    add_rows(sums_ref, (gain_sum, shift_sum, grad_sum, jnp.sum(cot, axis=0, keepdims=True)))

    @pl.when(step == LEN // ROWS - 1)
    def _():
        grad_out_ref[...] = mul(low_t[...], ctx_ref[...]).astype(jnp.bfloat16)


def middle_backward(middle, grad_rows, cot, context, gain, weights):
    rows = pl.BlockSpec((ROWS, D), lambda s: (s, 0))
    whole = pl.BlockSpec((D, D), lambda s: (0, 0), pipeline_mode=pl.Buffered(1))
    row = pl.BlockSpec((1, D), lambda s: (0, 0))
    sums = pl.BlockSpec((8, D), lambda s: (0, 0))
    return pl.pallas_call(
        middle_kernel,
        grid=(LEN // ROWS,),
        in_specs=[rows, rows, rows, whole, row, whole],
        out_specs=[rows, rows, whole, sums],
        out_shape=[
            jax.ShapeDtypeStruct((LEN, D), jnp.float32),
            jax.ShapeDtypeStruct((LEN, D), jnp.bfloat16),
            jax.ShapeDtypeStruct((D, D), jnp.bfloat16),
            jax.ShapeDtypeStruct((8, D), jnp.float32),
        ],
        scratch_shapes=[pltpu.VMEM((D, LEN), jnp.bfloat16)],
        compiler_params=pltpu.CompilerParams(vmem_limit_bytes=VMEM_LIMIT),
        cost_estimate=pl.CostEstimate(flops=4 * LEN * D * D, bytes_accessed=24 * 1024 * 1024, transcendentals=0),
    )(middle, grad_rows, cot, context, gain, weights)


def slot_rows(early_ref, late_ref, slot):
    index, kind = slot % 4, slot // 4
    if index < EARLY:
        return early_ref[2 * index + kind]
    return late_ref[2 * (index - EARLY) + kind]


def moment_kernel(
    early_ref,
    late_ref,
    m_qkv_ref,
    m_out_ref,
    m_up_ref,
    m_down_ref,
    g_qkv_ref,
    g_out_ref,
    g_up_ref,
    g_down_ref,
    n_qkv_ref,
    n_out_ref,
    n_up_ref,
    n_down_ref,
    slots_ref,
):
    first_packed = LATE_SLOTS - 3
    for pair in range(SLOT // PAIR):
        for part in range(3):
            column = (pair * 3 + part) * PAIR
            source = late_ref[first_packed + column // SLOT, :, column % SLOT : column % SLOT + PAIR]
            g_qkv_ref[part, :, pair * PAIR : (pair + 1) * PAIR] = source
    for part in range(3):
        moment = MOMENTUM_DECAY * m_qkv_ref[part] + g_qkv_ref[part]
        n_qkv_ref[part] = moment
        slots_ref[part] = moment.astype(jnp.bfloat16)
    grads = late_ref[first_packed - 1]
    g_out_ref[...] = grads
    moment = MOMENTUM_DECAY * m_out_ref[...] + grads
    n_out_ref[...] = moment
    slots_ref[3] = moment.astype(jnp.bfloat16)
    for kind, refs in enumerate(((m_up_ref, g_up_ref, n_up_ref), (m_down_ref, g_down_ref, n_down_ref))):
        old_ref, grads_ref, new_ref = refs
        for index in range(4):
            here = slice(index * SLOT, (index + 1) * SLOT)
            grads = slot_rows(early_ref, late_ref, 4 * kind + index)
            grads_ref[:, here] = grads
            moment = MOMENTUM_DECAY * old_ref[:, here] + grads
            new_ref[:, here] = moment
            slots_ref[4 + 4 * kind + index] = moment.astype(jnp.bfloat16)


def update_kernel(
    updates_ref,
    vec_sum_ref,
    w_qkv_ref,
    w_out_ref,
    w_up_ref,
    w_down_ref,
    vectors_ref,
    m_vec_ref,
    o_qkv_ref,
    o_out_ref,
    o_up_ref,
    o_down_ref,
    g_vec_ref,
    n_vec_ref,
    o_vec_ref,
):
    wide_rate = MATRIX_RATE * math.sqrt(FF / D)
    for part in range(3):
        o_qkv_ref[part] = w_qkv_ref[part] - MATRIX_RATE * updates_ref[part].astype(jnp.float32)
    o_out_ref[...] = w_out_ref[...] - MATRIX_RATE * updates_ref[3].astype(jnp.float32)
    for index in range(4):
        here = slice(index * SLOT, (index + 1) * SLOT)
        o_up_ref[:, here] = w_up_ref[:, here] - wide_rate * updates_ref[4 + index].astype(jnp.float32)
        o_down_ref[:, here] = w_down_ref[:, here] - wide_rate * updates_ref[8 + index].astype(jnp.float32)
    grads = vec_sum_ref[...]
    moment = MOMENTUM_DECAY * m_vec_ref[...] + grads
    square = jnp.mean(moment * moment, axis=1, keepdims=True)
    g_vec_ref[...] = grads
    n_vec_ref[...] = moment
    o_vec_ref[...] = vectors_ref[...] - VECTOR_RATE * moment * lax.rsqrt(square + SQUARE_EPSILON)


def like(arrays):
    return [jax.ShapeDtypeStruct(array.shape, jnp.float32) for array in arrays]


def features_first(arrays):
    qkv, out, up, down = arrays
    return qkv, out.T, up, down.T


def muon_step(early, late, vector_total, block_rows, token_grads, weights, vectors, momenta, m_vec):
    limit = pltpu.CompilerParams(vmem_limit_bytes=VMEM_LIMIT)
    weights, momenta = features_first(weights), features_first(momenta)
    slots_shape = jax.ShapeDtypeStruct((SLOTS,) + late.shape[1:], jnp.bfloat16)
    *stored, slots = pl.pallas_call(
        moment_kernel, out_shape=like(momenta) + like(momenta) + [slots_shape], compiler_params=limit
    )(early, late, *momenta)
    updates, vector_rows, output_pair, token_pair = muon_call(
        slots, vector_total.reshape(SLOTS, 8, 128), block_rows, token_grads
    )
    fresh = pl.pallas_call(
        update_kernel, out_shape=like(weights) + like([vectors] * 3), compiler_params=limit
    )(updates, vector_rows.reshape(12, D), *weights, vectors, m_vec)
    vector_grad, moment_vec, new_vec = fresh[4:]
    grads, moments, new = features_first(stored[:4]), features_first(stored[4:]), features_first(fresh[:4])
    return (output_pair, token_pair.astype(jnp.float32), *grads, vector_grad, *moments, moment_vec, *new, new_vec)


def by_slots(rows):
    return jnp.swapaxes(rows.reshape(rows.shape[0], -1, SLOT), 0, 1)


def narrow(rows):
    return rows.astype(jnp.bfloat16)


def contract(left, right, left_dim, right_dim):
    return lax.dot_general(
        left, right, (((left_dim,), (right_dim,)), ((), ())), preferred_element_type=jnp.float32
    )


def by_pairs(rows):
    count, height, width = rows.shape
    return jnp.transpose(rows.reshape(count, height, width // PAIR, PAIR), (1, 2, 0, 3)).reshape(height, -1)


def from_pairs(rows):
    height = rows.shape[0]
    return jnp.transpose(rows.reshape(height, -1, 3, PAIR), (2, 0, 1, 3)).reshape(3, height, -1)


def sequence_step(
    tokens,
    cotangent,
    piece_starts,
    w_qkv,
    w_out,
    w_up,
    w_down,
    vectors,
    m_qkv,
    m_out,
    m_up,
    m_down,
    m_vec,
):
    rank = lax.axis_index("tensor")
    slopes = jnp.exp2(-8.0 * jnp.arange(1, H + 1, dtype=jnp.float32) / H)
    starts = lax.dynamic_slice_in_dim(piece_starts[:, 0], rank, 1, 0)[0]
    shifts = by_pairs(jnp.stack([vectors[2], jnp.zeros((D,), jnp.float32), vectors[3]])[:, None])
    up_slots = by_slots(narrow(w_up))
    down_slots = by_slots(narrow(w_down).T)
    in_turn = jnp.stack([up_slots, down_slots], axis=1).reshape(2 * up_slots.shape[0], *up_slots.shape[1:])
    slots = jnp.concatenate([by_slots(by_pairs(narrow(w_qkv))), narrow(w_out).T[None], in_turn[: 2 * EARLY]])
    packed, context, exps, stats, normed_t, token_low, middle, normed_two, wholes, cotangent_low = attend_spread(
        starts, slopes, vectors[0:2], vectors[4:7], shifts, tokens, cotangent, slots
    )
    full_qkv, full_out, full_up, full_down = wholes
    block_rows, grad_normed_two, grad_up, grad_down, up_bias, early_sums = mlp_both(
        normed_two,
        cotangent_low,
        middle,
        vectors[11:12],
        vectors[7:11].reshape(1, FF),
        full_up,
        full_down,
        in_turn[2 * EARLY :],
    )
    grad_middle, grad_context, grad_out, middle_sums = middle_backward(
        middle, grad_normed_two, cotangent_low, context, vectors[5:6], full_out
    )
    sums, grad_token_low, token_sums, packed_grads = attend_sum(
        packed,
        context,
        grad_context,
        stats,
        full_qkv,
        normed_t,
        token_low,
        grad_middle,
        vectors[0:1],
        exps,
        grad_up,
        grad_down,
        grad_out,
    )
    packed_sums = from_pairs(packed_grads)[:, 0]
    vector_total = jnp.concatenate(
        [
            token_sums[0:2],
            packed_sums[0:1],
            packed_sums[2:3],
            middle_sums[2:3],
            middle_sums[0:2],
            up_bias.reshape(4, D),
            middle_sums[3:4],
        ]
    )
    weights = (w_qkv, w_out, w_up, w_down)
    momenta = (m_qkv, m_out, m_up, m_down)
    return muon_step(
        early_sums, sums, vector_total, block_rows, grad_token_low, weights, vectors, momenta, m_vec
    )


def solution(mesh):
    in_specs = (
        P(None, ("dp", "tensor"), None),
        P(None, ("dp", "tensor"), None),
        P(None, "dp", None),
        P(None, "dp", "tensor"),
        P("tensor", "dp"),
        P("dp", "tensor"),
        P("tensor", "dp"),
        P(),
        P(None, "dp", "tensor"),
        P("tensor", "dp"),
        P("dp", "tensor"),
        P("tensor", "dp"),
        P(),
    )
    out_specs = (
        P(None, ("dp", "tensor"), None),
        P(None, ("dp", "tensor"), None),
        P(None, "dp", "tensor"),
        P("tensor", "dp"),
        P("dp", "tensor"),
        P("tensor", "dp"),
        P(),
        P(None, "dp", "tensor"),
        P("tensor", "dp"),
        P("dp", "tensor"),
        P("tensor", "dp"),
        P(),
        P(None, "dp", "tensor"),
        P("tensor", "dp"),
        P("dp", "tensor"),
        P("tensor", "dp"),
        P(),
    )
    groups_fit = mesh.shape["tensor"] == MB and mesh.shape["dp"] == 16

    def pick(*arrays):
        if groups_fit and arrays[2].shape[1] == 1:
            return sequence_step(*arrays)
        return on_device(*arrays)

    return jax.shard_map(
        pick, mesh=mesh, in_specs=in_specs, out_specs=out_specs, check_vma=False
    )
```

```python
import math

import jax
import jax.numpy as jnp
from jax import lax
from jax.experimental import pallas as pl
from jax.experimental.pallas import tpu as pltpu
from jax.sharding import PartitionSpec as P

D = 1024
H = 16
HD = 64
FF = 4096
LEN = 1024
PIECE = 256
NPIECE = 2
MB = 2
NS_ITERS = 3


NORM_EPSILON = 1e-05
SQUARE_EPSILON = 1e-06
MASKED_SCORE = -1e30
SCHULZ_FIRST = 3.4445
SCHULZ_SECOND = -4.775
SCHULZ_THIRD = 2.0315
MOMENTUM_DECAY = 0.5
MATRIX_RATE = 0.5
VECTOR_RATE = 0.05


def layer_norm(inputs, gain_row, shift_row):
    average = jnp.mean(inputs, axis=-1, keepdims=True)
    centered = inputs - average
    variance = jnp.mean(centered * centered, axis=-1, keepdims=True)
    return centered * lax.rsqrt(variance + NORM_EPSILON) * gain_row + shift_row


def gelu_tanh(inputs):
    return jax.nn.gelu(inputs, approximate=True)


def score_layout(starts, slopes):
    positions = jnp.arange(LEN, dtype=jnp.int32)
    inside = (positions[None, :] >= starts[:, None]) & (
        positions[None, :] < starts[:, None] + PIECE
    )
    labels = jnp.arange(1, NPIECE + 1, dtype=jnp.int32)
    piece_label = jnp.sum(jnp.where(inside, labels[:, None], 0), axis=0)
    same_piece = (piece_label[:, None] == piece_label[None, :]) & (piece_label[:, None] > 0)
    visible = (positions[None, :] <= positions[:, None]) | same_piece
    distance = jnp.abs(positions[:, None] - positions[None, :]).astype(jnp.float32)
    penalty = -slopes[:, None, None] * distance[None, :, :]
    return (visible, penalty)


def head_scores(query_heads, key_heads, starts, slopes):
    visible, penalty = score_layout(starts, slopes)
    raw_scores = jnp.einsum(
        "qhd,khd->hqk", query_heads, key_heads, preferred_element_type=jnp.float32
    )
    scores = raw_scores * (1.0 / math.sqrt(HD)) + penalty
    return jnp.where(visible[None, :, :], scores, MASKED_SCORE)


def attend_forward(element, slopes):
    query_seq, key_seq, value_seq, starts = element
    heads_here = slopes.shape[0]
    query_heads = query_seq.reshape(LEN, heads_here, HD)
    key_heads = key_seq.reshape(LEN, heads_here, HD)
    value_heads = value_seq.reshape(LEN, heads_here, HD)
    scores = head_scores(query_heads, key_heads, starts, slopes)
    maximum = jnp.max(scores, axis=-1, keepdims=True)
    weights_raw = jnp.exp(scores - maximum)
    denominator = jnp.sum(weights_raw, axis=-1, keepdims=True)
    probabilities = weights_raw / denominator
    context = jnp.einsum(
        "hqk,khd->qhd",
        probabilities.astype(jnp.bfloat16),
        value_heads,
        preferred_element_type=jnp.float32,
    )
    logsum = (maximum + jnp.log(denominator))[..., 0]
    return (context.reshape(LEN, heads_here * HD), logsum)


def attend_backward(element, slopes):
    query_seq, key_seq, value_seq, context_grad, logsum, starts = element
    heads_here = slopes.shape[0]
    query_heads = query_seq.reshape(LEN, heads_here, HD)
    key_heads = key_seq.reshape(LEN, heads_here, HD)
    value_heads = value_seq.reshape(LEN, heads_here, HD)
    grad_heads = context_grad.reshape(LEN, heads_here, HD)
    scores = head_scores(query_heads, key_heads, starts, slopes)
    probabilities = jnp.exp(scores - logsum[..., None])
    grad_probs = jnp.einsum(
        "qhd,khd->hqk", grad_heads, value_heads, preferred_element_type=jnp.float32
    )
    inner_sum = jnp.sum(probabilities * grad_probs, axis=-1, keepdims=True)
    grad_scores = (probabilities * (grad_probs - inner_sum)).astype(jnp.bfloat16)
    scale_factor = 1.0 / math.sqrt(HD)
    grad_query = (
        jnp.einsum("hqk,khd->qhd", grad_scores, key_heads, preferred_element_type=jnp.float32)
        * scale_factor
    )
    grad_key = (
        jnp.einsum("hqk,qhd->khd", grad_scores, query_heads, preferred_element_type=jnp.float32)
        * scale_factor
    )
    grad_value = jnp.einsum(
        "hqk,qhd->khd",
        probabilities.astype(jnp.bfloat16),
        grad_heads,
        preferred_element_type=jnp.float32,
    )
    width_here = heads_here * HD
    return (
        grad_query.astype(jnp.bfloat16).reshape(LEN, width_here),
        grad_key.astype(jnp.bfloat16).reshape(LEN, width_here),
        grad_value.astype(jnp.bfloat16).reshape(LEN, width_here),
    )


def placed(values, offset, length):
    return lax.dynamic_update_slice_in_dim(jnp.zeros((length,), jnp.float32), values, offset, 0)


def accumulate(totals, addend):
    if totals is None:
        return addend
    return tuple((former + latter for former, latter in zip(totals, addend)))


def gram_term(narrow_rows, wide_rows):
    part_narrow = jnp.einsum(
        "mrc,mrd->cmd", narrow_rows, narrow_rows, preferred_element_type=jnp.float32
    )
    part_wide = jnp.einsum("mrc,mrd->cmd", wide_rows, wide_rows, preferred_element_type=jnp.float32)
    return jnp.concatenate([part_narrow, part_wide], axis=1)


def schulz_step(state, gram_matrix):
    turned = jnp.einsum("mrc,cmd->mrd", state, gram_matrix, preferred_element_type=jnp.float32)
    mixed = (SCHULZ_SECOND * state.astype(jnp.float32) + SCHULZ_THIRD * turned).astype(jnp.bfloat16)
    return (
        SCHULZ_FIRST * state.astype(jnp.float32)
        + jnp.einsum("mrc,cmd->mrd", mixed, gram_matrix, preferred_element_type=jnp.float32)
    ).astype(jnp.bfloat16)


def slice_term(source, weights, pattern):
    return jnp.einsum(pattern, source, weights, preferred_element_type=jnp.float32)


def on_device(
    tokens,
    cotangent,
    piece_starts,
    w_qkv,
    w_out,
    w_up,
    w_down,
    vectors,
    m_qkv,
    m_out,
    m_up,
    m_down,
    m_vec,
):
    tensor_count = lax.axis_size("tensor")
    tensor_rank = lax.axis_index("tensor")
    shard_rank = lax.axis_index("dp")
    heads_here = H // tensor_count
    width_here = heads_here * HD
    hidden_here = FF // tensor_count
    rows_here = tokens.shape[1]
    group_rows = rows_here * tensor_count
    seqs_here = piece_starts.shape[1]
    shard_rows = w_qkv.shape[1]
    head_ids = tensor_rank * heads_here + jnp.arange(heads_here, dtype=jnp.int32) + 1
    slopes = jnp.exp2(-8.0 * head_ids.astype(jnp.float32) / H)
    query_shift = lax.dynamic_slice_in_dim(vectors[2], tensor_rank * width_here, width_here, 0)
    value_shift = lax.dynamic_slice_in_dim(vectors[3], tensor_rank * width_here, width_here, 0)
    up_shift = lax.dynamic_slice_in_dim(
        vectors[7:11].reshape(FF), tensor_rank * hidden_here, hidden_here, 0
    )
    low_qkv = w_qkv.astype(jnp.bfloat16)
    low_out = w_out.astype(jnp.bfloat16)
    low_up = w_up.astype(jnp.bfloat16)
    low_down = w_down.astype(jnp.bfloat16)
    outputs_list = []
    input_grads = []
    vector_total = jnp.zeros((12, D), jnp.float32)
    grad_total = None

    def forward_one(element):
        return attend_forward(element, slopes)

    def backward_one(element):
        return attend_backward(element, slopes)

    for batch_index in range(MB):
        full_qkv, full_out, full_up, full_down = (
            lax.all_gather(low_qkv, "dp", axis=1, tiled=True),
            lax.all_gather(low_out, "dp", axis=1, tiled=True),
            lax.all_gather(low_up, "dp", axis=0, tiled=True),
            lax.all_gather(low_down, "dp", axis=1, tiled=True),
        )
        token_rows = tokens[batch_index].astype(jnp.float32)
        cotangent_rows = cotangent[batch_index]
        normed_one = layer_norm(token_rows, vectors[0], vectors[1])
        normed_all, cotangent_all = (
            lax.all_gather(normed_one.astype(jnp.bfloat16), "tensor", axis=0, tiled=True),
            lax.all_gather(cotangent_rows, "tensor", axis=0, tiled=True),
        )
        projected = jnp.einsum(
            "td,cde->cte", normed_all, full_qkv, preferred_element_type=jnp.float32
        )
        query_low = (projected[0] + query_shift).astype(jnp.bfloat16)
        key_low = projected[1].astype(jnp.bfloat16)
        value_low = (projected[2] + value_shift).astype(jnp.bfloat16)
        query_seqs = query_low.reshape(seqs_here, LEN, width_here)
        key_seqs = key_low.reshape(seqs_here, LEN, width_here)
        value_seqs = value_low.reshape(seqs_here, LEN, width_here)
        starts_here = piece_starts[batch_index]
        context_seq, logsum = lax.map(forward_one, (query_seqs, key_seqs, value_seqs, starts_here))
        context_low = context_seq.reshape(group_rows, width_here).astype(jnp.bfloat16)
        attended = lax.psum_scatter(
            slice_term(context_low, full_out, "tc,cd->td").astype(jnp.bfloat16),
            "tensor",
            scatter_dimension=0,
            tiled=True,
        ).astype(jnp.float32)
        middle = token_rows + attended + vectors[4]
        normed_two = layer_norm(middle, vectors[5], vectors[6])
        normed_two_all = lax.all_gather(
            normed_two.astype(jnp.bfloat16), "tensor", axis=0, tiled=True
        )
        before = jnp.dot(normed_two_all, full_up, preferred_element_type=jnp.float32) + up_shift
        activated = gelu_tanh(before).astype(jnp.bfloat16)
        expanded = lax.psum_scatter(
            slice_term(activated, full_down, "tf,fd->td").astype(jnp.bfloat16),
            "tensor",
            scatter_dimension=0,
            tiled=True,
        ).astype(jnp.float32)
        outputs_list.append((middle + expanded + vectors[11]).astype(jnp.bfloat16))
        grad_down = jnp.einsum(
            "tf,td->fd", activated, cotangent_all, preferred_element_type=jnp.float32
        )
        grad_activated = jnp.einsum(
            "td,fd->tf", cotangent_all, full_down, preferred_element_type=jnp.float32
        )
        gelu_pull = jax.vjp(gelu_tanh, before)[1]
        grad_before = gelu_pull(grad_activated)[0].astype(jnp.bfloat16)
        grad_up = jnp.einsum(
            "td,tf->df", normed_two_all, grad_before, preferred_element_type=jnp.float32
        )
        grad_normed_two = lax.psum_scatter(
            slice_term(grad_before, full_up, "tf,df->td").astype(jnp.bfloat16),
            "tensor",
            scatter_dimension=0,
            tiled=True,
        ).astype(jnp.float32)
        second_pull = jax.vjp(layer_norm, middle, vectors[5], vectors[6])[1]
        middle_from_norm, gain_two_grad, shift_two_grad = second_pull(grad_normed_two)
        grad_middle = cotangent_rows.astype(jnp.float32) + middle_from_norm
        grad_middle_all = lax.all_gather(
            grad_middle.astype(jnp.bfloat16), "tensor", axis=0, tiled=True
        )
        grad_out = jnp.einsum(
            "tc,td->cd", context_low, grad_middle_all, preferred_element_type=jnp.float32
        )
        grad_context = jnp.einsum(
            "td,cd->tc", grad_middle_all, full_out, preferred_element_type=jnp.float32
        ).astype(jnp.bfloat16)
        grad_query, grad_key, grad_value = lax.map(
            backward_one,
            (
                query_seqs,
                key_seqs,
                value_seqs,
                grad_context.reshape(seqs_here, LEN, width_here),
                logsum,
                starts_here,
            ),
        )
        grad_stack = jnp.stack(
            [
                grad_query.reshape(group_rows, width_here),
                grad_key.reshape(group_rows, width_here),
                grad_value.reshape(group_rows, width_here),
            ]
        )
        grad_qkv = jnp.einsum(
            "td,cte->cde", normed_all, grad_stack, preferred_element_type=jnp.float32
        )
        grad_normed_one = lax.psum_scatter(
            slice_term(grad_stack, full_qkv, "cte,cde->td").astype(jnp.bfloat16),
            "tensor",
            scatter_dimension=0,
            tiled=True,
        ).astype(jnp.float32)
        first_pull = jax.vjp(layer_norm, token_rows, vectors[0], vectors[1])[1]
        token_from_norm, gain_one_grad, shift_one_grad = first_pull(grad_normed_one)
        input_grads.append(grad_middle + token_from_norm)
        query_bias = jnp.sum(grad_stack[0], axis=0, dtype=jnp.float32)
        value_bias = jnp.sum(grad_stack[2], axis=0, dtype=jnp.float32)
        up_bias = jnp.sum(grad_before, axis=0, dtype=jnp.float32)
        head_rows = jnp.stack(
            [
                gain_one_grad,
                shift_one_grad,
                placed(query_bias, tensor_rank * width_here, D),
                placed(value_bias, tensor_rank * width_here, D),
                jnp.sum(grad_middle, axis=0),
                gain_two_grad,
                shift_two_grad,
            ]
        )
        up_rows = placed(up_bias, tensor_rank * hidden_here, FF).reshape(4, D)
        tail_row = jnp.sum(cotangent_rows, axis=0, dtype=jnp.float32)[None, :]
        vector_total = vector_total + jnp.concatenate([head_rows, up_rows, tail_row], axis=0)
        shard_grads = (
            lax.psum_scatter(
                grad_qkv.astype(jnp.bfloat16), "dp", scatter_dimension=1, tiled=True
            ).astype(jnp.float32),
            lax.psum_scatter(
                grad_out.astype(jnp.bfloat16), "dp", scatter_dimension=1, tiled=True
            ).astype(jnp.float32),
            lax.psum_scatter(
                grad_up.astype(jnp.bfloat16), "dp", scatter_dimension=0, tiled=True
            ).astype(jnp.float32),
            lax.psum_scatter(
                grad_down.astype(jnp.bfloat16), "dp", scatter_dimension=1, tiled=True
            ).astype(jnp.float32),
        )
        grad_total = accumulate(grad_total, shard_grads)
    grad_qkv_shard, grad_out_shard, grad_up_shard, grad_down_shard = grad_total
    moment_qkv = MOMENTUM_DECAY * m_qkv + grad_qkv_shard
    moment_out = MOMENTUM_DECAY * m_out + grad_out_shard
    moment_up = MOMENTUM_DECAY * m_up + grad_up_shard
    moment_down = MOMENTUM_DECAY * m_down + grad_down_shard
    squares = jnp.concatenate(
        [
            jnp.sum(moment_qkv * moment_qkv, axis=(1, 2)),
            jnp.stack(
                [
                    jnp.sum(moment_out * moment_out),
                    jnp.sum(moment_up * moment_up),
                    jnp.sum(moment_down * moment_down),
                ]
            ),
        ]
    )
    vector_grad, square_total = lax.psum((vector_total, squares), ("dp", "tensor"))
    factors = lax.rsqrt(square_total + SQUARE_EPSILON)
    scaled_qkv = (moment_qkv * factors[0:3][:, None, None]).astype(jnp.bfloat16)
    scaled_out = (moment_out * factors[3]).astype(jnp.bfloat16)
    scaled_up = (moment_up * factors[4]).astype(jnp.bfloat16)
    scaled_down = (moment_down * factors[5]).astype(jnp.bfloat16)
    gathered_qkv, gathered_out, gathered_up, gathered_down = (
        lax.all_gather(scaled_qkv, "dp", axis=1, tiled=True),
        lax.all_gather(scaled_out, "dp", axis=1, tiled=True),
        lax.all_gather(scaled_up, "dp", axis=0, tiled=True),
        lax.all_gather(scaled_down, "dp", axis=1, tiled=True),
    )
    offset = shard_rank * shard_rows
    narrow_rows = jnp.concatenate([jnp.swapaxes(gathered_qkv, 1, 2), gathered_out[None]], axis=0)
    wide_rows = jnp.stack([gathered_up.T, gathered_down])
    for sweep_index in range(NS_ITERS):
        gram_share = lax.psum_scatter(
            gram_term(narrow_rows, wide_rows).astype(jnp.bfloat16),
            "tensor",
            scatter_dimension=0,
            tiled=True,
        )
        gram_matrix = lax.all_gather(gram_share, "tensor", axis=0, tiled=True)
        narrow_rows = schulz_step(narrow_rows, gram_matrix[:, 0:4])
        wide_rows = schulz_step(wide_rows, gram_matrix[:, 4:6])
    final_narrow = narrow_rows.astype(jnp.float32)
    final_wide = wide_rows.astype(jnp.float32)
    update_qkv = lax.dynamic_slice_in_dim(
        jnp.swapaxes(final_narrow[0:3], 1, 2), offset, shard_rows, 1
    )
    update_out = lax.dynamic_slice_in_dim(final_narrow[3], offset, shard_rows, 1)
    update_up = lax.dynamic_slice_in_dim(final_wide[0].T, offset, shard_rows, 0)
    update_down = lax.dynamic_slice_in_dim(final_wide[1], offset, shard_rows, 1)
    wide_factor = math.sqrt(FF / D)
    new_qkv = w_qkv - MATRIX_RATE * update_qkv
    new_out = w_out - MATRIX_RATE * update_out
    new_up = w_up - MATRIX_RATE * wide_factor * update_up
    new_down = w_down - MATRIX_RATE * wide_factor * update_down
    moment_vec = MOMENTUM_DECAY * m_vec + vector_grad
    new_vec = vectors - VECTOR_RATE * moment_vec * lax.rsqrt(
        jnp.mean(moment_vec * moment_vec, axis=1, keepdims=True) + SQUARE_EPSILON
    )
    return (
        jnp.stack(outputs_list),
        jnp.stack(input_grads),
        grad_qkv_shard,
        grad_out_shard,
        grad_up_shard,
        grad_down_shard,
        vector_grad,
        moment_qkv,
        moment_out,
        moment_up,
        moment_down,
        moment_vec,
        new_qkv,
        new_out,
        new_up,
        new_down,
        new_vec,
    )


QB = 256
PAIR = 2 * HD
PAIRS = D // PAIR
VMEM_LIMIT = 56 * 1024 * 1024


def layout_grid(starts_ref, dist_ref):
    key_pos = lax.broadcasted_iota(jnp.int32, (LEN, LEN), 0)
    query_pos = lax.broadcasted_iota(jnp.int32, (LEN, LEN), 1)
    gap = query_pos - key_pos
    visible = gap >= 0
    for piece in range(NPIECE):
        start = starts_ref[piece]
        inside_key = (key_pos >= start) & (key_pos < start + PIECE)
        inside_query = (query_pos >= start) & (query_pos < start + PIECE)
        visible = visible | (inside_key & inside_query)
    dist_ref[...] = jnp.where(visible, jnp.abs(gap).astype(jnp.float32), -MASKED_SCORE)


def only_rows(pair, half):
    rows = lax.broadcasted_iota(jnp.int32, pair.shape, 0)
    return jnp.where((rows >= HD) if half else (rows < HD), pair, jnp.zeros_like(pair))


def only_cols(pair, half):
    cols = lax.broadcasted_iota(jnp.int32, pair.shape, 1)
    return jnp.where((cols >= HD) if half else (cols < HD), pair, jnp.zeros_like(pair))


def mul(left, right):
    return jnp.dot(left, right, preferred_element_type=jnp.float32)


def attend_pair(pair, slopes_ref, packed, dist_ref, ctx_ref, exps_ref, stat_ref, ctx_t, between):
    keys = packed[:, PAIR : 2 * PAIR]
    values_t = packed[:, 2 * PAIR :].T
    queries_t = (packed[:, :PAIR] * (1.0 / math.sqrt(HD))).T
    for half in (0, 1):
        slope = slopes_ref[2 * pair + half]
        queries = only_rows(queries_t, half)
        heads = slice(half * HD, half * HD + HD)
        for block in range(LEN // QB):
            span = min(LEN, QB * block + QB + PIECE)
            cols = slice(block * QB, block * QB + QB)
            scores = mul(keys[:span], queries[:, cols]) - slope * dist_ref[:span, cols]
            top = jnp.max(scores, axis=0, keepdims=True)
            raw = jnp.exp(scores - top)
            inverse = 1.0 / jnp.sum(raw, axis=0, keepdims=True)
            low = raw.astype(jnp.bfloat16)
            exps_ref[half, :span, cols] = low
            ctx_t[heads, cols] = mul(values_t[heads, :span], low) * inverse
            stat_ref[0, half : half + 1, cols] = inverse
        if half == 0:
            between()
    ctx_ref[...] = ctx_t[...].T.astype(jnp.bfloat16)


PACKED_COLS = pl.BlockSpec((LEN, 3 * PAIR), lambda p: (0, p))
PAIR_COLS = pl.BlockSpec((LEN, PAIR), lambda p: (0, p))
PAIR_GRID = pl.BlockSpec((2, LEN, LEN), lambda p: (p, 0, 0))
PAIR_STAT = pl.BlockSpec((1, 2, LEN), lambda p: (p, 0, 0))
SCALARS = pl.BlockSpec(memory_space=pltpu.SMEM)


HIDDEN = 512
CHUNK = 256
HIDDEN_STEPS = FF // HIDDEN
GELU_SLOPE = math.sqrt(2.0 / math.pi)
GELU_CUBE = 0.044715


def dot_last(left, right):
    return lax.dot_general(left, right, (((1,), (1,)), ((), ())), preferred_element_type=jnp.float32)


def gelu_both(rows):
    square = rows * rows
    bent = jnp.tanh(rows * (GELU_SLOPE + GELU_SLOPE * GELU_CUBE * square))
    half = 0.5 + 0.5 * bent
    slope = half + 0.5 * rows * (1.0 - bent * bent) * (GELU_SLOPE + 3.0 * GELU_SLOPE * GELU_CUBE * square)
    return rows * half, slope


def hidden_block(step):
    return (step % 2) * (HIDDEN_STEPS // 2) + step // 2


def mlp_kernel(
    rows_ref,
    cot_ref,
    base_ref,
    last_ref,
    bias_ref,
    up_ref,
    down_ref,
    slots_ref,
    block_ref,
    grad_rows_ref,
    grad_up_ref,
    grad_down_ref,
    bias_sum_ref,
    total_ref,
    rows_t,
    cot_t,
    total,
    up_part,
    down_part,
    active,
    grad_before,
    grad_early,
    first,
    second_y,
    second_x,
    third,
    fourth,
    sum_send,
    sum_recv,
    local_sem,
    spread_send,
    spread_recv,
    load_sem,
):
    step = pl.program_id(0)
    early_steps = 2 * EARLY
    table = []
    for index in range(HIDDEN_STEPS // 2 - EARLY):
        table += [(place_view(ref, 2 + 2 * index), HALF_SLOT) for ref in (up_part, down_part)]
    spread = Spread(slots_ref, table, local_sem, spread_send, spread_recv)

    def early_block(slot, part):
        return grad_early.at[slot % 2, 2 * (slot // 2) + part]

    def add_own(slot):
        for part in (0, 1):
            first[slot, part] = first[slot, part] + grad_early[slot % 2, 2 * (slot // 2) + part, :, :, summing.core]

    sources = [lambda part, slot=slot: early_block(slot, part) for slot in range(2 * EARLY)]
    buffers = (first, second_y, second_x, third, fourth)
    summing = Summing(sources, add_own, buffers, total_ref, (sum_send, sum_recv), 1)

    def loads(at):
        column = lax.rem(at, 2) * EARLY + at // 2
        cols = pl.ds(pl.multiple_of(column * HIDDEN, HIDDEN), HIDDEN)
        place = lax.rem(at, 2)
        return (
            pltpu.make_async_copy(up_ref.at[:, :, :, :, cols], up_part.at[place], load_sem.at[0, place]),
            pltpu.make_async_copy(down_ref.at[:, :, :, :, cols], down_part.at[place], load_sem.at[1, place]),
        )

    def sum_moves(moment):
        stages = (summing.stage_one, summing.stage_two, summing.stage_three, summing.stage_four)
        for slot in range(summing.count()):
            entry = 4 * (slot // 2 + 1) + slot % 2
            for number, stage in enumerate(stages):
                if moment == entry + 2 * number:
                    stage(slot)

    @pl.when(step == 0)
    def _():
        for copy in loads(step):
            copy.start()
        greet_neighbours([spread.sibling, spread.beside, spread.across] + spread.stations)
        spread.begin()
        rows_t[...] = rows_ref[...].T
        cot_t[...] = cot_ref[...].T
        total[...] = base_ref[...] + last_ref[...]
        grad_rows_ref[...] = jnp.zeros_like(grad_rows_ref)

    @pl.when(step < early_steps)
    def _():
        for copy in loads(step):
            copy.wait()

    @pl.when(step < early_steps - 1)
    def _():
        for copy in loads(step + 1):
            copy.start()

    for index in range(HIDDEN_STEPS // 2 - EARLY):

        @pl.when(step == early_steps + 2 * index)
        def _(index=index):
            spread.arrived(2 * index)
            spread.arrived(2 * index + 1)

    place = jnp.where(step < early_steps, lax.rem(step, 2), step - early_steps + 2)
    up = up_part[place].reshape(D, HIDDEN)
    down = down_part[place].reshape(D, HIDDEN)
    bias = bias_ref[...]
    bias_sum = jnp.zeros((1, HIDDEN), jnp.float32)
    for index in range(LEN // CHUNK):
        here = slice(index * CHUNK, index * CHUNK + CHUNK)
        value, slope = gelu_both(mul(rows_ref[here], up) + bias)
        value = value.astype(jnp.bfloat16)
        grads = (slope * mul(cot_ref[here], down)).astype(jnp.bfloat16)
        active[here] = value
        grad_before[here] = grads
        bias_sum += jnp.sum(grads.astype(jnp.float32), axis=0, keepdims=True)
        total[here] += dot_last(value, down)
        grad_rows_ref[here] += dot_last(grads, up)
        if index == LEN // CHUNK // 2 - 1:
            for number in range(spread.ticks()):
                pl.when(step == number)(lambda number=number: spread.tick(number))
            for number in range(HIDDEN_STEPS):
                pl.when(step == number)(lambda number=number: sum_moves(2 * number))
    bias_sum_ref[...] = bias_sum

    @pl.when(step < early_steps)
    def _():
        for index, (left, right) in enumerate(((rows_t, grad_before), (cot_t, active))):
            grads = mul(left[...], right[...]).astype(jnp.bfloat16)
            grad_early[index, step] = grads.reshape(grad_early.shape[2:])

    @pl.when(step >= early_steps)
    def _():
        grad_up_ref[...] = mul(rows_t[...], grad_before[...]).astype(jnp.bfloat16)
        grad_down_ref[...] = mul(cot_t[...], active[...]).astype(jnp.bfloat16)

    for number in range(HIDDEN_STEPS):

        @pl.when(step == number)
        def _(number=number):
            if number < early_steps and number % 2:
                summing.send_first(number - 1)
                summing.send_first(number)
            sum_moves(2 * number + 1)

    @pl.when(step == HIDDEN_STEPS - 1)
    def _():
        block_ref[...] = total[...].astype(jnp.bfloat16)
        summing.sent()
        spread.sent()


def late_block(step):
    late = HIDDEN_STEPS // 2 - EARLY
    return jnp.where(step < 2 * EARLY, 0, (step % 2) * late + step // 2 - EARLY)


def mlp_both(rows, cot, base, last, bias, up, down, slots):
    anywhere = pl.BlockSpec(memory_space=pl.ANY)
    once = pl.Buffered(1)
    whole = pl.BlockSpec((LEN, D), lambda s: (0, 0), pipeline_mode=once)
    hidden = pl.BlockSpec((D, HIDDEN), lambda s: (0, late_block(s)))
    hidden_row = pl.BlockSpec((1, HIDDEN), lambda s: (0, hidden_block(s)))
    low = jnp.bfloat16
    late = HIDDEN_STEPS // 2 - EARLY
    part = pltpu.VMEM((2 + 2 * late, 4, 2, 2, 64, HIDDEN), low)
    split = [weights.reshape(4, 2, 2, 64, -1) for weights in (up, down)]
    return pl.pallas_call(
        mlp_kernel,
        grid=(HIDDEN_STEPS,),
        in_specs=[whole, whole, whole, pl.BlockSpec((1, D), lambda s: (0, 0)), hidden_row, anywhere, anywhere, anywhere],
        out_specs=[
            whole,
            whole,
            hidden,
            hidden,
            hidden_row,
            pl.BlockSpec((2 * EARLY, 64, SLOT), lambda s: (0, 0, 0), pipeline_mode=once),
        ],
        out_shape=[
            jax.ShapeDtypeStruct((LEN, D), low),
            jax.ShapeDtypeStruct((LEN, D), jnp.float32),
            jax.ShapeDtypeStruct((D, 2 * late * HIDDEN), low),
            jax.ShapeDtypeStruct((D, 2 * late * HIDDEN), low),
            jax.ShapeDtypeStruct((1, FF), jnp.float32),
            jax.ShapeDtypeStruct((2 * EARLY, 64, SLOT), jnp.float32),
        ],
        scratch_shapes=[
            pltpu.VMEM((D, LEN), low),
            pltpu.VMEM((D, LEN), low),
            pltpu.VMEM((LEN, D), jnp.float32),
            part,
            part,
            pltpu.VMEM((LEN, HIDDEN), low),
            pltpu.VMEM((LEN, HIDDEN), low),
            pltpu.VMEM((2, 2 * EARLY, 4, 2, 2, 64, HIDDEN), low),
            *summing_buffers(2 * EARLY),
            *spread_semaphores(2 * late),
            pltpu.SemaphoreType.DMA((2, 2)),
        ],
        compiler_params=pltpu.CompilerParams(
            collective_id=5, has_side_effects=True, vmem_limit_bytes=62 * 1024 * 1024
        ),
        cost_estimate=pl.CostEstimate(
            flops=12 * LEN * D * FF, bytes_accessed=60 * 1024 * 1024, transcendentals=LEN * FF
        ),
    )(rows, cot, base, last, bias, *split, slots)


SLOTS = 12
SLOT = 512
HALF_SLOT = SLOT // 2
TILE = 256
GRAM_TILES = 5
POLY_TILE = 512
MESH_IDS = pl.DeviceIdType.MESH


def handler_of(slot):
    wide = slot - 4
    square = slot < 4
    dp_index = jnp.where(square, jnp.where(slot < 2, 2, 12), 4 + 6 * (wide // 4) + wide % 2)
    tensor_index = jnp.where(square, slot % 2, (wide // 2) % 2)
    return dp_index, tensor_index


def muon_kernel(
    moments_ref,
    vec_ref,
    block_ref,
    token_ref,
    updates_ref,
    vec_out_ref,
    block_pair_ref,
    token_pair_ref,
    pieces,
    turned,
    vec_pieces,
    vec_sum,
    gram,
    gram_low,
    poly_low,
    half_low,
    chain_low,
    chain_next,
    out_half,
    in_half,
    local_sem,
    send_sem,
    recv_sem,
    half_send,
    half_recv,
    swap_sem,
):
    groups = lax.axis_size("dp")
    parts = lax.axis_size("tensor")
    count = groups * parts
    dp_me = lax.axis_index("dp")
    t_me = lax.axis_index("tensor")
    me = t_me * groups + dp_me
    is_square = (dp_me == 2) | (dp_me == 12)
    is_up = (dp_me == 4) | (dp_me == 5)
    is_down = (dp_me == 10) | (dp_me == 11)
    is_wide = is_up | is_down
    is_handler = is_square | is_wide
    wide_slot = jnp.where(is_up, 4 + (dp_me - 4), 8 + (dp_me - 10)) + 2 * t_me
    slot_me = jnp.where(is_square, t_me + jnp.where(dp_me == 12, 2, 0), wide_slot)
    slot_me = jnp.where(is_handler, slot_me, 0)

    barrier = pltpu.get_barrier_semaphore()

    def greet(step, carry):
        other = lax.rem(me + step, count)
        pl.semaphore_signal(
            barrier, inc=1, device_id=(lax.rem(other, groups), other // groups), device_id_type=MESH_IDS
        )
        return carry

    lax.fori_loop(1, count, greet, 0)
    pl.semaphore_wait(barrier, count - 1)

    def give(step, carry):
        slot = lax.rem(me + step, SLOTS)
        dp_to, t_to = handler_of(slot)
        away = (dp_to != dp_me) | (t_to != t_me)

        @pl.when(away)
        def _():
            pltpu.make_async_remote_copy(
                src_ref=vec_ref.at[slot],
                dst_ref=vec_pieces.at[me],
                send_sem=send_sem.at[1],
                recv_sem=recv_sem.at[1],
                device_id=(dp_to, t_to),
                device_id_type=MESH_IDS,
            ).start()
            pltpu.make_async_remote_copy(
                src_ref=moments_ref.at[slot],
                dst_ref=pieces.at[me],
                send_sem=send_sem.at[0],
                recv_sem=recv_sem.at[0],
                device_id=(dp_to, t_to),
                device_id_type=MESH_IDS,
            ).start()

        return carry

    lax.fori_loop(0, SLOTS, give, 0)

    rows = block_ref.shape[0] // 2
    kept_rows = pl.ds(pl.multiple_of(t_me * rows, rows), rows)
    sent_rows = pl.ds(pl.multiple_of((1 - t_me) * rows, rows), rows)
    kept = []
    swaps = []
    for index, (whole, pair) in enumerate(((block_ref, block_pair_ref), (token_ref, token_pair_ref))):
        kept.append(pltpu.make_async_copy(whole.at[kept_rows], pair.at[t_me], swap_sem.at[2, index]))
        swaps.append(
            pltpu.make_async_remote_copy(
                src_ref=whole.at[sent_rows],
                dst_ref=pair.at[t_me],
                send_sem=swap_sem.at[0, index],
                recv_sem=swap_sem.at[1, index],
                device_id=(dp_me, 1 - t_me),
                device_id_type=MESH_IDS,
            )
        )

    for copy in kept:
        copy.start()

    @pl.when(jnp.logical_not(is_wide))
    def _():
        for copy in swaps:
            copy.start()

    def give_back(source, sem, target):
        def one(step, carry):
            other = lax.rem(me + step, count)
            pltpu.make_async_remote_copy(
                src_ref=source.at[other] if source is turned else source,
                dst_ref=target.at[slot_me],
                send_sem=send_sem.at[sem],
                recv_sem=recv_sem.at[sem],
                device_id=(lax.rem(other, groups), other // groups),
                device_id_type=MESH_IDS,
            ).start()
            return carry

        lax.fori_loop(1, count, one, 0)

    @pl.when(is_handler)
    def _():
        own = [
            pltpu.make_async_copy(vec_ref.at[slot_me], vec_pieces.at[me], local_sem.at[0]),
            pltpu.make_async_copy(moments_ref.at[slot_me], pieces.at[me], local_sem.at[1]),
        ]
        for copy in own:
            copy.start()
        for copy in own:
            copy.wait()
        rest = pl.ds(0, count - 1)
        pltpu.make_async_copy(vec_pieces.at[rest], vec_pieces.at[rest], recv_sem.at[1]).wait()
        vec_sum[...] = jnp.sum(vec_pieces[...], axis=0)
        give_back(vec_sum, 2, vec_out_ref)
        own_vec = pltpu.make_async_copy(vec_sum, vec_out_ref.at[slot_me], local_sem.at[0])
        own_vec.start()
        own_vec.wait()
        pltpu.make_async_copy(pieces.at[rest], pieces.at[rest], recv_sem.at[0]).wait()

        rows_of = TILE // 64

        def gram_tile(tile, carry):
            rows = pl.ds(pl.multiple_of(tile * TILE, TILE), TILE)
            total = jnp.zeros((TILE, D), jnp.float32)
            for part in range(parts):
                left = pieces[pl.ds(part * groups + tile * rows_of, rows_of)].reshape(TILE, SLOT)
                right = pieces[part * groups : (part + 1) * groups].reshape(D, SLOT)
                total += lax.dot_general(
                    left, right, (((1,), (1,)), ((), ())), preferred_element_type=jnp.float32
                )
            gram[rows, :] = total
            return carry

        lax.fori_loop(0, D // TILE, gram_tile, 0)

        @pl.when(is_wide)
        def _():
            core = lax.rem(dp_me, 2)
            sibling = (dp_me + 1 - 2 * core, t_me)
            across = (dp_me, 1 - t_me)

            def tile_at(index, owner):
                if index == 4:
                    row, col = jnp.where(owner == 0, 3, 2), 3
                elif index == 3:
                    row, col = jnp.where(owner == 0, 0, 2), jnp.where(owner == 0, 3, 2)
                else:
                    row, col = owner, owner + index
                return (
                    pl.ds(pl.multiple_of(row * TILE, TILE), TILE),
                    pl.ds(pl.multiple_of(col * TILE, TILE), TILE),
                )

            def exchange(stage, index, place):
                return pltpu.make_async_remote_copy(
                    src_ref=out_half.at[stage, index],
                    dst_ref=in_half.at[stage, index],
                    send_sem=half_send.at[stage, index],
                    recv_sem=half_recv.at[stage, index],
                    device_id=place,
                    device_id_type=MESH_IDS,
                )

            for index in range(GRAM_TILES):
                out_half[0, index] = gram[tile_at(index, 1 - core)].astype(jnp.bfloat16)
                exchange(0, index, sibling).start()
            for index in range(GRAM_TILES):
                exchange(0, index, sibling).wait_recv()
                total = gram[tile_at(index, core)] + in_half[0, index].astype(jnp.float32)
                out_half[1, index] = total.astype(jnp.bfloat16)
                exchange(1, index, across).start()
            for index in range(GRAM_TILES):
                exchange(1, index, across).wait_recv()
                total = out_half[1, index].astype(jnp.float32) + in_half[1, index].astype(jnp.float32)
                out_half[2, index] = total.astype(jnp.bfloat16)
                exchange(2, index, sibling).start()
                rows, cols = tile_at(index, core)
                gram[cols, rows] = out_half[2, index].astype(jnp.float32).T
                gram[rows, cols] = out_half[2, index].astype(jnp.float32)
            for index in range(GRAM_TILES):
                exchange(2, index, sibling).wait_recv()
                rows, cols = tile_at(index, 1 - core)
                gram[cols, rows] = in_half[2, index].astype(jnp.float32).T
                gram[rows, cols] = in_half[2, index].astype(jnp.float32)
            for index in range(GRAM_TILES):
                exchange(0, index, sibling).wait_send()
                exchange(1, index, across).wait_send()
                exchange(2, index, sibling).wait_send()
            for copy in swaps:
                copy.start()

        def trace_tile(tile, total):
            rows = pl.ds(pl.multiple_of(tile * TILE, TILE), TILE)
            row_ids = lax.broadcasted_iota(jnp.int32, (TILE, D), 0) + tile * TILE
            col_ids = lax.broadcasted_iota(jnp.int32, (TILE, D), 1)
            diagonal = jnp.where(row_ids == col_ids, gram[rows, :], 0.0)
            return total + jnp.sum(jnp.sum(diagonal, axis=0, keepdims=True), axis=1, keepdims=True)

        square_total = lax.fori_loop(0, D // TILE, trace_tile, jnp.zeros((1, 1), jnp.float32))
        factor = lax.rsqrt(square_total + SQUARE_EPSILON)
        gram_low[...] = (gram[...] * (factor * factor)).astype(jnp.bfloat16)

        first, second, third = SCHULZ_FIRST, SCHULZ_SECOND, SCHULZ_THIRD

        def tiles(body):
            def one(tile, carry):
                body(pl.ds(pl.multiple_of(tile * POLY_TILE, POLY_TILE), POLY_TILE))
                return carry

            lax.fori_loop(0, D // POLY_TILE, one, 0)

        chain = chain_low
        other = chain_next
        for sweep in range(NS_ITERS):
            target = chain if sweep == 0 else poly_low

            def poly(rows):
                square = mul(gram_low[rows, :], gram_low[...])
                grown = (second / first) * gram_low[rows, :].astype(jnp.float32) + (third / first) * square
                target[rows, :] = grown.astype(jnp.bfloat16)

            tiles(poly)
            if sweep > 0:

                def join(rows, chain=chain, other=other):
                    total = chain[rows, :].astype(jnp.float32) + poly_low[rows, :].astype(jnp.float32)
                    other[rows, :] = (total + mul(chain[rows, :], poly_low[...])).astype(jnp.bfloat16)

                tiles(join)
                chain, other = other, chain
            if sweep < NS_ITERS - 1:

                def half(rows):
                    grown = gram_low[rows, :].astype(jnp.float32) + mul(gram_low[rows, :], target[...])
                    half_low[rows, :] = grown.astype(jnp.bfloat16)

                def full(rows):
                    grown = half_low[rows, :].astype(jnp.float32) + mul(half_low[rows, :], target[...])
                    gram_low[rows, :] = (grown * (first * first)).astype(jnp.bfloat16)

                tiles(half)
                tiles(full)

        scale = factor * (first**NS_ITERS)

        def turn_tile(tile, carry):
            rows = pl.ds(pl.multiple_of(tile * TILE, TILE), TILE)
            for part in range(parts):
                at = pl.ds(part * groups + tile * rows_of, rows_of)
                whole = pieces[part * groups : (part + 1) * groups].reshape(D, SLOT)
                kept = pieces[at].reshape(TILE, SLOT).astype(jnp.float32)
                fresh = (kept + mul(chain[rows, :], whole)) * scale
                turned[at] = fresh.astype(jnp.bfloat16).reshape(rows_of, 64, SLOT)
            return carry

        lax.fori_loop(0, D // TILE, turn_tile, 0)
        give_back(turned, 3, updates_ref)
        own_turned = pltpu.make_async_copy(turned.at[me], updates_ref.at[slot_me], local_sem.at[1])
        own_turned.start()
        own_turned.wait()

    def finish(length):
        here = pl.ds(0, length)
        pltpu.make_async_copy(vec_ref.at[here], vec_ref.at[here], send_sem.at[1]).wait()
        pltpu.make_async_copy(moments_ref.at[here], moments_ref.at[here], send_sem.at[0]).wait()
        pltpu.make_async_copy(vec_out_ref.at[here], vec_out_ref.at[here], recv_sem.at[2]).wait()
        pltpu.make_async_copy(updates_ref.at[here], updates_ref.at[here], recv_sem.at[3]).wait()

    @pl.when(is_handler)
    def _():
        finish(SLOTS - 1)
        rest = pl.ds(0, count - 1)
        pltpu.make_async_copy(vec_pieces.at[rest], vec_pieces.at[rest], send_sem.at[2]).wait()
        pltpu.make_async_copy(turned.at[rest], turned.at[rest], send_sem.at[3]).wait()

    @pl.when(jnp.logical_not(is_handler))
    def _():
        finish(SLOTS)

    for copy in kept + swaps:
        copy.wait()


def muon_call(moments, vec_parts, block_rows, token_grads):
    count = lax.axis_size("dp") * lax.axis_size("tensor")
    rows = moments.shape[1]
    vmem = pl.BlockSpec(memory_space=pltpu.VMEM)
    anywhere = pl.BlockSpec(memory_space=pl.ANY)
    pair = jax.ShapeDtypeStruct((2, LEN // 2, D), jnp.bfloat16)
    low = pltpu.VMEM((D, D), jnp.bfloat16)
    return pl.pallas_call(
        muon_kernel,
        in_specs=[vmem, vmem, anywhere, anywhere],
        out_specs=[vmem, vmem, anywhere, anywhere],
        out_shape=[
            jax.ShapeDtypeStruct(moments.shape, jnp.bfloat16),
            jax.ShapeDtypeStruct(vec_parts.shape, jnp.float32),
            pair,
            pair,
        ],
        scratch_shapes=[
            pltpu.VMEM((count, rows, SLOT), jnp.bfloat16),
            pltpu.VMEM((count, rows, SLOT), jnp.bfloat16),
            pltpu.VMEM((count,) + vec_parts.shape[1:], jnp.float32),
            pltpu.VMEM(vec_parts.shape[1:], jnp.float32),
            pltpu.VMEM((D, D), jnp.float32),
            low,
            low,
            low,
            low,
            low,
            pltpu.VMEM((3, GRAM_TILES, TILE, TILE), jnp.bfloat16),
            pltpu.VMEM((3, GRAM_TILES, TILE, TILE), jnp.bfloat16),
            pltpu.SemaphoreType.DMA((2,)),
            pltpu.SemaphoreType.DMA((4,)),
            pltpu.SemaphoreType.DMA((4,)),
            pltpu.SemaphoreType.DMA((3, GRAM_TILES)),
            pltpu.SemaphoreType.DMA((3, GRAM_TILES)),
            pltpu.SemaphoreType.DMA((3, 2)),
        ],
        compiler_params=pltpu.CompilerParams(
            collective_id=1, has_side_effects=True, vmem_limit_bytes=VMEM_LIMIT
        ),
        cost_estimate=pl.CostEstimate(flops=12 * 2 * D**3, bytes_accessed=4 * 1024 * 1024, transcendentals=0),
    )(moments, vec_parts, block_rows, token_grads)


def neighbours():
    dp_me = lax.axis_index("dp")
    y = lax.axis_index("tensor")
    core = lax.rem(dp_me, 2)
    x = lax.rem(dp_me // 2, 2)
    z = dp_me // 4
    sibling = (dp_me + 1 - 2 * core, y)
    beside = (dp_me + 2 - 4 * x, y)
    across = (dp_me, 1 - y)
    stations = [(lax.rem(dp_me + 4 * hop, 16), y) for hop in (1, 2, 3)]
    return (z, x, core, y), sibling, beside, across, stations


def greet_neighbours(places):
    barrier = pltpu.get_barrier_semaphore()
    for place in places:
        pl.semaphore_signal(barrier, inc=1, device_id=place, device_id_type=MESH_IDS)
    pl.semaphore_wait(barrier, len(places))


EARLY = 2
AHEAD = 2


class Spread:
    def __init__(self, slots_ref, table, local_sem, send_sem, recv_sem):
        self.slots_ref, self.table = slots_ref, table
        self.local_sem, self.send_sem, self.recv_sem = local_sem, send_sem, recv_sem
        (self.z, self.x, self.core, self.y), self.sibling, self.beside, self.across, self.stations = neighbours()

    def remote(self, source, target, stage, slot, place):
        return pltpu.make_async_remote_copy(
            src_ref=source,
            dst_ref=target,
            send_sem=self.send_sem.at[stage, slot],
            recv_sem=self.recv_sem.at[stage, slot],
            device_id=place,
            device_id_type=MESH_IDS,
        )

    def own(self, slot):
        here = self.table[slot][0](self.y, 0, SLOT).at[self.z, self.x, self.core]
        return pltpu.make_async_copy(self.slots_ref.at[slot], here, self.local_sem.at[slot])

    def along_z(self, slot):
        here = self.table[slot][0](self.y, 0, SLOT).at[self.z, self.x, self.core]
        return [
            self.remote(self.slots_ref.at[slot], here, hop, slot, place)
            for hop, place in enumerate(self.stations)
        ]

    def second(self, slot):
        view, size = self.table[slot]
        copies = []
        if size:
            part = view(self.y, 0, size).at[:, self.x, self.core]
            copies.append(self.remote(part, part, 3, slot, self.beside))
        if size < SLOT:
            part = view(self.y, size, SLOT - size).at[:, self.x, self.core]
            copies.append(self.remote(part, part, 4, slot, self.across))
        return copies

    def third(self, slot):
        view, size = self.table[slot]
        copies = []
        if size:
            part = view(self.y, 0, size).at[:, :, self.core]
            copies.append(self.remote(part, part, 5, slot, self.across))
        if size < SLOT:
            for index in (0, 1):
                part = view(index, size, SLOT - size).at[:, self.x, self.core]
                copies.append(self.remote(part, part, 6 + index, slot, self.beside))
        return copies

    def fourth(self, slot):
        view, _ = self.table[slot]
        copies = []
        for index in (0, 1):
            part = view(index, 0, SLOT).at[:, :, self.core]
            copies.append(self.remote(part, part, 8 + index, slot, self.sibling))
        return copies

    def launch(self, slot):
        if slot < len(self.table):
            self.own(slot).start()
            for copy in self.along_z(slot):
                copy.start()

    def begin(self):
        for slot in range(AHEAD):
            self.launch(slot)

    def push_second(self, slot):
        self.own(slot).wait()
        for copy in self.along_z(slot):
            copy.wait_recv()
        for copy in self.second(slot):
            copy.start()

    def push_third(self, slot):
        for copy in self.second(slot):
            copy.wait_recv()
        for copy in self.third(slot):
            copy.start()

    def push_fourth(self, slot):
        for copy in self.third(slot):
            copy.wait_recv()
        for copy in self.fourth(slot):
            copy.start()

    def tick(self, index):
        count = len(self.table)
        self.launch(index + AHEAD)
        if index < count:
            self.push_second(index)
        if 0 <= index - 1 < count:
            self.push_third(index - 1)
        if 0 <= index - 2 < count:
            self.push_fourth(index - 2)

    def ticks(self):
        return len(self.table) + 2

    def arrived(self, slot):
        for copy in self.fourth(slot):
            copy.wait_recv()

    def sent(self):
        for slot in range(len(self.table)):
            for copy in self.along_z(slot) + self.second(slot) + self.third(slot) + self.fourth(slot):
                copy.wait_send()


def column_view(ref, column, distance):
    def view(part, start, size):
        first = column + part * distance + start
        if not isinstance(part, int):
            first = pl.multiple_of(first, 128)
        return ref.at[:, :, :, :, pl.ds(first, size)]

    return view


def place_view(ref, place):
    def view(part, start, size):
        return ref.at[place + part, :, :, :, :, pl.ds(start, size)]

    return view


def spread_semaphores(count):
    return [
        pltpu.SemaphoreType.DMA((count,)),
        pltpu.SemaphoreType.DMA((10, count)),
        pltpu.SemaphoreType.DMA((10, count)),
    ]


def pair_of(step):
    return (step % 2) * (PAIRS // 2) + step // 2


def fill_slots(w_qkv_ref, w_out_ref, w_up_ref, w_down_ref, slots_ref, later_ref):
    low = jnp.bfloat16
    for pair in range(SLOT // PAIR):
        for part in range(3):
            column = (pair * 3 + part) * PAIR
            source = w_qkv_ref[part, :, pair * PAIR : (pair + 1) * PAIR].astype(low)
            slots_ref[column // SLOT, :, column % SLOT : column % SLOT + PAIR] = source
    slots_ref[3] = w_out_ref[...].astype(low)
    for index in range(4):
        target, place = (slots_ref, 4 + 2 * index) if index < EARLY else (later_ref, 2 * (index - EARLY))
        for kind, ref in enumerate((w_up_ref, w_down_ref)):
            target[place + kind] = ref[:, index * SLOT : (index + 1) * SLOT].astype(low)


def attend_spread_kernel(
    starts_ref,
    slopes_ref,
    norm_ref,
    middle_rows_ref,
    shifts_ref,
    w_qkv_ref,
    w_out_ref,
    w_up_ref,
    w_down_ref,
    tokens_ref,
    cotangent_ref,
    packed_ref,
    ctx_ref,
    exps_ref,
    stat_ref,
    normed_t_ref,
    rows_ref,
    middle_ref,
    normed_two_ref,
    later_ref,
    qkv_ref,
    out_ref,
    up_ref,
    down_ref,
    cot_ref,
    slots_ref,
    dist_ref,
    ctx_t,
    ctx_all,
    out_weights,
    rows,
    normed,
    weights,
    local_sem,
    send_sem,
    recv_sem,
    swap_sem,
    load_sem,
):
    step = pl.program_id(0)
    pair = pair_of(step)
    table = [(column_view(qkv_ref, index * SLOT, 3 * SLOT), SLOT if index == 1 else 0) for index in range(3)]
    table += [(column_view(out_ref, 0, SLOT), 0)]
    for index in range(EARLY):
        for ref, over_x in ((up_ref, 0), (down_ref, HALF_SLOT if index else 0)):
            table += [(column_view(ref, index * SLOT, EARLY * SLOT), over_x)]
    count = len(table)
    spread = Spread(slots_ref, table, local_sem, send_sem, recv_sem)
    half_rows = pl.ds(pl.multiple_of(spread.y * (LEN // 2), LEN // 2), LEN // 2)
    own_rows = pltpu.make_async_copy(tokens_ref.at[spread.y], rows.at[half_rows], load_sem.at[2])

    def swap(source, target, index):
        return pltpu.make_async_remote_copy(
            src_ref=source.at[1 - spread.y],
            dst_ref=target,
            send_sem=swap_sem.at[0, index],
            recv_sem=swap_sem.at[1, index],
            device_id=spread.across,
            device_id_type=MESH_IDS,
        )

    token_swap = swap(tokens_ref, rows.at[half_rows], 0)
    cotangent_swap = swap(cotangent_ref, cot_ref.at[half_rows], 1)
    own_cotangent = pltpu.make_async_copy(cotangent_ref.at[spread.y], cot_ref.at[half_rows], load_sem.at[3])
    out_load = pltpu.make_async_copy(out_ref, out_weights, load_sem.at[4])

    def load(at):
        cols = pl.ds(pl.multiple_of(pair_of(at) * (3 * PAIR), PAIR), 3 * PAIR)
        place = lax.rem(at, 2)
        return pltpu.make_async_copy(qkv_ref.at[:, :, :, :, cols], weights.at[place], load_sem.at[place])

    @pl.when(step == 0)
    def _():
        fill_slots(w_qkv_ref, w_out_ref, w_up_ref, w_down_ref, slots_ref, later_ref)
        greet_neighbours([spread.sibling, spread.beside, spread.across] + spread.stations)
        own_rows.start()
        for slot in range(3):
            spread.launch(slot)
        spread.push_second(0)
        token_swap.start()
        spread.push_second(1)
        spread.push_third(0)
        spread.push_second(2)
        for slot in range(3, count):
            spread.launch(slot)
        layout_grid(starts_ref, dist_ref)
        spread.push_fourth(0)
        own_rows.wait()
        token_swap.wait_recv()
        spread.push_third(1)
        for index in range(LEN // CHUNK):
            here = slice(index * CHUNK, index * CHUNK + CHUNK)
            block = rows[here].astype(jnp.float32)
            low = layer_norm(block, norm_ref[0:1], norm_ref[1:2]).astype(jnp.bfloat16)
            normed[here] = low
            normed_t_ref[:, here] = low.T
            rows_ref[here] = rows[here]
        own_cotangent.start()

    for slot in range(3):

        @pl.when(step == 2 * slot)
        def _(slot=slot):
            spread.arrived(slot)

    @pl.when(lax.rem(step, 2) == 0)
    def _():
        load(step).start()

    load(step).wait()

    def between():
        @pl.when(lax.rem(step, 2) == 0)
        def _():
            load(step + 1).start()

        moves = (
            ((), (), 3),
            ((1,), (2,), 4),
            ((), (3,), 5),
            ((2,), (4,), 6),
            ((3,), (5,), 7),
            ((4,), (6,), None),
            ((5,), (7,), None),
            ((6,), (), None),
        )
        for index, (fourth, third, fresh) in enumerate(moves):

            @pl.when(step == index)
            def _(index=index, fourth=fourth, third=third, fresh=fresh):
                for slot in fourth:
                    spread.push_fourth(slot)
                for slot in third:
                    spread.push_third(slot)
                if fresh is not None:
                    spread.push_second(fresh)
                if fresh == count - 1:
                    cotangent_swap.start()

    packed = mul(normed[...], weights[lax.rem(step, 2)].reshape(D, 3 * PAIR)) + shifts_ref[...]
    packed = packed.astype(jnp.bfloat16)
    packed_ref[...] = packed
    @pl.when(step == PAIRS - 1)
    def _():
        spread.arrived(3)
        out_load.start()

    attend_pair(pair, slopes_ref, packed, dist_ref, ctx_ref, exps_ref, stat_ref, ctx_t, between)
    ctx_all[:, pl.ds(pl.multiple_of(pair * PAIR, PAIR), PAIR)] = ctx_ref[...]

    @pl.when(step == PAIRS - 1)
    def _():
        out_load.wait()
        for index in range(LEN // CHUNK):
            here = slice(index * CHUNK, index * CHUNK + CHUNK)
            attended = dot_last(ctx_all[here], out_weights[...].reshape(D, D))
            middle = rows[here].astype(jnp.float32) + attended + middle_rows_ref[0:1]
            middle_ref[here] = middle
            normed_two = layer_norm(middle, middle_rows_ref[1:2], middle_rows_ref[2:3])
            normed_two_ref[here] = normed_two.astype(jnp.bfloat16)
            if index == LEN // CHUNK // 2 - 1:
                spread.push_fourth(count - 1)
        for slot in range(4, count):
            spread.arrived(slot)
        spread.sent()
        token_swap.wait_send()
        cotangent_swap.wait()
        own_cotangent.wait()


def whole_shape(columns):
    return jax.ShapeDtypeStruct((4, 2, 2, 64, columns), jnp.bfloat16)


def attend_spread(starts, slopes, norm_rows, middle_rows, shifts, weights, tokens, cotangent):
    anywhere = pl.BlockSpec(memory_space=pl.ANY)
    once = pl.Buffered(1)
    whole = pl.BlockSpec((LEN, D), lambda s: (0, 0), pipeline_mode=once)
    low = jnp.bfloat16
    later = (2 * (4 - EARLY), 64, SLOT)
    *local, qkv, out, up, down, cotangent_rows = pl.pallas_call(
        attend_spread_kernel,
        grid=(PAIRS,),
        in_specs=[
            SCALARS,
            SCALARS,
            pl.BlockSpec((2, D), lambda s: (0, 0)),
            pl.BlockSpec((3, D), lambda s: (0, 0)),
            pl.BlockSpec((1, 3 * PAIR), lambda s: (0, pair_of(s))),
            pl.BlockSpec(weights[0].shape, lambda s: (0, 0, 0), pipeline_mode=once),
        ]
        + [pl.BlockSpec(weight.shape, lambda s: (0, 0), pipeline_mode=once) for weight in weights[1:]]
        + [anywhere] * 2,
        out_specs=[
            pl.BlockSpec((LEN, 3 * PAIR), lambda s: (0, pair_of(s))),
            pl.BlockSpec((LEN, PAIR), lambda s: (0, pair_of(s))),
            pl.BlockSpec((2, LEN, LEN), lambda s: (pair_of(s), 0, 0)),
            pl.BlockSpec((1, 2, LEN), lambda s: (pair_of(s), 0, 0)),
            whole,
            whole,
            whole,
            whole,
            pl.BlockSpec(later, lambda s: (0, 0, 0), pipeline_mode=once),
        ]
        + [anywhere] * 5,
        out_shape=[
            jax.ShapeDtypeStruct((LEN, 3 * D), low),
            jax.ShapeDtypeStruct((LEN, D), low),
            jax.ShapeDtypeStruct((H, LEN, LEN), low),
            jax.ShapeDtypeStruct((PAIRS, 2, LEN), jnp.float32),
            jax.ShapeDtypeStruct((D, LEN), low),
            jax.ShapeDtypeStruct((LEN, D), low),
            jax.ShapeDtypeStruct((LEN, D), jnp.float32),
            jax.ShapeDtypeStruct((LEN, D), low),
            jax.ShapeDtypeStruct(later, low),
            whole_shape(3 * D),
            whole_shape(D),
            whole_shape(2 * EARLY * SLOT),
            whole_shape(2 * EARLY * SLOT),
            jax.ShapeDtypeStruct((LEN, D), low),
        ],
        scratch_shapes=[
            pltpu.VMEM((4 + 2 * EARLY, 64, SLOT), low),
            pltpu.VMEM((LEN, LEN), jnp.float32),
            pltpu.VMEM((PAIR, LEN), jnp.float32),
            pltpu.VMEM((LEN, D), low),
            pltpu.VMEM((4, 2, 2, 64, D), low),
            pltpu.VMEM((LEN, D), low),
            pltpu.VMEM((LEN, D), low),
            pltpu.VMEM((2, 4, 2, 2, 64, 3 * PAIR), low),
        ]
        + spread_semaphores(4 + 2 * EARLY)
        + [pltpu.SemaphoreType.DMA((2, 2)), pltpu.SemaphoreType.DMA((5,))],
        compiler_params=pltpu.CompilerParams(
            collective_id=4, has_side_effects=True, vmem_limit_bytes=VMEM_LIMIT
        ),
        cost_estimate=pl.CostEstimate(
            flops=22 * LEN * LEN * D, bytes_accessed=90 * 1024 * 1024, transcendentals=H * LEN * LEN
        ),
    )(starts, slopes, norm_rows, middle_rows, shifts, *weights, tokens, cotangent)
    wholes = [whole.reshape(D, -1) for whole in (qkv, out, up, down)]
    return *local, wholes, cotangent_rows


class Summing:
    def __init__(self, sources, add_own, buffers, total_ref, sems, lag, ready=0, hold=0):
        self.sources, self.add_own, self.total_ref, self.lag = sources, add_own, total_ref, lag
        self.ready, self.hold = ready, hold
        self.first, self.second_y, self.second_x, self.third, self.fourth = buffers
        self.send_sem, self.recv_sem = sems
        (self.z, self.x, self.core, self.y), self.sibling, self.beside, self.across, self.stations = neighbours()
        self.low_cols = pl.ds(0, HALF_SLOT)
        self.high_cols = pl.ds(HALF_SLOT, HALF_SLOT)

    def count(self):
        return len(self.sources)

    def remote(self, source, target, stage, slot, place):
        return pltpu.make_async_remote_copy(
            src_ref=source,
            dst_ref=target,
            send_sem=self.send_sem.at[stage, slot],
            recv_sem=self.recv_sem.at[stage, slot],
            device_id=place,
            device_id_type=MESH_IDS,
        )

    def landed(self, ref, stage, slot):
        pltpu.make_async_copy(ref, ref, self.recv_sem.at[stage, slot]).wait()

    def send_first(self, slot):
        for part in (0, 1):
            source = self.sources[slot](part).at[:, :, 1 - self.core]
            self.remote(source, self.first.at[slot, part], 0, slot, self.sibling).start()

    def second_copies(self, slot):
        for_y = self.first.at[slot, 1 - self.y, :, :, :, self.low_cols]
        for_x = self.first.at[slot, :, :, 1 - self.x, :, self.high_cols]
        return (
            self.remote(for_y, self.second_y.at[slot], 1, slot, self.across),
            self.remote(for_x, self.second_x.at[slot], 2, slot, self.beside),
        )

    def third_copies(self, slot):
        for_x = self.second_y.at[slot, :, 1 - self.x]
        for_y = self.second_x.at[slot, 1 - self.y]
        return (
            self.remote(for_x, self.third.at[slot, :, :, self.low_cols], 3, slot, self.beside),
            self.remote(for_y, self.third.at[slot, :, :, self.high_cols], 4, slot, self.across),
        )

    def fourth_copies(self, slot):
        return tuple(
            self.remote(
                self.third.at[slot, lax.rem(self.z + hop, 4)], self.fourth.at[slot, hop - 1], 4 + hop, slot, place
            )
            for hop, place in zip((1, 2, 3), self.stations)
        )

    def stage_one(self, slot):
        self.landed(self.first.at[slot], 0, slot)
        self.add_own(slot)
        for copy in self.second_copies(slot):
            copy.start()

    def stage_two(self, slot):
        first, second_y, second_x = self.first, self.second_y, self.second_x
        self.landed(second_y.at[slot], 1, slot)
        second_y[slot] = second_y[slot] + first[slot, self.y, :, :, :, :HALF_SLOT]
        self.landed(second_x.at[slot], 2, slot)
        second_x[slot] = second_x[slot] + first[slot, :, :, self.x, :, HALF_SLOT:]
        for copy in self.third_copies(slot):
            copy.start()

    def stage_three(self, slot):
        third = self.third
        self.landed(third.at[slot, :, :, self.low_cols], 3, slot)
        self.landed(third.at[slot, :, :, self.high_cols], 4, slot)
        third[slot, :, :, :HALF_SLOT] = third[slot, :, :, :HALF_SLOT] + self.second_y[slot, :, self.x]
        third[slot, :, :, HALF_SLOT:] = third[slot, :, :, HALF_SLOT:] + self.second_x[slot, self.y]
        for copy in self.fourth_copies(slot):
            copy.start()

    def stage_four(self, slot):
        total = self.third[slot, self.z].astype(jnp.float32)
        for hop in (1, 2, 3):
            self.landed(self.fourth.at[slot, hop - 1], 4 + hop, slot)
            total = total + self.fourth[slot, hop - 1].astype(jnp.float32)
        self.total_ref[slot] = total

    def ticks(self):
        return self.count() + self.hold + 3 * self.lag

    def tick(self, index):
        for slot in range(self.count()):
            entry = slot + (self.hold if slot >= self.ready else 0)
            pl.when(index == entry)(lambda slot=slot: self.stage_one(slot))
        for number, stage in enumerate((self.stage_two, self.stage_three, self.stage_four)):
            entry = index - (number + 1) * self.lag
            slot = jnp.where(entry < self.ready, entry, entry - self.hold)
            late = (entry >= self.ready + self.hold) & (slot < self.count())
            early = (entry >= 0) & (entry < self.ready)
            pl.when(early | late)(lambda stage=stage, slot=slot: stage(slot))

    def sent(self):
        def one(slot, carry):
            pltpu.make_async_copy(self.first.at[slot], self.first.at[slot], self.send_sem.at[0, slot]).wait()
            for copy in self.second_copies(slot) + self.third_copies(slot) + self.fourth_copies(slot):
                copy.wait_send()
            return carry

        lax.fori_loop(0, self.count(), one, 0)


def summing_buffers(count):
    rows, low = 64, jnp.bfloat16
    return [
        pltpu.VMEM((count, 2, 4, 2, rows, SLOT), low),
        pltpu.VMEM((count, 4, 2, rows, HALF_SLOT), low),
        pltpu.VMEM((count, 2, 4, rows, HALF_SLOT), low),
        pltpu.VMEM((count, 4, rows, SLOT), low),
        pltpu.VMEM((count, 3, rows, SLOT), low),
        pltpu.SemaphoreType.DMA((8, count)),
        pltpu.SemaphoreType.DMA((8, count)),
    ]


LAG = 2
READY = 5
LATE_SLOTS = 8
RING = 4


def block_view(ref, column):
    return ref.at[:, :, :, :, pl.ds(column, SLOT)]


def attend_bwd_half(half, scale, values, keys_t, parts, exps, sums):
    half_t, half_rows, half_queries, inner = parts
    dq_t, dk_sum, dv_sum = sums
    heads = slice(half * HD, half * HD + HD)
    for block in range(LEN // QB):
        span = min(LEN, QB * block + QB + PIECE)
        cols = slice(block * QB, block * QB + QB)
        weights = exps[:span, cols]
        grad_probs = mul(values[:span], half_t[:, cols])
        grad_scores = (weights.astype(jnp.float32) * (grad_probs - inner[:, cols])).astype(jnp.bfloat16)
        dv_sum[:span, :] += mul(weights, half_rows[cols])
        dk_sum[:span, :] += mul(grad_scores, half_queries[cols])
        dq_t[heads, cols] = mul(keys_t[heads, :span], grad_scores) * scale


def attend_sum_kernel(
    packed_ref,
    ctx_ref,
    grad_ref,
    stat_ref,
    weights_ref,
    normed_t_ref,
    rows_ref,
    grad_middle_ref,
    gain_ref,
    exps_ref,
    up_ref,
    down_ref,
    out_ref,
    total_ref,
    token_grad_ref,
    sums_ref,
    packed_sum_ref,
    grad_normed,
    exps,
    dq_t,
    dk_sum,
    dv_sum,
    grad_qkv,
    mine,
    first,
    second_y,
    second_x,
    third,
    fourth,
    send_sem,
    recv_sem,
    exps_sem,
    load_sem,
):
    pair = pl.program_id(0)
    width = up_ref.shape[-1] // 2
    sources = []
    for index in range(width // SLOT):
        for ref in (up_ref, down_ref):
            sources.append(lambda part, ref=ref, index=index: block_view(ref, part * width + index * SLOT))
    sources.append(lambda part: block_view(out_ref, part * SLOT))
    for index in range(3):
        sources.append(lambda part, index=index: block_view(grad_qkv, (part * 3 + index) * SLOT))

    def load(slot, part):
        block = sources[slot](part).at[:, :, summing.core]
        return pltpu.make_async_copy(block, mine.at[slot % RING, part], load_sem.at[slot % RING])

    def add_own(slot):
        if slot < READY:
            place = slot % RING
            pltpu.make_async_copy(mine.at[place], mine.at[place], load_sem.at[place]).wait()
            first[slot] = first[slot] + mine[place]
            if slot + RING < READY:
                for part in (0, 1):
                    load(slot + RING, part).start()
        else:
            for part in (0, 1):
                cols = pl.ds((part * 3 + slot - READY) * SLOT, SLOT)
                first[slot, part] = first[slot, part] + grad_qkv[:, :, summing.core, :, cols]

    buffers = (first, second_y, second_x, third, fourth)
    summing = Summing(sources, add_own, buffers, total_ref, (send_sem, recv_sem), LAG, READY, 1)

    def exps_load(head, half):
        return pltpu.make_async_copy(exps_ref.at[head], exps.at[half], exps_sem.at[half])

    @pl.when(pair == 0)
    def _():
        for half in (0, 1):
            exps_load(half, half).start()
        for slot in range(RING):
            for part in (0, 1):
                load(slot, part).start()
        greet_neighbours([summing.sibling, summing.beside, summing.across] + summing.stations)
        for slot in range(READY):
            summing.send_first(slot)
        grad_normed[...] = jnp.zeros_like(grad_normed)
        sums_ref[...] = jnp.zeros_like(sums_ref)

    scale = 1.0 / math.sqrt(HD)
    queries = packed_ref[:, :PAIR]
    keys_t = packed_ref[:, PAIR : 2 * PAIR].T
    values = packed_ref[:, 2 * PAIR :]
    grads_t = grad_ref[...].T.astype(jnp.float32)
    context_t = ctx_ref[...].T.astype(jnp.float32)
    scaled = []
    inner_rows = []
    for half in (0, 1):
        heads = slice(half * HD, half * HD + HD)
        scaled.append(grads_t[heads] * stat_ref[0, half : half + 1, :])
        inner_rows.append(jnp.sum(scaled[half] * context_t[heads], axis=0, keepdims=True))
    scaled_t = jnp.concatenate(scaled, axis=0).astype(jnp.bfloat16)
    scaled_rows = scaled_t.T
    dk_sum[...] = jnp.zeros_like(dk_sum)
    dv_sum[...] = jnp.zeros_like(dv_sum)
    for half in (0, 1):
        exps_load(2 * pair + half, half).wait()
        parts = (
            only_rows(scaled_t, half),
            only_cols(scaled_rows, half),
            only_cols(queries, half),
            inner_rows[half],
        )
        attend_bwd_half(half, scale, values, keys_t, parts, exps.at[half], (dq_t, dk_sum, dv_sum))

        @pl.when(pair < PAIRS - 1)
        def _(half=half):
            exps_load(2 * pair + 2 + half, half).start()

        if half == 0:
            summing.tick(pair)
    grads = jnp.concatenate([dq_t[...].T, dk_sum[...] * scale, dv_sum[...]], axis=1).astype(jnp.bfloat16)
    packed_sum_ref[...] = jnp.sum(grads.astype(jnp.float32), axis=0, keepdims=True)
    cols = pl.ds(pl.multiple_of(pair * (3 * PAIR), PAIR), 3 * PAIR)
    grad_weights = mul(normed_t_ref[...], grads).astype(jnp.bfloat16)
    grad_qkv[:, :, :, :, cols] = grad_weights.reshape(4, 2, 2, 64, 3 * PAIR)
    grad_normed[...] += dot_last(grads, weights_ref[...])

    for slot in range(READY, LATE_SLOTS):
        pl.when(pair == PAIRS - LATE_SLOTS + slot)(lambda slot=slot: summing.send_first(slot))

    @pl.when(pair == PAIRS - 1)
    def _():
        def late(index, carry):
            summing.tick(index)
            chunk = index - PAIRS

            @pl.when(chunk < LEN // ROWS)
            def _():
                here = pl.ds(pl.multiple_of(chunk * ROWS, ROWS), ROWS)
                block = rows_ref[here, :].astype(jnp.float32)
                pulled, gain_sum, shift_sum = norm_pull(block, grad_normed[here, :], gain_ref[...])
                token_grad_ref[here, :] = (grad_middle_ref[here, :] + pulled).astype(jnp.bfloat16)
                add_rows(sums_ref, (gain_sum, shift_sum))

            return carry

        lax.fori_loop(PAIRS, summing.ticks(), late, 0)
        summing.sent()


def attend_sum(
    packed, context, grad_context, stats, weights, normed_t, rows_low, grad_middle, gain, exps, grad_up, grad_down, grad_out
):
    anywhere = pl.BlockSpec(memory_space=pl.ANY)
    rows = 64
    low = jnp.bfloat16
    once = pl.Buffered(1)
    tall = pl.BlockSpec((LEN, D), lambda p: (0, 0), pipeline_mode=once)
    split = [grad.reshape(4, 2, 2, rows, grad.shape[-1]) for grad in (grad_up, grad_down, grad_out)]
    return pl.pallas_call(
        attend_sum_kernel,
        grid=(PAIRS,),
        in_specs=[PACKED_COLS, PAIR_COLS, PAIR_COLS, PAIR_STAT, PACKED_COLS, tall, tall, tall]
        + [pl.BlockSpec((1, D), lambda p: (0, 0))]
        + [anywhere] * 4,
        out_specs=[
            pl.BlockSpec((LATE_SLOTS, rows, SLOT), lambda p: (0, 0, 0), pipeline_mode=once),
            tall,
            pl.BlockSpec((8, D), lambda p: (0, 0)),
            pl.BlockSpec((1, 3 * PAIR), lambda p: (0, p)),
        ],
        out_shape=[
            jax.ShapeDtypeStruct((LATE_SLOTS, rows, SLOT), jnp.float32),
            jax.ShapeDtypeStruct((LEN, D), low),
            jax.ShapeDtypeStruct((8, D), jnp.float32),
            jax.ShapeDtypeStruct((1, 3 * D), jnp.float32),
        ],
        scratch_shapes=[
            pltpu.VMEM((LEN, D), jnp.float32),
            pltpu.VMEM((2, LEN, LEN), low),
            pltpu.VMEM((PAIR, LEN), jnp.float32),
            pltpu.VMEM((LEN, PAIR), jnp.float32),
            pltpu.VMEM((LEN, PAIR), jnp.float32),
            pltpu.VMEM((4, 2, 2, rows, 3 * D), low),
            pltpu.VMEM((RING, 2, 4, 2, rows, SLOT), low),
            *summing_buffers(LATE_SLOTS),
            pltpu.SemaphoreType.DMA((2,)),
            pltpu.SemaphoreType.DMA((RING,)),
        ],
        compiler_params=pltpu.CompilerParams(
            collective_id=2, has_side_effects=True, vmem_limit_bytes=62 * 1024 * 1024
        ),
        cost_estimate=pl.CostEstimate(
            flops=44 * LEN * LEN * D, bytes_accessed=400 * 1024 * 1024, transcendentals=0
        ),
    )(packed, context, grad_context, stats, weights, normed_t, rows_low, grad_middle, gain, exps, *split)


ROWS = 256


def norm_pull(rows, grads, gain):
    centered = rows - jnp.mean(rows, axis=-1, keepdims=True)
    inverse = lax.rsqrt(jnp.mean(centered * centered, axis=-1, keepdims=True) + NORM_EPSILON)
    normed = centered * inverse
    scaled = grads * gain
    along = jnp.mean(scaled * normed, axis=-1, keepdims=True)
    pulled = inverse * (scaled - jnp.mean(scaled, axis=-1, keepdims=True) - normed * along)
    gain_sum = jnp.sum(grads * normed, axis=0, keepdims=True)
    return pulled, gain_sum, jnp.sum(grads, axis=0, keepdims=True)


def add_rows(sums_ref, rows):
    for index, row in enumerate(rows):
        sums_ref[index : index + 1, :] += row


def middle_kernel(
    middle_ref, grad_ref, cot_ref, ctx_ref, gain_ref, weights_ref, grad_middle_ref, grad_ctx_ref, grad_out_ref, sums_ref, low_t
):
    step = pl.program_id(0)

    @pl.when(step == 0)
    def _():
        sums_ref[...] = jnp.zeros_like(sums_ref)

    cot = cot_ref[...].astype(jnp.float32)
    pulled, gain_sum, shift_sum = norm_pull(middle_ref[...], grad_ref[...], gain_ref[...])
    grads = cot + pulled
    low = grads.astype(jnp.bfloat16)
    grad_middle_ref[...] = grads
    grad_ctx_ref[...] = mul(low, weights_ref[...]).astype(jnp.bfloat16)
    low_t[:, pl.ds(pl.multiple_of(step * ROWS, ROWS), ROWS)] = low.T
    grad_sum = jnp.sum(grads, axis=0, keepdims=True)
    add_rows(sums_ref, (gain_sum, shift_sum, grad_sum, jnp.sum(cot, axis=0, keepdims=True)))

    @pl.when(step == LEN // ROWS - 1)
    def _():
        grad_out_ref[...] = mul(low_t[...], ctx_ref[...]).astype(jnp.bfloat16)


def middle_backward(middle, grad_rows, cot, context, gain, weights):
    rows = pl.BlockSpec((ROWS, D), lambda s: (s, 0))
    whole = pl.BlockSpec((D, D), lambda s: (0, 0), pipeline_mode=pl.Buffered(1))
    row = pl.BlockSpec((1, D), lambda s: (0, 0))
    sums = pl.BlockSpec((8, D), lambda s: (0, 0))
    return pl.pallas_call(
        middle_kernel,
        grid=(LEN // ROWS,),
        in_specs=[rows, rows, rows, whole, row, whole],
        out_specs=[rows, rows, whole, sums],
        out_shape=[
            jax.ShapeDtypeStruct((LEN, D), jnp.float32),
            jax.ShapeDtypeStruct((LEN, D), jnp.bfloat16),
            jax.ShapeDtypeStruct((D, D), jnp.bfloat16),
            jax.ShapeDtypeStruct((8, D), jnp.float32),
        ],
        scratch_shapes=[pltpu.VMEM((D, LEN), jnp.bfloat16)],
        compiler_params=pltpu.CompilerParams(vmem_limit_bytes=VMEM_LIMIT),
        cost_estimate=pl.CostEstimate(flops=4 * LEN * D * D, bytes_accessed=24 * 1024 * 1024, transcendentals=0),
    )(middle, grad_rows, cot, context, gain, weights)


def slot_rows(early_ref, late_ref, slot):
    index, kind = slot % 4, slot // 4
    if index < EARLY:
        return early_ref[2 * index + kind]
    return late_ref[2 * (index - EARLY) + kind]


def moment_kernel(
    early_ref,
    late_ref,
    m_qkv_ref,
    m_out_ref,
    m_up_ref,
    m_down_ref,
    g_qkv_ref,
    g_out_ref,
    g_up_ref,
    g_down_ref,
    n_qkv_ref,
    n_out_ref,
    n_up_ref,
    n_down_ref,
    slots_ref,
):
    first_packed = LATE_SLOTS - 3
    for pair in range(SLOT // PAIR):
        for part in range(3):
            column = (pair * 3 + part) * PAIR
            source = late_ref[first_packed + column // SLOT, :, column % SLOT : column % SLOT + PAIR]
            g_qkv_ref[part, :, pair * PAIR : (pair + 1) * PAIR] = source
    for part in range(3):
        moment = MOMENTUM_DECAY * m_qkv_ref[part] + g_qkv_ref[part]
        n_qkv_ref[part] = moment
        slots_ref[part] = moment.astype(jnp.bfloat16)
    grads = late_ref[first_packed - 1]
    g_out_ref[...] = grads
    moment = MOMENTUM_DECAY * m_out_ref[...] + grads
    n_out_ref[...] = moment
    slots_ref[3] = moment.astype(jnp.bfloat16)
    for kind, refs in enumerate(((m_up_ref, g_up_ref, n_up_ref), (m_down_ref, g_down_ref, n_down_ref))):
        old_ref, grads_ref, new_ref = refs
        for index in range(4):
            here = slice(index * SLOT, (index + 1) * SLOT)
            grads = slot_rows(early_ref, late_ref, 4 * kind + index)
            grads_ref[:, here] = grads
            moment = MOMENTUM_DECAY * old_ref[:, here] + grads
            new_ref[:, here] = moment
            slots_ref[4 + 4 * kind + index] = moment.astype(jnp.bfloat16)


def update_kernel(
    updates_ref,
    vec_sum_ref,
    w_qkv_ref,
    w_out_ref,
    w_up_ref,
    w_down_ref,
    vectors_ref,
    m_vec_ref,
    o_qkv_ref,
    o_out_ref,
    o_up_ref,
    o_down_ref,
    g_vec_ref,
    n_vec_ref,
    o_vec_ref,
):
    wide_rate = MATRIX_RATE * math.sqrt(FF / D)
    for part in range(3):
        o_qkv_ref[part] = w_qkv_ref[part] - MATRIX_RATE * updates_ref[part].astype(jnp.float32)
    o_out_ref[...] = w_out_ref[...] - MATRIX_RATE * updates_ref[3].astype(jnp.float32)
    for index in range(4):
        here = slice(index * SLOT, (index + 1) * SLOT)
        o_up_ref[:, here] = w_up_ref[:, here] - wide_rate * updates_ref[4 + index].astype(jnp.float32)
        o_down_ref[:, here] = w_down_ref[:, here] - wide_rate * updates_ref[8 + index].astype(jnp.float32)
    grads = vec_sum_ref[...]
    moment = MOMENTUM_DECAY * m_vec_ref[...] + grads
    square = jnp.mean(moment * moment, axis=1, keepdims=True)
    g_vec_ref[...] = grads
    n_vec_ref[...] = moment
    o_vec_ref[...] = vectors_ref[...] - VECTOR_RATE * moment * lax.rsqrt(square + SQUARE_EPSILON)


def like(arrays):
    return [jax.ShapeDtypeStruct(array.shape, jnp.float32) for array in arrays]


def features_first(arrays):
    qkv, out, up, down = arrays
    return qkv, out.T, up, down.T


def muon_step(early, late, vector_total, block_rows, token_grads, weights, vectors, momenta, m_vec):
    limit = pltpu.CompilerParams(vmem_limit_bytes=VMEM_LIMIT)
    weights, momenta = features_first(weights), features_first(momenta)
    slots_shape = jax.ShapeDtypeStruct((SLOTS,) + late.shape[1:], jnp.bfloat16)
    *stored, slots = pl.pallas_call(
        moment_kernel, out_shape=like(momenta) + like(momenta) + [slots_shape], compiler_params=limit
    )(early, late, *momenta)
    updates, vector_rows, output_pair, token_pair = muon_call(
        slots, vector_total.reshape(SLOTS, 8, 128), block_rows, token_grads
    )
    fresh = pl.pallas_call(
        update_kernel, out_shape=like(weights) + like([vectors] * 3), compiler_params=limit
    )(updates, vector_rows.reshape(12, D), *weights, vectors, m_vec)
    vector_grad, moment_vec, new_vec = fresh[4:]
    grads, moments, new = features_first(stored[:4]), features_first(stored[4:]), features_first(fresh[:4])
    return (output_pair, token_pair.astype(jnp.float32), *grads, vector_grad, *moments, moment_vec, *new, new_vec)


def narrow(rows):
    return rows.astype(jnp.bfloat16)


def contract(left, right, left_dim, right_dim):
    return lax.dot_general(
        left, right, (((left_dim,), (right_dim,)), ((), ())), preferred_element_type=jnp.float32
    )


def by_pairs(rows):
    count, height, width = rows.shape
    return jnp.transpose(rows.reshape(count, height, width // PAIR, PAIR), (1, 2, 0, 3)).reshape(height, -1)


def from_pairs(rows):
    height = rows.shape[0]
    return jnp.transpose(rows.reshape(height, -1, 3, PAIR), (2, 0, 1, 3)).reshape(3, height, -1)


def sequence_step(
    tokens,
    cotangent,
    piece_starts,
    w_qkv,
    w_out,
    w_up,
    w_down,
    vectors,
    m_qkv,
    m_out,
    m_up,
    m_down,
    m_vec,
):
    rank = lax.axis_index("tensor")
    slopes = jnp.exp2(-8.0 * jnp.arange(1, H + 1, dtype=jnp.float32) / H)
    starts = lax.dynamic_slice_in_dim(piece_starts[:, 0], rank, 1, 0)[0]
    shifts = by_pairs(jnp.stack([vectors[2], jnp.zeros((D,), jnp.float32), vectors[3]])[:, None])
    weights = (w_qkv, w_out, w_up, w_down)
    packed, context, exps, stats, normed_t, token_low, middle, normed_two, later, wholes, cotangent_low = attend_spread(
        starts, slopes, vectors[0:2], vectors[4:7], shifts, features_first(weights), tokens, cotangent
    )
    full_qkv, full_out, full_up, full_down = wholes
    block_rows, grad_normed_two, grad_up, grad_down, up_bias, early_sums = mlp_both(
        normed_two,
        cotangent_low,
        middle,
        vectors[11:12],
        vectors[7:11].reshape(1, FF),
        full_up,
        full_down,
        later,
    )
    grad_middle, grad_context, grad_out, middle_sums = middle_backward(
        middle, grad_normed_two, cotangent_low, context, vectors[5:6], full_out
    )
    sums, grad_token_low, token_sums, packed_grads = attend_sum(
        packed,
        context,
        grad_context,
        stats,
        full_qkv,
        normed_t,
        token_low,
        grad_middle,
        vectors[0:1],
        exps,
        grad_up,
        grad_down,
        grad_out,
    )
    packed_sums = from_pairs(packed_grads)[:, 0]
    vector_total = jnp.concatenate(
        [
            token_sums[0:2],
            packed_sums[0:1],
            packed_sums[2:3],
            middle_sums[2:3],
            middle_sums[0:2],
            up_bias.reshape(4, D),
            middle_sums[3:4],
        ]
    )
    momenta = (m_qkv, m_out, m_up, m_down)
    return muon_step(
        early_sums, sums, vector_total, block_rows, grad_token_low, weights, vectors, momenta, m_vec
    )


def solution(mesh):
    in_specs = (
        P(None, ("dp", "tensor"), None),
        P(None, ("dp", "tensor"), None),
        P(None, "dp", None),
        P(None, "dp", "tensor"),
        P("tensor", "dp"),
        P("dp", "tensor"),
        P("tensor", "dp"),
        P(),
        P(None, "dp", "tensor"),
        P("tensor", "dp"),
        P("dp", "tensor"),
        P("tensor", "dp"),
        P(),
    )
    out_specs = (
        P(None, ("dp", "tensor"), None),
        P(None, ("dp", "tensor"), None),
        P(None, "dp", "tensor"),
        P("tensor", "dp"),
        P("dp", "tensor"),
        P("tensor", "dp"),
        P(),
        P(None, "dp", "tensor"),
        P("tensor", "dp"),
        P("dp", "tensor"),
        P("tensor", "dp"),
        P(),
        P(None, "dp", "tensor"),
        P("tensor", "dp"),
        P("dp", "tensor"),
        P("tensor", "dp"),
        P(),
    )
    groups_fit = mesh.shape["tensor"] == MB and mesh.shape["dp"] == 16

    def pick(*arrays):
        if groups_fit and arrays[2].shape[1] == 1:
            return sequence_step(*arrays)
        return on_device(*arrays)

    return jax.shard_map(
        pick, mesh=mesh, in_specs=in_specs, out_specs=out_specs, check_vma=False
    )
```

```python
import math

import jax
import jax.numpy as jnp
from jax import lax
from jax.experimental import pallas as pl
from jax.experimental.pallas import tpu as pltpu
from jax.sharding import PartitionSpec as P

D = 1024
H = 16
HD = 64
FF = 4096
LEN = 1024
PIECE = 256
NPIECE = 2
MB = 2
NS_ITERS = 3


NORM_EPSILON = 1e-05
SQUARE_EPSILON = 1e-06
MASKED_SCORE = -1e30
SCHULZ_FIRST = 3.4445
SCHULZ_SECOND = -4.775
SCHULZ_THIRD = 2.0315
MOMENTUM_DECAY = 0.5
MATRIX_RATE = 0.5
VECTOR_RATE = 0.05


def layer_norm(inputs, gain_row, shift_row):
    average = jnp.mean(inputs, axis=-1, keepdims=True)
    centered = inputs - average
    variance = jnp.mean(centered * centered, axis=-1, keepdims=True)
    return centered * lax.rsqrt(variance + NORM_EPSILON) * gain_row + shift_row


def gelu_tanh(inputs):
    return jax.nn.gelu(inputs, approximate=True)


def score_layout(starts, slopes):
    positions = jnp.arange(LEN, dtype=jnp.int32)
    inside = (positions[None, :] >= starts[:, None]) & (
        positions[None, :] < starts[:, None] + PIECE
    )
    labels = jnp.arange(1, NPIECE + 1, dtype=jnp.int32)
    piece_label = jnp.sum(jnp.where(inside, labels[:, None], 0), axis=0)
    same_piece = (piece_label[:, None] == piece_label[None, :]) & (piece_label[:, None] > 0)
    visible = (positions[None, :] <= positions[:, None]) | same_piece
    distance = jnp.abs(positions[:, None] - positions[None, :]).astype(jnp.float32)
    penalty = -slopes[:, None, None] * distance[None, :, :]
    return (visible, penalty)


def head_scores(query_heads, key_heads, starts, slopes):
    visible, penalty = score_layout(starts, slopes)
    raw_scores = jnp.einsum(
        "qhd,khd->hqk", query_heads, key_heads, preferred_element_type=jnp.float32
    )
    scores = raw_scores * (1.0 / math.sqrt(HD)) + penalty
    return jnp.where(visible[None, :, :], scores, MASKED_SCORE)


def attend_forward(element, slopes):
    query_seq, key_seq, value_seq, starts = element
    heads_here = slopes.shape[0]
    query_heads = query_seq.reshape(LEN, heads_here, HD)
    key_heads = key_seq.reshape(LEN, heads_here, HD)
    value_heads = value_seq.reshape(LEN, heads_here, HD)
    scores = head_scores(query_heads, key_heads, starts, slopes)
    maximum = jnp.max(scores, axis=-1, keepdims=True)
    weights_raw = jnp.exp(scores - maximum)
    denominator = jnp.sum(weights_raw, axis=-1, keepdims=True)
    probabilities = weights_raw / denominator
    context = jnp.einsum(
        "hqk,khd->qhd",
        probabilities.astype(jnp.bfloat16),
        value_heads,
        preferred_element_type=jnp.float32,
    )
    logsum = (maximum + jnp.log(denominator))[..., 0]
    return (context.reshape(LEN, heads_here * HD), logsum)


def attend_backward(element, slopes):
    query_seq, key_seq, value_seq, context_grad, logsum, starts = element
    heads_here = slopes.shape[0]
    query_heads = query_seq.reshape(LEN, heads_here, HD)
    key_heads = key_seq.reshape(LEN, heads_here, HD)
    value_heads = value_seq.reshape(LEN, heads_here, HD)
    grad_heads = context_grad.reshape(LEN, heads_here, HD)
    scores = head_scores(query_heads, key_heads, starts, slopes)
    probabilities = jnp.exp(scores - logsum[..., None])
    grad_probs = jnp.einsum(
        "qhd,khd->hqk", grad_heads, value_heads, preferred_element_type=jnp.float32
    )
    inner_sum = jnp.sum(probabilities * grad_probs, axis=-1, keepdims=True)
    grad_scores = (probabilities * (grad_probs - inner_sum)).astype(jnp.bfloat16)
    scale_factor = 1.0 / math.sqrt(HD)
    grad_query = (
        jnp.einsum("hqk,khd->qhd", grad_scores, key_heads, preferred_element_type=jnp.float32)
        * scale_factor
    )
    grad_key = (
        jnp.einsum("hqk,qhd->khd", grad_scores, query_heads, preferred_element_type=jnp.float32)
        * scale_factor
    )
    grad_value = jnp.einsum(
        "hqk,qhd->khd",
        probabilities.astype(jnp.bfloat16),
        grad_heads,
        preferred_element_type=jnp.float32,
    )
    width_here = heads_here * HD
    return (
        grad_query.astype(jnp.bfloat16).reshape(LEN, width_here),
        grad_key.astype(jnp.bfloat16).reshape(LEN, width_here),
        grad_value.astype(jnp.bfloat16).reshape(LEN, width_here),
    )


def placed(values, offset, length):
    return lax.dynamic_update_slice_in_dim(jnp.zeros((length,), jnp.float32), values, offset, 0)


def accumulate(totals, addend):
    if totals is None:
        return addend
    return tuple((former + latter for former, latter in zip(totals, addend)))


def gram_term(narrow_rows, wide_rows):
    part_narrow = jnp.einsum(
        "mrc,mrd->cmd", narrow_rows, narrow_rows, preferred_element_type=jnp.float32
    )
    part_wide = jnp.einsum("mrc,mrd->cmd", wide_rows, wide_rows, preferred_element_type=jnp.float32)
    return jnp.concatenate([part_narrow, part_wide], axis=1)


def schulz_step(state, gram_matrix):
    turned = jnp.einsum("mrc,cmd->mrd", state, gram_matrix, preferred_element_type=jnp.float32)
    mixed = (SCHULZ_SECOND * state.astype(jnp.float32) + SCHULZ_THIRD * turned).astype(jnp.bfloat16)
    return (
        SCHULZ_FIRST * state.astype(jnp.float32)
        + jnp.einsum("mrc,cmd->mrd", mixed, gram_matrix, preferred_element_type=jnp.float32)
    ).astype(jnp.bfloat16)


def slice_term(source, weights, pattern):
    return jnp.einsum(pattern, source, weights, preferred_element_type=jnp.float32)


def on_device(
    tokens,
    cotangent,
    piece_starts,
    w_qkv,
    w_out,
    w_up,
    w_down,
    vectors,
    m_qkv,
    m_out,
    m_up,
    m_down,
    m_vec,
):
    tensor_count = lax.axis_size("tensor")
    tensor_rank = lax.axis_index("tensor")
    shard_rank = lax.axis_index("dp")
    heads_here = H // tensor_count
    width_here = heads_here * HD
    hidden_here = FF // tensor_count
    rows_here = tokens.shape[1]
    group_rows = rows_here * tensor_count
    seqs_here = piece_starts.shape[1]
    shard_rows = w_qkv.shape[1]
    head_ids = tensor_rank * heads_here + jnp.arange(heads_here, dtype=jnp.int32) + 1
    slopes = jnp.exp2(-8.0 * head_ids.astype(jnp.float32) / H)
    query_shift = lax.dynamic_slice_in_dim(vectors[2], tensor_rank * width_here, width_here, 0)
    value_shift = lax.dynamic_slice_in_dim(vectors[3], tensor_rank * width_here, width_here, 0)
    up_shift = lax.dynamic_slice_in_dim(
        vectors[7:11].reshape(FF), tensor_rank * hidden_here, hidden_here, 0
    )
    low_qkv = w_qkv.astype(jnp.bfloat16)
    low_out = w_out.astype(jnp.bfloat16)
    low_up = w_up.astype(jnp.bfloat16)
    low_down = w_down.astype(jnp.bfloat16)
    outputs_list = []
    input_grads = []
    vector_total = jnp.zeros((12, D), jnp.float32)
    grad_total = None

    def forward_one(element):
        return attend_forward(element, slopes)

    def backward_one(element):
        return attend_backward(element, slopes)

    for batch_index in range(MB):
        full_qkv, full_out, full_up, full_down = (
            lax.all_gather(low_qkv, "dp", axis=1, tiled=True),
            lax.all_gather(low_out, "dp", axis=1, tiled=True),
            lax.all_gather(low_up, "dp", axis=0, tiled=True),
            lax.all_gather(low_down, "dp", axis=1, tiled=True),
        )
        token_rows = tokens[batch_index].astype(jnp.float32)
        cotangent_rows = cotangent[batch_index]
        normed_one = layer_norm(token_rows, vectors[0], vectors[1])
        normed_all, cotangent_all = (
            lax.all_gather(normed_one.astype(jnp.bfloat16), "tensor", axis=0, tiled=True),
            lax.all_gather(cotangent_rows, "tensor", axis=0, tiled=True),
        )
        projected = jnp.einsum(
            "td,cde->cte", normed_all, full_qkv, preferred_element_type=jnp.float32
        )
        query_low = (projected[0] + query_shift).astype(jnp.bfloat16)
        key_low = projected[1].astype(jnp.bfloat16)
        value_low = (projected[2] + value_shift).astype(jnp.bfloat16)
        query_seqs = query_low.reshape(seqs_here, LEN, width_here)
        key_seqs = key_low.reshape(seqs_here, LEN, width_here)
        value_seqs = value_low.reshape(seqs_here, LEN, width_here)
        starts_here = piece_starts[batch_index]
        context_seq, logsum = lax.map(forward_one, (query_seqs, key_seqs, value_seqs, starts_here))
        context_low = context_seq.reshape(group_rows, width_here).astype(jnp.bfloat16)
        attended = lax.psum_scatter(
            slice_term(context_low, full_out, "tc,cd->td").astype(jnp.bfloat16),
            "tensor",
            scatter_dimension=0,
            tiled=True,
        ).astype(jnp.float32)
        middle = token_rows + attended + vectors[4]
        normed_two = layer_norm(middle, vectors[5], vectors[6])
        normed_two_all = lax.all_gather(
            normed_two.astype(jnp.bfloat16), "tensor", axis=0, tiled=True
        )
        before = jnp.dot(normed_two_all, full_up, preferred_element_type=jnp.float32) + up_shift
        activated = gelu_tanh(before).astype(jnp.bfloat16)
        expanded = lax.psum_scatter(
            slice_term(activated, full_down, "tf,fd->td").astype(jnp.bfloat16),
            "tensor",
            scatter_dimension=0,
            tiled=True,
        ).astype(jnp.float32)
        outputs_list.append((middle + expanded + vectors[11]).astype(jnp.bfloat16))
        grad_down = jnp.einsum(
            "tf,td->fd", activated, cotangent_all, preferred_element_type=jnp.float32
        )
        grad_activated = jnp.einsum(
            "td,fd->tf", cotangent_all, full_down, preferred_element_type=jnp.float32
        )
        gelu_pull = jax.vjp(gelu_tanh, before)[1]
        grad_before = gelu_pull(grad_activated)[0].astype(jnp.bfloat16)
        grad_up = jnp.einsum(
            "td,tf->df", normed_two_all, grad_before, preferred_element_type=jnp.float32
        )
        grad_normed_two = lax.psum_scatter(
            slice_term(grad_before, full_up, "tf,df->td").astype(jnp.bfloat16),
            "tensor",
            scatter_dimension=0,
            tiled=True,
        ).astype(jnp.float32)
        second_pull = jax.vjp(layer_norm, middle, vectors[5], vectors[6])[1]
        middle_from_norm, gain_two_grad, shift_two_grad = second_pull(grad_normed_two)
        grad_middle = cotangent_rows.astype(jnp.float32) + middle_from_norm
        grad_middle_all = lax.all_gather(
            grad_middle.astype(jnp.bfloat16), "tensor", axis=0, tiled=True
        )
        grad_out = jnp.einsum(
            "tc,td->cd", context_low, grad_middle_all, preferred_element_type=jnp.float32
        )
        grad_context = jnp.einsum(
            "td,cd->tc", grad_middle_all, full_out, preferred_element_type=jnp.float32
        ).astype(jnp.bfloat16)
        grad_query, grad_key, grad_value = lax.map(
            backward_one,
            (
                query_seqs,
                key_seqs,
                value_seqs,
                grad_context.reshape(seqs_here, LEN, width_here),
                logsum,
                starts_here,
            ),
        )
        grad_stack = jnp.stack(
            [
                grad_query.reshape(group_rows, width_here),
                grad_key.reshape(group_rows, width_here),
                grad_value.reshape(group_rows, width_here),
            ]
        )
        grad_qkv = jnp.einsum(
            "td,cte->cde", normed_all, grad_stack, preferred_element_type=jnp.float32
        )
        grad_normed_one = lax.psum_scatter(
            slice_term(grad_stack, full_qkv, "cte,cde->td").astype(jnp.bfloat16),
            "tensor",
            scatter_dimension=0,
            tiled=True,
        ).astype(jnp.float32)
        first_pull = jax.vjp(layer_norm, token_rows, vectors[0], vectors[1])[1]
        token_from_norm, gain_one_grad, shift_one_grad = first_pull(grad_normed_one)
        input_grads.append(grad_middle + token_from_norm)
        query_bias = jnp.sum(grad_stack[0], axis=0, dtype=jnp.float32)
        value_bias = jnp.sum(grad_stack[2], axis=0, dtype=jnp.float32)
        up_bias = jnp.sum(grad_before, axis=0, dtype=jnp.float32)
        head_rows = jnp.stack(
            [
                gain_one_grad,
                shift_one_grad,
                placed(query_bias, tensor_rank * width_here, D),
                placed(value_bias, tensor_rank * width_here, D),
                jnp.sum(grad_middle, axis=0),
                gain_two_grad,
                shift_two_grad,
            ]
        )
        up_rows = placed(up_bias, tensor_rank * hidden_here, FF).reshape(4, D)
        tail_row = jnp.sum(cotangent_rows, axis=0, dtype=jnp.float32)[None, :]
        vector_total = vector_total + jnp.concatenate([head_rows, up_rows, tail_row], axis=0)
        shard_grads = (
            lax.psum_scatter(
                grad_qkv.astype(jnp.bfloat16), "dp", scatter_dimension=1, tiled=True
            ).astype(jnp.float32),
            lax.psum_scatter(
                grad_out.astype(jnp.bfloat16), "dp", scatter_dimension=1, tiled=True
            ).astype(jnp.float32),
            lax.psum_scatter(
                grad_up.astype(jnp.bfloat16), "dp", scatter_dimension=0, tiled=True
            ).astype(jnp.float32),
            lax.psum_scatter(
                grad_down.astype(jnp.bfloat16), "dp", scatter_dimension=1, tiled=True
            ).astype(jnp.float32),
        )
        grad_total = accumulate(grad_total, shard_grads)
    grad_qkv_shard, grad_out_shard, grad_up_shard, grad_down_shard = grad_total
    moment_qkv = MOMENTUM_DECAY * m_qkv + grad_qkv_shard
    moment_out = MOMENTUM_DECAY * m_out + grad_out_shard
    moment_up = MOMENTUM_DECAY * m_up + grad_up_shard
    moment_down = MOMENTUM_DECAY * m_down + grad_down_shard
    squares = jnp.concatenate(
        [
            jnp.sum(moment_qkv * moment_qkv, axis=(1, 2)),
            jnp.stack(
                [
                    jnp.sum(moment_out * moment_out),
                    jnp.sum(moment_up * moment_up),
                    jnp.sum(moment_down * moment_down),
                ]
            ),
        ]
    )
    vector_grad, square_total = lax.psum((vector_total, squares), ("dp", "tensor"))
    factors = lax.rsqrt(square_total + SQUARE_EPSILON)
    scaled_qkv = (moment_qkv * factors[0:3][:, None, None]).astype(jnp.bfloat16)
    scaled_out = (moment_out * factors[3]).astype(jnp.bfloat16)
    scaled_up = (moment_up * factors[4]).astype(jnp.bfloat16)
    scaled_down = (moment_down * factors[5]).astype(jnp.bfloat16)
    gathered_qkv, gathered_out, gathered_up, gathered_down = (
        lax.all_gather(scaled_qkv, "dp", axis=1, tiled=True),
        lax.all_gather(scaled_out, "dp", axis=1, tiled=True),
        lax.all_gather(scaled_up, "dp", axis=0, tiled=True),
        lax.all_gather(scaled_down, "dp", axis=1, tiled=True),
    )
    offset = shard_rank * shard_rows
    narrow_rows = jnp.concatenate([jnp.swapaxes(gathered_qkv, 1, 2), gathered_out[None]], axis=0)
    wide_rows = jnp.stack([gathered_up.T, gathered_down])
    for sweep_index in range(NS_ITERS):
        gram_share = lax.psum_scatter(
            gram_term(narrow_rows, wide_rows).astype(jnp.bfloat16),
            "tensor",
            scatter_dimension=0,
            tiled=True,
        )
        gram_matrix = lax.all_gather(gram_share, "tensor", axis=0, tiled=True)
        narrow_rows = schulz_step(narrow_rows, gram_matrix[:, 0:4])
        wide_rows = schulz_step(wide_rows, gram_matrix[:, 4:6])
    final_narrow = narrow_rows.astype(jnp.float32)
    final_wide = wide_rows.astype(jnp.float32)
    update_qkv = lax.dynamic_slice_in_dim(
        jnp.swapaxes(final_narrow[0:3], 1, 2), offset, shard_rows, 1
    )
    update_out = lax.dynamic_slice_in_dim(final_narrow[3], offset, shard_rows, 1)
    update_up = lax.dynamic_slice_in_dim(final_wide[0].T, offset, shard_rows, 0)
    update_down = lax.dynamic_slice_in_dim(final_wide[1], offset, shard_rows, 1)
    wide_factor = math.sqrt(FF / D)
    new_qkv = w_qkv - MATRIX_RATE * update_qkv
    new_out = w_out - MATRIX_RATE * update_out
    new_up = w_up - MATRIX_RATE * wide_factor * update_up
    new_down = w_down - MATRIX_RATE * wide_factor * update_down
    moment_vec = MOMENTUM_DECAY * m_vec + vector_grad
    new_vec = vectors - VECTOR_RATE * moment_vec * lax.rsqrt(
        jnp.mean(moment_vec * moment_vec, axis=1, keepdims=True) + SQUARE_EPSILON
    )
    return (
        jnp.stack(outputs_list),
        jnp.stack(input_grads),
        grad_qkv_shard,
        grad_out_shard,
        grad_up_shard,
        grad_down_shard,
        vector_grad,
        moment_qkv,
        moment_out,
        moment_up,
        moment_down,
        moment_vec,
        new_qkv,
        new_out,
        new_up,
        new_down,
        new_vec,
    )


QB = 256
PAIR = 2 * HD
PAIRS = D // PAIR
VMEM_LIMIT = 56 * 1024 * 1024


def layout_grid(starts_ref, dist_ref):
    key_pos = lax.broadcasted_iota(jnp.int32, (LEN, LEN), 0)
    query_pos = lax.broadcasted_iota(jnp.int32, (LEN, LEN), 1)
    gap = query_pos - key_pos
    visible = gap >= 0
    for piece in range(NPIECE):
        start = starts_ref[piece]
        inside_key = (key_pos >= start) & (key_pos < start + PIECE)
        inside_query = (query_pos >= start) & (query_pos < start + PIECE)
        visible = visible | (inside_key & inside_query)
    dist_ref[...] = jnp.where(visible, jnp.abs(gap).astype(jnp.float32), -MASKED_SCORE)


def only_rows(pair, half):
    rows = lax.broadcasted_iota(jnp.int32, pair.shape, 0)
    return jnp.where((rows >= HD) if half else (rows < HD), pair, jnp.zeros_like(pair))


def only_cols(pair, half):
    cols = lax.broadcasted_iota(jnp.int32, pair.shape, 1)
    return jnp.where((cols >= HD) if half else (cols < HD), pair, jnp.zeros_like(pair))


def mul(left, right):
    return jnp.dot(left, right, preferred_element_type=jnp.float32)


def attend_pair(pair, slopes_ref, packed, dist_ref, ctx_ref, exps_ref, stat_ref, ctx_t, between):
    keys = packed[:, PAIR : 2 * PAIR]
    values_t = packed[:, 2 * PAIR :].T
    queries_t = (packed[:, :PAIR] * (1.0 / math.sqrt(HD))).T
    for half in (0, 1):
        slope = slopes_ref[2 * pair + half]
        queries = only_rows(queries_t, half)
        heads = slice(half * HD, half * HD + HD)
        for block in range(LEN // QB):
            span = min(LEN, QB * block + QB + PIECE)
            cols = slice(block * QB, block * QB + QB)
            scores = mul(keys[:span], queries[:, cols]) - slope * dist_ref[:span, cols]
            top = jnp.max(scores, axis=0, keepdims=True)
            raw = jnp.exp(scores - top)
            inverse = 1.0 / jnp.sum(raw, axis=0, keepdims=True)
            low = raw.astype(jnp.bfloat16)
            exps_ref[half, :span, cols] = low
            ctx_t[heads, cols] = mul(values_t[heads, :span], low) * inverse
            stat_ref[0, half : half + 1, cols] = inverse
        if half == 0:
            between()
    ctx_ref[...] = ctx_t[...].T.astype(jnp.bfloat16)


PACKED_COLS = pl.BlockSpec((LEN, 3 * PAIR), lambda p: (0, p))
PAIR_COLS = pl.BlockSpec((LEN, PAIR), lambda p: (0, p))
PAIR_GRID = pl.BlockSpec((2, LEN, LEN), lambda p: (p, 0, 0))
PAIR_STAT = pl.BlockSpec((1, 2, LEN), lambda p: (p, 0, 0))
SCALARS = pl.BlockSpec(memory_space=pltpu.SMEM)


HIDDEN = 512
CHUNK = 256
HIDDEN_STEPS = FF // HIDDEN
GELU_SLOPE = math.sqrt(2.0 / math.pi)
GELU_CUBE = 0.044715


def dot_last(left, right):
    return lax.dot_general(left, right, (((1,), (1,)), ((), ())), preferred_element_type=jnp.float32)


def gelu_both(rows):
    square = rows * rows
    bent = jnp.tanh(rows * (GELU_SLOPE + GELU_SLOPE * GELU_CUBE * square))
    half = 0.5 + 0.5 * bent
    slope = half + 0.5 * rows * (1.0 - bent * bent) * (GELU_SLOPE + 3.0 * GELU_SLOPE * GELU_CUBE * square)
    return rows * half, slope


def hidden_block(step):
    return (step % 2) * (HIDDEN_STEPS // 2) + step // 2


def mlp_kernel(
    rows_ref,
    cot_ref,
    base_ref,
    last_ref,
    bias_ref,
    up_ref,
    down_ref,
    slots_ref,
    block_ref,
    grad_rows_ref,
    grad_up_ref,
    grad_down_ref,
    bias_sum_ref,
    total_ref,
    rows_t,
    cot_t,
    total,
    up_part,
    down_part,
    active,
    grad_before,
    grad_early,
    first,
    second_y,
    second_x,
    third,
    fourth,
    sum_send,
    sum_recv,
    local_sem,
    spread_send,
    spread_recv,
    load_sem,
):
    step = pl.program_id(0)
    early_steps = 2 * EARLY
    table = []
    for index in range(HIDDEN_STEPS // 2 - EARLY):
        table += [(place_view(ref, 2 + 2 * index), HALF_SLOT) for ref in (up_part, down_part)]
    spread = Spread(slots_ref, table, local_sem, spread_send, spread_recv)

    def early_block(slot, part):
        return grad_early.at[slot % 2, 2 * (slot // 2) + part]

    def add_own(slot):
        for part in (0, 1):
            first[slot, part] = first[slot, part] + grad_early[slot % 2, 2 * (slot // 2) + part, :, :, summing.core]

    sources = [lambda part, slot=slot: early_block(slot, part) for slot in range(2 * EARLY)]
    buffers = (first, second_y, second_x, third, fourth)
    summing = Summing(sources, add_own, buffers, total_ref, (sum_send, sum_recv), 1)

    def loads(at):
        column = lax.rem(at, 2) * EARLY + at // 2
        cols = pl.ds(pl.multiple_of(column * HIDDEN, HIDDEN), HIDDEN)
        place = lax.rem(at, 2)
        return (
            pltpu.make_async_copy(up_ref.at[:, :, :, :, cols], up_part.at[place], load_sem.at[0, place]),
            pltpu.make_async_copy(down_ref.at[:, :, :, :, cols], down_part.at[place], load_sem.at[1, place]),
        )

    def sum_moves(moment):
        stages = (summing.stage_one, summing.stage_two, summing.stage_three, summing.stage_four)
        for slot in range(summing.count()):
            entry = 4 * (slot // 2 + 1) + slot % 2
            for number, stage in enumerate(stages):
                if moment == entry + 2 * number:
                    stage(slot)

    @pl.when(step == 0)
    def _():
        for copy in loads(step):
            copy.start()
        greet_neighbours([spread.sibling, spread.beside, spread.across] + spread.stations)
        spread.begin()
        rows_t[...] = rows_ref[...].T
        cot_t[...] = cot_ref[...].T
        total[...] = base_ref[...] + last_ref[...]
        grad_rows_ref[...] = jnp.zeros_like(grad_rows_ref)

    @pl.when(step < early_steps)
    def _():
        for copy in loads(step):
            copy.wait()

    @pl.when(step < early_steps - 1)
    def _():
        for copy in loads(step + 1):
            copy.start()

    for index in range(HIDDEN_STEPS // 2 - EARLY):

        @pl.when(step == early_steps + 2 * index)
        def _(index=index):
            spread.arrived(2 * index)
            spread.arrived(2 * index + 1)

    place = jnp.where(step < early_steps, lax.rem(step, 2), step - early_steps + 2)
    up = up_part[place].reshape(D, HIDDEN)
    down = down_part[place].reshape(D, HIDDEN)
    bias = bias_ref[...]
    bias_sum = jnp.zeros((1, HIDDEN), jnp.float32)
    for index in range(LEN // CHUNK):
        here = slice(index * CHUNK, index * CHUNK + CHUNK)
        value, slope = gelu_both(mul(rows_ref[here], up) + bias)
        value = value.astype(jnp.bfloat16)
        grads = (slope * mul(cot_ref[here], down)).astype(jnp.bfloat16)
        active[here] = value
        grad_before[here] = grads
        bias_sum += jnp.sum(grads.astype(jnp.float32), axis=0, keepdims=True)
        total[here] += dot_last(value, down)
        grad_rows_ref[here] += dot_last(grads, up)
        if index == LEN // CHUNK // 2 - 1:
            for number in range(spread.ticks()):
                pl.when(step == number)(lambda number=number: spread.tick(number))
            for number in range(HIDDEN_STEPS):
                pl.when(step == number)(lambda number=number: sum_moves(2 * number))
    bias_sum_ref[...] = bias_sum

    @pl.when(step < early_steps)
    def _():
        for index, (left, right) in enumerate(((rows_t, grad_before), (cot_t, active))):
            grads = mul(left[...], right[...]).astype(jnp.bfloat16)
            grad_early[index, step] = grads.reshape(grad_early.shape[2:])

    @pl.when(step >= early_steps)
    def _():
        grad_up_ref[...] = mul(rows_t[...], grad_before[...]).astype(jnp.bfloat16)
        grad_down_ref[...] = mul(cot_t[...], active[...]).astype(jnp.bfloat16)

    for number in range(HIDDEN_STEPS):

        @pl.when(step == number)
        def _(number=number):
            if number < early_steps and number % 2:
                summing.send_first(number - 1)
                summing.send_first(number)
            sum_moves(2 * number + 1)

    @pl.when(step == HIDDEN_STEPS - 1)
    def _():
        block_ref[...] = total[...].astype(jnp.bfloat16)
        summing.sent()
        spread.sent()


def late_block(step):
    late = HIDDEN_STEPS // 2 - EARLY
    return jnp.where(step < 2 * EARLY, 0, (step % 2) * late + step // 2 - EARLY)


def mlp_both(rows, cot, base, last, bias, up, down, slots):
    anywhere = pl.BlockSpec(memory_space=pl.ANY)
    once = pl.Buffered(1)
    whole = pl.BlockSpec((LEN, D), lambda s: (0, 0), pipeline_mode=once)
    hidden = pl.BlockSpec((D, HIDDEN), lambda s: (0, late_block(s)))
    hidden_row = pl.BlockSpec((1, HIDDEN), lambda s: (0, hidden_block(s)))
    low = jnp.bfloat16
    late = HIDDEN_STEPS // 2 - EARLY
    part = pltpu.VMEM((2 + 2 * late, 4, 2, 2, 64, HIDDEN), low)
    split = [weights.reshape(4, 2, 2, 64, -1) for weights in (up, down)]
    return pl.pallas_call(
        mlp_kernel,
        grid=(HIDDEN_STEPS,),
        in_specs=[whole, whole, whole, pl.BlockSpec((1, D), lambda s: (0, 0)), hidden_row, anywhere, anywhere, anywhere],
        out_specs=[
            whole,
            whole,
            hidden,
            hidden,
            hidden_row,
            pl.BlockSpec((2 * EARLY, 64, SLOT), lambda s: (0, 0, 0), pipeline_mode=once),
        ],
        out_shape=[
            jax.ShapeDtypeStruct((LEN, D), low),
            jax.ShapeDtypeStruct((LEN, D), jnp.float32),
            jax.ShapeDtypeStruct((D, 2 * late * HIDDEN), low),
            jax.ShapeDtypeStruct((D, 2 * late * HIDDEN), low),
            jax.ShapeDtypeStruct((1, FF), jnp.float32),
            jax.ShapeDtypeStruct((2 * EARLY, 64, SLOT), jnp.float32),
        ],
        scratch_shapes=[
            pltpu.VMEM((D, LEN), low),
            pltpu.VMEM((D, LEN), low),
            pltpu.VMEM((LEN, D), jnp.float32),
            part,
            part,
            pltpu.VMEM((LEN, HIDDEN), low),
            pltpu.VMEM((LEN, HIDDEN), low),
            pltpu.VMEM((2, 2 * EARLY, 4, 2, 2, 64, HIDDEN), low),
            *summing_buffers(2 * EARLY),
            *spread_semaphores(2 * late),
            pltpu.SemaphoreType.DMA((2, 2)),
        ],
        compiler_params=pltpu.CompilerParams(
            collective_id=5, has_side_effects=True, vmem_limit_bytes=62 * 1024 * 1024
        ),
        cost_estimate=pl.CostEstimate(
            flops=12 * LEN * D * FF, bytes_accessed=60 * 1024 * 1024, transcendentals=LEN * FF
        ),
    )(rows, cot, base, last, bias, *split, slots)


SLOTS = 12
SLOT = 512
HALF_SLOT = SLOT // 2
TILE = 256
GRAM_TILES = 5
POLY_TILE = 512
MESH_IDS = pl.DeviceIdType.MESH


def handler_of(slot):
    wide = slot - 4
    square = slot < 4
    dp_index = jnp.where(square, jnp.where(slot < 2, 2, 12), 4 + 6 * (wide // 4) + wide % 2)
    tensor_index = jnp.where(square, slot % 2, (wide // 2) % 2)
    return dp_index, tensor_index


def muon_kernel(
    moments_ref,
    vec_ref,
    block_ref,
    token_ref,
    updates_ref,
    vec_out_ref,
    block_pair_ref,
    token_pair_ref,
    pieces,
    turned,
    vec_pieces,
    vec_sum,
    gram,
    gram_low,
    poly_low,
    half_low,
    chain_low,
    chain_next,
    out_half,
    in_half,
    local_sem,
    send_sem,
    recv_sem,
    half_send,
    half_recv,
    swap_sem,
):
    groups = lax.axis_size("dp")
    parts = lax.axis_size("tensor")
    count = groups * parts
    dp_me = lax.axis_index("dp")
    t_me = lax.axis_index("tensor")
    me = t_me * groups + dp_me
    is_square = (dp_me == 2) | (dp_me == 12)
    is_up = (dp_me == 4) | (dp_me == 5)
    is_down = (dp_me == 10) | (dp_me == 11)
    is_wide = is_up | is_down
    is_handler = is_square | is_wide
    wide_slot = jnp.where(is_up, 4 + (dp_me - 4), 8 + (dp_me - 10)) + 2 * t_me
    slot_me = jnp.where(is_square, t_me + jnp.where(dp_me == 12, 2, 0), wide_slot)
    slot_me = jnp.where(is_handler, slot_me, 0)

    barrier = pltpu.get_barrier_semaphore()

    def greet(step, carry):
        other = lax.rem(me + step, count)
        pl.semaphore_signal(
            barrier, inc=1, device_id=(lax.rem(other, groups), other // groups), device_id_type=MESH_IDS
        )
        return carry

    lax.fori_loop(1, count, greet, 0)
    pl.semaphore_wait(barrier, count - 1)

    def give(step, carry):
        slot = lax.rem(me + step, SLOTS)
        dp_to, t_to = handler_of(slot)
        away = (dp_to != dp_me) | (t_to != t_me)

        @pl.when(away)
        def _():
            pltpu.make_async_remote_copy(
                src_ref=vec_ref.at[slot],
                dst_ref=vec_pieces.at[me],
                send_sem=send_sem.at[1],
                recv_sem=recv_sem.at[1],
                device_id=(dp_to, t_to),
                device_id_type=MESH_IDS,
            ).start()
            pltpu.make_async_remote_copy(
                src_ref=moments_ref.at[slot],
                dst_ref=pieces.at[me],
                send_sem=send_sem.at[0],
                recv_sem=recv_sem.at[0],
                device_id=(dp_to, t_to),
                device_id_type=MESH_IDS,
            ).start()

        return carry

    lax.fori_loop(0, SLOTS, give, 0)

    rows = block_ref.shape[0] // 2
    kept_rows = pl.ds(pl.multiple_of(t_me * rows, rows), rows)
    sent_rows = pl.ds(pl.multiple_of((1 - t_me) * rows, rows), rows)
    kept = []
    swaps = []
    for index, (whole, pair) in enumerate(((block_ref, block_pair_ref), (token_ref, token_pair_ref))):
        kept.append(pltpu.make_async_copy(whole.at[kept_rows], pair.at[t_me], swap_sem.at[2, index]))
        swaps.append(
            pltpu.make_async_remote_copy(
                src_ref=whole.at[sent_rows],
                dst_ref=pair.at[t_me],
                send_sem=swap_sem.at[0, index],
                recv_sem=swap_sem.at[1, index],
                device_id=(dp_me, 1 - t_me),
                device_id_type=MESH_IDS,
            )
        )

    for copy in kept:
        copy.start()

    @pl.when(jnp.logical_not(is_wide))
    def _():
        for copy in swaps:
            copy.start()

    def give_back(source, sem, target):
        def one(step, carry):
            other = lax.rem(me + step, count)
            pltpu.make_async_remote_copy(
                src_ref=source.at[other] if source is turned else source,
                dst_ref=target.at[slot_me],
                send_sem=send_sem.at[sem],
                recv_sem=recv_sem.at[sem],
                device_id=(lax.rem(other, groups), other // groups),
                device_id_type=MESH_IDS,
            ).start()
            return carry

        lax.fori_loop(1, count, one, 0)

    @pl.when(is_handler)
    def _():
        own = [
            pltpu.make_async_copy(vec_ref.at[slot_me], vec_pieces.at[me], local_sem.at[0]),
            pltpu.make_async_copy(moments_ref.at[slot_me], pieces.at[me], local_sem.at[1]),
        ]
        for copy in own:
            copy.start()
        for copy in own:
            copy.wait()
        rest = pl.ds(0, count - 1)
        pltpu.make_async_copy(vec_pieces.at[rest], vec_pieces.at[rest], recv_sem.at[1]).wait()
        vec_sum[...] = jnp.sum(vec_pieces[...], axis=0)
        give_back(vec_sum, 2, vec_out_ref)
        own_vec = pltpu.make_async_copy(vec_sum, vec_out_ref.at[slot_me], local_sem.at[0])
        own_vec.start()
        own_vec.wait()
        pltpu.make_async_copy(pieces.at[rest], pieces.at[rest], recv_sem.at[0]).wait()

        rows_of = TILE // 64

        def gram_tile(tile, carry):
            rows = pl.ds(pl.multiple_of(tile * TILE, TILE), TILE)
            total = jnp.zeros((TILE, D), jnp.float32)
            for part in range(parts):
                left = pieces[pl.ds(part * groups + tile * rows_of, rows_of)].reshape(TILE, SLOT)
                right = pieces[part * groups : (part + 1) * groups].reshape(D, SLOT)
                total += lax.dot_general(
                    left, right, (((1,), (1,)), ((), ())), preferred_element_type=jnp.float32
                )
            gram[rows, :] = total
            return carry

        lax.fori_loop(0, D // TILE, gram_tile, 0)

        @pl.when(is_wide)
        def _():
            core = lax.rem(dp_me, 2)
            sibling = (dp_me + 1 - 2 * core, t_me)
            across = (dp_me, 1 - t_me)

            def tile_at(index, owner):
                if index == 4:
                    row, col = jnp.where(owner == 0, 3, 2), 3
                elif index == 3:
                    row, col = jnp.where(owner == 0, 0, 2), jnp.where(owner == 0, 3, 2)
                else:
                    row, col = owner, owner + index
                return (
                    pl.ds(pl.multiple_of(row * TILE, TILE), TILE),
                    pl.ds(pl.multiple_of(col * TILE, TILE), TILE),
                )

            def exchange(stage, index, place):
                return pltpu.make_async_remote_copy(
                    src_ref=out_half.at[stage, index],
                    dst_ref=in_half.at[stage, index],
                    send_sem=half_send.at[stage, index],
                    recv_sem=half_recv.at[stage, index],
                    device_id=place,
                    device_id_type=MESH_IDS,
                )

            for index in range(GRAM_TILES):
                out_half[0, index] = gram[tile_at(index, 1 - core)].astype(jnp.bfloat16)
                exchange(0, index, sibling).start()
            for index in range(GRAM_TILES):
                exchange(0, index, sibling).wait_recv()
                total = gram[tile_at(index, core)] + in_half[0, index].astype(jnp.float32)
                out_half[1, index] = total.astype(jnp.bfloat16)
                exchange(1, index, across).start()
            for index in range(GRAM_TILES):
                exchange(1, index, across).wait_recv()
                total = out_half[1, index].astype(jnp.float32) + in_half[1, index].astype(jnp.float32)
                out_half[2, index] = total.astype(jnp.bfloat16)
                exchange(2, index, sibling).start()
                rows, cols = tile_at(index, core)
                gram[cols, rows] = out_half[2, index].astype(jnp.float32).T
                gram[rows, cols] = out_half[2, index].astype(jnp.float32)
            for index in range(GRAM_TILES):
                exchange(2, index, sibling).wait_recv()
                rows, cols = tile_at(index, 1 - core)
                gram[cols, rows] = in_half[2, index].astype(jnp.float32).T
                gram[rows, cols] = in_half[2, index].astype(jnp.float32)
            for index in range(GRAM_TILES):
                exchange(0, index, sibling).wait_send()
                exchange(1, index, across).wait_send()
                exchange(2, index, sibling).wait_send()
            for copy in swaps:
                copy.start()

        def trace_tile(tile, total):
            rows = pl.ds(pl.multiple_of(tile * TILE, TILE), TILE)
            row_ids = lax.broadcasted_iota(jnp.int32, (TILE, D), 0) + tile * TILE
            col_ids = lax.broadcasted_iota(jnp.int32, (TILE, D), 1)
            diagonal = jnp.where(row_ids == col_ids, gram[rows, :], 0.0)
            return total + jnp.sum(jnp.sum(diagonal, axis=0, keepdims=True), axis=1, keepdims=True)

        square_total = lax.fori_loop(0, D // TILE, trace_tile, jnp.zeros((1, 1), jnp.float32))
        factor = lax.rsqrt(square_total + SQUARE_EPSILON)
        gram_low[...] = (gram[...] * (factor * factor)).astype(jnp.bfloat16)

        first, second, third = SCHULZ_FIRST, SCHULZ_SECOND, SCHULZ_THIRD

        def tiles(body):
            def one(tile, carry):
                body(pl.ds(pl.multiple_of(tile * POLY_TILE, POLY_TILE), POLY_TILE))
                return carry

            lax.fori_loop(0, D // POLY_TILE, one, 0)

        chain = chain_low
        other = chain_next
        for sweep in range(NS_ITERS):
            target = chain if sweep == 0 else poly_low

            def poly(rows):
                square = mul(gram_low[rows, :], gram_low[...])
                grown = (second / first) * gram_low[rows, :].astype(jnp.float32) + (third / first) * square
                target[rows, :] = grown.astype(jnp.bfloat16)

            tiles(poly)
            if sweep > 0:

                def join(rows, chain=chain, other=other):
                    total = chain[rows, :].astype(jnp.float32) + poly_low[rows, :].astype(jnp.float32)
                    other[rows, :] = (total + mul(chain[rows, :], poly_low[...])).astype(jnp.bfloat16)

                tiles(join)
                chain, other = other, chain
            if sweep < NS_ITERS - 1:

                def half(rows):
                    grown = gram_low[rows, :].astype(jnp.float32) + mul(gram_low[rows, :], target[...])
                    half_low[rows, :] = grown.astype(jnp.bfloat16)

                def full(rows):
                    grown = half_low[rows, :].astype(jnp.float32) + mul(half_low[rows, :], target[...])
                    gram_low[rows, :] = (grown * (first * first)).astype(jnp.bfloat16)

                tiles(half)
                tiles(full)

        scale = factor * (first**NS_ITERS)

        def turn_tile(tile, carry):
            rows = pl.ds(pl.multiple_of(tile * TILE, TILE), TILE)
            for part in range(parts):
                at = pl.ds(part * groups + tile * rows_of, rows_of)
                whole = pieces[part * groups : (part + 1) * groups].reshape(D, SLOT)
                kept = pieces[at].reshape(TILE, SLOT).astype(jnp.float32)
                fresh = (kept + mul(chain[rows, :], whole)) * scale
                turned[at] = fresh.astype(jnp.bfloat16).reshape(rows_of, 64, SLOT)
            return carry

        lax.fori_loop(0, D // TILE, turn_tile, 0)
        give_back(turned, 3, updates_ref)
        own_turned = pltpu.make_async_copy(turned.at[me], updates_ref.at[slot_me], local_sem.at[1])
        own_turned.start()
        own_turned.wait()

    def finish(length):
        here = pl.ds(0, length)
        pltpu.make_async_copy(vec_ref.at[here], vec_ref.at[here], send_sem.at[1]).wait()
        pltpu.make_async_copy(moments_ref.at[here], moments_ref.at[here], send_sem.at[0]).wait()
        pltpu.make_async_copy(vec_out_ref.at[here], vec_out_ref.at[here], recv_sem.at[2]).wait()
        pltpu.make_async_copy(updates_ref.at[here], updates_ref.at[here], recv_sem.at[3]).wait()

    @pl.when(is_handler)
    def _():
        finish(SLOTS - 1)
        rest = pl.ds(0, count - 1)
        pltpu.make_async_copy(vec_pieces.at[rest], vec_pieces.at[rest], send_sem.at[2]).wait()
        pltpu.make_async_copy(turned.at[rest], turned.at[rest], send_sem.at[3]).wait()

    @pl.when(jnp.logical_not(is_handler))
    def _():
        finish(SLOTS)

    for copy in kept + swaps:
        copy.wait()


def muon_call(moments, vec_parts, block_rows, token_grads):
    count = lax.axis_size("dp") * lax.axis_size("tensor")
    rows = moments.shape[1]
    vmem = pl.BlockSpec(memory_space=pltpu.VMEM)
    anywhere = pl.BlockSpec(memory_space=pl.ANY)
    pair = jax.ShapeDtypeStruct((2, LEN // 2, D), jnp.bfloat16)
    low = pltpu.VMEM((D, D), jnp.bfloat16)
    return pl.pallas_call(
        muon_kernel,
        in_specs=[vmem, vmem, anywhere, anywhere],
        out_specs=[vmem, vmem, anywhere, anywhere],
        out_shape=[
            jax.ShapeDtypeStruct(moments.shape, jnp.bfloat16),
            jax.ShapeDtypeStruct(vec_parts.shape, jnp.float32),
            pair,
            pair,
        ],
        scratch_shapes=[
            pltpu.VMEM((count, rows, SLOT), jnp.bfloat16),
            pltpu.VMEM((count, rows, SLOT), jnp.bfloat16),
            pltpu.VMEM((count,) + vec_parts.shape[1:], jnp.float32),
            pltpu.VMEM(vec_parts.shape[1:], jnp.float32),
            pltpu.VMEM((D, D), jnp.float32),
            low,
            low,
            low,
            low,
            low,
            pltpu.VMEM((3, GRAM_TILES, TILE, TILE), jnp.bfloat16),
            pltpu.VMEM((3, GRAM_TILES, TILE, TILE), jnp.bfloat16),
            pltpu.SemaphoreType.DMA((2,)),
            pltpu.SemaphoreType.DMA((4,)),
            pltpu.SemaphoreType.DMA((4,)),
            pltpu.SemaphoreType.DMA((3, GRAM_TILES)),
            pltpu.SemaphoreType.DMA((3, GRAM_TILES)),
            pltpu.SemaphoreType.DMA((3, 2)),
        ],
        compiler_params=pltpu.CompilerParams(
            collective_id=1, has_side_effects=True, vmem_limit_bytes=VMEM_LIMIT
        ),
        cost_estimate=pl.CostEstimate(flops=12 * 2 * D**3, bytes_accessed=4 * 1024 * 1024, transcendentals=0),
    )(moments, vec_parts, block_rows, token_grads)


def neighbours():
    dp_me = lax.axis_index("dp")
    y = lax.axis_index("tensor")
    core = lax.rem(dp_me, 2)
    x = lax.rem(dp_me // 2, 2)
    z = dp_me // 4
    sibling = (dp_me + 1 - 2 * core, y)
    beside = (dp_me + 2 - 4 * x, y)
    across = (dp_me, 1 - y)
    stations = [(lax.rem(dp_me + 4 * hop, 16), y) for hop in (1, 2, 3)]
    return (z, x, core, y), sibling, beside, across, stations


def greet_neighbours(places):
    barrier = pltpu.get_barrier_semaphore()
    for place in places:
        pl.semaphore_signal(barrier, inc=1, device_id=place, device_id_type=MESH_IDS)
    pl.semaphore_wait(barrier, len(places))


EARLY = 2
AHEAD = 2


class Spread:
    def __init__(self, slots_ref, table, local_sem, send_sem, recv_sem):
        self.slots_ref, self.table = slots_ref, table
        self.local_sem, self.send_sem, self.recv_sem = local_sem, send_sem, recv_sem
        (self.z, self.x, self.core, self.y), self.sibling, self.beside, self.across, self.stations = neighbours()

    def remote(self, source, target, stage, slot, place):
        return pltpu.make_async_remote_copy(
            src_ref=source,
            dst_ref=target,
            send_sem=self.send_sem.at[stage, slot],
            recv_sem=self.recv_sem.at[stage, slot],
            device_id=place,
            device_id_type=MESH_IDS,
        )

    def own(self, slot):
        here = self.table[slot][0](self.y, 0, SLOT).at[self.z, self.x, self.core]
        return pltpu.make_async_copy(self.slots_ref.at[slot], here, self.local_sem.at[slot])

    def along_z(self, slot):
        here = self.table[slot][0](self.y, 0, SLOT).at[self.z, self.x, self.core]
        return [
            self.remote(self.slots_ref.at[slot], here, hop, slot, place)
            for hop, place in enumerate(self.stations)
        ]

    def second(self, slot):
        view, size = self.table[slot]
        copies = []
        if size:
            part = view(self.y, 0, size).at[:, self.x, self.core]
            copies.append(self.remote(part, part, 3, slot, self.beside))
        if size < SLOT:
            part = view(self.y, size, SLOT - size).at[:, self.x, self.core]
            copies.append(self.remote(part, part, 4, slot, self.across))
        return copies

    def third(self, slot):
        view, size = self.table[slot]
        copies = []
        if size:
            part = view(self.y, 0, size).at[:, :, self.core]
            copies.append(self.remote(part, part, 5, slot, self.across))
        if size < SLOT:
            for index in (0, 1):
                part = view(index, size, SLOT - size).at[:, self.x, self.core]
                copies.append(self.remote(part, part, 6 + index, slot, self.beside))
        return copies

    def fourth(self, slot):
        view, _ = self.table[slot]
        copies = []
        for index in (0, 1):
            part = view(index, 0, SLOT).at[:, :, self.core]
            copies.append(self.remote(part, part, 8 + index, slot, self.sibling))
        return copies

    def launch(self, slot):
        if slot < len(self.table):
            self.own(slot).start()
            for copy in self.along_z(slot):
                copy.start()

    def begin(self):
        for slot in range(AHEAD):
            self.launch(slot)

    def push_second(self, slot):
        self.own(slot).wait()
        for copy in self.along_z(slot):
            copy.wait_recv()
        for copy in self.second(slot):
            copy.start()

    def push_third(self, slot):
        for copy in self.second(slot):
            copy.wait_recv()
        for copy in self.third(slot):
            copy.start()

    def push_fourth(self, slot):
        for copy in self.third(slot):
            copy.wait_recv()
        for copy in self.fourth(slot):
            copy.start()

    def tick(self, index):
        count = len(self.table)
        self.launch(index + AHEAD)
        if index < count:
            self.push_second(index)
        if 0 <= index - 1 < count:
            self.push_third(index - 1)
        if 0 <= index - 2 < count:
            self.push_fourth(index - 2)

    def ticks(self):
        return len(self.table) + 2

    def arrived(self, slot):
        for copy in self.fourth(slot):
            copy.wait_recv()

    def sent(self):
        for slot in range(len(self.table)):
            for copy in self.along_z(slot) + self.second(slot) + self.third(slot) + self.fourth(slot):
                copy.wait_send()


def column_view(ref, column, distance):
    def view(part, start, size):
        first = column + part * distance + start
        if not isinstance(part, int):
            first = pl.multiple_of(first, 128)
        return ref.at[:, :, :, :, pl.ds(first, size)]

    return view


def place_view(ref, place):
    def view(part, start, size):
        return ref.at[place + part, :, :, :, :, pl.ds(start, size)]

    return view


def spread_semaphores(count):
    return [
        pltpu.SemaphoreType.DMA((count,)),
        pltpu.SemaphoreType.DMA((10, count)),
        pltpu.SemaphoreType.DMA((10, count)),
    ]


def pair_of(step):
    return (step % 2) * (PAIRS // 2) + step // 2


def fill_slots(w_qkv_ref, w_out_ref, w_up_ref, w_down_ref, slots_ref, later_ref):
    low = jnp.bfloat16
    for pair in range(SLOT // PAIR):
        for part in range(3):
            column = (pair * 3 + part) * PAIR
            source = w_qkv_ref[part, :, pair * PAIR : (pair + 1) * PAIR].astype(low)
            slots_ref[column // SLOT, :, column % SLOT : column % SLOT + PAIR] = source
    slots_ref[3] = w_out_ref[...].astype(low)
    for index in range(4):
        target, place = (slots_ref, 4 + 2 * index) if index < EARLY else (later_ref, 2 * (index - EARLY))
        for kind, ref in enumerate((w_up_ref, w_down_ref)):
            target[place + kind] = ref[:, index * SLOT : (index + 1) * SLOT].astype(low)


def attend_spread_kernel(
    starts_ref,
    slopes_ref,
    norm_ref,
    middle_rows_ref,
    shifts_ref,
    w_qkv_ref,
    w_out_ref,
    w_up_ref,
    w_down_ref,
    tokens_ref,
    cotangent_ref,
    packed_ref,
    ctx_ref,
    exps_ref,
    stat_ref,
    normed_t_ref,
    rows_ref,
    middle_ref,
    normed_two_ref,
    later_ref,
    qkv_ref,
    out_ref,
    up_ref,
    down_ref,
    cot_ref,
    slots_ref,
    dist_ref,
    ctx_t,
    ctx_all,
    out_weights,
    rows,
    normed,
    weights,
    local_sem,
    send_sem,
    recv_sem,
    swap_sem,
    load_sem,
):
    step = pl.program_id(0)
    pair = pair_of(step)
    table = [(column_view(qkv_ref, index * SLOT, 3 * SLOT), SLOT if index == 1 else 0) for index in range(3)]
    table += [(column_view(out_ref, 0, SLOT), 0)]
    for index in range(EARLY):
        for ref, over_x in ((up_ref, HALF_SLOT if index else 0), (down_ref, HALF_SLOT if index else 0)):
            table += [(column_view(ref, index * SLOT, EARLY * SLOT), over_x)]
    count = len(table)
    spread = Spread(slots_ref, table, local_sem, send_sem, recv_sem)
    half_rows = pl.ds(pl.multiple_of(spread.y * (LEN // 2), LEN // 2), LEN // 2)
    own_rows = pltpu.make_async_copy(tokens_ref.at[spread.y], rows.at[half_rows], load_sem.at[2])

    def swap(source, target, index):
        return pltpu.make_async_remote_copy(
            src_ref=source.at[1 - spread.y],
            dst_ref=target,
            send_sem=swap_sem.at[0, index],
            recv_sem=swap_sem.at[1, index],
            device_id=spread.across,
            device_id_type=MESH_IDS,
        )

    token_swap = swap(tokens_ref, rows.at[half_rows], 0)
    cotangent_swap = swap(cotangent_ref, cot_ref.at[half_rows], 1)
    own_cotangent = pltpu.make_async_copy(cotangent_ref.at[spread.y], cot_ref.at[half_rows], load_sem.at[3])
    out_load = pltpu.make_async_copy(out_ref, out_weights, load_sem.at[4])

    def load(at):
        cols = pl.ds(pl.multiple_of(pair_of(at) * (3 * PAIR), PAIR), 3 * PAIR)
        place = lax.rem(at, 2)
        return pltpu.make_async_copy(qkv_ref.at[:, :, :, :, cols], weights.at[place], load_sem.at[place])

    @pl.when(step == 0)
    def _():
        fill_slots(w_qkv_ref, w_out_ref, w_up_ref, w_down_ref, slots_ref, later_ref)
        greet_neighbours([spread.sibling, spread.beside, spread.across] + spread.stations)
        own_rows.start()
        for slot in range(3):
            spread.launch(slot)
        spread.push_second(0)
        token_swap.start()
        spread.push_second(1)
        spread.push_third(0)
        spread.push_second(2)
        for slot in range(3, count):
            spread.launch(slot)
        layout_grid(starts_ref, dist_ref)
        spread.push_fourth(0)
        own_rows.wait()
        token_swap.wait_recv()
        spread.push_third(1)
        for index in range(LEN // CHUNK):
            here = slice(index * CHUNK, index * CHUNK + CHUNK)
            block = rows[here].astype(jnp.float32)
            low = layer_norm(block, norm_ref[0:1], norm_ref[1:2]).astype(jnp.bfloat16)
            normed[here] = low
            normed_t_ref[:, here] = low.T
            rows_ref[here] = rows[here]
        own_cotangent.start()

    for slot in range(3):

        @pl.when(step == 2 * slot)
        def _(slot=slot):
            spread.arrived(slot)

    @pl.when(lax.rem(step, 2) == 0)
    def _():
        load(step).start()

    load(step).wait()

    def between():
        @pl.when(lax.rem(step, 2) == 0)
        def _():
            load(step + 1).start()

        moves = (
            ((), (), 3),
            ((1,), (2,), 4),
            ((), (3,), 5),
            ((2,), (4,), 6),
            ((3,), (5,), 7),
            ((4,), (6,), None),
            ((5,), (7,), None),
            ((6,), (), None),
        )
        for index, (fourth, third, fresh) in enumerate(moves):

            @pl.when(step == index)
            def _(index=index, fourth=fourth, third=third, fresh=fresh):
                for slot in fourth:
                    spread.push_fourth(slot)
                for slot in third:
                    spread.push_third(slot)
                if fresh is not None:
                    spread.push_second(fresh)
                if fresh == count - 1:
                    cotangent_swap.start()

    packed = mul(normed[...], weights[lax.rem(step, 2)].reshape(D, 3 * PAIR)) + shifts_ref[...]
    packed = packed.astype(jnp.bfloat16)
    packed_ref[...] = packed
    @pl.when(step == PAIRS - 1)
    def _():
        spread.arrived(3)
        out_load.start()

    attend_pair(pair, slopes_ref, packed, dist_ref, ctx_ref, exps_ref, stat_ref, ctx_t, between)
    ctx_all[:, pl.ds(pl.multiple_of(pair * PAIR, PAIR), PAIR)] = ctx_ref[...]

    @pl.when(step == PAIRS - 1)
    def _():
        out_load.wait()
        for index in range(LEN // CHUNK):
            here = slice(index * CHUNK, index * CHUNK + CHUNK)
            attended = dot_last(ctx_all[here], out_weights[...].reshape(D, D))
            middle = rows[here].astype(jnp.float32) + attended + middle_rows_ref[0:1]
            middle_ref[here] = middle
            normed_two = layer_norm(middle, middle_rows_ref[1:2], middle_rows_ref[2:3])
            normed_two_ref[here] = normed_two.astype(jnp.bfloat16)
            if index == LEN // CHUNK // 2 - 1:
                spread.push_fourth(count - 1)
        for slot in range(4, count):
            spread.arrived(slot)
        spread.sent()
        token_swap.wait_send()
        cotangent_swap.wait()
        own_cotangent.wait()


def whole_shape(columns):
    return jax.ShapeDtypeStruct((4, 2, 2, 64, columns), jnp.bfloat16)


def attend_spread(starts, slopes, norm_rows, middle_rows, shifts, weights, tokens, cotangent):
    anywhere = pl.BlockSpec(memory_space=pl.ANY)
    once = pl.Buffered(1)
    whole = pl.BlockSpec((LEN, D), lambda s: (0, 0), pipeline_mode=once)
    low = jnp.bfloat16
    later = (2 * (4 - EARLY), 64, SLOT)
    *local, qkv, out, up, down, cotangent_rows = pl.pallas_call(
        attend_spread_kernel,
        grid=(PAIRS,),
        in_specs=[
            SCALARS,
            SCALARS,
            pl.BlockSpec((2, D), lambda s: (0, 0)),
            pl.BlockSpec((3, D), lambda s: (0, 0)),
            pl.BlockSpec((1, 3 * PAIR), lambda s: (0, pair_of(s))),
            pl.BlockSpec(weights[0].shape, lambda s: (0, 0, 0), pipeline_mode=once),
        ]
        + [pl.BlockSpec(weight.shape, lambda s: (0, 0), pipeline_mode=once) for weight in weights[1:]]
        + [anywhere] * 2,
        out_specs=[
            pl.BlockSpec((LEN, 3 * PAIR), lambda s: (0, pair_of(s))),
            pl.BlockSpec((LEN, PAIR), lambda s: (0, pair_of(s))),
            pl.BlockSpec((2, LEN, LEN), lambda s: (pair_of(s), 0, 0)),
            pl.BlockSpec((1, 2, LEN), lambda s: (pair_of(s), 0, 0)),
            whole,
            whole,
            whole,
            whole,
            pl.BlockSpec(later, lambda s: (0, 0, 0), pipeline_mode=once),
        ]
        + [anywhere] * 5,
        out_shape=[
            jax.ShapeDtypeStruct((LEN, 3 * D), low),
            jax.ShapeDtypeStruct((LEN, D), low),
            jax.ShapeDtypeStruct((H, LEN, LEN), low),
            jax.ShapeDtypeStruct((PAIRS, 2, LEN), jnp.float32),
            jax.ShapeDtypeStruct((D, LEN), low),
            jax.ShapeDtypeStruct((LEN, D), low),
            jax.ShapeDtypeStruct((LEN, D), jnp.float32),
            jax.ShapeDtypeStruct((LEN, D), low),
            jax.ShapeDtypeStruct(later, low),
            whole_shape(3 * D),
            whole_shape(D),
            whole_shape(2 * EARLY * SLOT),
            whole_shape(2 * EARLY * SLOT),
            jax.ShapeDtypeStruct((LEN, D), low),
        ],
        scratch_shapes=[
            pltpu.VMEM((4 + 2 * EARLY, 64, SLOT), low),
            pltpu.VMEM((LEN, LEN), jnp.float32),
            pltpu.VMEM((PAIR, LEN), jnp.float32),
            pltpu.VMEM((LEN, D), low),
            pltpu.VMEM((4, 2, 2, 64, D), low),
            pltpu.VMEM((LEN, D), low),
            pltpu.VMEM((LEN, D), low),
            pltpu.VMEM((2, 4, 2, 2, 64, 3 * PAIR), low),
        ]
        + spread_semaphores(4 + 2 * EARLY)
        + [pltpu.SemaphoreType.DMA((2, 2)), pltpu.SemaphoreType.DMA((5,))],
        compiler_params=pltpu.CompilerParams(
            collective_id=4, has_side_effects=True, vmem_limit_bytes=VMEM_LIMIT
        ),
        cost_estimate=pl.CostEstimate(
            flops=22 * LEN * LEN * D, bytes_accessed=90 * 1024 * 1024, transcendentals=H * LEN * LEN
        ),
    )(starts, slopes, norm_rows, middle_rows, shifts, *weights, tokens, cotangent)
    wholes = [whole.reshape(D, -1) for whole in (qkv, out, up, down)]
    return *local, wholes, cotangent_rows


class Summing:
    def __init__(self, sources, add_own, buffers, total_ref, sems, lag, ready=0, hold=0):
        self.sources, self.add_own, self.total_ref, self.lag = sources, add_own, total_ref, lag
        self.ready, self.hold = ready, hold
        self.first, self.second_y, self.second_x, self.third, self.fourth = buffers
        self.send_sem, self.recv_sem = sems
        (self.z, self.x, self.core, self.y), self.sibling, self.beside, self.across, self.stations = neighbours()
        self.low_cols = pl.ds(0, HALF_SLOT)
        self.high_cols = pl.ds(HALF_SLOT, HALF_SLOT)

    def count(self):
        return len(self.sources)

    def remote(self, source, target, stage, slot, place):
        return pltpu.make_async_remote_copy(
            src_ref=source,
            dst_ref=target,
            send_sem=self.send_sem.at[stage, slot],
            recv_sem=self.recv_sem.at[stage, slot],
            device_id=place,
            device_id_type=MESH_IDS,
        )

    def landed(self, ref, stage, slot):
        pltpu.make_async_copy(ref, ref, self.recv_sem.at[stage, slot]).wait()

    def send_first(self, slot):
        for part in (0, 1):
            source = self.sources[slot](part).at[:, :, 1 - self.core]
            self.remote(source, self.first.at[slot, part], 0, slot, self.sibling).start()

    def second_copies(self, slot):
        for_y = self.first.at[slot, 1 - self.y, :, :, :, self.low_cols]
        for_x = self.first.at[slot, :, :, 1 - self.x, :, self.high_cols]
        return (
            self.remote(for_y, self.second_y.at[slot], 1, slot, self.across),
            self.remote(for_x, self.second_x.at[slot], 2, slot, self.beside),
        )

    def third_copies(self, slot):
        for_x = self.second_y.at[slot, :, 1 - self.x]
        for_y = self.second_x.at[slot, 1 - self.y]
        return (
            self.remote(for_x, self.third.at[slot, :, :, self.low_cols], 3, slot, self.beside),
            self.remote(for_y, self.third.at[slot, :, :, self.high_cols], 4, slot, self.across),
        )

    def fourth_copies(self, slot):
        return tuple(
            self.remote(
                self.third.at[slot, lax.rem(self.z + hop, 4)], self.fourth.at[slot, hop - 1], 4 + hop, slot, place
            )
            for hop, place in zip((1, 2, 3), self.stations)
        )

    def stage_one(self, slot):
        self.landed(self.first.at[slot], 0, slot)
        self.add_own(slot)
        for copy in self.second_copies(slot):
            copy.start()

    def stage_two(self, slot):
        first, second_y, second_x = self.first, self.second_y, self.second_x
        self.landed(second_y.at[slot], 1, slot)
        second_y[slot] = second_y[slot] + first[slot, self.y, :, :, :, :HALF_SLOT]
        self.landed(second_x.at[slot], 2, slot)
        second_x[slot] = second_x[slot] + first[slot, :, :, self.x, :, HALF_SLOT:]
        for copy in self.third_copies(slot):
            copy.start()

    def stage_three(self, slot):
        third = self.third
        self.landed(third.at[slot, :, :, self.low_cols], 3, slot)
        self.landed(third.at[slot, :, :, self.high_cols], 4, slot)
        third[slot, :, :, :HALF_SLOT] = third[slot, :, :, :HALF_SLOT] + self.second_y[slot, :, self.x]
        third[slot, :, :, HALF_SLOT:] = third[slot, :, :, HALF_SLOT:] + self.second_x[slot, self.y]
        for copy in self.fourth_copies(slot):
            copy.start()

    def stage_four(self, slot):
        total = self.third[slot, self.z].astype(jnp.float32)
        for hop in (1, 2, 3):
            self.landed(self.fourth.at[slot, hop - 1], 4 + hop, slot)
            total = total + self.fourth[slot, hop - 1].astype(jnp.float32)
        self.total_ref[slot] = total

    def ticks(self):
        return self.count() + self.hold + 3 * self.lag

    def tick(self, index):
        for slot in range(self.count()):
            entry = slot + (self.hold if slot >= self.ready else 0)
            pl.when(index == entry)(lambda slot=slot: self.stage_one(slot))
        for number, stage in enumerate((self.stage_two, self.stage_three, self.stage_four)):
            entry = index - (number + 1) * self.lag
            slot = jnp.where(entry < self.ready, entry, entry - self.hold)
            late = (entry >= self.ready + self.hold) & (slot < self.count())
            early = (entry >= 0) & (entry < self.ready)
            pl.when(early | late)(lambda stage=stage, slot=slot: stage(slot))

    def sent(self):
        def one(slot, carry):
            pltpu.make_async_copy(self.first.at[slot], self.first.at[slot], self.send_sem.at[0, slot]).wait()
            for copy in self.second_copies(slot) + self.third_copies(slot) + self.fourth_copies(slot):
                copy.wait_send()
            return carry

        lax.fori_loop(0, self.count(), one, 0)


def summing_buffers(count):
    rows, low = 64, jnp.bfloat16
    return [
        pltpu.VMEM((count, 2, 4, 2, rows, SLOT), low),
        pltpu.VMEM((count, 4, 2, rows, HALF_SLOT), low),
        pltpu.VMEM((count, 2, 4, rows, HALF_SLOT), low),
        pltpu.VMEM((count, 4, rows, SLOT), low),
        pltpu.VMEM((count, 3, rows, SLOT), low),
        pltpu.SemaphoreType.DMA((8, count)),
        pltpu.SemaphoreType.DMA((8, count)),
    ]


LAG = 2
READY = 5
LATE_SLOTS = 8
RING = 4


def block_view(ref, column):
    return ref.at[:, :, :, :, pl.ds(column, SLOT)]


def attend_bwd_half(half, scale, values, keys_t, parts, exps, sums):
    half_t, half_rows, half_queries, inner = parts
    dq_t, dk_sum, dv_sum = sums
    heads = slice(half * HD, half * HD + HD)
    for block in range(LEN // QB):
        span = min(LEN, QB * block + QB + PIECE)
        cols = slice(block * QB, block * QB + QB)
        weights = exps[:span, cols]
        grad_probs = mul(values[:span], half_t[:, cols])
        grad_scores = (weights.astype(jnp.float32) * (grad_probs - inner[:, cols])).astype(jnp.bfloat16)
        dv_sum[:span, :] += mul(weights, half_rows[cols])
        dk_sum[:span, :] += mul(grad_scores, half_queries[cols])
        dq_t[heads, cols] = mul(keys_t[heads, :span], grad_scores) * scale


def attend_sum_kernel(
    packed_ref,
    ctx_ref,
    grad_ref,
    stat_ref,
    weights_ref,
    normed_t_ref,
    rows_ref,
    grad_middle_ref,
    gain_ref,
    exps_ref,
    up_ref,
    down_ref,
    out_ref,
    total_ref,
    token_grad_ref,
    sums_ref,
    packed_sum_ref,
    grad_normed,
    exps,
    dq_t,
    dk_sum,
    dv_sum,
    grad_qkv,
    mine,
    first,
    second_y,
    second_x,
    third,
    fourth,
    send_sem,
    recv_sem,
    exps_sem,
    load_sem,
):
    pair = pl.program_id(0)
    width = up_ref.shape[-1] // 2
    sources = []
    for index in range(width // SLOT):
        for ref in (up_ref, down_ref):
            sources.append(lambda part, ref=ref, index=index: block_view(ref, part * width + index * SLOT))
    sources.append(lambda part: block_view(out_ref, part * SLOT))
    for index in range(3):
        sources.append(lambda part, index=index: block_view(grad_qkv, (part * 3 + index) * SLOT))

    def load(slot, part):
        block = sources[slot](part).at[:, :, summing.core]
        return pltpu.make_async_copy(block, mine.at[slot % RING, part], load_sem.at[slot % RING])

    def add_own(slot):
        if slot < READY:
            place = slot % RING
            pltpu.make_async_copy(mine.at[place], mine.at[place], load_sem.at[place]).wait()
            first[slot] = first[slot] + mine[place]
            if slot + RING < READY:
                for part in (0, 1):
                    load(slot + RING, part).start()
        else:
            for part in (0, 1):
                cols = pl.ds((part * 3 + slot - READY) * SLOT, SLOT)
                first[slot, part] = first[slot, part] + grad_qkv[:, :, summing.core, :, cols]

    buffers = (first, second_y, second_x, third, fourth)
    summing = Summing(sources, add_own, buffers, total_ref, (send_sem, recv_sem), LAG, READY, 1)

    def exps_load(head, half):
        return pltpu.make_async_copy(exps_ref.at[head], exps.at[half], exps_sem.at[half])

    @pl.when(pair == 0)
    def _():
        for half in (0, 1):
            exps_load(half, half).start()
        for slot in range(RING):
            for part in (0, 1):
                load(slot, part).start()
        greet_neighbours([summing.sibling, summing.beside, summing.across] + summing.stations)
        for slot in range(READY):
            summing.send_first(slot)
        grad_normed[...] = jnp.zeros_like(grad_normed)
        sums_ref[...] = jnp.zeros_like(sums_ref)

    scale = 1.0 / math.sqrt(HD)
    queries = packed_ref[:, :PAIR]
    keys_t = packed_ref[:, PAIR : 2 * PAIR].T
    values = packed_ref[:, 2 * PAIR :]
    grads_t = grad_ref[...].T.astype(jnp.float32)
    context_t = ctx_ref[...].T.astype(jnp.float32)
    scaled = []
    inner_rows = []
    for half in (0, 1):
        heads = slice(half * HD, half * HD + HD)
        scaled.append(grads_t[heads] * stat_ref[0, half : half + 1, :])
        inner_rows.append(jnp.sum(scaled[half] * context_t[heads], axis=0, keepdims=True))
    scaled_t = jnp.concatenate(scaled, axis=0).astype(jnp.bfloat16)
    scaled_rows = scaled_t.T
    dk_sum[...] = jnp.zeros_like(dk_sum)
    dv_sum[...] = jnp.zeros_like(dv_sum)
    for half in (0, 1):
        exps_load(2 * pair + half, half).wait()
        parts = (
            only_rows(scaled_t, half),
            only_cols(scaled_rows, half),
            only_cols(queries, half),
            inner_rows[half],
        )
        attend_bwd_half(half, scale, values, keys_t, parts, exps.at[half], (dq_t, dk_sum, dv_sum))

        @pl.when(pair < PAIRS - 1)
        def _(half=half):
            exps_load(2 * pair + 2 + half, half).start()

        if half == 0:
            summing.tick(pair)
    grads = jnp.concatenate([dq_t[...].T, dk_sum[...] * scale, dv_sum[...]], axis=1).astype(jnp.bfloat16)
    packed_sum_ref[...] = jnp.sum(grads.astype(jnp.float32), axis=0, keepdims=True)
    cols = pl.ds(pl.multiple_of(pair * (3 * PAIR), PAIR), 3 * PAIR)
    grad_weights = mul(normed_t_ref[...], grads).astype(jnp.bfloat16)
    grad_qkv[:, :, :, :, cols] = grad_weights.reshape(4, 2, 2, 64, 3 * PAIR)
    grad_normed[...] += dot_last(grads, weights_ref[...])

    for slot in range(READY, LATE_SLOTS):
        pl.when(pair == PAIRS - LATE_SLOTS + slot)(lambda slot=slot: summing.send_first(slot))

    @pl.when(pair == PAIRS - 1)
    def _():
        def late(index, carry):
            summing.tick(index)
            chunk = index - PAIRS

            @pl.when(chunk < LEN // ROWS)
            def _():
                here = pl.ds(pl.multiple_of(chunk * ROWS, ROWS), ROWS)
                block = rows_ref[here, :].astype(jnp.float32)
                pulled, gain_sum, shift_sum = norm_pull(block, grad_normed[here, :], gain_ref[...])
                token_grad_ref[here, :] = (grad_middle_ref[here, :] + pulled).astype(jnp.bfloat16)
                add_rows(sums_ref, (gain_sum, shift_sum))

            return carry

        lax.fori_loop(PAIRS, summing.ticks(), late, 0)
        summing.sent()


def attend_sum(
    packed, context, grad_context, stats, weights, normed_t, rows_low, grad_middle, gain, exps, grad_up, grad_down, grad_out
):
    anywhere = pl.BlockSpec(memory_space=pl.ANY)
    rows = 64
    low = jnp.bfloat16
    once = pl.Buffered(1)
    tall = pl.BlockSpec((LEN, D), lambda p: (0, 0), pipeline_mode=once)
    split = [grad.reshape(4, 2, 2, rows, grad.shape[-1]) for grad in (grad_up, grad_down, grad_out)]
    return pl.pallas_call(
        attend_sum_kernel,
        grid=(PAIRS,),
        in_specs=[PACKED_COLS, PAIR_COLS, PAIR_COLS, PAIR_STAT, PACKED_COLS, tall, tall, tall]
        + [pl.BlockSpec((1, D), lambda p: (0, 0))]
        + [anywhere] * 4,
        out_specs=[
            pl.BlockSpec((LATE_SLOTS, rows, SLOT), lambda p: (0, 0, 0), pipeline_mode=once),
            tall,
            pl.BlockSpec((8, D), lambda p: (0, 0)),
            pl.BlockSpec((1, 3 * PAIR), lambda p: (0, p)),
        ],
        out_shape=[
            jax.ShapeDtypeStruct((LATE_SLOTS, rows, SLOT), jnp.float32),
            jax.ShapeDtypeStruct((LEN, D), low),
            jax.ShapeDtypeStruct((8, D), jnp.float32),
            jax.ShapeDtypeStruct((1, 3 * D), jnp.float32),
        ],
        scratch_shapes=[
            pltpu.VMEM((LEN, D), jnp.float32),
            pltpu.VMEM((2, LEN, LEN), low),
            pltpu.VMEM((PAIR, LEN), jnp.float32),
            pltpu.VMEM((LEN, PAIR), jnp.float32),
            pltpu.VMEM((LEN, PAIR), jnp.float32),
            pltpu.VMEM((4, 2, 2, rows, 3 * D), low),
            pltpu.VMEM((RING, 2, 4, 2, rows, SLOT), low),
            *summing_buffers(LATE_SLOTS),
            pltpu.SemaphoreType.DMA((2,)),
            pltpu.SemaphoreType.DMA((RING,)),
        ],
        compiler_params=pltpu.CompilerParams(
            collective_id=2, has_side_effects=True, vmem_limit_bytes=62 * 1024 * 1024
        ),
        cost_estimate=pl.CostEstimate(
            flops=44 * LEN * LEN * D, bytes_accessed=400 * 1024 * 1024, transcendentals=0
        ),
    )(packed, context, grad_context, stats, weights, normed_t, rows_low, grad_middle, gain, exps, *split)


ROWS = 256


def norm_pull(rows, grads, gain):
    centered = rows - jnp.mean(rows, axis=-1, keepdims=True)
    inverse = lax.rsqrt(jnp.mean(centered * centered, axis=-1, keepdims=True) + NORM_EPSILON)
    normed = centered * inverse
    scaled = grads * gain
    along = jnp.mean(scaled * normed, axis=-1, keepdims=True)
    pulled = inverse * (scaled - jnp.mean(scaled, axis=-1, keepdims=True) - normed * along)
    gain_sum = jnp.sum(grads * normed, axis=0, keepdims=True)
    return pulled, gain_sum, jnp.sum(grads, axis=0, keepdims=True)


def add_rows(sums_ref, rows):
    for index, row in enumerate(rows):
        sums_ref[index : index + 1, :] += row


def middle_kernel(
    middle_ref, grad_ref, cot_ref, ctx_ref, gain_ref, weights_ref, grad_middle_ref, grad_ctx_ref, grad_out_ref, sums_ref, low_t
):
    step = pl.program_id(0)

    @pl.when(step == 0)
    def _():
        sums_ref[...] = jnp.zeros_like(sums_ref)

    cot = cot_ref[...].astype(jnp.float32)
    pulled, gain_sum, shift_sum = norm_pull(middle_ref[...], grad_ref[...], gain_ref[...])
    grads = cot + pulled
    low = grads.astype(jnp.bfloat16)
    grad_middle_ref[...] = grads
    grad_ctx_ref[...] = mul(low, weights_ref[...]).astype(jnp.bfloat16)
    low_t[:, pl.ds(pl.multiple_of(step * ROWS, ROWS), ROWS)] = low.T
    grad_sum = jnp.sum(grads, axis=0, keepdims=True)
    add_rows(sums_ref, (gain_sum, shift_sum, grad_sum, jnp.sum(cot, axis=0, keepdims=True)))

    @pl.when(step == LEN // ROWS - 1)
    def _():
        grad_out_ref[...] = mul(low_t[...], ctx_ref[...]).astype(jnp.bfloat16)


def middle_backward(middle, grad_rows, cot, context, gain, weights):
    rows = pl.BlockSpec((ROWS, D), lambda s: (s, 0))
    whole = pl.BlockSpec((D, D), lambda s: (0, 0), pipeline_mode=pl.Buffered(1))
    row = pl.BlockSpec((1, D), lambda s: (0, 0))
    sums = pl.BlockSpec((8, D), lambda s: (0, 0))
    return pl.pallas_call(
        middle_kernel,
        grid=(LEN // ROWS,),
        in_specs=[rows, rows, rows, whole, row, whole],
        out_specs=[rows, rows, whole, sums],
        out_shape=[
            jax.ShapeDtypeStruct((LEN, D), jnp.float32),
            jax.ShapeDtypeStruct((LEN, D), jnp.bfloat16),
            jax.ShapeDtypeStruct((D, D), jnp.bfloat16),
            jax.ShapeDtypeStruct((8, D), jnp.float32),
        ],
        scratch_shapes=[pltpu.VMEM((D, LEN), jnp.bfloat16)],
        compiler_params=pltpu.CompilerParams(vmem_limit_bytes=VMEM_LIMIT),
        cost_estimate=pl.CostEstimate(flops=4 * LEN * D * D, bytes_accessed=24 * 1024 * 1024, transcendentals=0),
    )(middle, grad_rows, cot, context, gain, weights)


def slot_rows(early_ref, late_ref, slot):
    index, kind = slot % 4, slot // 4
    if index < EARLY:
        return early_ref[2 * index + kind]
    return late_ref[2 * (index - EARLY) + kind]


def moment_kernel(
    early_ref,
    late_ref,
    m_qkv_ref,
    m_out_ref,
    m_up_ref,
    m_down_ref,
    g_qkv_ref,
    g_out_ref,
    g_up_ref,
    g_down_ref,
    n_qkv_ref,
    n_out_ref,
    n_up_ref,
    n_down_ref,
    slots_ref,
):
    first_packed = LATE_SLOTS - 3
    for pair in range(SLOT // PAIR):
        for part in range(3):
            column = (pair * 3 + part) * PAIR
            source = late_ref[first_packed + column // SLOT, :, column % SLOT : column % SLOT + PAIR]
            g_qkv_ref[part, :, pair * PAIR : (pair + 1) * PAIR] = source
    for part in range(3):
        moment = MOMENTUM_DECAY * m_qkv_ref[part] + g_qkv_ref[part]
        n_qkv_ref[part] = moment
        slots_ref[part] = moment.astype(jnp.bfloat16)
    grads = late_ref[first_packed - 1]
    g_out_ref[...] = grads
    moment = MOMENTUM_DECAY * m_out_ref[...] + grads
    n_out_ref[...] = moment
    slots_ref[3] = moment.astype(jnp.bfloat16)
    for kind, refs in enumerate(((m_up_ref, g_up_ref, n_up_ref), (m_down_ref, g_down_ref, n_down_ref))):
        old_ref, grads_ref, new_ref = refs
        for index in range(4):
            here = slice(index * SLOT, (index + 1) * SLOT)
            grads = slot_rows(early_ref, late_ref, 4 * kind + index)
            grads_ref[:, here] = grads
            moment = MOMENTUM_DECAY * old_ref[:, here] + grads
            new_ref[:, here] = moment
            slots_ref[4 + 4 * kind + index] = moment.astype(jnp.bfloat16)


def update_kernel(
    updates_ref,
    vec_sum_ref,
    w_qkv_ref,
    w_out_ref,
    w_up_ref,
    w_down_ref,
    vectors_ref,
    m_vec_ref,
    o_qkv_ref,
    o_out_ref,
    o_up_ref,
    o_down_ref,
    g_vec_ref,
    n_vec_ref,
    o_vec_ref,
):
    wide_rate = MATRIX_RATE * math.sqrt(FF / D)
    for part in range(3):
        o_qkv_ref[part] = w_qkv_ref[part] - MATRIX_RATE * updates_ref[part].astype(jnp.float32)
    o_out_ref[...] = w_out_ref[...] - MATRIX_RATE * updates_ref[3].astype(jnp.float32)
    for index in range(4):
        here = slice(index * SLOT, (index + 1) * SLOT)
        o_up_ref[:, here] = w_up_ref[:, here] - wide_rate * updates_ref[4 + index].astype(jnp.float32)
        o_down_ref[:, here] = w_down_ref[:, here] - wide_rate * updates_ref[8 + index].astype(jnp.float32)
    grads = vec_sum_ref[...]
    moment = MOMENTUM_DECAY * m_vec_ref[...] + grads
    square = jnp.mean(moment * moment, axis=1, keepdims=True)
    g_vec_ref[...] = grads
    n_vec_ref[...] = moment
    o_vec_ref[...] = vectors_ref[...] - VECTOR_RATE * moment * lax.rsqrt(square + SQUARE_EPSILON)


def like(arrays):
    return [jax.ShapeDtypeStruct(array.shape, jnp.float32) for array in arrays]


def features_first(arrays):
    qkv, out, up, down = arrays
    return qkv, out.T, up, down.T


def muon_step(early, late, vector_total, block_rows, token_grads, weights, vectors, momenta, m_vec):
    limit = pltpu.CompilerParams(vmem_limit_bytes=VMEM_LIMIT)
    weights, momenta = features_first(weights), features_first(momenta)
    slots_shape = jax.ShapeDtypeStruct((SLOTS,) + late.shape[1:], jnp.bfloat16)
    *stored, slots = pl.pallas_call(
        moment_kernel, out_shape=like(momenta) + like(momenta) + [slots_shape], compiler_params=limit
    )(early, late, *momenta)
    updates, vector_rows, output_pair, token_pair = muon_call(
        slots, vector_total.reshape(SLOTS, 8, 128), block_rows, token_grads
    )
    fresh = pl.pallas_call(
        update_kernel, out_shape=like(weights) + like([vectors] * 3), compiler_params=limit
    )(updates, vector_rows.reshape(12, D), *weights, vectors, m_vec)
    vector_grad, moment_vec, new_vec = fresh[4:]
    grads, moments, new = features_first(stored[:4]), features_first(stored[4:]), features_first(fresh[:4])
    return (output_pair, token_pair.astype(jnp.float32), *grads, vector_grad, *moments, moment_vec, *new, new_vec)


def narrow(rows):
    return rows.astype(jnp.bfloat16)


def contract(left, right, left_dim, right_dim):
    return lax.dot_general(
        left, right, (((left_dim,), (right_dim,)), ((), ())), preferred_element_type=jnp.float32
    )


def by_pairs(rows):
    count, height, width = rows.shape
    return jnp.transpose(rows.reshape(count, height, width // PAIR, PAIR), (1, 2, 0, 3)).reshape(height, -1)


def from_pairs(rows):
    height = rows.shape[0]
    return jnp.transpose(rows.reshape(height, -1, 3, PAIR), (2, 0, 1, 3)).reshape(3, height, -1)


def sequence_step(
    tokens,
    cotangent,
    piece_starts,
    w_qkv,
    w_out,
    w_up,
    w_down,
    vectors,
    m_qkv,
    m_out,
    m_up,
    m_down,
    m_vec,
):
    rank = lax.axis_index("tensor")
    slopes = jnp.exp2(-8.0 * jnp.arange(1, H + 1, dtype=jnp.float32) / H)
    starts = lax.dynamic_slice_in_dim(piece_starts[:, 0], rank, 1, 0)[0]
    shifts = by_pairs(jnp.stack([vectors[2], jnp.zeros((D,), jnp.float32), vectors[3]])[:, None])
    weights = (w_qkv, w_out, w_up, w_down)
    packed, context, exps, stats, normed_t, token_low, middle, normed_two, later, wholes, cotangent_low = attend_spread(
        starts, slopes, vectors[0:2], vectors[4:7], shifts, features_first(weights), tokens, cotangent
    )
    full_qkv, full_out, full_up, full_down = wholes
    block_rows, grad_normed_two, grad_up, grad_down, up_bias, early_sums = mlp_both(
        normed_two,
        cotangent_low,
        middle,
        vectors[11:12],
        vectors[7:11].reshape(1, FF),
        full_up,
        full_down,
        later,
    )
    grad_middle, grad_context, grad_out, middle_sums = middle_backward(
        middle, grad_normed_two, cotangent_low, context, vectors[5:6], full_out
    )
    sums, grad_token_low, token_sums, packed_grads = attend_sum(
        packed,
        context,
        grad_context,
        stats,
        full_qkv,
        normed_t,
        token_low,
        grad_middle,
        vectors[0:1],
        exps,
        grad_up,
        grad_down,
        grad_out,
    )
    packed_sums = from_pairs(packed_grads)[:, 0]
    vector_total = jnp.concatenate(
        [
            token_sums[0:2],
            packed_sums[0:1],
            packed_sums[2:3],
            middle_sums[2:3],
            middle_sums[0:2],
            up_bias.reshape(4, D),
            middle_sums[3:4],
        ]
    )
    momenta = (m_qkv, m_out, m_up, m_down)
    return muon_step(
        early_sums, sums, vector_total, block_rows, grad_token_low, weights, vectors, momenta, m_vec
    )


def solution(mesh):
    in_specs = (
        P(None, ("dp", "tensor"), None),
        P(None, ("dp", "tensor"), None),
        P(None, "dp", None),
        P(None, "dp", "tensor"),
        P("tensor", "dp"),
        P("dp", "tensor"),
        P("tensor", "dp"),
        P(),
        P(None, "dp", "tensor"),
        P("tensor", "dp"),
        P("dp", "tensor"),
        P("tensor", "dp"),
        P(),
    )
    out_specs = (
        P(None, ("dp", "tensor"), None),
        P(None, ("dp", "tensor"), None),
        P(None, "dp", "tensor"),
        P("tensor", "dp"),
        P("dp", "tensor"),
        P("tensor", "dp"),
        P(),
        P(None, "dp", "tensor"),
        P("tensor", "dp"),
        P("dp", "tensor"),
        P("tensor", "dp"),
        P(),
        P(None, "dp", "tensor"),
        P("tensor", "dp"),
        P("dp", "tensor"),
        P("tensor", "dp"),
        P(),
    )
    groups_fit = mesh.shape["tensor"] == MB and mesh.shape["dp"] == 16

    def pick(*arrays):
        if groups_fit and arrays[2].shape[1] == 1:
            return sequence_step(*arrays)
        return on_device(*arrays)

    return jax.shard_map(
        pick, mesh=mesh, in_specs=in_specs, out_specs=out_specs, check_vma=False
    )
```
